32 devices in a mesh: phase: 2 (over core), dp: 16 (over z, y, x).
Axes of the slice: x: 2, y: 2, z: 4, core: 2. Of those that a mesh axis runs over, the one named last changes fastest.
Arguments:
- char_ids: int32 [2, 16, 4096], P(None, 'dp'), may hold values from 0 to 255
- char_counts: int32 [2, 16, 256], P(None, 'dp'), may hold values from 1 to 16
- segment_ids: int32 [2, 16, 256], P(None, 'dp'), may hold values from 0 to 3, never falling along the last dimension, each value on 1 to 128 neighbouring positions
- out_cotangent: bfloat16 [2, 16, 256, 512], P(None, 'dp'), may hold values from -6 to 6
- char_table: bfloat16 [256, 256], replicated, may hold values from -6 to 6
- char_gain_one: bfloat16 [256], replicated, may hold values from 0.099609375 to 1.8984375
- char_query: bfloat16 [256, 256], replicated, may hold values from -0.375 to 0.375
- char_key: bfloat16 [256, 256], replicated, may hold values from -0.375 to 0.375
- char_value: bfloat16 [256, 256], replicated, may hold values from -0.375 to 0.375
- char_output: bfloat16 [256, 256], replicated, may hold values from -1 to 1
- char_gain_two: bfloat16 [256], replicated, may hold values from 0.099609375 to 1.8984375
- char_up: bfloat16 [256, 1024], replicated, may hold values from -0.375 to 0.375
- char_down: bfloat16 [1024, 256], replicated, may hold values from -0.25 to 0.25
- char_project: bfloat16 [256, 512], replicated, may hold values from -0.375 to 0.375
- word_gain_one: bfloat16 [512], replicated, may hold values from 0.099609375 to 1.8984375
- word_query: bfloat16 [512, 512], replicated, may hold values from -0.25 to 0.25
- word_key: bfloat16 [512, 512], replicated, may hold values from -0.25 to 0.25
- word_value: bfloat16 [512, 512], replicated, may hold values from -0.25 to 0.25
- word_output: bfloat16 [512, 512], replicated, may hold values from -1.5 to 1.5
- word_gain_two: bfloat16 [512], replicated, may hold values from 0.099609375 to 1.8984375
- word_up: bfloat16 [512, 2048], replicated, may hold values from -0.25 to 0.25
- word_down: bfloat16 [2048, 512], replicated, may hold values from -0.1875 to 0.1875
Outputs:
- word_out: bfloat16 [2, 16, 256, 512], P(None, 'dp', None, 'phase')
- gradient_char_table: float32 [256, 256], P('dp', 'phase')
- gradient_char_gain_one: float32 [256], P('dp')
- gradient_char_query: float32 [256, 256], P('dp', 'phase')
- gradient_char_key: float32 [256, 256], P('dp', 'phase')
- gradient_char_value: float32 [256, 256], P('dp', 'phase')
- gradient_char_output: float32 [256, 256], P('dp', 'phase')
- gradient_char_gain_two: float32 [256], P('dp')
- gradient_char_up: float32 [256, 1024], P('dp', 'phase')
- gradient_char_down: float32 [1024, 256], P('dp', 'phase')
- gradient_char_project: float32 [256, 512], P('dp', 'phase')
- gradient_word_gain_one: float32 [512], P('dp')
- gradient_word_query: float32 [512, 512], P('dp', 'phase')
- gradient_word_key: float32 [512, 512], P('dp', 'phase')
- gradient_word_value: float32 [512, 512], P('dp', 'phase')
- gradient_word_output: float32 [512, 512], P('dp', 'phase')
- gradient_word_gain_two: float32 [512], P('dp')
- gradient_word_up: float32 [512, 2048], P('dp', 'phase')
- gradient_word_down: float32 [2048, 512], P('dp', 'phase')
The draws below stay inside these ranges and needn't reach their ends.
Inputs may be any that keep to these rules, and one draw needn't show every extreme that they name: `char_counts`: the number of characters of each word; slots past it are padding. `segment_ids`: segment numbers never fall along a row; each number names 1 to 128 consecutive words, and one names exactly 128.
All inputs are finite; a program needn't handle non-finite values.
Results may differ from the reference program's by a relative error of at most 0.023.
Values may be sent and summed in bfloat16 or wider, within the bound.
No kernel may reach another device: no remote copies, remote signals or barrier semaphores. Data moves between devices by JAX's collectives and lax.ppermute only.
A program may use at most 192 MiB of HBM per device.

```python
import math
import jax
import jax.numpy as jnp
import numpy as np
from jax import lax

HEAD_DIM = 64
CHAR_HEADS = 4
CD = 256
CFF = 1024
CPW = 16
CVOC = 256
WORD_HEADS = 8
WD = 512
WFF = 2048
WORDS = 256
MICRO = 2
ROWS = 16


def plant(entries, stream_key, least, largest):
    longest = entries.shape.index(max(entries.shape))
    spots = []
    for shift in (0, 1):
        where = [jax.random.randint(jax.random.fold_in(stream_key, axis), (), 0, length) for axis, length in enumerate(entries.shape)]
        where[longest] = (where[longest] + shift) % entries.shape[longest]
        spots.append(tuple(where))
    return entries.at[spots[0]].set(least).at[spots[1]].set(largest)


def levels(rng, shape, shards, smallest, high):
    def one(dim, blocks):
        steps = jax.random.uniform(jax.random.fold_in(jax.random.fold_in(rng, 6), dim), (blocks,), jnp.float32, smallest / len(shards), high / len(shards))
        return jnp.repeat(jnp.exp(steps), shape[dim] // blocks).reshape((-1,) + (1,) * (len(shape) - dim - 1))

    gain = one(*shards[0])
    for cut in shards[1:]:
        gain = gain * one(*cut)
    return gain


def rank_bounds(number_of, slope):
    portions = [(1 << 20) // math.isqrt(rank ** slope) + 1 for rank in range(1, number_of + 1)]
    deviation = 1 + sum(portions) // (1 << 30)
    return np.cumsum(np.array([max(1, weight // deviation) for weight in portions]))


def ranked_ids(key, extent, number_of, slope):
    table = rank_bounds(number_of, slope)
    ticket = jax.random.randint(jax.random.fold_in(key, 1), extent, 0, int(table[number_of - 1]))
    rank = jnp.searchsorted(jnp.asarray(table, jnp.int32), ticket, side="right")
    return jax.random.permutation(jax.random.fold_in(key, 2), number_of)[rank].astype(jnp.int32)


def length_profile(count, total, bound, skew):
    weights = [(1 << 20) // math.isqrt(standing ** skew) + 1 for standing in range(2, count + 1)]
    surplus, holding = total - bound - (count - 1), [1] * (count - 1)
    while surplus > 0:
        candidates = [i for i in range(count - 1) if holding[i] < bound]
        mass, left = sum([weights[i] for i in candidates]), surplus
        for i in candidates:
            extra = min(bound - holding[i], max(1, left * weights[i] // mass), surplus)
            holding[i] = holding[i] + extra
            surplus = surplus - extra
    return np.array([bound] + holding)


def ragged_sizes(rng, amount, total, bound, lean):
    if amount == 2:
        one = jax.random.randint(rng, (), max(1, total - bound), min(bound, total - 1) + 1)
        return jnp.stack([one, total - one])
    tallies = jnp.asarray(length_profile(amount, total, bound, lean), jnp.int32)
    twos = (amount - 1) // 2
    giver, taker = tallies[1:1 + 2 * twos:2], tallies[2:2 + 2 * twos:2]
    room = jnp.minimum(giver - 1, bound - taker)
    shifted = jax.random.randint(jax.random.fold_in(rng, 1), (twos,), 0, 1 << 20) % (room + 1)
    tallies = tallies.at[1:1 + 2 * twos:2].set(giver - shifted).at[2:2 + 2 * twos:2].set(taker + shifted)
    return tallies[jax.random.permutation(jax.random.fold_in(rng, 2), amount)]


def noise(rng, extent, spread, bound, pieces=(), kind=jnp.bfloat16):
    values = spread * jax.random.normal(rng, extent, jnp.float32)
    if pieces:
        values = values * levels(rng, extent, pieces, -0.22, 0.18)
    return jnp.clip(values, -bound, bound).astype(kind)


def setup_inputs(seed: int = 0) -> dict:
    key_list = jax.random.split(jax.random.key(seed), 23)
    return {
        "char_ids": plant(ranked_ids(key_list[0], (MICRO, ROWS, WORDS * CPW), CVOC, 2), jax.random.fold_in(key_list[0], 3), 0, CVOC - 1).astype(jnp.int32),
        "char_counts": plant(jax.random.randint(key_list[1], (MICRO, ROWS, WORDS), 1, CPW + 1), jax.random.fold_in(key_list[1], 1), 1, CPW).astype(jnp.int32),
        "segment_ids": jax.vmap(lambda own: jnp.searchsorted(jnp.cumsum(ragged_sizes(own, 4, WORDS, WORDS // 2, 1)), jnp.arange(WORDS), side="right"))(jax.random.split(key_list[2], MICRO * ROWS)).reshape((MICRO, ROWS, WORDS)).astype(jnp.int32),
        "out_cotangent": noise(key_list[3], (MICRO, ROWS, WORDS, WD), 1.0, 6.0, ((1, 16),)),
        "char_table": noise(key_list[4], (CVOC, CD), 1.0, 6.0),
        "char_gain_one": jnp.clip(1.0 + 0.18 * jax.random.normal(key_list[5], (CD,), jnp.float32), 0.099609375, 1.8984375).astype(jnp.bfloat16),
        "char_query": noise(key_list[6], (CD, CD), CD ** -0.5, 0.375),
        "char_key": noise(key_list[7], (CD, CD), CD ** -0.5, 0.375),
        "char_value": noise(key_list[8], (CD, CD), CD ** -0.5, 0.375),
        "char_output": noise(key_list[9], (CD, CD), (CD // 8) ** -0.5, 1.0),
        "char_gain_two": jnp.clip(1.0 + 0.18 * jax.random.normal(key_list[10], (CD,), jnp.float32), 0.099609375, 1.8984375).astype(jnp.bfloat16),
        "char_up": noise(key_list[11], (CD, CFF), CD ** -0.5, 0.375),
        "char_down": noise(key_list[12], (CFF, CD), (CFF // 2) ** -0.5, 0.25),
        "char_project": noise(key_list[13], (CD, WD), CD ** -0.5, 0.375),
        "word_gain_one": jnp.clip(1.0 + 0.18 * jax.random.normal(key_list[14], (WD,), jnp.float32), 0.099609375, 1.8984375).astype(jnp.bfloat16),
        "word_query": noise(key_list[15], (WD, WD), WD ** -0.5, 0.25),
        "word_key": noise(key_list[16], (WD, WD), WD ** -0.5, 0.25),
        "word_value": noise(key_list[17], (WD, WD), WD ** -0.5, 0.25),
        "word_output": noise(key_list[18], (WD, WD), (WD // 32) ** -0.5, 1.5),
        "word_gain_two": jnp.clip(1.0 + 0.18 * jax.random.normal(key_list[19], (WD,), jnp.float32), 0.099609375, 1.8984375).astype(jnp.bfloat16),
        "word_up": noise(key_list[20], (WD, WFF), WD ** -0.5, 0.25),
        "word_down": noise(key_list[21], (WFF, WD), (WFF // 2) ** -0.5, 0.1875),
    }


epsilon = 1e-06
half_root = 0.7071067811865476
floor_score = -1e+30
score_scale = 0.125
char_forms = ('wqhd,wkhd->hqkw', 'hqkw,wkhd->wqhd')
word_forms = ('qhd,khd->hqk', 'hqk,khd->qhd')

@jax.custom_vjp
def low(v):
    return lax.optimization_barrier(v.astype(jnp.bfloat16)).astype(jnp.float32)

@jax.custom_vjp
def low_back(v):
    return v

def low_keep(v):
    return (low(v), None)

def low_pass(kept, grad):
    return (grad,)

def back_keep(v):
    return (v, None)

def back_low(kept, grad):
    return (low(grad),)
low.defvjp(low_keep, low_pass)
low_back.defvjp(back_keep, back_low)

def highest(left, right):
    return jnp.dot(left, right, precision=lax.Precision.HIGHEST)

def rms_norm(values, scaling):
    return values * lax.rsqrt(lax.optimization_barrier(jnp.mean(values * values, axis=-1, keepdims=True)) + epsilon) * scaling

def gelu_value(values):
    return 0.5 * values * (1.0 + jax.scipy.special.erf(values * half_root))

def attention(query_in, key_in, value_in, setup):
    allowed, head_shape, einsum_forms = setup
    query_heads = query_in.reshape(head_shape)
    key_heads = key_in.reshape(head_shape)
    value_heads = value_in.reshape(head_shape)
    raw_scores = low_back(jnp.einsum(einsum_forms[0], query_heads, key_heads, precision=lax.Precision.HIGHEST) * score_scale)
    masked = jnp.where(allowed, raw_scores, floor_score)
    highest_score = lax.optimization_barrier(jnp.max(masked, axis=2, keepdims=True))
    expanded = jnp.exp(masked - highest_score)
    soft_low = low(expanded / lax.optimization_barrier(jnp.sum(expanded, axis=2, keepdims=True)))
    mixed = jnp.einsum(einsum_forms[1], soft_low, value_heads, precision=lax.Precision.HIGHEST)
    return low(low_back(mixed.reshape(query_in.shape)))

def layer(inputs, weights, setup):
    gain_one, w_query, w_key, w_value, w_output, gain_two, w_up, w_down = weights
    normed = low(rms_norm(inputs, gain_one))
    query_low = low(low_back(highest(normed, w_query)))
    key_low = low(low_back(highest(normed, w_key)))
    value_low = low(low_back(highest(normed, w_value)))
    mixed = attention(query_low, key_low, value_low, setup)
    middle = inputs + low_back(highest(mixed, w_output))
    normed_two = low(rms_norm(middle, gain_two))
    before = low_back(highest(normed_two, w_up))
    active = low(gelu_value(before))
    return middle + low_back(highest(active, w_down))

def row_forward(parameters, row):
    identifiers, counts, segments = row
    char_table = parameters[0]
    char_weights = parameters[1:9]
    char_project = parameters[9]
    word_weights = parameters[10:18]
    embedded = char_table[identifiers]
    char_allowed = (lax.broadcasted_iota(jnp.int32, (CPW, WORDS), 0) < counts[None, :])[None, None]
    chars = layer(embedded, char_weights, (char_allowed, (WORDS, CPW, CHAR_HEADS, HEAD_DIM), char_forms))
    present = (lax.broadcasted_iota(jnp.int32, (WORDS, CPW), 1) < counts[:, None]).astype(jnp.float32)
    pooled = lax.optimization_barrier(jnp.sum(chars.reshape(WORDS, CPW, CD) * present[:, :, None], axis=1)) / counts[:, None].astype(jnp.float32)
    vectors = low(low_back(highest(low(pooled), char_project)))
    query_place = lax.broadcasted_iota(jnp.int32, (WORDS, WORDS), 0)
    key_place = lax.broadcasted_iota(jnp.int32, (WORDS, WORDS), 1)
    word_allowed = ((key_place <= query_place) & (segments[:, None] == segments[None, :]))[None]
    return layer(vectors, word_weights, (word_allowed, (WORDS, WORD_HEADS, HEAD_DIM), word_forms))

def reference(char_ids, char_counts, segment_ids, out_cotangent, char_table, char_gain_one, char_query, char_key, char_value, char_output, char_gain_two, char_up, char_down, char_project, word_gain_one, word_query, word_key, word_value, word_output, word_gain_two, word_up, word_down):
    weights = tuple((member.astype(jnp.float32) for member in (char_table, char_gain_one, char_query, char_key, char_value, char_output, char_gain_two, char_up, char_down, char_project, word_gain_one, word_query, word_key, word_value, word_output, word_gain_two, word_up, word_down)))
    identifiers = char_ids.reshape(MICRO * ROWS, WORDS * CPW)
    counts = char_counts.reshape(MICRO * ROWS, WORDS)
    segments = segment_ids.reshape(MICRO * ROWS, WORDS)
    row_pass = jax.checkpoint(row_forward)

    def forward(parameters):

        def one_row(row):
            return row_pass(parameters, row)
        return lax.map(one_row, (identifiers, counts, segments))
    results, pullback = jax.vjp(forward, weights)
    deltas, = pullback(out_cotangent.reshape(MICRO * ROWS, WORDS, WD).astype(jnp.float32))
    word_out = results.reshape(MICRO, ROWS, WORDS, WD).astype(jnp.bfloat16)
    return (word_out, deltas[0], deltas[1], deltas[2], deltas[3], deltas[4], deltas[5], deltas[6], deltas[7], deltas[8], deltas[9], deltas[10], deltas[11], deltas[12], deltas[13], deltas[14], deltas[15], deltas[16], deltas[17])
```

```python
from functools import partial

import jax
import jax.numpy as jnp
from jax import lax
from jax.experimental import pallas as pl
from jax.experimental.pallas import tpu as pltpu
from jax.sharding import PartitionSpec as P

F32 = jnp.float32
LOW = jnp.bfloat16

CD = 256
CFF = 1024
CPW = 16
CVOC = 256
CHAR_HEADS = 4
HEAD = 64
WD = 512
WFF = 2048
WORD_HEADS = 8
WORDS = 256

SPAN = 256
STEP = 240
BLOCKS = (WORDS * CPW - 1) // STEP + 1

epsilon = 1e-06
half_root = 0.7071067811865476
density = 0.3989422804014327
floor_score = -1e30

R_EMB, R_Q, R_K, R_V, R_P, R_MIX, R_SLOPE = 0, 256, 512, 768, 1024, 2048, 2304
KEPT_LOW = 3328
KEPT_F32 = 264

W_Q, W_K, W_V, W_O, W_UP, W_DOWN, W_CDOWN, W_PROJ = 0, 32, 64, 96, 128, 256, 384, 416
W_ROWS = 432
C_TABLE, C_Q, C_K, C_V, C_O, C_UP, C_GAIN = 0, 16, 32, 48, 64, 80, 144
C_ROWS = 160
SHARES = 16


def nn(left, right):
    return lax.dot_general(left, right, (((1,), (0,)), ((), ())), preferred_element_type=F32)


def nt(left, right):
    return lax.dot_general(left, right, (((1,), (1,)), ((), ())), preferred_element_type=F32)


def iota(shape, axis):
    return lax.broadcasted_iota(jnp.int32, shape, axis)


def eye(n):
    return iota((n, n), 0) == iota((n, n), 1)


def row_to_column(row):
    n = row.shape[1]
    return jnp.sum(jnp.where(eye(n), row, 0.0), axis=1, keepdims=True)


def gelu_pair(v):
    full = 0.5 + 0.5 * lax.erf(v * half_root)
    return v * full, full + v * (density * jnp.exp(-0.5 * v * v))


def share_order(d):
    return (d % 4) * 4 + d // 4


def membership(starts, counts, base):
    place = iota((1, SPAN), 1).astype(F32) + base
    own = jnp.where((starts >= base) & (starts < base + STEP), starts, 1e6)
    inside = (own <= place) & (place < own + counts)
    return jnp.where(inside, 1.0, 0.0).astype(LOW)


def word_starts(counts_row):
    earlier = iota((WORDS, WORDS), 1) < iota((WORDS, WORDS), 0)
    starts = jnp.sum(jnp.where(earlier, counts_row, 0.0), axis=1, keepdims=True)
    counts = row_to_column(counts_row)
    return starts, counts


def kernel_a(
    counts_ref, ids_ref, segs_ref, cot_hbm,
    table_ref, g1_ref, wq_ref, wk_ref, wv_ref, wo_ref, g2_ref, up_ref, down_ref, proj_ref,
    wg1_ref, wwq_hbm, wwk_hbm, wwv_hbm, wwo_hbm, wg2_ref, wup_hbm, wdown_hbm,
    keptl_hbm, keptf_hbm, gw_ref, keep_hbm, send_hbm, out_ref, gains_ref,
    cot, wwq, wwk, wwv, wwo, wup, wdown,
    tab_t, wqkv_t, wo_t, up_t, ids_t, slow, sf32, pa, pm, rowinfo,
    bundle, xs, midw, pw, actw, slopew,
    wsem, ksem, osem,
):
    phase = lax.axis_index("phase")
    loads = [
        pltpu.make_async_copy(src, dst, wsem.at[i])
        for i, (src, dst) in enumerate(
            ((wwq_hbm, wwq), (wwk_hbm, wwk), (wwv_hbm, wwv), (wwo_hbm, wwo),
             (wup_hbm, wup), (wdown_hbm, wdown), (cot_hbm.at[phase, 0], cot))
        )
    ]
    for load in loads:
        load.start()

    tab_t[...] = table_ref[...].T
    wqkv_t[0:CD] = (wq_ref[...] * 0.125).T
    wqkv_t[CD:2 * CD] = wk_ref[...].T
    wqkv_t[2 * CD:] = wv_ref[...].T
    wo_t[...] = wo_ref[...].T
    up_t[...] = up_ref[...].T
    g1 = row_to_column(g1_ref[...].astype(F32))
    g2 = row_to_column(g2_ref[...].astype(F32))
    counts_row = counts_ref[phase].astype(F32)
    starts, counts = word_starts(counts_row)
    last = jnp.max(starts)
    n_blocks = (last.astype(jnp.int32)) // STEP + 1
    ids = ids_ref[phase]
    ids_t[...] = jnp.concatenate(
        [ids[:, 128 * a:128 * a + 128] for a in range(32)], axis=0
    ).astype(F32).T.astype(LOW)
    starts_row = jnp.sum(
        jnp.where(iota((WORDS, WORDS), 0) < iota((WORDS, WORDS), 1), counts, 0.0), axis=0, keepdims=True
    )
    high = jnp.floor(starts_row * 0.0625)
    number = iota((1, WORDS), 1).astype(F32)
    rowinfo[...] = jnp.concatenate(
        [high, starts_row - 16.0 * high, number, jnp.ones((1, WORDS), F32), jnp.zeros((12, WORDS), F32)], axis=0
    ).astype(LOW)
    pa[...] = jnp.zeros_like(pa)
    pm[...] = jnp.zeros_like(pm)

    def kept_copies(b, slot):
        return (
            pltpu.make_async_copy(slow.at[slot], keptl_hbm.at[b], ksem.at[0, slot]),
            pltpu.make_async_copy(sf32.at[slot], keptf_hbm.at[b], ksem.at[1, slot]),
        )

    def block(b, carry):
        slot = lax.rem(b, 2)
        base = (b * STEP).astype(F32)

        @pl.when(b >= 2)
        def _():
            for c in kept_copies(b - 2, slot):
                c.wait()

        member = membership(starts, counts, base)
        info = nn(rowinfo[...], member)
        wid = info[2:3]
        valid = info[3:4] > 0.5
        place = iota((1, SPAN), 1).astype(F32) + base
        flat = (wid * 16.0 + place - (info[0:1] * 16.0 + info[1:2])).astype(jnp.int32)
        pick = jnp.where(iota((32, SPAN), 0) == (flat >> 7), 1.0, 0.0).astype(LOW)
        lanes = nn(ids_t[...], pick)
        ident = jnp.sum(jnp.where(iota((128, SPAN), 0) == (flat & 127), lanes, 0.0), axis=0, keepdims=True)
        ident = jnp.where(valid, ident, -1.0)
        hot = jnp.where(iota((CVOC, SPAN), 0).astype(F32) == ident, 1.0, 0.0).astype(LOW)
        emb = nn(tab_t[...], hot)
        inv1 = lax.rsqrt(jnp.mean(emb * emb, axis=0, keepdims=True) + epsilon)
        normed = (emb * inv1 * g1).astype(LOW)
        qkv = nn(wqkv_t[...], normed).astype(LOW)
        slow[slot, R_EMB:R_EMB + CD] = emb.astype(LOW)
        slow[slot, R_Q:R_Q + 2 * CD] = qkv[:2 * CD]
        key_rows = qkv[CD:2 * CD].T
        value_t = qkv[2 * CD:]
        slow[slot, R_V:R_V + SPAN] = value_t.T
        same = lax.dot_general(member, member, (((0,), (0,)), ((), ())), preferred_element_type=F32) > 0.5
        mixed = []
        for h in range(CHAR_HEADS):
            hs = slice(h * HEAD, (h + 1) * HEAD)
            s = nn(key_rows[:, hs], qkv[hs])
            s = jnp.where(same, s, floor_score)
            e = jnp.exp(s - jnp.max(s, axis=0, keepdims=True))
            p = (e * (1.0 / jnp.sum(e, axis=0, keepdims=True))).astype(LOW)
            slow[slot, R_P + h * SPAN:R_P + (h + 1) * SPAN] = p
            mixed.append(nn(value_t[hs], p).astype(LOW))
        mixed = jnp.concatenate(mixed, axis=0)
        slow[slot, R_MIX:R_MIX + CD] = mixed
        middle = emb + nn(wo_t[...], mixed)
        inv2 = lax.rsqrt(jnp.mean(middle * middle, axis=0, keepdims=True) + epsilon)
        sf32[slot, 0:CD] = middle
        sf32[slot, CD:] = jnp.concatenate([inv1, inv2, ident, jnp.zeros((5, SPAN), F32)], axis=0)
        normed_two = (middle * inv2 * g2).astype(LOW)
        for c in range(CFF // 256):
            cs = slice(c * 256, (c + 1) * 256)
            before = nn(up_t[cs], normed_two)
            act, slope = gelu_pair(before)
            slow[slot, R_SLOPE + c * 256:R_SLOPE + (c + 1) * 256] = slope.astype(LOW)
            pa[:, cs] += nt(member, act.astype(LOW))
        middle_hi = middle.astype(LOW)
        middle_lo = (middle - middle_hi.astype(F32)).astype(LOW)
        pm[...] += nt(member, middle_hi) + nt(member, middle_lo)
        for c in kept_copies(b, slot):
            c.start()
        return carry

    lax.fori_loop(0, n_blocks, block, 0)

    pa_hi = pa[...].astype(LOW)
    pa_lo = (pa[...] - pa_hi.astype(F32)).astype(LOW)
    per_count = 1.0 / counts
    pooled = (pm[...] + nn(pa_hi, down_ref[...]) + nn(pa_lo, down_ref[...])) * per_count
    pooled_low = pooled.astype(LOW)
    x = nn(pooled_low, proj_ref[...]).astype(LOW).astype(F32)
    xs[...] = x
    for load in loads:
        load.wait()
    wg1 = wg1_ref[...].astype(F32)
    wg2 = wg2_ref[...].astype(F32)
    winv1 = lax.rsqrt(jnp.mean(x * x, axis=1, keepdims=True) + epsilon)
    normed = (x * winv1 * wg1).astype(LOW)
    q = (nn(normed, wwq[...]) * 0.125).astype(LOW)
    k = nn(normed, wwk[...]).astype(LOW)
    v = nn(normed, wwv[...]).astype(LOW)
    seg_row = segs_ref[phase].astype(F32)
    seg_col = row_to_column(seg_row)
    allowed = (seg_row == seg_col) & (iota((WORDS, WORDS), 0) <= iota((WORDS, WORDS), 1))
    k_t = k.T
    v_t = v.T
    mixed_t = []
    for h in range(WORD_HEADS):
        hs = slice(h * HEAD, (h + 1) * HEAD)
        s = nt(k[:, hs], q[:, hs])
        s = jnp.where(allowed, s, floor_score)
        e = jnp.exp(s - jnp.max(s, axis=0, keepdims=True))
        p = (e * (1.0 / jnp.sum(e, axis=0, keepdims=True))).astype(LOW)
        pw[h] = p
        mixed_t.append(nn(v_t[hs], p).astype(LOW))
    mixed_t = jnp.concatenate(mixed_t, axis=0)
    middle = x + nn(mixed_t.T, wwo[...])
    midw[...] = middle
    winv2 = lax.rsqrt(jnp.mean(middle * middle, axis=1, keepdims=True) + epsilon)
    normed_two = (middle * winv2 * wg2).astype(LOW)
    result = middle
    for c in range(WFF // 512):
        cs = slice(c * 512, (c + 1) * 512)
        act, slope = gelu_pair(nn(normed_two, wup[:, cs]))
        act = act.astype(LOW)
        actw[:, cs] = act
        slopew[:, cs] = slope.astype(LOW)
        result = result + nn(act, wdown[cs, :])
    out_ref[...] = result.astype(LOW)

    mine = phase
    def place(row, value, width):
        n = value.shape[0] // SHARES
        low = value.astype(LOW)
        for half in range(2):
            side = jnp.bitwise_xor(mine, half)
            for piece in range(max(1, width // 256)):
                cols = low[:, half * width + piece * 256:half * width + piece * 256 + min(width, 256)]
                for d in range(SHARES):
                    part = cols[d * n:(d + 1) * n]
                    if width == 128:
                        part = jnp.concatenate([part[:n // 2], part[n // 2:]], axis=1)
                    m = part.shape[0]
                    bundle[side, share_order(d), row + piece * n:row + piece * n + m, :] = part

    cot_low = cot[...]
    n2d = jnp.zeros((WORDS, WD), F32)
    n2_t = normed_two.T
    for c in range(WFF // 512):
        cs = slice(c * 512, (c + 1) * 512)
        gd = nn(actw[:, cs].T, cot_low)
        low = gd.astype(LOW)
        for half in range(2):
            side = jnp.bitwise_xor(mine, half)
            for i in range(4):
                d = c * 4 + i
                bundle[side, share_order(d), W_DOWN:W_DOWN + 128, :] = low[i * 128:(i + 1) * 128, half * 256:half * 256 + 256]
        bd = (nt(cot_low, wdown[cs, :]) * slopew[:, cs].astype(F32)).astype(LOW)
        gu = nn(n2_t, bd).astype(LOW)
        half = c // 2
        side = jnp.bitwise_xor(mine, half)
        for piece in range(2):
            row = W_UP + ((c % 2) * 2 + piece) * 32
            for d in range(SHARES):
                bundle[side, share_order(d), row:row + 32, :] = gu[d * 32:(d + 1) * 32, piece * 256:piece * 256 + 256]
        n2d = n2d + nt(bd, wup[:, cs])
    middle = midw[...]
    vhat = middle * winv2
    gain2 = jnp.sum(n2d * vhat, axis=0, keepdims=True)
    lifted = n2d * wg2
    md = cot_low.astype(F32) + winv2 * (lifted - vhat * jnp.mean(lifted * vhat, axis=1, keepdims=True))
    md_low = md.astype(LOW)
    place(W_O, nn(mixed_t, md_low), 256)
    do = nt(md_low, wwo[...]).astype(LOW)
    dq_t, dk, dv = [], [], []
    for h in range(WORD_HEADS):
        hs = slice(h * HEAD, (h + 1) * HEAD)
        p = pw[h]
        pf = p.astype(F32)
        dp = nt(v[:, hs], do[:, hs])
        ds = (pf * (dp - jnp.sum(pf * dp, axis=0, keepdims=True))).astype(LOW)
        dq_t.append(nn(k_t[hs], ds))
        dk.append(nn(ds, q[:, hs]))
        dv.append(nn(p, do[:, hs]))
    dq = (jnp.concatenate(dq_t, axis=0) * 0.125).astype(LOW).T
    dk = jnp.concatenate(dk, axis=1).astype(LOW)
    dv = jnp.concatenate(dv, axis=1).astype(LOW)
    normed_t = normed.T
    place(W_Q, nn(normed_t, dq), 256)
    place(W_K, nn(normed_t, dk), 256)
    place(W_V, nn(normed_t, dv), 256)
    nd = nt(dq, wwq[...]) + nt(dk, wwk[...]) + nt(dv, wwv[...])
    vhat = xs[...] * winv1
    gain1 = jnp.sum(nd * vhat, axis=0, keepdims=True)
    lifted = nd * wg1
    xd = md + winv1 * (lifted - vhat * jnp.mean(lifted * vhat, axis=1, keepdims=True))
    vd = xd.astype(LOW)
    place(W_PROJ, nn(pooled_low.T, vd), 256)
    gw = (nt(vd, proj_ref[...]) * per_count).astype(LOW)
    gw_ref[...] = gw.T
    place(W_CDOWN, nn(pa_hi.T, gw), 128)
    gains_ref[...] = jnp.concatenate([gain1, gain2, jnp.zeros((6, WD), F32)], axis=0)
    stores = [
        pltpu.make_async_copy(bundle.at[0], keep_hbm, osem.at[0]),
        pltpu.make_async_copy(bundle.at[1], send_hbm, osem.at[1]),
    ]
    for s in stores:
        s.start()

    def drain(b, carry):
        for c in kept_copies(b, lax.rem(b, 2)):
            c.wait()
        return carry

    lax.fori_loop(jnp.maximum(n_blocks - 2, 0), n_blocks, drain, 0)
    for s in stores:
        s.wait()


def kernel_b(
    counts_ref, gw_ref, wgains_ref, g1_ref, wq_ref, wk_ref, wv_ref, wo_ref, g2_ref, up_ref, down_ref,
    keptl_hbm, keptf_hbm,
    keep_hbm, send_hbm,
    slow, sf32, wqkv, aup, aqkv, ao, atab, ag1, ag2, bundle, ksem, osem,
):
    phase = lax.axis_index("phase")
    counts_row = counts_ref[phase].astype(F32)
    starts, counts = word_starts(counts_row)
    n_blocks = jnp.max(starts).astype(jnp.int32) // STEP + 1

    def kept_copies(b, slot):
        return (
            pltpu.make_async_copy(keptl_hbm.at[b], slow.at[slot], ksem.at[0, slot]),
            pltpu.make_async_copy(keptf_hbm.at[b], sf32.at[slot], ksem.at[1, slot]),
        )

    for c in kept_copies(0, 0):
        c.start()
    g1 = row_to_column(g1_ref[...].astype(F32))
    g2 = row_to_column(g2_ref[...].astype(F32))
    for i, w in enumerate((wq_ref, wk_ref, wv_ref)):
        wqkv[:, i * CD:(i + 1) * CD] = w[...]
    for acc in (aup, aqkv, ao, atab, ag1, ag2):
        acc[...] = jnp.zeros_like(acc)

    def block(b, carry):
        slot = lax.rem(b, 2)
        base = (b * STEP).astype(F32)

        @pl.when(b + 1 < n_blocks)
        def _():
            for c in kept_copies(b + 1, 1 - slot):
                c.start()

        for c in kept_copies(b, slot):
            c.wait()
        member = membership(starts, counts, base)
        middle = sf32[slot, 0:CD]
        inv1 = sf32[slot, CD:CD + 1]
        inv2 = sf32[slot, CD + 1:CD + 2]
        ident = sf32[slot, CD + 2:CD + 3]
        g_low = nn(gw_ref[...], member).astype(LOW)
        vhat = middle * inv2
        normed_two = (vhat * g2).astype(LOW)
        n2d = jnp.zeros((CD, SPAN), F32)
        for c in range(CFF // 256):
            cs = slice(c * 256, (c + 1) * 256)
            slope = slow[slot, R_SLOPE + c * 256:R_SLOPE + (c + 1) * 256].astype(F32)
            bd = (nn(down_ref[cs, :], g_low) * slope).astype(LOW)
            aup[:, cs] += nt(normed_two, bd)
            n2d = n2d + nn(up_ref[:, cs], bd)
        ag2[...] += n2d * vhat
        lifted = n2d * g2
        md = g_low.astype(F32) + inv2 * (lifted - vhat * jnp.mean(lifted * vhat, axis=0, keepdims=True))
        md_low = md.astype(LOW)
        ao[...] += nt(slow[slot, R_MIX:R_MIX + CD], md_low)
        do = nn(wo_ref[...], md_low).astype(LOW)
        dq, dk, dv = [], [], []
        v = slow[slot, R_V:R_V + SPAN]
        for h in range(CHAR_HEADS):
            hs = slice(h * HEAD, (h + 1) * HEAD)
            p = slow[slot, R_P + h * SPAN:R_P + (h + 1) * SPAN]
            pf = p.astype(F32)
            dp = nn(v[:, hs], do[hs])
            ds = (pf * (dp - jnp.sum(pf * dp, axis=0, keepdims=True))).astype(LOW)
            dq.append((nn(slow[slot, R_K + h * HEAD:R_K + (h + 1) * HEAD], ds) * 0.125).astype(LOW))
            dk.append(nt(slow[slot, R_Q + h * HEAD:R_Q + (h + 1) * HEAD], ds).astype(LOW))
            dv.append(nt(do[hs], p).astype(LOW))
        dqkv = jnp.concatenate(dq + dk + dv, axis=0)
        emb = slow[slot, R_EMB:R_EMB + CD].astype(F32)
        ehat = emb * inv1
        normed = (ehat * g1).astype(LOW)
        aqkv[...] += nt(normed, dqkv)
        nd = nn(wqkv[...], dqkv)
        ag1[...] += nd * ehat
        lifted = nd * g1
        ed = md + inv1 * (lifted - ehat * jnp.mean(lifted * ehat, axis=0, keepdims=True))
        hot = jnp.where(iota((CVOC, SPAN), 0).astype(F32) == ident, 1.0, 0.0).astype(LOW)
        atab[...] += nt(hot, ed.astype(LOW))
        return carry

    lax.fori_loop(0, n_blocks, block, 0)

    def place(row, value, width):
        n = value.shape[0] // SHARES
        low = value.astype(LOW)
        for half in range(2):
            side = jnp.bitwise_xor(phase, half)
            for piece in range(width // 128):
                cols = low[:, half * width + piece * 128:half * width + piece * 128 + 128]
                for d in range(SHARES):
                    bundle[side, share_order(d), row + piece * n:row + piece * n + n, :] = cols[d * n:(d + 1) * n]

    place(C_TABLE, atab[...], 128)
    place(C_Q, aqkv[:, 0:CD], 128)
    place(C_K, aqkv[:, CD:2 * CD], 128)
    place(C_V, aqkv[:, 2 * CD:], 128)
    place(C_O, ao[...], 128)
    place(C_UP, aup[...], 512)
    cg = jnp.concatenate(
        [jnp.sum(ag1[...], axis=1, keepdims=True), jnp.sum(ag2[...], axis=1, keepdims=True)], axis=1
    )
    cg = jnp.concatenate([cg, jnp.zeros((CD, 126), F32)], axis=1).T
    wg = wgains_ref[...]
    for d in range(SHARES):
        rows = [
            jnp.concatenate([cg[0:1, d * 16:d * 16 + 16], jnp.zeros((1, 112), F32)], axis=1),
            jnp.concatenate([cg[1:2, d * 16:d * 16 + 16], jnp.zeros((1, 112), F32)], axis=1),
            jnp.concatenate([wg[0:1, d * 32:d * 32 + 32], jnp.zeros((1, 96), F32)], axis=1),
            jnp.concatenate([wg[1:2, d * 32:d * 32 + 32], jnp.zeros((1, 96), F32)], axis=1),
            jnp.zeros((12, 128), F32),
        ]
        tile = jnp.concatenate(rows, axis=0).astype(LOW)
        bundle[0, share_order(d), C_GAIN:C_GAIN + 16, :] = tile
        bundle[1, share_order(d), C_GAIN:C_GAIN + 16, :] = tile
    stores = [
        pltpu.make_async_copy(bundle.at[0], keep_hbm, osem.at[0]),
        pltpu.make_async_copy(bundle.at[1], send_hbm, osem.at[1]),
    ]
    for s in stores:
        s.start()
    for s in stores:
        s.wait()


ANYWHERE = pl.BlockSpec(memory_space=pl.ANY)
INSIDE = pl.BlockSpec(memory_space=pltpu.VMEM)


def call_a(char_counts, char_ids, segment_ids, out_cotangent, weights):
    shape = jax.ShapeDtypeStruct
    v = pltpu.VMEM
    return pl.pallas_call(
        kernel_a,
        out_shape=(
            shape((BLOCKS, KEPT_LOW, SPAN), LOW),
            shape((BLOCKS, KEPT_F32, SPAN), F32),
            shape((CD, WORDS), LOW),
            shape((SHARES, W_ROWS, 256), LOW),
            shape((SHARES, W_ROWS, 256), LOW),
            shape((WORDS, WD), LOW),
            shape((8, WD), F32),
        ),
        in_specs=[INSIDE] * 3 + [ANYWHERE] + [INSIDE] * 10 + [INSIDE] + [ANYWHERE] * 4 + [INSIDE] + [ANYWHERE] * 2,
        out_specs=(ANYWHERE, ANYWHERE, INSIDE, ANYWHERE, ANYWHERE, INSIDE, INSIDE),
        scratch_shapes=[
            v((WORDS, WD), LOW),
            v((WD, WD), LOW), v((WD, WD), LOW), v((WD, WD), LOW), v((WD, WD), LOW),
            v((WD, WFF), LOW), v((WFF, WD), LOW),
            v((CD, CVOC), LOW), v((3 * CD, CD), LOW), v((CD, CD), LOW), v((CFF, CD), LOW), v((128, 32), LOW),
            v((2, KEPT_LOW, SPAN), LOW), v((2, KEPT_F32, SPAN), F32),
            v((WORDS, CFF), F32), v((WORDS, CD), F32), v((16, WORDS), LOW),
            v((2, SHARES, W_ROWS, 256), LOW),
            v((WORDS, WD), F32), v((WORDS, WD), F32),
            v((WORD_HEADS, WORDS, WORDS), LOW), v((WORDS, WFF), LOW), v((WORDS, WFF), LOW),
            pltpu.SemaphoreType.DMA((7,)),
            pltpu.SemaphoreType.DMA((2, 2)),
            pltpu.SemaphoreType.DMA((2,)),
        ],
        compiler_params=pltpu.CompilerParams(vmem_limit_bytes=60 * 2**20),
        cost_estimate=pl.CostEstimate(flops=20 * 10**9, bytes_accessed=60 * 10**6, transcendentals=10**6),
        name="forward_and_words",
    )(char_counts, char_ids, segment_ids, out_cotangent, *weights)


def call_b(char_counts, gw, wgains, weights, keptl, keptf):
    shape = jax.ShapeDtypeStruct
    v = pltpu.VMEM
    return pl.pallas_call(
        kernel_b,
        out_shape=(shape((SHARES, C_ROWS, 128), LOW), shape((SHARES, C_ROWS, 128), LOW)),
        in_specs=[INSIDE] * 11 + [ANYWHERE] * 2,
        out_specs=(ANYWHERE, ANYWHERE),
        scratch_shapes=[
            v((2, KEPT_LOW, SPAN), LOW), v((2, KEPT_F32, SPAN), F32),
            v((CD, 3 * CD), LOW),
            v((CD, CFF), F32), v((CD, 3 * CD), F32), v((CD, CD), F32), v((CVOC, CD), F32),
            v((CD, SPAN), F32), v((CD, SPAN), F32),
            v((2, SHARES, C_ROWS, 128), LOW),
            pltpu.SemaphoreType.DMA((2, 2)),
            pltpu.SemaphoreType.DMA((2,)),
        ],
        compiler_params=pltpu.CompilerParams(vmem_limit_bytes=60 * 2**20),
        cost_estimate=pl.CostEstimate(flops=20 * 10**9, bytes_accessed=60 * 10**6, transcendentals=10**6),
        name="character_backward",
    )(char_counts, gw, wgains, *weights, keptl, keptf)


def flip(value, axis, bits):
    count = lax.axis_size(axis)
    return lax.ppermute(value, axis, [(i, i ^ bits) for i in range(count)])


def pick(value, index):
    return lax.dynamic_index_in_dim(value, index, 0, keepdims=False)


def scatter_sum(keep, send):
    rows, width = keep.shape[1:]
    got = flip(send, "phase", 1)
    total = (keep.astype(F32) + got.astype(F32)).astype(LOW).reshape(4, 4, rows, width)
    dp = lax.axis_index("dp")
    plane, line = lax.rem(dp, 4), lax.div(dp, 4)
    got = [flip(pick(total, lax.bitwise_xor(plane, k)), "dp", k) for k in range(1, 4)]
    total = pick(total, plane).astype(F32)
    for g in got:
        total = total + g.astype(F32)
    total = total.astype(LOW)
    got = [flip(pick(total, lax.bitwise_xor(line, k)), "dp", 4 * k) for k in range(1, 4)]
    total = pick(total, line).astype(F32)
    for g in got:
        total = total + g.astype(F32)
    return total


def body(
    char_ids, char_counts, segment_ids, out_cotangent,
    char_table, char_gain_one, char_query, char_key, char_value, char_output, char_gain_two, char_up, char_down,
    char_project,
    word_gain_one, word_query, word_key, word_value, word_output, word_gain_two, word_up, word_down,
):
    phase = lax.axis_index("phase")
    g1, g2 = char_gain_one.reshape(1, CD), char_gain_two.reshape(1, CD)
    wg1, wg2 = word_gain_one.reshape(1, WD), word_gain_two.reshape(1, WD)
    keptl, keptf, gw, wkeep, wsend, word_out, wgains = call_a(
        char_counts, char_ids, segment_ids, out_cotangent,
        (char_table, g1, char_query, char_key, char_value, char_output, g2, char_up, char_down, char_project,
         wg1, word_query, word_key, word_value, word_output, wg2, word_up, word_down),
    )
    ckeep, csend = call_b(
        char_counts, gw, wgains,
        (g1, char_query, char_key, char_value, char_output, g2, char_up, char_down), keptl, keptf,
    )
    halves = word_out.reshape(WORDS, 2, WD // 2).transpose(1, 0, 2)
    got = flip(pick(halves, 1 - phase), "phase", 1)
    own = pick(halves, phase)
    first = phase == 0
    outs = jnp.stack([jnp.where(first, own, got), jnp.where(first, got, own)])[:, None]
    if lax.axis_size("dp") == SHARES:
        w = scatter_sum(wkeep, wsend)
        c = scatter_sum(ckeep, csend)
        cdown = w[W_CDOWN:W_CDOWN + 32]
        cdown = jnp.concatenate([cdown[:, :128], cdown[:, 128:]], axis=0)

        def wide(rows, pieces, n):
            return jnp.concatenate([rows[i * n:(i + 1) * n] for i in range(pieces)], axis=1)

        return (
            outs,
            c[C_TABLE:C_TABLE + 16], c[C_GAIN, :16],
            c[C_Q:C_Q + 16], c[C_K:C_K + 16], c[C_V:C_V + 16], c[C_O:C_O + 16], c[C_GAIN + 1, :16],
            wide(c[C_UP:C_UP + 64], 4, 16), cdown, w[W_PROJ:W_PROJ + 16],
            c[C_GAIN + 2, :32],
            w[W_Q:W_Q + 32], w[W_K:W_K + 32], w[W_V:W_V + 32], w[W_O:W_O + 32], c[C_GAIN + 3, :32],
            wide(w[W_UP:W_UP + 128], 4, 32), w[W_DOWN:W_DOWN + 128],
        )
    return general_sums(outs, wkeep, wsend, ckeep, csend)


def general_sums(outs, wkeep, wsend, ckeep, csend):
    order = jnp.asarray([share_order(d) for d in range(SHARES)])

    def natural(keep, send):
        total = keep.astype(F32) + flip(send, "phase", 1).astype(F32)
        return jnp.take(total, order, axis=0)

    w, c = natural(wkeep, wsend), natural(ckeep, csend)

    def whole(rows):
        return rows.reshape(-1, rows.shape[-1])

    def wide(rows, pieces):
        n = rows.shape[1] // pieces
        return whole(rows.reshape(SHARES, pieces, n, rows.shape[-1]).transpose(0, 2, 1, 3).reshape(SHARES, n, -1))

    cdown = w[:, W_CDOWN:W_CDOWN + 32]
    cdown = jnp.concatenate([cdown[..., :128], cdown[..., 128:]], axis=1)
    parts = (
        whole(c[:, C_TABLE:C_TABLE + 16]), c[:, C_GAIN, :16].reshape(-1),
        whole(c[:, C_Q:C_Q + 16]), whole(c[:, C_K:C_K + 16]), whole(c[:, C_V:C_V + 16]), whole(c[:, C_O:C_O + 16]),
        c[:, C_GAIN + 1, :16].reshape(-1),
        wide(c[:, C_UP:C_UP + 64], 4), whole(cdown), whole(w[:, W_PROJ:W_PROJ + 16]),
        c[:, C_GAIN + 2, :32].reshape(-1),
        whole(w[:, W_Q:W_Q + 32]), whole(w[:, W_K:W_K + 32]), whole(w[:, W_V:W_V + 32]), whole(w[:, W_O:W_O + 32]),
        c[:, C_GAIN + 3, :32].reshape(-1),
        wide(w[:, W_UP:W_UP + 128], 4), whole(w[:, W_DOWN:W_DOWN + 128]),
    )
    return (outs,) + tuple(lax.psum_scatter(p, "dp", scatter_dimension=0, tiled=True) for p in parts)


def solution(mesh):
    rows = P(None, "dp", None)
    both = P("dp", "phase")
    one = P("dp")
    return jax.shard_map(
        body,
        mesh=mesh,
        in_specs=(rows, rows, rows, P(None, "dp", None, None)) + (P(),) * 18,
        out_specs=(
            P(None, "dp", None, "phase"),
            both, one, both, both, both, both, one, both, both, both,
            one, both, both, both, both, one, both, both,
        ),
        check_vma=False,
    )
```

```python
from functools import partial

import jax
import jax.numpy as jnp
from jax import lax
from jax.experimental import pallas as pl
from jax.experimental.pallas import tpu as pltpu
from jax.sharding import PartitionSpec as P

F32 = jnp.float32
LOW = jnp.bfloat16

CD = 256
CFF = 1024
CPW = 16
CVOC = 256
CHAR_HEADS = 4
HEAD = 64
WD = 512
WFF = 2048
WORD_HEADS = 8
WORDS = 256

SPAN = 256
STEP = 240
WIDE = 2 * SPAN
TURNS = ((WORDS * CPW - 1) // STEP + 2) // 2

epsilon = 1e-06
half_root = 0.7071067811865476
density = 0.3989422804014327
floor_score = -1e30

R_EMB, R_Q, R_K, R_V, R_P, R_MIX = 0, 256, 512, 768, 1024, 2048
KEPT_LOW = 2304
KEPT_ALL = KEPT_LOW + CFF
I_INV1, I_INV2, I_IDENT, I_WORD = 0, 1, 2, 3
BAND = 144
WINDOW = 96

X_Q, X_K, X_V, X_O, X_UP, X_CDOWN = 0, 32, 64, 96, 128, 256
X_ROWS = 288
Z_DOWN, Z_PROJ = 0, 128
Z_ROWS = 144
C_TABLE, C_Q, C_K, C_V, C_O, C_UP, C_GAIN = 0, 16, 32, 48, 64, 80, 144
C_ROWS = 160
SHARES = 16


def nn(left, right):
    return lax.dot_general(left, right, (((1,), (0,)), ((), ())), preferred_element_type=F32)


def nt(left, right):
    return lax.dot_general(left, right, (((1,), (1,)), ((), ())), preferred_element_type=F32)


def iota(shape, axis):
    return lax.broadcasted_iota(jnp.int32, shape, axis)


def eye(n):
    return iota((n, n), 0) == iota((n, n), 1)


def row_to_column(row):
    n = row.shape[1]
    return jnp.sum(jnp.where(eye(n), row, 0.0), axis=1, keepdims=True)


def gelu_pair(v):
    full = 0.5 + 0.5 * lax.erf(v * half_root)
    return v * full, full + v * (density * jnp.exp(-0.5 * v * v))


def plane_first(d):
    return (d % 4) * 4 + d // 4


def line_first(d):
    return d


def lane_places(turn):
    lane = iota((1, WIDE), 1)
    second = lane >= SPAN
    base = (turn * (2 * STEP)).astype(F32) + jnp.where(second, float(STEP), 0.0)
    return (lane - jnp.where(second, SPAN, 0)).astype(F32) + base, base


def members(word, first, count):
    return jnp.where((iota((count, WIDE), 0) + first).astype(F32) == word, 1.0, 0.0).astype(LOW)


def word_starts(counts_row):
    earlier = iota((WORDS, WORDS), 1) < iota((WORDS, WORDS), 0)
    starts = jnp.sum(jnp.where(earlier, counts_row, 0.0), axis=1, keepdims=True)
    counts = row_to_column(counts_row)
    return starts, counts


def put(bundle, phase, order, row, value, width, share_rows):
    low = value.astype(LOW)
    lanes = bundle.shape[-1]
    for half in range(2):
        side = jnp.bitwise_xor(phase, half)
        for piece in range(max(1, width // lanes)):
            take = min(width, lanes)
            cols = low[:, half * width + piece * lanes:half * width + piece * lanes + take]
            for i in range(value.shape[0] // share_rows):
                part = cols[i * share_rows:(i + 1) * share_rows]
                if take < lanes:
                    part = jnp.concatenate([part[:share_rows // 2], part[share_rows // 2:]], axis=1)
                m = part.shape[0]
                bundle[side, order(i), row + piece * share_rows:row + piece * share_rows + m, :] = part


def band(t):
    keys = slice(0, BAND) if t % 2 == 0 else slice(SPAN - BAND, SPAN)
    return t // 2, keys, slice(t * 128, (t + 1) * 128)


def two_heads(pair):
    zero = jnp.zeros((HEAD, pair.shape[1]), LOW)
    first = jnp.concatenate([pair[:HEAD], zero], axis=0)
    second = jnp.concatenate([zero, pair[HEAD:]], axis=0)
    return jnp.concatenate([first, second], axis=1)


def two_heads_rows(pair):
    left = iota(pair.shape, 1) < HEAD
    zero = jnp.zeros(pair.shape, LOW)
    return jnp.concatenate([jnp.where(left, pair, zero), jnp.where(left, zero, pair)], axis=0)


def softmax_keys(s):
    e = jnp.exp(s - jnp.max(s, axis=0, keepdims=True))
    return (e * (1.0 / jnp.sum(e, axis=0, keepdims=True))).astype(LOW)


def kernel_a(
    counts_ref, ids_ref, segs_ref, cot_hbm,
    table_ref, g1_ref, wq_ref, wk_ref, wv_ref, wo_ref, g2_ref, up_ref, down_ref, proj_ref,
    wg1_ref, wwq_hbm, wwk_hbm, wwv_hbm, wwo_hbm, wg2_ref, wup_hbm, wdown_hbm,
    keptl_hbm, kepts_hbm, keptm_hbm, kepti_hbm, turns_ref, gw_ref,
    xkeep_hbm, xsend_hbm, zkeep_hbm, zsend_hbm, outk_ref, outs_ref, gains_ref,
    cot, wwq, wwk, wwv, wwo, wup, wdown,
    tab_t, wqkv_t, wo_t, up_t, ids_t, slow, smid, sinfo, pa, pm, rowinfo, firsts_v, firsts, before_s, act_s, prob_s, found_s,
    xbundle, zbundle, xs, midw, pw, actw, slopew,
    wsem, ksem, osem,
):
    phase = lax.axis_index("phase")
    loads = [
        pltpu.make_async_copy(src, dst, wsem.at[i])
        for i, (src, dst) in enumerate(
            ((wwq_hbm, wwq), (wwk_hbm, wwk), (wwv_hbm, wwv), (wwo_hbm, wwo),
             (wup_hbm, wup), (wdown_hbm, wdown), (cot_hbm.at[phase, 0], cot))
        )
    ]
    for load in loads:
        load.start()

    counts_row = counts_ref[phase].astype(F32)
    starts, counts = word_starts(counts_row)
    last = jnp.max(starts)
    n_turns = last.astype(jnp.int32) // (2 * STEP) + 1
    turns_ref[0] = n_turns
    bases = (iota((1, 128), 1) * (2 * STEP)).astype(F32)
    first = jnp.sum(jnp.where(starts < bases, 1.0, 0.0), axis=0, keepdims=True)
    firsts_v[...] = jnp.broadcast_to(first, (8, 128)).astype(jnp.int32)
    first_copy = pltpu.make_async_copy(firsts_v, firsts, wsem.at[7])
    first_copy.start()
    tab_t[...] = table_ref[...].T
    wqkv_t[0:CD] = (wq_ref[...] * 0.125).T
    wqkv_t[CD:2 * CD] = wk_ref[...].T
    wqkv_t[2 * CD:] = wv_ref[...].T
    wo_t[...] = wo_ref[...].T
    up_t[...] = up_ref[...].T
    g1 = row_to_column(g1_ref[...].astype(F32)[None, :])
    g2 = row_to_column(g2_ref[...].astype(F32)[None, :])
    ids = ids_ref[phase]
    ids_t[...] = jnp.concatenate(
        [ids[:, 128 * a:128 * a + 128] for a in range(32)], axis=0
    ).astype(F32).T.astype(LOW)
    starts_row = jnp.sum(
        jnp.where(iota((WORDS, WORDS), 0) < iota((WORDS, WORDS), 1), counts, 0.0), axis=0, keepdims=True
    )
    high = jnp.floor(starts_row * 0.0625)
    number = iota((1, WORDS), 1).astype(F32)
    rowinfo[...] = jnp.concatenate(
        [high, starts_row - 16.0 * high, number, jnp.ones((1, WORDS), F32), jnp.zeros((12, WORDS), F32)], axis=0
    ).astype(LOW)
    pa[...] = jnp.zeros_like(pa)
    pm[...] = jnp.zeros_like(pm)
    prob_s[...] = jnp.zeros_like(prob_s)
    for slot in range(2):
        slow[slot, R_P:R_P + CHAR_HEADS * SPAN] = jnp.zeros((CHAR_HEADS * SPAN, WIDE), LOW)
    first_copy.wait()

    def find(turn):
        place, base = lane_places(turn)
        own = (starts >= base) & (starts < base + STEP) & (starts <= place) & (place < starts + counts)
        info = nn(rowinfo[...], jnp.where(own, 1.0, 0.0).astype(LOW))
        word = info[2:3]
        flat = (word * 16.0 + place - (info[0:1] * 16.0 + info[1:2])).astype(jnp.int32)
        chosen = jnp.where(iota((32, WIDE), 0) == (flat >> 7), 1.0, 0.0).astype(LOW)
        lanes = nn(ids_t[...], chosen)
        ident = jnp.sum(jnp.where(iota((128, WIDE), 0) == (flat & 127), lanes, 0.0), axis=0, keepdims=True)
        valid = info[3:4] > 0.5
        none = jnp.full((6, WIDE), -1.0, F32)
        return jnp.concatenate([jnp.where(valid, ident, -1.0), jnp.where(valid, word, -1.0), none], axis=0)

    found_s[...] = find(jnp.int32(0))

    def kept_copies(b, slot):
        return (
            pltpu.make_async_copy(slow.at[slot, pl.ds(0, KEPT_LOW)], keptl_hbm.at[b], ksem.at[0, slot]),
            pltpu.make_async_copy(slow.at[slot, pl.ds(KEPT_LOW, CFF)], kepts_hbm.at[b], ksem.at[1, slot]),
            pltpu.make_async_copy(smid.at[slot], keptm_hbm.at[b], ksem.at[2, slot]),
            pltpu.make_async_copy(sinfo.at[slot], kepti_hbm.at[b], ksem.at[3, slot]),
        )

    def turn(b, carry):
        slot = lax.rem(b, 2)

        @pl.when(b >= 2)
        def _():
            for c in kept_copies(b - 2, slot):
                c.wait()

        ident = found_s[0:1]
        word = found_s[1:2]
        hot = jnp.where(iota((CVOC, WIDE), 0).astype(F32) == ident, 1.0, 0.0).astype(LOW)
        emb = nn(tab_t[...], hot)
        inv1 = lax.rsqrt(jnp.mean(emb * emb, axis=0, keepdims=True) + epsilon)
        normed = (emb * inv1 * g1).astype(LOW)
        qkv = nn(wqkv_t[...], normed).astype(LOW)
        key_rows = [qkv[CD:2 * CD, u * SPAN:(u + 1) * SPAN].T for u in range(2)]
        value_t = qkv[2 * CD:]
        word_col = jnp.broadcast_to(jnp.where(word < 0.0, -2.0, word), (8, WIDE)).T[:, 0:1]
        for t in range(4):
            u, ks, ql = band(t)
            bias = jnp.where(word_col[u * SPAN + ks.start:u * SPAN + ks.stop] == word[:, ql], 0.0, floor_score)
            for pair in range(CHAR_HEADS // 2):
                fs = slice(pair * 128, pair * 128 + 128)
                s = nn(key_rows[u][ks, fs], two_heads(qkv[fs, ql]))
                for i in range(2):
                    p = softmax_keys(s[:, i * 128:i * 128 + 128] + bias)
                    row = (pair * 2 + i) * SPAN
                    prob_s[row + ks.start:row + ks.stop, ql] = p
                    slow[slot, R_P + row + ks.start:R_P + row + ks.stop, ql] = p
        slow[slot, R_EMB:R_EMB + CD] = emb.astype(LOW)
        slow[slot, R_Q:R_Q + 2 * CD] = qkv[:2 * CD]
        for u in range(2):
            us = slice(u * SPAN, (u + 1) * SPAN)
            slow[slot, R_V:R_V + SPAN, us] = value_t[:, us].T
        mixed = []
        for h in range(CHAR_HEADS):
            hs = slice(h * HEAD, (h + 1) * HEAD)
            both = []
            for u in range(2):
                us = slice(u * SPAN, (u + 1) * SPAN)
                both.append(nn(value_t[hs, us], prob_s[h * SPAN:(h + 1) * SPAN, us]).astype(LOW))
            mixed.append(jnp.concatenate(both, axis=1))
        mixed = jnp.concatenate(mixed, axis=0)
        slow[slot, R_MIX:R_MIX + CD] = mixed
        middle = emb + nn(wo_t[...], mixed)
        inv2 = lax.rsqrt(jnp.mean(middle * middle, axis=0, keepdims=True) + epsilon)
        smid[slot] = middle
        sinfo[slot] = jnp.concatenate([inv1, inv2, ident, word, jnp.zeros((4, WIDE), F32)], axis=0)
        normed_two = (middle * inv2 * g2).astype(LOW)
        before_s[...] = nn(up_t[...], normed_two)
        found_s[...] = find(b + 1)
        for c in range(CFF // 32):
            cs = slice(c * 32, (c + 1) * 32)
            act, slope = gelu_pair(before_s[cs])
            slow[slot, KEPT_LOW + c * 32:KEPT_LOW + (c + 1) * 32] = slope.astype(LOW)
            act_s[cs] = act.astype(LOW)
        middle_hi = middle.astype(LOW)
        middle_lo = (middle - middle_hi.astype(F32)).astype(LOW)
        w0 = (firsts[0, b] // 16) * 16
        windows = (firsts[0, b + 1] - w0 + WINDOW - 1) // WINDOW

        def pool(i, carry):
            first = w0 + i * WINDOW
            w = pl.ds(pl.multiple_of(first, 16), WINDOW)
            near = members(word, first, WINDOW)
            pa[w, :] += nt(near, act_s[...])
            pm[w, :] += nt(near, middle_hi) + nt(near, middle_lo)
            return carry

        pool(0, 0)
        lax.fori_loop(1, windows, pool, 0)
        for c in kept_copies(b, slot):
            c.start()
        return carry

    lax.fori_loop(0, n_turns, turn, 0)

    pa_hi = pa[0:WORDS].astype(LOW)
    pa_lo = (pa[0:WORDS] - pa_hi.astype(F32)).astype(LOW)
    per_count = 1.0 / counts
    pooled = (pm[0:WORDS] + nn(pa_hi, down_ref[...]) + nn(pa_lo, down_ref[...])) * per_count
    pooled_low = pooled.astype(LOW)
    x = nn(pooled_low, proj_ref[...]).astype(LOW).astype(F32)
    xs[...] = x
    for load in loads:
        load.wait()
    wg1 = wg1_ref[...].astype(F32)[None, :]
    wg2 = wg2_ref[...].astype(F32)[None, :]
    winv1 = lax.rsqrt(jnp.mean(x * x, axis=1, keepdims=True) + epsilon)
    normed = (x * winv1 * wg1).astype(LOW)
    q = (nn(normed, wwq[...]) * 0.125).astype(LOW)
    k = nn(normed, wwk[...]).astype(LOW)
    v = nn(normed, wwv[...]).astype(LOW)
    seg_row = segs_ref[phase].astype(F32)
    seg_col = row_to_column(seg_row)
    allowed = (seg_row == seg_col) & (iota((WORDS, WORDS), 0) <= iota((WORDS, WORDS), 1))
    bias = jnp.where(allowed, 0.0, floor_score)
    k_t = k.T
    v_t = v.T
    for h in range(WORD_HEADS):
        pw[h, 128:, 0:128] = jnp.zeros((128, 128), LOW)
    for t in range(2):
        ks, ql = slice(0, 128 * (t + 1)), slice(128 * t, 128 * (t + 1))
        for pair in range(WORD_HEADS // 2):
            fs = slice(pair * 128, pair * 128 + 128)
            s = nt(k[ks, fs], two_heads_rows(q[ql, fs]))
            for i in range(2):
                pw[pair * 2 + i, ks, ql] = softmax_keys(s[:, i * 128:i * 128 + 128] + bias[ks, ql])
    mixed_t = jnp.concatenate(
        [nn(v_t[h * HEAD:(h + 1) * HEAD], pw[h]).astype(LOW) for h in range(WORD_HEADS)], axis=0
    )
    middle = x + nn(mixed_t.T, wwo[...])
    midw[...] = middle
    winv2 = lax.rsqrt(jnp.mean(middle * middle, axis=1, keepdims=True) + epsilon)
    normed_two = (middle * winv2 * wg2).astype(LOW)
    result = middle
    for c in range(WFF // 512):
        cs = slice(c * 512, (c + 1) * 512)
        act, slope = gelu_pair(nn(normed_two, wup[:, cs]))
        act = act.astype(LOW)
        actw[:, cs] = act
        slopew[:, cs] = slope.astype(LOW)
        result = result + nn(act, wdown[cs, :])
    result = result.astype(LOW)
    front = phase == 0
    outk_ref[...] = jnp.where(front, result[:, :256], result[:, 256:])
    outs_ref[...] = jnp.where(front, result[:, 256:], result[:, :256])

    cot_low = cot[...]
    n2d = jnp.zeros((WORDS, WD), F32)
    n2_t = normed_two.T
    for c in range(WFF // 512):
        cs = slice(c * 512, (c + 1) * 512)
        gd = nn(actw[:, cs].T, cot_low)
        put(zbundle, phase, lambda i: line_first(c * 4 + i), Z_DOWN, gd, 256, 128)
        bd = (nt(cot_low, wdown[cs, :]) * slopew[:, cs].astype(F32)).astype(LOW)
        gu = nn(n2_t, bd).astype(LOW)
        side = jnp.bitwise_xor(phase, c // 2)
        for piece in range(2):
            row = X_UP + ((c % 2) * 2 + piece) * 32
            for d in range(SHARES):
                xbundle[side, plane_first(d), row:row + 32, :] = gu[d * 32:(d + 1) * 32, piece * 256:piece * 256 + 256]
        n2d = n2d + nt(bd, wup[:, cs])
    middle = midw[...]
    vhat = middle * winv2
    gain2 = jnp.sum(n2d * vhat, axis=0, keepdims=True)
    lifted = n2d * wg2
    md = cot_low.astype(F32) + winv2 * (lifted - vhat * jnp.mean(lifted * vhat, axis=1, keepdims=True))
    md_low = md.astype(LOW)
    put(xbundle, phase, plane_first, X_O, nn(mixed_t, md_low), 256, 32)
    do = nt(md_low, wwo[...]).astype(LOW)
    dq_t, dk, dv = [], [], []
    left = iota((WORDS, 128), 1) < HEAD
    for pair in range(WORD_HEADS // 2):
        fs = slice(pair * 128, pair * 128 + 128)
        ds = []
        for t in range(2):
            ks, ql = slice(0, 128 * (t + 1)), slice(128 * t, 128 * (t + 1))
            dp = nt(v[ks, fs], two_heads_rows(do[ql, fs]))
            for i in range(2):
                pf = pw[pair * 2 + i, ks, ql].astype(F32)
                dph = dp[:, i * 128:i * 128 + 128]
                d = (pf * (dph - jnp.sum(pf * dph, axis=0, keepdims=True))).astype(LOW)
                ds.append(d if t else jnp.concatenate([d, jnp.zeros((128, 128), LOW)], axis=0))
        both = [jnp.concatenate([ds[i], ds[i + 2]], axis=1) for i in range(2)]
        for i in range(2):
            h = pair * 2 + i
            dq_t.append(nn(k_t[h * HEAD:(h + 1) * HEAD], both[i]))
        dk.append(jnp.where(left, nn(both[0], q[:, fs]), nn(both[1], q[:, fs])).astype(LOW))
        dv.append(jnp.where(left, nn(pw[pair * 2], do[:, fs]), nn(pw[pair * 2 + 1], do[:, fs])).astype(LOW))
    dq = (jnp.concatenate(dq_t, axis=0) * 0.125).astype(LOW).T
    dk = jnp.concatenate(dk, axis=1)
    dv = jnp.concatenate(dv, axis=1)
    normed_t = normed.T
    put(xbundle, phase, plane_first, X_Q, nn(normed_t, dq), 256, 32)
    put(xbundle, phase, plane_first, X_K, nn(normed_t, dk), 256, 32)
    put(xbundle, phase, plane_first, X_V, nn(normed_t, dv), 256, 32)
    nd = nt(dq, wwq[...]) + nt(dk, wwk[...]) + nt(dv, wwv[...])
    vhat = xs[...] * winv1
    gain1 = jnp.sum(nd * vhat, axis=0, keepdims=True)
    lifted = nd * wg1
    xd = md + winv1 * (lifted - vhat * jnp.mean(lifted * vhat, axis=1, keepdims=True))
    vd = xd.astype(LOW)
    put(zbundle, phase, line_first, Z_PROJ, nn(pooled_low.T, vd), 256, 16)
    gw = (nt(vd, proj_ref[...]) * per_count).astype(LOW)
    gw_ref[...] = gw.T
    put(xbundle, phase, plane_first, X_CDOWN, nn(pa_hi.T, gw), 128, 64)
    gains_ref[...] = jnp.concatenate([gain1, gain2, jnp.zeros((6, WD), F32)], axis=0)
    stores = [
        pltpu.make_async_copy(xbundle.at[0], xkeep_hbm, osem.at[0]),
        pltpu.make_async_copy(xbundle.at[1], xsend_hbm, osem.at[1]),
        pltpu.make_async_copy(zbundle.at[0], zkeep_hbm, osem.at[2]),
        pltpu.make_async_copy(zbundle.at[1], zsend_hbm, osem.at[3]),
    ]
    for s in stores:
        s.start()

    def drain(b, carry):
        for c in kept_copies(b, lax.rem(b, 2)):
            c.wait()
        return carry

    lax.fori_loop(jnp.maximum(n_turns - 2, 0), n_turns, drain, 0)
    for s in stores:
        s.wait()


def kernel_b1(
    turns_ref, gw_ref, g2_ref, up_ref, down_ref, kepts_hbm, keptm_hbm, kepti_hbm,
    keptd_hbm, aup_ref, gain_ref,
    sslope, smid, sinfo, sdelta, aup, ag2, ksem, dsem,
):
    n_turns = turns_ref[0]

    def kept_copies(b, slot):
        return (
            pltpu.make_async_copy(kepts_hbm.at[b], sslope.at[slot], ksem.at[0, slot]),
            pltpu.make_async_copy(keptm_hbm.at[b], smid.at[slot], ksem.at[1, slot]),
            pltpu.make_async_copy(kepti_hbm.at[b], sinfo.at[slot], ksem.at[2, slot]),
        )

    def delta_copy(b, slot):
        return pltpu.make_async_copy(sdelta.at[slot], keptd_hbm.at[b], dsem.at[slot])

    for c in kept_copies(0, 0):
        c.start()
    g2 = row_to_column(g2_ref[...].astype(F32)[None, :])
    aup[...] = jnp.zeros_like(aup)
    ag2[...] = jnp.zeros_like(ag2)

    def turn(b, carry):
        slot = lax.rem(b, 2)

        @pl.when(b + 1 < n_turns)
        def _():
            for c in kept_copies(b + 1, 1 - slot):
                c.start()

        @pl.when(b >= 2)
        def _():
            delta_copy(b - 2, slot).wait()

        for c in kept_copies(b, slot):
            c.wait()
        inv2 = sinfo[slot, I_INV2:I_INV2 + 1]
        g_low = nn(gw_ref[...], members(sinfo[slot, I_WORD:I_WORD + 1], 0, WORDS)).astype(LOW)
        vhat = smid[slot] * inv2
        normed_two = (vhat * g2).astype(LOW)
        n2d = jnp.zeros((CD, WIDE), F32)
        for c in range(CFF // 256):
            cs = slice(c * 256, (c + 1) * 256)
            bd = (nn(down_ref[cs, :], g_low) * sslope[slot, cs].astype(F32)).astype(LOW)
            aup[:, cs] += nt(normed_two, bd)
            n2d = n2d + nn(up_ref[:, cs], bd)
        ag2[...] += n2d * vhat
        lifted = n2d * g2
        md = g_low.astype(F32) + inv2 * (lifted - vhat * jnp.mean(lifted * vhat, axis=0, keepdims=True))
        sdelta[slot] = md.astype(LOW)
        delta_copy(b, slot).start()
        return carry

    lax.fori_loop(0, n_turns, turn, 0)
    aup_ref[...] = aup[...].astype(LOW)
    gain_ref[...] = jnp.broadcast_to(jnp.sum(ag2[...], axis=1, keepdims=True), (CD, 8)).T

    def drain(b, carry):
        delta_copy(b, lax.rem(b, 2)).wait()
        return carry

    lax.fori_loop(jnp.maximum(n_turns - 2, 0), n_turns, drain, 0)


def kernel_b2(
    turns_ref, wgains_ref, gain2_ref, aup_ref, g1_ref, wq_ref, wk_ref, wv_ref, wo_ref,
    keptl_hbm, keptd_hbm, kepti_hbm,
    keep_hbm, send_hbm,
    slow, sinfo, sdelta, dscore, wqkv, aqkv, ao, atab, ag1, bundle, ksem, osem,
):
    phase = lax.axis_index("phase")
    n_turns = turns_ref[0]

    def kept_copies(b, slot):
        return (
            pltpu.make_async_copy(keptl_hbm.at[b], slow.at[slot], ksem.at[0, slot]),
            pltpu.make_async_copy(keptd_hbm.at[b], sdelta.at[slot], ksem.at[1, slot]),
            pltpu.make_async_copy(kepti_hbm.at[b], sinfo.at[slot], ksem.at[2, slot]),
        )

    for c in kept_copies(0, 0):
        c.start()
    g1 = row_to_column(g1_ref[...].astype(F32)[None, :])
    for i, w in enumerate((wq_ref, wk_ref, wv_ref)):
        wqkv[:, i * CD:(i + 1) * CD] = w[...]
    for acc in (aqkv, ao, atab, ag1, dscore):
        acc[...] = jnp.zeros_like(acc)

    def turn(b, carry):
        slot = lax.rem(b, 2)

        @pl.when(b + 1 < n_turns)
        def _():
            for c in kept_copies(b + 1, 1 - slot):
                c.start()

        for c in kept_copies(b, slot):
            c.wait()
        inv1 = sinfo[slot, I_INV1:I_INV1 + 1]
        ident = sinfo[slot, I_IDENT:I_IDENT + 1]
        md_low = sdelta[slot]
        ao[...] += nt(slow[slot, R_MIX:R_MIX + CD], md_low)
        do = nn(wo_ref[...], md_low).astype(LOW)
        for t in range(4):
            u, ks, ql = band(t)
            for pair in range(CHAR_HEADS // 2):
                fs = slice(u * SPAN + pair * 128, u * SPAN + pair * 128 + 128)
                dp = nn(
                    slow[slot, R_V + ks.start:R_V + ks.stop, fs], two_heads(do[pair * 128:pair * 128 + 128, ql])
                )
                for i in range(2):
                    row = (pair * 2 + i) * SPAN
                    pf = slow[slot, R_P + row + ks.start:R_P + row + ks.stop, ql].astype(F32)
                    dph = dp[:, i * 128:i * 128 + 128]
                    d = pf * (dph - jnp.sum(pf * dph, axis=0, keepdims=True))
                    dscore[row + ks.start:row + ks.stop, ql] = d.astype(LOW)
        dq, dk, dv = [], [], []
        for h in range(CHAR_HEADS):
            hs = slice(h * HEAD, (h + 1) * HEAD)
            one, two, three = [], [], []
            for u in range(2):
                us = slice(u * SPAN, (u + 1) * SPAN)
                p = slow[slot, R_P + h * SPAN:R_P + (h + 1) * SPAN, us]
                ds = dscore[h * SPAN:(h + 1) * SPAN, us]
                one.append((nn(slow[slot, R_K + h * HEAD:R_K + (h + 1) * HEAD, us], ds) * 0.125).astype(LOW))
                two.append(nt(slow[slot, R_Q + h * HEAD:R_Q + (h + 1) * HEAD, us], ds).astype(LOW))
                three.append(nt(do[hs, us], p).astype(LOW))
            for part, pair in ((dq, one), (dk, two), (dv, three)):
                part.append(jnp.concatenate(pair, axis=1))
        dqkv = jnp.concatenate(dq + dk + dv, axis=0)
        emb = slow[slot, R_EMB:R_EMB + CD].astype(F32)
        ehat = emb * inv1
        normed = (ehat * g1).astype(LOW)
        aqkv[...] += nt(normed, dqkv)
        nd = nn(wqkv[...], dqkv)
        ag1[...] += nd * ehat
        lifted = nd * g1
        ed = md_low.astype(F32) + inv1 * (lifted - ehat * jnp.mean(lifted * ehat, axis=0, keepdims=True))
        hot = jnp.where(iota((CVOC, WIDE), 0).astype(F32) == ident, 1.0, 0.0).astype(LOW)
        atab[...] += nt(hot, ed.astype(LOW))
        return carry

    lax.fori_loop(0, n_turns, turn, 0)

    put(bundle, phase, plane_first, C_TABLE, atab[...], 128, 16)
    put(bundle, phase, plane_first, C_Q, aqkv[:, 0:CD], 128, 16)
    put(bundle, phase, plane_first, C_K, aqkv[:, CD:2 * CD], 128, 16)
    put(bundle, phase, plane_first, C_V, aqkv[:, 2 * CD:], 128, 16)
    put(bundle, phase, plane_first, C_O, ao[...], 128, 16)
    put(bundle, phase, plane_first, C_UP, aup_ref[...], 512, 16)
    cg1 = jnp.broadcast_to(jnp.sum(ag1[...], axis=1, keepdims=True), (CD, 8)).T[0:1]
    cg2 = gain2_ref[0:1]
    wg = wgains_ref[...]
    for d in range(SHARES):
        rows = [
            jnp.concatenate([cg1[:, d * 16:d * 16 + 16], jnp.zeros((1, 112), F32)], axis=1),
            jnp.concatenate([cg2[:, d * 16:d * 16 + 16], jnp.zeros((1, 112), F32)], axis=1),
            jnp.concatenate([wg[0:1, d * 32:d * 32 + 32], jnp.zeros((1, 96), F32)], axis=1),
            jnp.concatenate([wg[1:2, d * 32:d * 32 + 32], jnp.zeros((1, 96), F32)], axis=1),
            jnp.zeros((12, 128), F32),
        ]
        tile = jnp.concatenate(rows, axis=0).astype(LOW)
        bundle[0, plane_first(d), C_GAIN:C_GAIN + 16, :] = tile
        bundle[1, plane_first(d), C_GAIN:C_GAIN + 16, :] = tile
    stores = [
        pltpu.make_async_copy(bundle.at[0], keep_hbm, osem.at[0]),
        pltpu.make_async_copy(bundle.at[1], send_hbm, osem.at[1]),
    ]
    for s in stores:
        s.start()
    for s in stores:
        s.wait()


def kernel_f(
    xown_hbm, xg1, xg2, xg3, zown_hbm, zg1, zg2, zg3, cown_hbm, cg1, cg2, cg3, outk, outg,
    word_out, d_table, d_g1, d_q, d_k, d_v, d_o, d_g2, d_up, d_down, d_proj,
    e_g1, e_q, e_k, e_v, e_o, e_g2, e_up, e_down,
    xown, zown, cown, sem,
):
    phase = lax.axis_index("phase")
    dp = lax.axis_index("dp")
    plane, line = lax.rem(dp, 4), lax.div(dp, 4)
    loads = [
        pltpu.make_async_copy(xown_hbm.at[line], xown, sem.at[0]),
        pltpu.make_async_copy(zown_hbm.at[plane], zown, sem.at[1]),
        pltpu.make_async_copy(cown_hbm.at[line], cown, sem.at[2]),
    ]
    for load in loads:
        load.start()
    word_out[phase, 0] = outk[...]
    word_out[1 - phase, 0] = outg[...]
    for load in loads:
        load.wait()

    def total(own, parts, rows):
        t = own[rows].astype(F32)
        for p in parts:
            t = t + p[rows].astype(F32)
        return t

    def x(row, n):
        return total(xown, (xg1, xg2, xg3), slice(row, row + n))

    def z(row, n):
        return total(zown, (zg1, zg2, zg3), slice(row, row + n))

    def c(row, n):
        return total(cown, (cg1, cg2, cg3), slice(row, row + n))

    d_table[...] = c(C_TABLE, 16)
    d_q[...] = c(C_Q, 16)
    d_k[...] = c(C_K, 16)
    d_v[...] = c(C_V, 16)
    d_o[...] = c(C_O, 16)
    for i in range(4):
        d_up[:, i * 128:(i + 1) * 128] = c(C_UP + i * 16, 16)
        e_up[:, i * 256:(i + 1) * 256] = x(X_UP + i * 32, 32)
    gains = c(C_GAIN, 16)
    d_g1[...] = gains[0, :16]
    d_g2[...] = gains[1, :16]
    e_g1[...] = gains[2, :32]
    e_g2[...] = gains[3, :32]
    cd = x(X_CDOWN, 32)
    d_down[0:32] = cd[:, :128]
    d_down[32:64] = cd[:, 128:]
    d_proj[...] = z(Z_PROJ, 16)
    e_q[...] = x(X_Q, 32)
    e_k[...] = x(X_K, 32)
    e_v[...] = x(X_V, 32)
    e_o[...] = x(X_O, 32)
    e_down[...] = z(Z_DOWN, 128)


ANYWHERE = pl.BlockSpec(memory_space=pl.ANY)
INSIDE = pl.BlockSpec(memory_space=pltpu.VMEM)
SCALARS = pl.BlockSpec(memory_space=pltpu.SMEM)
shape = jax.ShapeDtypeStruct


def params():
    return pltpu.CompilerParams(vmem_limit_bytes=60 * 2**20)


def call_a(char_counts, char_ids, segment_ids, out_cotangent, weights):
    v = pltpu.VMEM
    return pl.pallas_call(
        kernel_a,
        out_shape=(
            shape((TURNS, KEPT_LOW, WIDE), LOW),
            shape((TURNS, CFF, WIDE), LOW),
            shape((TURNS, CD, WIDE), F32),
            shape((TURNS, 8, WIDE), F32),
            shape((1,), jnp.int32),
            shape((CD, WORDS), LOW),
            shape((SHARES, X_ROWS, 256), LOW),
            shape((SHARES, X_ROWS, 256), LOW),
            shape((SHARES, Z_ROWS, 256), LOW),
            shape((SHARES, Z_ROWS, 256), LOW),
            shape((WORDS, WD // 2), LOW),
            shape((WORDS, WD // 2), LOW),
            shape((8, WD), F32),
        ),
        in_specs=[INSIDE] * 3 + [ANYWHERE] + [INSIDE] * 10 + [INSIDE] + [ANYWHERE] * 4 + [INSIDE] + [ANYWHERE] * 2,
        out_specs=(ANYWHERE,) * 4 + (SCALARS, INSIDE) + (ANYWHERE,) * 4 + (INSIDE,) * 3,
        scratch_shapes=[
            v((WORDS, WD), LOW),
            v((WD, WD), LOW), v((WD, WD), LOW), v((WD, WD), LOW), v((WD, WD), LOW),
            v((WD, WFF), LOW), v((WFF, WD), LOW),
            v((CD, CVOC), LOW), v((3 * CD, CD), LOW), v((CD, CD), LOW), v((CFF, CD), LOW), v((128, 32), LOW),
            v((2, KEPT_ALL, WIDE), LOW), v((2, CD, WIDE), F32), v((2, 8, WIDE), F32),
            v((WORDS + WINDOW, CFF), F32), v((WORDS + WINDOW, CD), F32), v((16, WORDS), LOW),
            v((8, 128), jnp.int32), pltpu.SMEM((8, 128), jnp.int32),
            v((CFF, WIDE), F32), v((CFF, WIDE), LOW), v((CHAR_HEADS * SPAN, WIDE), LOW), v((8, WIDE), F32),
            v((2, SHARES, X_ROWS, 256), LOW), v((2, SHARES, Z_ROWS, 256), LOW),
            v((WORDS, WD), F32), v((WORDS, WD), F32),
            v((WORD_HEADS, WORDS, WORDS), LOW), v((WORDS, WFF), LOW), v((WORDS, WFF), LOW),
            pltpu.SemaphoreType.DMA((8,)),
            pltpu.SemaphoreType.DMA((4, 2)),
            pltpu.SemaphoreType.DMA((4,)),
        ],
        compiler_params=params(),
        cost_estimate=pl.CostEstimate(flops=200 * 10**9, bytes_accessed=60 * 10**6, transcendentals=10**6),
        name="forward_and_words",
    )(char_counts, char_ids, segment_ids, out_cotangent, *weights)


def call_b1(turns, gw, gain, up, down, kepts, keptm, kepti):
    v = pltpu.VMEM
    return pl.pallas_call(
        kernel_b1,
        out_shape=(shape((TURNS, CD, WIDE), LOW), shape((CD, CFF), LOW), shape((8, CD), F32)),
        in_specs=[SCALARS] + [INSIDE] * 4 + [ANYWHERE] * 3,
        out_specs=(ANYWHERE, INSIDE, INSIDE),
        scratch_shapes=[
            v((2, CFF, WIDE), LOW), v((2, CD, WIDE), F32), v((2, 8, WIDE), F32), v((2, CD, WIDE), LOW),
            v((CD, CFF), F32), v((CD, WIDE), F32),
            pltpu.SemaphoreType.DMA((3, 2)),
            pltpu.SemaphoreType.DMA((2,)),
        ],
        compiler_params=params(),
        cost_estimate=pl.CostEstimate(flops=200 * 10**9, bytes_accessed=20 * 10**6, transcendentals=10**6),
        name="character_backward_one",
    )(turns, gw, gain, up, down, kepts, keptm, kepti)


def call_b2(turns, wgains, gain2, aup, weights, keptl, keptd, kepti):
    v = pltpu.VMEM
    return pl.pallas_call(
        kernel_b2,
        out_shape=(shape((SHARES, C_ROWS, 128), LOW), shape((SHARES, C_ROWS, 128), LOW)),
        in_specs=[SCALARS] + [INSIDE] * 8 + [ANYWHERE] * 3,
        out_specs=(ANYWHERE, ANYWHERE),
        scratch_shapes=[
            v((2, KEPT_LOW, WIDE), LOW), v((2, 8, WIDE), F32), v((2, CD, WIDE), LOW),
            v((CHAR_HEADS * SPAN, WIDE), LOW),
            v((CD, 3 * CD), LOW),
            v((CD, 3 * CD), F32), v((CD, CD), F32), v((CVOC, CD), F32), v((CD, WIDE), F32),
            v((2, SHARES, C_ROWS, 128), LOW),
            pltpu.SemaphoreType.DMA((3, 2)),
            pltpu.SemaphoreType.DMA((2,)),
        ],
        compiler_params=params(),
        cost_estimate=pl.CostEstimate(flops=200 * 10**9, bytes_accessed=40 * 10**6, transcendentals=10**6),
        name="character_backward_two",
    )(turns, wgains, gain2, aup, *weights, keptl, keptd, kepti)


def call_f(x, z, c, outk, outg):
    v = pltpu.VMEM
    outs = ((CVOC, CD), (CD,), (CD, CD), (CD, CD), (CD, CD), (CD, CD), (CD,), (CD, CFF), (CFF, CD), (CD, WD),
            (WD,), (WD, WD), (WD, WD), (WD, WD), (WD, WD), (WD,), (WD, WFF), (WFF, WD))
    outs = [(s[0] // SHARES,) + tuple(n // 2 for n in s[1:]) for s in outs]
    return pl.pallas_call(
        kernel_f,
        out_shape=(shape((2, 1, WORDS, WD // 2), LOW),) + tuple(shape(s, F32) for s in outs),
        in_specs=([ANYWHERE] + [INSIDE] * 3) * 3 + [INSIDE] * 2,
        out_specs=(INSIDE,) * 19,
        scratch_shapes=[
            v((X_ROWS, 256), LOW), v((Z_ROWS, 256), LOW), v((C_ROWS, 128), LOW), pltpu.SemaphoreType.DMA((3,)),
        ],
        compiler_params=params(),
        name="finish",
    )(x[0], *x[1], z[0], *z[1], c[0], *c[1], outk, outg)


def flip(value, axis, bits):
    count = lax.axis_size(axis)
    return lax.ppermute(value, axis, [(i, i ^ bits) for i in range(count)])


def pick(value, index):
    return lax.dynamic_index_in_dim(value, index, 0, keepdims=False)


def plus(first, *others):
    total = first.astype(F32)
    for other in others:
        total = total + other.astype(F32)
    return total.astype(LOW)


def quarters(total, place):
    return [pick(total, lax.bitwise_xor(place, k)) for k in range(1, 4)]


def over_plane(parts):
    return [flip(part, "dp", k) for k, part in enumerate(parts, 1)]


def over_line(parts):
    return [flip(part, "dp", 4 * k) for k, part in enumerate(parts, 1)]


def after(value, *others):
    return lax.optimization_barrier((value,) + others)[0]


def body(
    char_ids, char_counts, segment_ids, out_cotangent,
    char_table, char_gain_one, char_query, char_key, char_value, char_output, char_gain_two, char_up, char_down,
    char_project,
    word_gain_one, word_query, word_key, word_value, word_output, word_gain_two, word_up, word_down,
):
    keptl, kepts, keptm, kepti, turns, gw, xkeep, xsend, zkeep, zsend, outk, outs, wgains = call_a(
        char_counts, char_ids, segment_ids, out_cotangent,
        (char_table, char_gain_one, char_query, char_key, char_value, char_output, char_gain_two, char_up, char_down,
         char_project,
         word_gain_one, word_query, word_key, word_value, word_output, word_gain_two, word_up, word_down),
    )
    fast = lax.axis_size("dp") == SHARES
    dp = lax.axis_index("dp")
    plane, line = lax.rem(dp, 4), lax.div(dp, 4)
    zgot, xgot, outg = flip(zsend, "phase", 1), flip(xsend, "phase", 1), flip(outs, "phase", 1)
    keptd, aup, gain2 = call_b1(turns, gw, char_gain_two, char_up, char_down, kepts, keptm, kepti)
    attention = (char_gain_one, char_query, char_key, char_value, char_output)
    if not fast:
        ckeep, csend = call_b2(turns, wgains, gain2, aup, attention, keptl, keptd, kepti)
        return general_sums(outk, outg, (xkeep, xgot), (zkeep, zgot), (ckeep, flip(csend, "phase", 1)))
    xgot, zgot = after(xgot, keptd), after(zgot, keptd)
    xsum = plus(xkeep, xgot).reshape(4, 4, X_ROWS, 256)
    zsum = plus(zkeep, zgot).reshape(4, 4, Z_ROWS, 256)
    xparts, zparts = quarters(xsum, plane), quarters(zsum, line)
    keptd = after(keptd, *xparts, *zparts)
    xparts, zparts = over_plane(xparts), over_line(zparts)
    ckeep, csend = call_b2(turns, wgains, gain2, aup, attention, keptl, keptd, kepti)
    ckeep, csend, xparts, zparts, xsum, zsum = lax.optimization_barrier((ckeep, csend, xparts, zparts, xsum, zsum))
    cgot = flip(csend, "phase", 1)
    xsum = plus(pick(xsum, plane), *xparts)
    zsum = plus(pick(zsum, line), *zparts)
    xparts = over_line(quarters(xsum, line))
    zparts = over_plane(quarters(zsum, plane))
    csum = plus(ckeep, cgot).reshape(4, 4, C_ROWS, 128)
    csum = plus(pick(csum, plane), *over_plane(quarters(csum, plane)))
    cparts = over_line(quarters(csum, line))
    return call_f((xsum, xparts), (zsum, zparts), (csum, cparts), outk, outg)


def general_sums(outk, outg, xs, zs, cs):
    first = lax.axis_index("phase") == 0
    outs = jnp.stack([jnp.where(first, outk, outg), jnp.where(first, outg, outk)])[:, None]
    order = jnp.asarray([plane_first(d) for d in range(SHARES)])

    def natural(pair):
        return pair[0].astype(F32) + pair[1].astype(F32)

    x, c = (jnp.take(natural(pair), order, axis=0) for pair in (xs, cs))
    z = natural(zs)

    def whole(rows):
        return rows.reshape(-1, rows.shape[-1])

    def wide(rows, pieces):
        n = rows.shape[1] // pieces
        return whole(rows.reshape(SHARES, pieces, n, rows.shape[-1]).transpose(0, 2, 1, 3).reshape(SHARES, n, -1))

    cdown = x[:, X_CDOWN:X_CDOWN + 32]
    cdown = jnp.concatenate([cdown[..., :128], cdown[..., 128:]], axis=1)
    parts = (
        whole(c[:, C_TABLE:C_TABLE + 16]), c[:, C_GAIN, :16].reshape(-1),
        whole(c[:, C_Q:C_Q + 16]), whole(c[:, C_K:C_K + 16]), whole(c[:, C_V:C_V + 16]), whole(c[:, C_O:C_O + 16]),
        c[:, C_GAIN + 1, :16].reshape(-1),
        wide(c[:, C_UP:C_UP + 64], 4), whole(cdown), whole(z[:, Z_PROJ:Z_PROJ + 16]),
        c[:, C_GAIN + 2, :32].reshape(-1),
        whole(x[:, X_Q:X_Q + 32]), whole(x[:, X_K:X_K + 32]), whole(x[:, X_V:X_V + 32]), whole(x[:, X_O:X_O + 32]),
        c[:, C_GAIN + 3, :32].reshape(-1),
        wide(x[:, X_UP:X_UP + 128], 4), whole(z[:, Z_DOWN:Z_DOWN + 128]),
    )
    return (outs,) + tuple(lax.psum_scatter(p, "dp", scatter_dimension=0, tiled=True) for p in parts)


def solution(mesh):
    rows = P(None, "dp", None)
    both = P("dp", "phase")
    one = P("dp")
    return jax.shard_map(
        body,
        mesh=mesh,
        in_specs=(rows, rows, rows, P(None, "dp", None, None)) + (P(),) * 18,
        out_specs=(
            P(None, "dp", None, "phase"),
            both, one, both, both, both, both, one, both, both, both,
            one, both, both, both, both, one, both, both,
        ),
        check_vma=False,
    )
```

```python
from functools import partial

import jax
import jax.numpy as jnp
from jax import lax
from jax.experimental import pallas as pl
from jax.experimental.pallas import tpu as pltpu
from jax.sharding import PartitionSpec as P

F32 = jnp.float32
LOW = jnp.bfloat16

CD = 256
CFF = 1024
CPW = 16
CVOC = 256
CHAR_HEADS = 4
HEAD = 64
WD = 512
WFF = 2048
WORD_HEADS = 8
WORDS = 256

SPAN = 256
STEP = 240
WIDE = 2 * SPAN
TURNS = ((WORDS * CPW - 1) // STEP + 2) // 2

epsilon = 1e-06
half_root = 0.7071067811865476
density = 0.3989422804014327
floor_score = -1e30
log2_e = 1.4426950408889634

R_EMB, R_Q, R_K, R_V, R_P, R_MIX = 0, 256, 512, 768, 1024, 2048
KEPT_LOW = 2304
I_INV1, I_INV2, I_IDENT, I_WORD = 0, 1, 2, 3
BAND = 144
WINDOW = 96

F_UP, F_DOWN = 0, 128
F_ROWS = 256
T_Q, T_K, T_V, T_O, T_CDOWN, T_PROJ = 0, 32, 64, 96, 128, 160
T_ROWS = 176
C_TABLE, C_Q, C_K, C_V, C_O, C_UP, C_GAIN = 0, 16, 32, 48, 64, 80, 144
C_ROWS = 160
SHARES = 16


def nn(left, right):
    return lax.dot_general(left, right, (((1,), (0,)), ((), ())), preferred_element_type=F32)


def nt(left, right):
    return lax.dot_general(left, right, (((1,), (1,)), ((), ())), preferred_element_type=F32)


def iota(shape, axis):
    return lax.broadcasted_iota(jnp.int32, shape, axis)


def eye(n):
    return iota((n, n), 0) == iota((n, n), 1)


def row_to_column(row):
    n = row.shape[1]
    return jnp.sum(jnp.where(eye(n), row, 0.0), axis=1, keepdims=True)


def gelu_pair(v):
    e = lax.erf(v * half_root)
    half = 0.5 * v
    bell = jnp.exp2(v * v * (-0.5 * log2_e))
    return half + half * e, 0.5 + 0.5 * e + (density * v) * bell


def gelu_twice(v):
    u = v * half_root
    whole = 1.0 + lax.erf(u)
    bell = jnp.exp2(u * u * (-log2_e))
    return v * whole, whole + (2.0 * density * v) * bell


def bits(d):
    return d % 2, d // 2 % 2, d // 4 % 2, d // 8


def plane_first(d, core=0):
    return (d % 4) * 4 + d // 4


def by_core(d, core):
    x, y, low, high = bits(d)
    return (y * 8 + x * 4 if core else x * 8 + y * 4) + low * 2 + high


def members(word, first, count, weight=1.0):
    return jnp.where((iota((count, WIDE), 0) + first).astype(F32) == word, weight, 0.0).astype(LOW)


def word_starts(counts_row):
    earlier = iota((WORDS, WORDS), 1) < iota((WORDS, WORDS), 0)
    return jnp.sum(jnp.where(earlier, counts_row, 0.0), axis=1, keepdims=True)


def column_to_row(column):
    return jnp.sum(jnp.where(eye(column.shape[0]), column, 0.0), axis=0, keepdims=True)


def put(bundle, phase, order, row, value, width, share_rows):
    low = value.astype(LOW)
    lanes = bundle.shape[-1]
    for half in range(2):
        side = jnp.bitwise_xor(phase, half)
        for piece in range(max(1, width // lanes)):
            take = min(width, lanes)
            cols = low[:, half * width + piece * lanes:half * width + piece * lanes + take]
            for i in range(value.shape[0] // share_rows):
                part = cols[i * share_rows:(i + 1) * share_rows]
                if take < lanes:
                    part = jnp.concatenate([part[:share_rows // 2], part[share_rows // 2:]], axis=1)
                m = part.shape[0]
                bundle[side, order(i, half), row + piece * share_rows:row + piece * share_rows + m, :] = part


def band(t):
    keys = slice(0, BAND) if t % 2 == 0 else slice(SPAN - BAND, SPAN)
    return t // 2, keys, slice(t * 128, (t + 1) * 128)


def two_heads(pair):
    zero = jnp.zeros((HEAD, pair.shape[1]), LOW)
    first = jnp.concatenate([pair[:HEAD], zero], axis=0)
    second = jnp.concatenate([zero, pair[HEAD:]], axis=0)
    return jnp.concatenate([first, second], axis=1)


def two_heads_rows(pair):
    left = iota(pair.shape, 1) < HEAD
    zero = jnp.zeros(pair.shape, LOW)
    return jnp.concatenate([jnp.where(left, pair, zero), jnp.where(left, zero, pair)], axis=0)


def softmax_keys(s):
    e = jnp.exp(s - jnp.max(s, axis=0, keepdims=True))
    return (e * (1.0 / jnp.sum(e, axis=0, keepdims=True))).astype(LOW)


def kernel_a(
    counts_hbm, ids_hbm, segs_hbm, cot_hbm,
    table_hbm, g1_hbm, wq_hbm, wk_hbm, wv_hbm, wo_hbm, g2_hbm, up_hbm, down_hbm, proj_hbm,
    wg1_hbm, wwq_hbm, wwk_hbm, wwv_hbm, wwo_hbm, wg2_hbm, wup_hbm, wdown_hbm,
    keptl_hbm, kepts_hbm, keptm_hbm, kepti_hbm, turns_ref,
    keep_hbm, send_hbm, outk_ref, outs_ref, gain_ref,
    q_ref, k_ref, v_ref, probs_ref, mixt_ref, normed_ref, xhat_ref, winv_ref, md_ref, pooled_ref, pa_ref,
    counts_ref, ids_ref, segs_ref,
    table_ref, g1_ref, wq_ref, wk_ref, wv_ref, wo_ref, g2_ref, up_ref, down_ref, proj_ref, wg1_ref, wg2_ref,
    cot, wwq, wwk, wwv, wwo, wup, wdown,
    tab_t, wqkv_t, wo_t, up_t, ids_t, slow, sslope, smid, sinfo, pa, pm, rowinfo, firsts_v, firsts, before_s, act_s, prob_s, found_s,
    next_s, mid_s, word_s,
    bundle, actw, slopew,
    csem, wsem, ksem, osem,
):
    phase = lax.axis_index("phase")
    tiny = [
        pltpu.make_async_copy(src.at[phase], dst, csem.at[12 + i])
        for i, (src, dst) in enumerate(((counts_hbm, counts_ref), (ids_hbm, ids_ref), (segs_hbm, segs_ref)))
    ]
    for load in tiny:
        load.start()
    early = [
        pltpu.make_async_copy(src, dst, csem.at[i])
        for i, (src, dst) in enumerate(
            ((g1_hbm, g1_ref), (g2_hbm, g2_ref), (table_hbm, table_ref), (wq_hbm, wq_ref), (wk_hbm, wk_ref),
             (wv_hbm, wv_ref), (wo_hbm, wo_ref), (up_hbm, up_ref), (down_hbm, down_ref), (proj_hbm, proj_ref),
             (wg1_hbm, wg1_ref), (wg2_hbm, wg2_ref))
        )
    ]
    for load in early:
        load.start()
    loads = [
        pltpu.make_async_copy(src, dst, wsem.at[i])
        for i, (src, dst) in enumerate(
            ((wwq_hbm, wwq), (wwk_hbm, wwk), (wwv_hbm, wwv), (wwo_hbm, wwo),
             (wup_hbm, wup), (wdown_hbm, wdown), (cot_hbm.at[phase, 0], cot))
        )
    ]
    for load in tiny:
        load.wait()
    counts_row = counts_ref[...].astype(F32)
    starts = word_starts(counts_row)
    counts = row_to_column(counts_row)
    blocks = jnp.floor((starts + 0.5) * (1.0 / STEP))
    places = starts + (SPAN - STEP) * blocks
    n_turns = jnp.max(places).astype(jnp.int32) // WIDE + 1
    turns_ref[0] = n_turns
    bases = (iota((1, 128), 1) * WIDE).astype(F32)
    first = jnp.sum(jnp.where(places < bases, 1.0, 0.0), axis=0, keepdims=True)
    firsts_v[...] = jnp.broadcast_to(first, (8, 128)).astype(jnp.int32)
    first_copy = pltpu.make_async_copy(firsts_v, firsts, wsem.at[7])
    first_copy.start()
    ids = ids_ref[...]
    ids_t[...] = jnp.concatenate(
        [ids[:, 128 * a:128 * a + 128] for a in range(32)], axis=0
    ).astype(F32).T.astype(LOW)
    places_row = column_to_row(places)
    none = jnp.zeros((1, 1), F32)
    rowinfo[...] = jnp.concatenate(
        [places_row - jnp.concatenate([none, places_row[:, :-1]], axis=1),
         counts_row - jnp.concatenate([none, counts_row[:, :-1]], axis=1),
         jnp.ones((1, WORDS), F32), jnp.zeros((13, WORDS), F32)], axis=0
    ).astype(LOW)
    pa[...] = jnp.zeros_like(pa)
    pm[...] = jnp.zeros_like(pm)
    for load in early:
        load.wait()
    for load in loads:
        load.start()
    tab_t[...] = table_ref[...].T
    wqkv_t[0:CD] = (wq_ref[...] * 0.125).T
    wqkv_t[CD:2 * CD] = wk_ref[...].T
    wqkv_t[2 * CD:] = wv_ref[...].T
    wo_t[...] = wo_ref[...].T
    up_t[...] = up_ref[...].T
    g1 = row_to_column(g1_ref[...].astype(F32)[None, :])
    g2 = row_to_column(g2_ref[...].astype(F32)[None, :])
    prob_s[...] = jnp.zeros_like(prob_s)
    for slot in range(2):
        slow[slot, R_P:R_P + CHAR_HEADS * SPAN] = jnp.zeros((CHAR_HEADS * SPAN, WIDE), LOW)
    first_copy.wait()

    def find(turn):
        place = (iota((1, WIDE), 1) + turn * WIDE).astype(F32)
        begun = jnp.where(places <= place, 1.0, 0.0).astype(LOW)
        info = nn(rowinfo[...], begun)
        word = info[2:3] - 1.0
        slot = place - info[0:1]
        flat = (word * 16.0 + slot).astype(jnp.int32)
        chosen = jnp.where(iota((32, WIDE), 0) == (flat >> 7), 1.0, 0.0).astype(LOW)
        lanes = nn(ids_t[...], chosen)
        ident = jnp.sum(jnp.where(iota((128, WIDE), 0) == (flat & 127), lanes, 0.0), axis=0, keepdims=True)
        valid = slot < info[1:2]
        none = jnp.full((6, WIDE), -1.0, F32)
        return jnp.concatenate([jnp.where(valid, ident, -1.0), jnp.where(valid, word, -1.0), none], axis=0)

    found_s[...] = find(jnp.int32(0))

    def copies(b):
        slot = lax.rem(b, 2)
        return (
            pltpu.make_async_copy(slow.at[slot], keptl_hbm.at[b], ksem.at[0, slot]),
            pltpu.make_async_copy(sslope.at[slot], kepts_hbm.at[b], ksem.at[1, slot]),
            pltpu.make_async_copy(smid.at[slot], keptm_hbm.at[b], ksem.at[2, slot]),
            pltpu.make_async_copy(sinfo.at[slot], kepti_hbm.at[b], ksem.at[3, slot]),
        )

    def start(copies):
        for c in copies:
            c.start()

    def wait(copies):
        for c in copies:
            c.wait()

    def near_words(b):
        first = (firsts[0, b] // 16) * 16
        return first, (firsts[0, b + 1] - first + WINDOW - 1) // WINDOW

    def window(first):
        return pl.ds(pl.multiple_of(first, 16), WINDOW)

    def attend(b):
        slot = lax.rem(b, 2)
        ident = found_s[0:1]
        word = found_s[1:2]
        hot = jnp.where(iota((CVOC, WIDE), 0).astype(F32) == ident, 1.0, 0.0).astype(LOW)
        emb = nn(tab_t[...], hot)
        inv1 = lax.rsqrt(jnp.mean(emb * emb, axis=0, keepdims=True) + epsilon)
        normed = (emb * inv1 * g1).astype(LOW)
        yield
        qkv = nn(wqkv_t[...], normed).astype(LOW)
        key_rows = [qkv[CD:2 * CD, u * SPAN:(u + 1) * SPAN].T for u in range(2)]
        value_t = qkv[2 * CD:]
        word_col = jnp.broadcast_to(jnp.where(word < 0.0, -2.0, word), (8, WIDE)).T[:, 0:1]
        yield
        for t in range(4):
            u, ks, ql = band(t)
            bias = jnp.where(word_col[u * SPAN + ks.start:u * SPAN + ks.stop] == word[:, ql], 0.0, floor_score)
            for pair in range(CHAR_HEADS // 2):
                fs = slice(pair * 128, pair * 128 + 128)
                s = nn(key_rows[u][ks, fs], two_heads(qkv[fs, ql]))
                for i in range(2):
                    p = softmax_keys(s[:, i * 128:i * 128 + 128] + bias)
                    row = (pair * 2 + i) * SPAN
                    prob_s[row + ks.start:row + ks.stop, ql] = p
                    slow[slot, R_P + row + ks.start:R_P + row + ks.stop, ql] = p
                yield
        slow[slot, R_EMB:R_EMB + CD] = emb.astype(LOW)
        slow[slot, R_Q:R_Q + 2 * CD] = qkv[:2 * CD]
        for u in range(2):
            us = slice(u * SPAN, (u + 1) * SPAN)
            slow[slot, R_V:R_V + SPAN, us] = value_t[:, us].T
        mixed = []
        for h in range(CHAR_HEADS):
            hs = slice(h * HEAD, (h + 1) * HEAD)
            both = []
            for u in range(2):
                us = slice(u * SPAN, (u + 1) * SPAN)
                both.append(nn(value_t[hs, us], prob_s[h * SPAN:(h + 1) * SPAN, us]).astype(LOW))
            mixed.append(jnp.concatenate(both, axis=1))
        mixed = jnp.concatenate(mixed, axis=0)
        slow[slot, R_MIX:R_MIX + CD] = mixed
        yield
        middle = emb + nn(wo_t[...], mixed)
        inv2 = lax.rsqrt(jnp.mean(middle * middle, axis=0, keepdims=True) + epsilon)
        smid[slot] = middle
        sinfo[slot] = jnp.concatenate([inv1, inv2, ident, word, jnp.zeros((4, WIDE), F32)], axis=0)
        normed_two = (middle * inv2 * g2).astype(LOW)
        yield
        first, _ = near_words(b)
        near = members(word, first, WINDOW)
        middle_low = middle.astype(LOW)
        pm[window(first), :] += nt(near, middle_low)
        mid_s[...] = middle_low
        next_s[...] = normed_two
        word_s[0:1] = word
        found_s[...] = find(b + 1)
        yield

    def feed(b):
        slot = lax.rem(b, 2)
        word = word_s[0:1]
        before_s[...] = nn(up_t[...], next_s[...])
        yield
        for c in range(CFF // 32):
            cs = slice(c * 32, (c + 1) * 32)
            act, slope = gelu_twice(before_s[cs])
            sslope[slot, cs] = slope.astype(LOW)
            act_s[cs] = act.astype(LOW)
            if c % 4 == 3:
                yield
        first, _ = near_words(b)
        pa[window(first), :] += nt(members(word, first, WINDOW, 0.5), act_s[...])
        yield

    def run(*parts):
        parts = list(parts)
        while parts:
            for part in tuple(parts):
                if next(part, parts) is parts:
                    parts.remove(part)

    def turn(b, carry):
        @pl.when(b >= 2)
        def _():
            wait(copies(b - 2))

        run(attend(b))
        run(feed(b))
        first, windows = near_words(b)

        def more(i, carry):
            at = first + i * WINDOW
            pm[window(at), :] += nt(members(word_s[0:1], at, WINDOW), mid_s[...])
            pa[window(at), :] += nt(members(word_s[0:1], at, WINDOW, 0.5), act_s[...])
            return carry

        lax.fori_loop(1, windows, more, 0)
        start(copies(b))
        return carry

    lax.fori_loop(0, n_turns, turn, 0)

    pa_hi = pa[0:WORDS].astype(LOW)
    pa_lo = (pa[0:WORDS] - pa_hi.astype(F32)).astype(LOW)
    per_count = 1.0 / counts
    pooled = (pm[0:WORDS] + nn(pa_hi, down_ref[...]) + nn(pa_lo, down_ref[...])) * per_count
    pooled_low = pooled.astype(LOW)
    pooled_ref[...] = pooled_low
    pa_ref[...] = pa_hi
    x = nn(pooled_low, proj_ref[...]).astype(LOW).astype(F32)
    for load in loads:
        load.wait()
    wg1 = wg1_ref[...].astype(F32)[None, :]
    wg2 = wg2_ref[...].astype(F32)[None, :]
    winv1 = lax.rsqrt(jnp.mean(x * x, axis=1, keepdims=True) + epsilon)
    xhat = x * winv1
    normed = (xhat * wg1).astype(LOW)
    xhat_ref[...] = xhat
    winv_ref[...] = jnp.broadcast_to(winv1, (WORDS, 128))
    normed_ref[...] = normed
    q = (nn(normed, wwq[...]) * 0.125).astype(LOW)
    k = nn(normed, wwk[...]).astype(LOW)
    v = nn(normed, wwv[...]).astype(LOW)
    seg_row = segs_ref[...].astype(F32)
    seg_col = row_to_column(seg_row)
    allowed = (seg_row == seg_col) & (iota((WORDS, WORDS), 0) <= iota((WORDS, WORDS), 1))
    bias = jnp.where(allowed, 0.0, floor_score)
    q_ref[...] = q
    k_ref[...] = k
    v_ref[...] = v
    v_t = v.T
    for h in range(WORD_HEADS):
        probs_ref[h, 128:, 0:128] = jnp.zeros((128, 128), LOW)
    for t in range(2):
        ks, ql = slice(0, 128 * (t + 1)), slice(128 * t, 128 * (t + 1))
        for pair in range(WORD_HEADS // 2):
            fs = slice(pair * 128, pair * 128 + 128)
            s = nt(k[ks, fs], two_heads_rows(q[ql, fs]))
            for i in range(2):
                probs_ref[pair * 2 + i, ks, ql] = softmax_keys(s[:, i * 128:i * 128 + 128] + bias[ks, ql])
    mixed_t = jnp.concatenate(
        [nn(v_t[h * HEAD:(h + 1) * HEAD], probs_ref[h]).astype(LOW) for h in range(WORD_HEADS)], axis=0
    )
    mixt_ref[...] = mixed_t
    middle = x + nn(mixed_t.T, wwo[...])
    winv2 = lax.rsqrt(jnp.mean(middle * middle, axis=1, keepdims=True) + epsilon)
    normed_two = (middle * winv2 * wg2).astype(LOW)
    result = middle
    for c in range(WFF // 512):
        cs = slice(c * 512, (c + 1) * 512)
        act, slope = gelu_pair(nn(normed_two, wup[:, cs]))
        act = act.astype(LOW)
        actw[:, cs] = act
        slopew[:, cs] = slope.astype(LOW)
        result = result + nn(act, wdown[cs, :])
    result = result.astype(LOW)
    front = phase == 0
    outk_ref[...] = jnp.where(front, result[:, :256], result[:, 256:])
    outs_ref[...] = jnp.where(front, result[:, 256:], result[:, :256])

    cot_low = cot[...]
    n2d = jnp.zeros((WORDS, WD), F32)
    n2_t = normed_two.T
    for c in range(WFF // 512):
        cs = slice(c * 512, (c + 1) * 512)
        gd = nn(actw[:, cs].T, cot_low)
        put(bundle, phase, lambda i, p: by_core(c * 4 + i, p), F_DOWN, gd, 256, 128)
        bd = (nt(cot_low, wdown[cs, :]) * slopew[:, cs].astype(F32)).astype(LOW)
        gu = nn(n2_t, bd).astype(LOW)
        side = jnp.bitwise_xor(phase, c // 2)
        for piece in range(2):
            row = F_UP + ((c % 2) * 2 + piece) * 32
            for d in range(SHARES):
                bundle[side, by_core(d, c // 2), row:row + 32, :] = gu[d * 32:(d + 1) * 32, piece * 256:piece * 256 + 256]
        n2d = n2d + nt(bd, wup[:, cs])
    stores = [
        pltpu.make_async_copy(bundle.at[0], keep_hbm, osem.at[0]),
        pltpu.make_async_copy(bundle.at[1], send_hbm, osem.at[1]),
    ]
    for s in stores:
        s.start()
    vhat = middle * winv2
    gain_ref[...] = jnp.broadcast_to(jnp.sum(n2d * vhat, axis=0, keepdims=True), (8, WD))
    lifted = n2d * wg2
    md_ref[...] = cot[...].astype(F32) + winv2 * (lifted - vhat * jnp.mean(lifted * vhat, axis=1, keepdims=True))

    def drain(b, carry):
        wait(copies(b))
        return carry

    lax.fori_loop(jnp.maximum(n_turns - 2, 0), n_turns, drain, 0)
    for s in stores:
        s.wait()


def kernel_a2(
    counts_ref, q_ref, k_ref, v_ref, pw, mixt_ref, normed_ref, xhat_ref, winv_ref, md_ref, pooled_ref, pa_ref,
    wg1_ref, proj_ref, wwq_hbm, wwk_hbm, wwv_hbm, wwo_hbm,
    gw_ref, keep_hbm, send_hbm, gain_ref,
    wwq, wwk, wwv, wwo, bundle, wsem, osem,
):
    phase = lax.axis_index("phase")
    loads = [
        pltpu.make_async_copy(src, dst, wsem.at[i])
        for i, (src, dst) in enumerate(((wwo_hbm, wwo), (wwq_hbm, wwq), (wwk_hbm, wwk), (wwv_hbm, wwv)))
    ]
    for load in loads:
        load.start()
    wg1 = wg1_ref[...].astype(F32)[None, :]
    q, k, v, normed, pooled_low = q_ref[...], k_ref[...], v_ref[...], normed_ref[...], pooled_ref[...]
    per_count = 1.0 / row_to_column(counts_ref[phase].astype(F32))
    md = md_ref[...]
    md_low = md.astype(LOW)
    put(bundle, phase, by_core, T_O, nn(mixt_ref[...], md_low), 256, 32)
    k_t = k.T
    loads[0].wait()
    do = nt(md_low, wwo[...]).astype(LOW)
    dq_t, dk, dv = [], [], []
    left = iota((WORDS, 128), 1) < HEAD
    for pair in range(WORD_HEADS // 2):
        fs = slice(pair * 128, pair * 128 + 128)
        ds = []
        for t in range(2):
            ks, ql = slice(0, 128 * (t + 1)), slice(128 * t, 128 * (t + 1))
            dp = nt(v[ks, fs], two_heads_rows(do[ql, fs]))
            for i in range(2):
                pf = pw[pair * 2 + i, ks, ql].astype(F32)
                dph = dp[:, i * 128:i * 128 + 128]
                d = (pf * (dph - jnp.sum(pf * dph, axis=0, keepdims=True))).astype(LOW)
                ds.append(d if t else jnp.concatenate([d, jnp.zeros((128, 128), LOW)], axis=0))
        both = [jnp.concatenate([ds[i], ds[i + 2]], axis=1) for i in range(2)]
        for i in range(2):
            h = pair * 2 + i
            dq_t.append(nn(k_t[h * HEAD:(h + 1) * HEAD], both[i]))
        dk.append(jnp.where(left, nn(both[0], q[:, fs]), nn(both[1], q[:, fs])).astype(LOW))
        dv.append(jnp.where(left, nn(pw[pair * 2], do[:, fs]), nn(pw[pair * 2 + 1], do[:, fs])).astype(LOW))
    dq = (jnp.concatenate(dq_t, axis=0) * 0.125).astype(LOW).T
    dk = jnp.concatenate(dk, axis=1)
    dv = jnp.concatenate(dv, axis=1)
    normed_t = normed.T
    for load in loads[1:]:
        load.wait()
    nd = nt(dq, wwq[...]) + nt(dk, wwk[...]) + nt(dv, wwv[...])
    put(bundle, phase, by_core, T_Q, nn(normed_t, dq), 256, 32)
    put(bundle, phase, by_core, T_K, nn(normed_t, dk), 256, 32)
    put(bundle, phase, by_core, T_V, nn(normed_t, dv), 256, 32)
    vhat = xhat_ref[...]
    gain_ref[...] = jnp.broadcast_to(jnp.sum(nd * vhat, axis=0, keepdims=True), (8, WD))
    lifted = nd * wg1
    xd = md + winv_ref[:, 0:1] * (lifted - vhat * jnp.mean(lifted * vhat, axis=1, keepdims=True))
    vd = xd.astype(LOW)
    put(bundle, phase, by_core, T_PROJ, nn(pooled_low.T, vd), 256, 16)
    gw = (nt(vd, proj_ref[...]) * per_count).astype(LOW)
    gw_ref[...] = gw.T
    put(bundle, phase, by_core, T_CDOWN, nn(pa_ref[...].T, gw), 128, 64)
    stores = [
        pltpu.make_async_copy(bundle.at[0], keep_hbm, osem.at[0]),
        pltpu.make_async_copy(bundle.at[1], send_hbm, osem.at[1]),
    ]
    for s in stores:
        s.start()
    for s in stores:
        s.wait()


def kernel_b1(
    turns_ref, gw_ref, g2_ref, up_ref, down_ref, kepts_hbm, keptm_hbm, kepti_hbm,
    keptd_hbm, aup_ref, gain_ref,
    sslope, smid, sinfo, sdelta, aup, ag2, down, ksem, dsem,
):
    n_turns = turns_ref[0]

    def kept_copies(b, slot):
        return (
            pltpu.make_async_copy(kepts_hbm.at[b], sslope.at[slot], ksem.at[0, slot]),
            pltpu.make_async_copy(keptm_hbm.at[b], smid.at[slot], ksem.at[1, slot]),
            pltpu.make_async_copy(kepti_hbm.at[b], sinfo.at[slot], ksem.at[2, slot]),
        )

    def delta_copy(b, slot):
        return pltpu.make_async_copy(sdelta.at[slot], keptd_hbm.at[b], dsem.at[slot])

    for c in kept_copies(0, 0):
        c.start()
    g2 = row_to_column(g2_ref[...].astype(F32)[None, :])
    down[...] = down_ref[...] * 0.5
    aup[...] = jnp.zeros_like(aup)
    ag2[...] = jnp.zeros_like(ag2)

    def turn(b, carry):
        slot = lax.rem(b, 2)

        @pl.when(b + 1 < n_turns)
        def _():
            for c in kept_copies(b + 1, 1 - slot):
                c.start()

        @pl.when(b >= 2)
        def _():
            delta_copy(b - 2, slot).wait()

        for c in kept_copies(b, slot):
            c.wait()
        inv2 = sinfo[slot, I_INV2:I_INV2 + 1]
        g_low = nn(gw_ref[...], members(sinfo[slot, I_WORD:I_WORD + 1], 0, WORDS)).astype(LOW)
        vhat = smid[slot] * inv2
        normed_two = (vhat * g2).astype(LOW)
        n2d = jnp.zeros((CD, WIDE), F32)
        for c in range(CFF // 256):
            cs = slice(c * 256, (c + 1) * 256)
            bd = (nn(down[cs, :], g_low) * sslope[slot, cs].astype(F32)).astype(LOW)
            aup[:, cs] += nt(normed_two, bd)
            n2d = n2d + nn(up_ref[:, cs], bd)
        ag2[...] += n2d * vhat
        lifted = n2d * g2
        md = g_low.astype(F32) + inv2 * (lifted - vhat * jnp.mean(lifted * vhat, axis=0, keepdims=True))
        sdelta[slot] = md.astype(LOW)
        delta_copy(b, slot).start()
        return carry

    lax.fori_loop(0, n_turns, turn, 0)
    aup_ref[...] = aup[...].astype(LOW)
    gain_ref[...] = jnp.broadcast_to(jnp.sum(ag2[...], axis=1, keepdims=True), (CD, 8)).T

    def drain(b, carry):
        delta_copy(b, lax.rem(b, 2)).wait()
        return carry

    lax.fori_loop(jnp.maximum(n_turns - 2, 0), n_turns, drain, 0)


def kernel_b2(
    turns_ref, wgain1_ref, wgain2_ref, gain2_ref, aup_ref, g1_ref, wq_ref, wk_ref, wv_ref, wo_ref,
    keptl_hbm, keptd_hbm, kepti_hbm,
    keep_hbm, send_hbm,
    slow, sinfo, sdelta, dscore, wqkv, aqkv, ao, atab, ag1, bundle, ksem, osem,
):
    phase = lax.axis_index("phase")
    n_turns = turns_ref[0]

    def kept_copies(b, slot):
        return (
            pltpu.make_async_copy(keptl_hbm.at[b], slow.at[slot], ksem.at[0, slot]),
            pltpu.make_async_copy(keptd_hbm.at[b], sdelta.at[slot], ksem.at[1, slot]),
            pltpu.make_async_copy(kepti_hbm.at[b], sinfo.at[slot], ksem.at[2, slot]),
        )

    for c in kept_copies(0, 0):
        c.start()
    g1 = row_to_column(g1_ref[...].astype(F32)[None, :])
    for i, w in enumerate((wq_ref, wk_ref, wv_ref)):
        wqkv[:, i * CD:(i + 1) * CD] = w[...]
    for acc in (aqkv, ao, atab, ag1, dscore):
        acc[...] = jnp.zeros_like(acc)

    def turn(b, carry):
        slot = lax.rem(b, 2)

        @pl.when(b + 1 < n_turns)
        def _():
            for c in kept_copies(b + 1, 1 - slot):
                c.start()

        for c in kept_copies(b, slot):
            c.wait()
        inv1 = sinfo[slot, I_INV1:I_INV1 + 1]
        ident = sinfo[slot, I_IDENT:I_IDENT + 1]
        md_low = sdelta[slot]
        ao[...] += nt(slow[slot, R_MIX:R_MIX + CD], md_low)
        do = nn(wo_ref[...], md_low).astype(LOW)
        for t in range(4):
            u, ks, ql = band(t)
            for pair in range(CHAR_HEADS // 2):
                fs = slice(u * SPAN + pair * 128, u * SPAN + pair * 128 + 128)
                dp = nn(
                    slow[slot, R_V + ks.start:R_V + ks.stop, fs], two_heads(do[pair * 128:pair * 128 + 128, ql])
                )
                for i in range(2):
                    row = (pair * 2 + i) * SPAN
                    pf = slow[slot, R_P + row + ks.start:R_P + row + ks.stop, ql].astype(F32)
                    dph = dp[:, i * 128:i * 128 + 128]
                    d = pf * (dph - jnp.sum(pf * dph, axis=0, keepdims=True))
                    dscore[row + ks.start:row + ks.stop, ql] = d.astype(LOW)
        dq, dk, dv = [], [], []
        for h in range(CHAR_HEADS):
            hs = slice(h * HEAD, (h + 1) * HEAD)
            one, two, three = [], [], []
            for u in range(2):
                us = slice(u * SPAN, (u + 1) * SPAN)
                p = slow[slot, R_P + h * SPAN:R_P + (h + 1) * SPAN, us]
                ds = dscore[h * SPAN:(h + 1) * SPAN, us]
                one.append((nn(slow[slot, R_K + h * HEAD:R_K + (h + 1) * HEAD, us], ds) * 0.125).astype(LOW))
                two.append(nt(slow[slot, R_Q + h * HEAD:R_Q + (h + 1) * HEAD, us], ds).astype(LOW))
                three.append(nt(do[hs, us], p).astype(LOW))
            for part, pair in ((dq, one), (dk, two), (dv, three)):
                part.append(jnp.concatenate(pair, axis=1))
        dqkv = jnp.concatenate(dq + dk + dv, axis=0)
        emb = slow[slot, R_EMB:R_EMB + CD].astype(F32)
        ehat = emb * inv1
        normed = (ehat * g1).astype(LOW)
        aqkv[...] += nt(normed, dqkv)
        nd = nn(wqkv[...], dqkv)
        ag1[...] += nd * ehat
        lifted = nd * g1
        ed = md_low.astype(F32) + inv1 * (lifted - ehat * jnp.mean(lifted * ehat, axis=0, keepdims=True))
        hot = jnp.where(iota((CVOC, WIDE), 0).astype(F32) == ident, 1.0, 0.0).astype(LOW)
        atab[...] += nt(hot, ed.astype(LOW))
        return carry

    lax.fori_loop(0, n_turns, turn, 0)

    put(bundle, phase, plane_first, C_TABLE, atab[...], 128, 16)
    put(bundle, phase, plane_first, C_Q, aqkv[:, 0:CD], 128, 16)
    put(bundle, phase, plane_first, C_K, aqkv[:, CD:2 * CD], 128, 16)
    put(bundle, phase, plane_first, C_V, aqkv[:, 2 * CD:], 128, 16)
    put(bundle, phase, plane_first, C_O, ao[...], 128, 16)
    put(bundle, phase, plane_first, C_UP, aup_ref[...], 512, 16)
    cg1 = jnp.broadcast_to(jnp.sum(ag1[...], axis=1, keepdims=True), (CD, 8)).T[0:1]
    cg2 = gain2_ref[0:1]
    for d in range(SHARES):
        rows = [
            jnp.concatenate([cg1[:, d * 16:d * 16 + 16], jnp.zeros((1, 112), F32)], axis=1),
            jnp.concatenate([cg2[:, d * 16:d * 16 + 16], jnp.zeros((1, 112), F32)], axis=1),
            jnp.concatenate([wgain1_ref[0:1, d * 32:d * 32 + 32], jnp.zeros((1, 96), F32)], axis=1),
            jnp.concatenate([wgain2_ref[0:1, d * 32:d * 32 + 32], jnp.zeros((1, 96), F32)], axis=1),
            jnp.zeros((12, 128), F32),
        ]
        tile = jnp.concatenate(rows, axis=0).astype(LOW)
        bundle[0, plane_first(d), C_GAIN:C_GAIN + 16, :] = tile
        bundle[1, plane_first(d), C_GAIN:C_GAIN + 16, :] = tile
    stores = [
        pltpu.make_async_copy(bundle.at[0], keep_hbm, osem.at[0]),
        pltpu.make_async_copy(bundle.at[1], send_hbm, osem.at[1]),
    ]
    for s in stores:
        s.start()
    for s in stores:
        s.wait()


def kernel_f(
    f0, f1, f2, f3, f4, f5, t0, t1, t2, t3, t4, t5, c0, c1, c2, c3, c4, c5, c6, c7, outk, outg,
    word_out, d_table, d_g1, d_q, d_k, d_v, d_o, d_g2, d_up, d_down, d_proj,
    e_g1, e_q, e_k, e_v, e_o, e_g2, e_up, e_down,
    fs, ts, cs, sem,
):
    phase = lax.axis_index("phase")
    dp = lax.axis_index("dp")
    x, y, low, high = (lax.rem(lax.div(dp, n), 2) for n in (1, 2, 4, 8))
    a, b = jnp.where(phase == 0, x, y), jnp.where(phase == 0, y, x)
    loads = []
    at = a * 8 + b * 4 + low * 2 + high
    line = lax.div(dp, 4)
    both = (at, at, lax.rem(at, 8), lax.rem(at, 4), lax.rem(at, 2), 0)
    place = lax.rem(dp, 4) * 4 + line
    for i, (parts, places, here) in enumerate((
        ((f0, f1, f2, f3, f4, f5), both, fs),
        ((t0, t1, t2, t3, t4, t5), both, ts),
        ((c0, c1, c2, c3, c4), (place, place, line, line, line), cs),
    )):
        for j, (part, n) in enumerate(zip(parts, places)):
            loads.append(pltpu.make_async_copy(part.at[n], here.at[j], sem.at[i]))
    for j, part in enumerate((c5, c6, c7)):
        loads.append(pltpu.make_async_copy(part, cs.at[5 + j], sem.at[2]))
    for load in loads:
        load.start()
    word_out[phase, 0] = outk[...]
    word_out[1 - phase, 0] = outg[...]
    for load in loads:
        load.wait()

    def total(parts, row, n):
        t = parts[0, row:row + n].astype(F32) + parts[1, row:row + n].astype(F32)
        for j in range(2, parts.shape[0]):
            t = t + parts[j, row:row + n].astype(F32)
        return t

    f, t, c = partial(total, fs), partial(total, ts), partial(total, cs)
    d_table[...] = c(C_TABLE, 16)
    d_q[...] = c(C_Q, 16)
    d_k[...] = c(C_K, 16)
    d_v[...] = c(C_V, 16)
    d_o[...] = c(C_O, 16)
    for i in range(4):
        d_up[:, i * 128:(i + 1) * 128] = c(C_UP + i * 16, 16)
        e_up[:, i * 256:(i + 1) * 256] = f(F_UP + i * 32, 32)
    gains = c(C_GAIN, 16)
    d_g1[...] = gains[0, :16]
    d_g2[...] = gains[1, :16]
    e_g1[...] = gains[2, :32]
    e_g2[...] = gains[3, :32]
    cd = t(T_CDOWN, 32)
    d_down[0:32] = cd[:, :128]
    d_down[32:64] = cd[:, 128:]
    d_proj[...] = t(T_PROJ, 16)
    e_q[...] = t(T_Q, 32)
    e_k[...] = t(T_K, 32)
    e_v[...] = t(T_V, 32)
    e_o[...] = t(T_O, 32)
    e_down[...] = f(F_DOWN, 128)


ANYWHERE = pl.BlockSpec(memory_space=pltpu.HBM)
INSIDE = pl.BlockSpec(memory_space=pltpu.VMEM)
SCALARS = pl.BlockSpec(memory_space=pltpu.SMEM)
shape = jax.ShapeDtypeStruct


def params(mib):
    return pltpu.CompilerParams(vmem_limit_bytes=mib * 2**20)


def outside(dims, dtype):
    return pltpu.HBM(dims, dtype)


def kept_outside(*values):
    return tuple(pltpu.with_memory_space_constraint(v, pltpu.HBM) for v in values)


def call_a(char_counts, char_ids, segment_ids, out_cotangent, weights):
    v = pltpu.VMEM
    return pl.pallas_call(
        kernel_a,
        out_shape=(
            outside((TURNS, KEPT_LOW, WIDE), LOW),
            outside((TURNS, CFF, WIDE), LOW),
            outside((TURNS, CD, WIDE), F32),
            outside((TURNS, 8, WIDE), F32),
            shape((1,), jnp.int32),
            outside((SHARES, F_ROWS, 256), LOW),
            outside((SHARES, F_ROWS, 256), LOW),
            shape((WORDS, WD // 2), LOW),
            shape((WORDS, WD // 2), LOW),
            shape((8, WD), F32),
            shape((WORDS, WD), LOW), shape((WORDS, WD), LOW), shape((WORDS, WD), LOW),
            shape((WORD_HEADS, WORDS, WORDS), LOW), shape((WD, WORDS), LOW), shape((WORDS, WD), LOW),
            shape((WORDS, WD), F32), shape((WORDS, 128), F32), shape((WORDS, WD), F32),
            shape((WORDS, CD), LOW), shape((WORDS, CFF), LOW),
        ),
        in_specs=[ANYWHERE] * 22,
        out_specs=(ANYWHERE,) * 4 + (SCALARS,) + (ANYWHERE,) * 2 + (INSIDE,) * 14,
        scratch_shapes=[
            v((1, WORDS), jnp.int32), v((1, WORDS * CPW), jnp.int32), v((1, WORDS), jnp.int32),
            v((CVOC, CD), LOW), v((CD,), LOW), v((CD, CD), LOW), v((CD, CD), LOW), v((CD, CD), LOW), v((CD, CD), LOW),
            v((CD,), LOW), v((CD, CFF), LOW), v((CFF, CD), LOW), v((CD, WD), LOW), v((WD,), LOW), v((WD,), LOW),
            v((WORDS, WD), LOW),
            v((WD, WD), LOW), v((WD, WD), LOW), v((WD, WD), LOW), v((WD, WD), LOW),
            v((WD, WFF), LOW), v((WFF, WD), LOW),
            v((CD, CVOC), LOW), v((3 * CD, CD), LOW), v((CD, CD), LOW), v((CFF, CD), LOW), v((128, 32), LOW),
            v((2, KEPT_LOW, WIDE), LOW), v((2, CFF, WIDE), LOW), v((2, CD, WIDE), F32), v((2, 8, WIDE), F32),
            v((WORDS + WINDOW, CFF), F32), v((WORDS + WINDOW, CD), F32), v((16, WORDS), LOW),
            v((8, 128), jnp.int32), pltpu.SMEM((8, 128), jnp.int32),
            v((CFF, WIDE), F32), v((CFF, WIDE), LOW), v((CHAR_HEADS * SPAN, WIDE), LOW), v((8, WIDE), F32),
            v((CD, WIDE), LOW), v((CD, WIDE), LOW), v((8, WIDE), F32),
            v((2, SHARES, F_ROWS, 256), LOW),
            v((WORDS, WFF), LOW), v((WORDS, WFF), LOW),
            pltpu.SemaphoreType.DMA((15,)),
            pltpu.SemaphoreType.DMA((8,)),
            pltpu.SemaphoreType.DMA((4, 2)),
            pltpu.SemaphoreType.DMA((2,)),
        ],
        compiler_params=params(44),
        cost_estimate=pl.CostEstimate(flops=200 * 10**9, bytes_accessed=60 * 10**6, transcendentals=10**6),
        name="forward_and_words",
    )(*kept_outside(char_counts, char_ids, segment_ids, out_cotangent, *weights))


def call_a2(char_counts, kept, gain, project, weights):
    v = pltpu.VMEM
    return pl.pallas_call(
        kernel_a2,
        out_shape=(
            shape((CD, WORDS), LOW),
            outside((SHARES, T_ROWS, 256), LOW),
            outside((SHARES, T_ROWS, 256), LOW),
            shape((8, WD), F32),
        ),
        in_specs=[INSIDE] * 14 + [ANYWHERE] * 4,
        out_specs=(INSIDE, ANYWHERE, ANYWHERE, INSIDE),
        scratch_shapes=[
            v((WD, WD), LOW), v((WD, WD), LOW), v((WD, WD), LOW), v((WD, WD), LOW),
            v((2, SHARES, T_ROWS, 256), LOW),
            pltpu.SemaphoreType.DMA((4,)),
            pltpu.SemaphoreType.DMA((2,)),
        ],
        compiler_params=params(20),
        cost_estimate=pl.CostEstimate(flops=200 * 10**9, bytes_accessed=10 * 10**6, transcendentals=10**6),
        name="word_attention_backward",
    )(char_counts, *kept, gain, project, *kept_outside(*weights))


def call_b1(turns, gw, gain, up, down, kepts, keptm, kepti):
    v = pltpu.VMEM
    return pl.pallas_call(
        kernel_b1,
        out_shape=(outside((TURNS, CD, WIDE), LOW), shape((CD, CFF), LOW), shape((8, CD), F32)),
        in_specs=[SCALARS] + [INSIDE] * 4 + [ANYWHERE] * 3,
        out_specs=(ANYWHERE, INSIDE, INSIDE),
        scratch_shapes=[
            v((2, CFF, WIDE), LOW), v((2, CD, WIDE), F32), v((2, 8, WIDE), F32), v((2, CD, WIDE), LOW),
            v((CD, CFF), F32), v((CD, WIDE), F32), v((CFF, CD), LOW),
            pltpu.SemaphoreType.DMA((3, 2)),
            pltpu.SemaphoreType.DMA((2,)),
        ],
        compiler_params=params(16),
        cost_estimate=pl.CostEstimate(flops=200 * 10**9, bytes_accessed=20 * 10**6, transcendentals=10**6),
        name="character_backward_one",
    )(turns, gw, gain, up, down, *kept_outside(kepts, keptm, kepti))


def call_b2(turns, wgain1, wgain2, gain2, aup, weights, keptl, keptd, kepti):
    v = pltpu.VMEM
    return pl.pallas_call(
        kernel_b2,
        out_shape=(outside((SHARES, C_ROWS, 128), LOW), outside((SHARES, C_ROWS, 128), LOW)),
        in_specs=[SCALARS] + [INSIDE] * 9 + [ANYWHERE] * 3,
        out_specs=(ANYWHERE, ANYWHERE),
        scratch_shapes=[
            v((2, KEPT_LOW, WIDE), LOW), v((2, 8, WIDE), F32), v((2, CD, WIDE), LOW),
            v((CHAR_HEADS * SPAN, WIDE), LOW),
            v((CD, 3 * CD), LOW),
            v((CD, 3 * CD), F32), v((CD, CD), F32), v((CVOC, CD), F32), v((CD, WIDE), F32),
            v((2, SHARES, C_ROWS, 128), LOW),
            pltpu.SemaphoreType.DMA((3, 2)),
            pltpu.SemaphoreType.DMA((2,)),
        ],
        compiler_params=params(20),
        cost_estimate=pl.CostEstimate(flops=200 * 10**9, bytes_accessed=40 * 10**6, transcendentals=10**6),
        name="character_backward_two",
    )(turns, wgain1, wgain2, gain2, aup, *weights, *kept_outside(keptl, keptd, kepti))


def call_f(f, t, c, outk, outg):
    v = pltpu.VMEM
    outs = ((CVOC, CD), (CD,), (CD, CD), (CD, CD), (CD, CD), (CD, CD), (CD,), (CD, CFF), (CFF, CD), (CD, WD),
            (WD,), (WD, WD), (WD, WD), (WD, WD), (WD, WD), (WD,), (WD, WFF), (WFF, WD))
    outs = [(s[0] // SHARES,) + tuple(n // 2 for n in s[1:]) for s in outs]
    return pl.pallas_call(
        kernel_f,
        out_shape=(shape((2, 1, WORDS, WD // 2), LOW),) + tuple(shape(s, F32) for s in outs),
        in_specs=[ANYWHERE] * 20 + [INSIDE] * 2,
        out_specs=(INSIDE,) * 19,
        scratch_shapes=[
            v((6, F_ROWS, 256), LOW), v((6, T_ROWS, 256), LOW), v((8, C_ROWS, 128), LOW), pltpu.SemaphoreType.DMA((3,)),
        ],
        compiler_params=params(8),
        name="finish",
    )(*kept_outside(*f, *t, *c), outk, outg)


def flip(value, axis, bits):
    count = lax.axis_size(axis)
    return lax.ppermute(value, axis, [(i, i ^ bits) for i in range(count)])


def flip_both(value, first, second):
    pairs = [(i, i ^ first) for i in range(SHARES)] + [(SHARES + i, SHARES + (i ^ second)) for i in range(SHARES)]
    return lax.ppermute(value, ("phase", "dp"), pairs)


def pick(value, index):
    return lax.dynamic_index_in_dim(value, index, 0, keepdims=False)


def plus(*parts):
    total = parts[0].astype(F32)
    for part in parts[1:]:
        total = total + part.astype(F32)
    return total.astype(LOW)


class Sum:
    def __init__(self, keep):
        phase, dp = lax.axis_index("phase"), lax.axis_index("dp")
        x, y, low, high = (lax.rem(lax.div(dp, n), 2) for n in (1, 2, 4, 8))
        self.bits = [jnp.where(phase == 0, x, y), jnp.where(phase == 0, y, x), low, high]
        self.flips = [(1, 2), (2, 1), (4, 4), (8, 8)]
        self.parts = [keep]

    def send(self):
        step = len(self.parts) - 2
        half = SHARES >> (step + 1)
        total = None
        for part in self.parts:
            at, size = 0, part.shape[0]
            for bit, n in zip(self.bits[:step], (8, 4, 2, 1)):
                if n < size:
                    at = at + bit * n
            at = at + (1 - self.bits[step]) * half
            piece = lax.dynamic_slice_in_dim(part, at, half, 0).astype(F32)
            total = piece if total is None else total + piece
        return total.astype(LOW)

    def across(self, value):
        return flip_both(value, *self.flips[len(self.parts) - 2])


def together(*values):
    return lax.optimization_barrier(values)


def body(
    char_ids, char_counts, segment_ids, out_cotangent,
    char_table, char_gain_one, char_query, char_key, char_value, char_output, char_gain_two, char_up, char_down,
    char_project,
    word_gain_one, word_query, word_key, word_value, word_output, word_gain_two, word_up, word_down,
):
    keptl, kepts, keptm, kepti, turns, fkeep, fsend, outk, outs, wgain2, *words = call_a(
        char_counts, char_ids, segment_ids, out_cotangent,
        (char_table, char_gain_one, char_query, char_key, char_value, char_output, char_gain_two, char_up, char_down,
         char_project,
         word_gain_one, word_query, word_key, word_value, word_output, word_gain_two, word_up, word_down),
    )
    fgot = flip(fsend, "phase", 1)
    outg = flip(outs, "phase", 1)
    gw, tkeep, tsend, wgain1 = call_a2(
        char_counts, words, word_gain_one, char_project, (word_query, word_key, word_value, word_output)
    )
    one = (char_gain_two, char_up, char_down, kepts, keptm, kepti)
    two = (char_gain_one, char_query, char_key, char_value, char_output)
    if lax.axis_size("dp") != SHARES:
        keptd, aup, gain2 = call_b1(turns, gw, *one)
        ckeep, csend = call_b2(turns, wgain1, wgain2, gain2, aup, two, keptl, keptd, kepti)
        got = [flip(v, "phase", 1) for v in (tsend, csend)]
        return general_sums(outk, outg, (fkeep, fgot), (tkeep, got[0]), (ckeep, got[1]))
    f, t = Sum(fkeep), Sum(tkeep)
    gw, tsend, fgot, outg = together(gw, tsend, fgot, outg)
    f.parts.append(fgot)
    send = f.send()
    gw, send = together(gw, send)
    fgot, tgot = f.across(send), flip(tsend, "phase", 1)
    keptd, aup, gain2 = call_b1(turns, gw, *one)
    keptd, fgot, tgot = together(keptd, fgot, tgot)
    f.parts.append(fgot)
    t.parts.append(tgot)
    fsend, tsend = f.send(), t.send()
    keptd, fsend, tsend = together(keptd, fsend, tsend)
    fgot, tgot = f.across(fsend), t.across(tsend)
    ckeep, csend = call_b2(turns, wgain1, wgain2, gain2, aup, two, keptl, keptd, kepti)
    ckeep, csend, fgot, tgot = together(ckeep, csend, fgot, tgot)
    f.parts.append(fgot)
    t.parts.append(tgot)
    cphase, fgot, tgot = flip(csend, "phase", 1), f.across(f.send()), t.across(t.send())
    f.parts.append(fgot)
    t.parts.append(tgot)
    dp = lax.axis_index("dp")
    plane, line = lax.rem(dp, 4), lax.div(dp, 4)
    c = [ckeep.reshape(4, 4, C_ROWS, 128), cphase.reshape(4, 4, C_ROWS, 128)]
    sends = [plus(*(pick(part, lax.bitwise_xor(plane, k)) for part in c)) for k in range(1, 4)]
    cgot, fgot, tgot = (
        [flip(send, "dp", k) for k, send in enumerate(sends, 1)], f.across(f.send()), t.across(t.send())
    )
    f.parts.append(fgot)
    t.parts.append(tgot)
    c = [pick(part, plane) for part in c] + cgot
    sends = [plus(*(pick(part, lax.bitwise_xor(line, k)) for part in c)) for k in range(1, 4)]
    cline, tgot = [flip(send, "dp", 4 * k) for k, send in enumerate(sends, 1)], t.across(t.send())
    t.parts.append(tgot)
    return call_f(f.parts, t.parts, (ckeep, cphase, *cgot, *cline), outk, outg)


def general_sums(outk, outg, fs, ts, cs):
    phase = lax.axis_index("phase")
    first = phase == 0
    outs = jnp.stack([jnp.where(first, outk, outg), jnp.where(first, outg, outk)])[:, None]
    plain, swapped = (jnp.asarray([by_core(d, core) for d in range(SHARES)]) for core in range(2))

    def natural(pair, order):
        return jnp.take(pair[0].astype(F32) + pair[1].astype(F32), order, axis=0)

    order = jnp.where(first, plain, swapped)
    f, t, c = natural(fs, order), natural(ts, order), natural(cs, jnp.asarray([plane_first(d) for d in range(SHARES)]))

    def whole(rows):
        return rows.reshape(-1, rows.shape[-1])

    def wide(rows, pieces):
        n = rows.shape[1] // pieces
        return whole(rows.reshape(SHARES, pieces, n, rows.shape[-1]).transpose(0, 2, 1, 3).reshape(SHARES, n, -1))

    cdown = t[:, T_CDOWN:T_CDOWN + 32]
    cdown = jnp.concatenate([cdown[..., :128], cdown[..., 128:]], axis=1)
    parts = (
        whole(c[:, C_TABLE:C_TABLE + 16]), c[:, C_GAIN, :16].reshape(-1),
        whole(c[:, C_Q:C_Q + 16]), whole(c[:, C_K:C_K + 16]), whole(c[:, C_V:C_V + 16]), whole(c[:, C_O:C_O + 16]),
        c[:, C_GAIN + 1, :16].reshape(-1),
        wide(c[:, C_UP:C_UP + 64], 4), whole(cdown), whole(t[:, T_PROJ:T_PROJ + 16]),
        c[:, C_GAIN + 2, :32].reshape(-1),
        whole(t[:, T_Q:T_Q + 32]), whole(t[:, T_K:T_K + 32]), whole(t[:, T_V:T_V + 32]), whole(t[:, T_O:T_O + 32]),
        c[:, C_GAIN + 3, :32].reshape(-1),
        wide(f[:, F_UP:F_UP + 128], 4), whole(f[:, F_DOWN:F_DOWN + 128]),
    )
    return (outs,) + tuple(lax.psum_scatter(p, "dp", scatter_dimension=0, tiled=True) for p in parts)


def solution(mesh):
    rows = P(None, "dp", None)
    both = P("dp", "phase")
    one = P("dp")
    return jax.shard_map(
        body,
        mesh=mesh,
        in_specs=(rows, rows, rows, P(None, "dp", None, None)) + (P(),) * 18,
        out_specs=(
            P(None, "dp", None, "phase"),
            both, one, both, both, both, both, one, both, both, both,
            one, both, both, both, both, one, both, both,
        ),
        check_vma=False,
    )
```

```python
from functools import partial

import jax
import jax.numpy as jnp
from jax import lax
from jax.experimental import pallas as pl
from jax.experimental.pallas import tpu as pltpu
from jax.sharding import PartitionSpec as P

F32 = jnp.float32
LOW = jnp.bfloat16

CD = 256
CFF = 1024
CPW = 16
CVOC = 256
CHAR_HEADS = 4
HEAD = 64
WD = 512
WFF = 2048
WORD_HEADS = 8
WORDS = 256

SPAN = 256
STEP = 241
WIDE = 2 * SPAN
TURNS = ((WORDS * CPW - 1) // STEP + 2) // 2

epsilon = 1e-06
half_root = 0.7071067811865476
density = 0.3989422804014327
floor_score = -1e30
log2_e = 1.4426950408889634

R_EMB, R_Q, R_K, R_V, R_P, R_MIX = 0, 256, 512, 768, 1024, 2048
KEPT_LOW = 2304
I_INV1, I_INV2, I_IDENT, I_WORD = 0, 1, 2, 3
BAND = 144
WINDOW = 96

F_UP, F_DOWN = 0, 128
F_ROWS = 256
T_Q, T_K, T_V, T_O, T_CDOWN, T_PROJ = 0, 32, 64, 96, 128, 160
T_ROWS = 176
C_TABLE, C_Q, C_K, C_V, C_O, C_UP, C_GAIN = 0, 16, 32, 48, 64, 80, 144
C_ROWS = 160
SHARES = 16


def nn(left, right):
    return lax.dot_general(left, right, (((1,), (0,)), ((), ())), preferred_element_type=F32)


def nt(left, right):
    return lax.dot_general(left, right, (((1,), (1,)), ((), ())), preferred_element_type=F32)


def iota(shape, axis):
    return lax.broadcasted_iota(jnp.int32, shape, axis)


def eye(n):
    return iota((n, n), 0) == iota((n, n), 1)


def row_to_column(row):
    n = row.shape[1]
    return jnp.sum(jnp.where(eye(n), row, 0.0), axis=1, keepdims=True)


def gelu_pair(v):
    e = lax.erf(v * half_root)
    half = 0.5 * v
    bell = jnp.exp2(v * v * (-0.5 * log2_e))
    return half + half * e, 0.5 + 0.5 * e + (density * v) * bell


def gelu_twice(v):
    u = v * half_root
    whole = 1.0 + lax.erf(u)
    bell = jnp.exp2(u * u * (-log2_e))
    return v * whole, whole + (2.0 * density * v) * bell


def bits(d):
    return d % 2, d // 2 % 2, d // 4 % 2, d // 8


def plane_first(d, core=0):
    return (d % 4) * 4 + d // 4


def feed_order(d, core):
    x, y, low, high = bits(d)
    return (y * 8 + x * 2 if core else x * 8 + y * 2) + low * 4 + high


def word_order(d, core=0):
    _, _, low, high = bits(d)
    return (d % 4) * 4 + low * 2 + high


def own_bits():
    phase, dp = lax.axis_index("phase"), lax.axis_index("dp")
    x, y, low, high = (lax.rem(lax.div(dp, n), 2) for n in (1, 2, 4, 8))
    return jnp.where(phase == 0, x, y), jnp.where(phase == 0, y, x), low, high


def own_plane():
    return lax.rem(lax.axis_index("dp"), 4)


def add_up(out, *parts):
    for i in range(out.shape[0]):
        total = parts[0][i].astype(F32)
        for part in parts[1:]:
            total = total + part[i].astype(F32)
        out[i] = total.astype(LOW)


def members(word, first, count, weight=1.0):
    return jnp.where((iota((count, WIDE), 0) + first).astype(F32) == word, weight, 0.0).astype(LOW)


def word_starts(counts_row):
    earlier = iota((WORDS, WORDS), 1) < iota((WORDS, WORDS), 0)
    return jnp.sum(jnp.where(earlier, counts_row, 0.0), axis=1, keepdims=True)


def column_to_row(column):
    return jnp.sum(jnp.where(eye(column.shape[0]), column, 0.0), axis=0, keepdims=True)


def put(bundle, phase, order, row, value, width, share_rows):
    low = value.astype(LOW)
    lanes = bundle.shape[-1]
    for half in range(2):
        side = jnp.bitwise_xor(phase, half)
        for piece in range(max(1, width // lanes)):
            take = min(width, lanes)
            cols = low[:, half * width + piece * lanes:half * width + piece * lanes + take]
            for i in range(value.shape[0] // share_rows):
                part = cols[i * share_rows:(i + 1) * share_rows]
                if take < lanes:
                    part = jnp.concatenate([part[:share_rows // 2], part[share_rows // 2:]], axis=1)
                m = part.shape[0]
                bundle[side, order(i, half), row + piece * share_rows:row + piece * share_rows + m, :] = part


def band(t):
    keys = slice(0, BAND) if t % 2 == 0 else slice(SPAN - BAND, SPAN)
    return t // 2, keys, slice(t * 128, (t + 1) * 128)


def two_heads(pair):
    zero = jnp.zeros((HEAD, pair.shape[1]), LOW)
    first = jnp.concatenate([pair[:HEAD], zero], axis=0)
    second = jnp.concatenate([zero, pair[HEAD:]], axis=0)
    return jnp.concatenate([first, second], axis=1)


def two_heads_rows(pair):
    left = iota(pair.shape, 1) < HEAD
    zero = jnp.zeros(pair.shape, LOW)
    return jnp.concatenate([jnp.where(left, pair, zero), jnp.where(left, zero, pair)], axis=0)


def softmax_keys(s):
    e = jnp.exp(s - jnp.max(s, axis=0, keepdims=True))
    return (e * (1.0 / jnp.sum(e, axis=0, keepdims=True))).astype(LOW)


def kernel_a(
    counts_hbm, ids_hbm, segs_hbm, cot_hbm,
    table_hbm, g1_hbm, wq_hbm, wk_hbm, wv_hbm, wo_hbm, g2_hbm, up_hbm, down_hbm, proj_hbm,
    wg1_hbm, wwq_hbm, wwk_hbm, wwv_hbm, wwo_hbm, wg2_hbm, wup_hbm, wdown_hbm,
    keptl_hbm, kepts_hbm, keptm_hbm, kepti_hbm, turns_ref,
    keep_hbm, send_hbm, outk_ref, outs_ref, gain_ref,
    q_ref, k_ref, v_ref, probs_ref, mixt_ref, normed_ref, xhat_ref, winv_ref, md_ref, pooled_ref, pa_ref,
    counts_ref, ids_ref, segs_ref,
    table_ref, g1_ref, wq_ref, wk_ref, wv_ref, wo_ref, g2_ref, up_ref, down_ref, proj_ref, wg1_ref, wg2_ref,
    cot, wwq, wwk, wwv, wwo, wup, wdown,
    tab_t, wqkv_t, wo_t, up_t, ids_t, slow, sslope, smid, sinfo, pa, pm, rowinfo, firsts_v, firsts, before_s, act_s, prob_s, found_s,
    next_s, mid_s, word_s,
    bundle, actw, slopew,
    csem, wsem, ksem, osem,
):
    phase = lax.axis_index("phase")
    tiny = [
        pltpu.make_async_copy(src.at[phase], dst, csem.at[12 + i])
        for i, (src, dst) in enumerate(((counts_hbm, counts_ref), (ids_hbm, ids_ref), (segs_hbm, segs_ref)))
    ]
    for load in tiny:
        load.start()
    early = [
        pltpu.make_async_copy(src, dst, csem.at[i])
        for i, (src, dst) in enumerate(
            ((g1_hbm, g1_ref), (g2_hbm, g2_ref), (table_hbm, table_ref), (wq_hbm, wq_ref), (wk_hbm, wk_ref),
             (wv_hbm, wv_ref), (wo_hbm, wo_ref), (up_hbm, up_ref), (down_hbm, down_ref), (proj_hbm, proj_ref),
             (wg1_hbm, wg1_ref), (wg2_hbm, wg2_ref))
        )
    ]
    for load in early:
        load.start()
    loads = [
        pltpu.make_async_copy(src, dst, wsem.at[i])
        for i, (src, dst) in enumerate(
            ((wwq_hbm, wwq), (wwk_hbm, wwk), (wwv_hbm, wwv), (wwo_hbm, wwo),
             (wup_hbm, wup), (wdown_hbm, wdown), (cot_hbm.at[phase, 0], cot))
        )
    ]
    pa[...] = jnp.zeros_like(pa)
    pm[...] = jnp.zeros_like(pm)
    prob_s[...] = jnp.zeros_like(prob_s)
    for slot in range(2):
        slow[slot, R_P:R_P + CHAR_HEADS * SPAN] = jnp.zeros((CHAR_HEADS * SPAN, WIDE), LOW)
    for load in tiny:
        load.wait()
    counts_row = counts_ref[...].astype(F32)
    starts = word_starts(counts_row)
    counts = row_to_column(counts_row)
    blocks = jnp.floor((starts + 0.5) * (1.0 / STEP))
    places = starts + (SPAN - STEP) * blocks
    n_turns = jnp.max(places).astype(jnp.int32) // WIDE + 1
    turns_ref[0] = n_turns
    bases = (iota((1, 128), 1) * WIDE).astype(F32)
    first = jnp.sum(jnp.where(places < bases, 1.0, 0.0), axis=0, keepdims=True)
    firsts_v[...] = jnp.broadcast_to(first, (8, 128)).astype(jnp.int32)
    first_copy = pltpu.make_async_copy(firsts_v, firsts, wsem.at[7])
    first_copy.start()
    ids = ids_ref[...]
    ids_t[...] = jnp.concatenate(
        [ids[:, 128 * a:128 * a + 128] for a in range(32)], axis=0
    ).astype(F32).T.astype(LOW)
    places_row = column_to_row(places)
    none = jnp.zeros((1, 1), F32)
    rowinfo[...] = jnp.concatenate(
        [places_row - jnp.concatenate([none, places_row[:, :-1]], axis=1),
         counts_row - jnp.concatenate([none, counts_row[:, :-1]], axis=1),
         jnp.ones((1, WORDS), F32), jnp.zeros((13, WORDS), F32)], axis=0
    ).astype(LOW)
    for load in early:
        load.wait()
    for load in loads:
        load.start()
    tab_t[...] = table_ref[...].T
    wqkv_t[0:CD] = (wq_ref[...] * 0.125).T
    wqkv_t[CD:2 * CD] = wk_ref[...].T
    wqkv_t[2 * CD:] = wv_ref[...].T
    wo_t[...] = wo_ref[...].T
    up_t[...] = up_ref[...].T
    g1 = row_to_column(g1_ref[...].astype(F32)[None, :])
    g2 = row_to_column(g2_ref[...].astype(F32)[None, :])
    first_copy.wait()

    def find(turn):
        place = (iota((1, WIDE), 1) + turn * WIDE).astype(F32)
        begun = jnp.where(places <= place, 1.0, 0.0).astype(LOW)
        info = nn(rowinfo[...], begun)
        word = info[2:3] - 1.0
        slot = place - info[0:1]
        flat = (word * 16.0 + slot).astype(jnp.int32)
        chosen = jnp.where(iota((32, WIDE), 0) == (flat >> 7), 1.0, 0.0).astype(LOW)
        lanes = nn(ids_t[...], chosen)
        ident = jnp.sum(jnp.where(iota((128, WIDE), 0) == (flat & 127), lanes, 0.0), axis=0, keepdims=True)
        valid = slot < info[1:2]
        none = jnp.full((6, WIDE), -1.0, F32)
        return jnp.concatenate([jnp.where(valid, ident, -1.0), jnp.where(valid, word, -1.0), none], axis=0)

    found_s[...] = find(jnp.int32(0))

    def copies(b):
        slot = lax.rem(b, 2)
        return (
            pltpu.make_async_copy(slow.at[slot], keptl_hbm.at[b], ksem.at[0, slot]),
            pltpu.make_async_copy(sslope.at[slot], kepts_hbm.at[b], ksem.at[1, slot]),
            pltpu.make_async_copy(smid.at[slot], keptm_hbm.at[b], ksem.at[2, slot]),
            pltpu.make_async_copy(sinfo.at[slot], kepti_hbm.at[b], ksem.at[3, slot]),
        )

    def start(copies):
        for c in copies:
            c.start()

    def wait(copies):
        for c in copies:
            c.wait()

    def near_words(b):
        first = (firsts[0, b] // 16) * 16
        return first, (firsts[0, b + 1] - first + WINDOW - 1) // WINDOW

    def window(first):
        return pl.ds(pl.multiple_of(first, 16), WINDOW)

    def attend(b):
        slot = lax.rem(b, 2)
        ident = found_s[0:1]
        word = found_s[1:2]
        hot = jnp.where(iota((CVOC, WIDE), 0).astype(F32) == ident, 1.0, 0.0).astype(LOW)
        emb = nn(tab_t[...], hot)
        inv1 = lax.rsqrt(jnp.mean(emb * emb, axis=0, keepdims=True) + epsilon)
        normed = (emb * inv1 * g1).astype(LOW)
        yield
        qkv = nn(wqkv_t[...], normed).astype(LOW)
        key_rows = [qkv[CD:2 * CD, u * SPAN:(u + 1) * SPAN].T for u in range(2)]
        value_t = qkv[2 * CD:]
        word_col = jnp.broadcast_to(jnp.where(word < 0.0, -2.0, word), (8, WIDE)).T[:, 0:1]
        yield
        for t in range(4):
            u, ks, ql = band(t)
            bias = jnp.where(word_col[u * SPAN + ks.start:u * SPAN + ks.stop] == word[:, ql], 0.0, floor_score)
            for pair in range(CHAR_HEADS // 2):
                fs = slice(pair * 128, pair * 128 + 128)
                s = nn(key_rows[u][ks, fs], two_heads(qkv[fs, ql]))
                for i in range(2):
                    p = softmax_keys(s[:, i * 128:i * 128 + 128] + bias)
                    row = (pair * 2 + i) * SPAN
                    prob_s[row + ks.start:row + ks.stop, ql] = p
                    slow[slot, R_P + row + ks.start:R_P + row + ks.stop, ql] = p
                yield
        slow[slot, R_EMB:R_EMB + CD] = emb.astype(LOW)
        slow[slot, R_Q:R_Q + 2 * CD] = qkv[:2 * CD]
        for u in range(2):
            us = slice(u * SPAN, (u + 1) * SPAN)
            slow[slot, R_V:R_V + SPAN, us] = value_t[:, us].T
        mixed = []
        for h in range(CHAR_HEADS):
            hs = slice(h * HEAD, (h + 1) * HEAD)
            both = []
            for u in range(2):
                us = slice(u * SPAN, (u + 1) * SPAN)
                both.append(nn(value_t[hs, us], prob_s[h * SPAN:(h + 1) * SPAN, us]).astype(LOW))
            mixed.append(jnp.concatenate(both, axis=1))
        mixed = jnp.concatenate(mixed, axis=0)
        slow[slot, R_MIX:R_MIX + CD] = mixed
        yield
        middle = emb + nn(wo_t[...], mixed)
        inv2 = lax.rsqrt(jnp.mean(middle * middle, axis=0, keepdims=True) + epsilon)
        smid[slot] = middle
        sinfo[slot] = jnp.concatenate([inv1, inv2, ident, word, jnp.zeros((4, WIDE), F32)], axis=0)
        normed_two = (middle * inv2 * g2).astype(LOW)
        yield
        first, _ = near_words(b)
        near = members(word, first, WINDOW)
        middle_low = middle.astype(LOW)
        pm[window(first), :] += nt(near, middle_low)
        mid_s[...] = middle_low
        next_s[...] = normed_two
        word_s[0:1] = word
        found_s[...] = find(b + 1)
        yield

    def feed(b):
        slot = lax.rem(b, 2)
        word = word_s[0:1]
        before_s[...] = nn(up_t[...], next_s[...])
        yield
        for c in range(CFF // 32):
            cs = slice(c * 32, (c + 1) * 32)
            act, slope = gelu_twice(before_s[cs])
            sslope[slot, cs] = slope.astype(LOW)
            act_s[cs] = act.astype(LOW)
            if c % 4 == 3:
                yield
        first, _ = near_words(b)
        pa[window(first), :] += nt(members(word, first, WINDOW, 0.5), act_s[...])
        yield

    def run(*parts):
        parts = list(parts)
        while parts:
            for part in tuple(parts):
                if next(part, parts) is parts:
                    parts.remove(part)

    def turn(b, carry):
        @pl.when(b >= 2)
        def _():
            wait(copies(b - 2))

        run(attend(b))
        run(feed(b))
        first, windows = near_words(b)

        def more(i, carry):
            at = first + i * WINDOW
            pm[window(at), :] += nt(members(word_s[0:1], at, WINDOW), mid_s[...])
            pa[window(at), :] += nt(members(word_s[0:1], at, WINDOW, 0.5), act_s[...])
            return carry

        lax.fori_loop(1, windows, more, 0)
        start(copies(b))
        return carry

    lax.fori_loop(0, n_turns, turn, 0)

    pa_hi = pa[0:WORDS].astype(LOW)
    pa_lo = (pa[0:WORDS] - pa_hi.astype(F32)).astype(LOW)
    per_count = 1.0 / counts
    pooled = (pm[0:WORDS] + nn(pa_hi, down_ref[...]) + nn(pa_lo, down_ref[...])) * per_count
    pooled_low = pooled.astype(LOW)
    pooled_ref[...] = pooled_low
    pa_ref[...] = pa_hi
    x = nn(pooled_low, proj_ref[...]).astype(LOW).astype(F32)
    for load in loads:
        load.wait()
    wg1 = wg1_ref[...].astype(F32)[None, :]
    wg2 = wg2_ref[...].astype(F32)[None, :]
    winv1 = lax.rsqrt(jnp.mean(x * x, axis=1, keepdims=True) + epsilon)
    xhat = x * winv1
    normed = (xhat * wg1).astype(LOW)
    xhat_ref[...] = xhat
    winv_ref[...] = jnp.broadcast_to(winv1, (WORDS, 128))
    normed_ref[...] = normed
    q = (nn(normed, wwq[...]) * 0.125).astype(LOW)
    k = nn(normed, wwk[...]).astype(LOW)
    v = nn(normed, wwv[...]).astype(LOW)
    seg_row = segs_ref[...].astype(F32)
    seg_col = row_to_column(seg_row)
    allowed = (seg_row == seg_col) & (iota((WORDS, WORDS), 0) <= iota((WORDS, WORDS), 1))
    bias = jnp.where(allowed, 0.0, floor_score)
    q_ref[...] = q
    k_ref[...] = k
    v_ref[...] = v
    v_t = v.T
    for h in range(WORD_HEADS):
        probs_ref[h, 128:, 0:128] = jnp.zeros((128, 128), LOW)
    for t in range(2):
        ks, ql = slice(0, 128 * (t + 1)), slice(128 * t, 128 * (t + 1))
        for pair in range(WORD_HEADS // 2):
            fs = slice(pair * 128, pair * 128 + 128)
            s = nt(k[ks, fs], two_heads_rows(q[ql, fs]))
            for i in range(2):
                probs_ref[pair * 2 + i, ks, ql] = softmax_keys(s[:, i * 128:i * 128 + 128] + bias[ks, ql])
    mixed_t = jnp.concatenate(
        [nn(v_t[h * HEAD:(h + 1) * HEAD], probs_ref[h]).astype(LOW) for h in range(WORD_HEADS)], axis=0
    )
    mixt_ref[...] = mixed_t
    middle = x + nn(mixed_t.T, wwo[...])
    winv2 = lax.rsqrt(jnp.mean(middle * middle, axis=1, keepdims=True) + epsilon)
    normed_two = (middle * winv2 * wg2).astype(LOW)
    result = middle
    for c in range(WFF // 512):
        cs = slice(c * 512, (c + 1) * 512)
        act, slope = gelu_pair(nn(normed_two, wup[:, cs]))
        act = act.astype(LOW)
        actw[:, cs] = act
        slopew[:, cs] = slope.astype(LOW)
        result = result + nn(act, wdown[cs, :])
    result = result.astype(LOW)
    front = phase == 0
    outk_ref[...] = jnp.where(front, result[:, :256], result[:, 256:])
    outs_ref[...] = jnp.where(front, result[:, 256:], result[:, :256])

    cot_low = cot[...]
    n2d = jnp.zeros((WORDS, WD), F32)
    n2_t = normed_two.T
    for c in range(WFF // 512):
        cs = slice(c * 512, (c + 1) * 512)
        gd = nn(actw[:, cs].T, cot_low)
        put(bundle, phase, lambda i, p: feed_order(c * 4 + i, p), F_DOWN, gd, 256, 128)
        bd = (nt(cot_low, wdown[cs, :]) * slopew[:, cs].astype(F32)).astype(LOW)
        gu = nn(n2_t, bd).astype(LOW)
        side = jnp.bitwise_xor(phase, c // 2)
        for piece in range(2):
            row = F_UP + ((c % 2) * 2 + piece) * 32
            for d in range(SHARES):
                bundle[side, feed_order(d, c // 2), row:row + 32, :] = gu[d * 32:(d + 1) * 32, piece * 256:piece * 256 + 256]
        n2d = n2d + nt(bd, wup[:, cs])
    stores = [
        pltpu.make_async_copy(bundle.at[0], keep_hbm, osem.at[0]),
        pltpu.make_async_copy(bundle.at[1], send_hbm, osem.at[1]),
    ]
    for s in stores:
        s.start()
    vhat = middle * winv2
    gain_ref[...] = jnp.broadcast_to(jnp.sum(n2d * vhat, axis=0, keepdims=True), (8, WD))
    lifted = n2d * wg2
    md_ref[...] = cot[...].astype(F32) + winv2 * (lifted - vhat * jnp.mean(lifted * vhat, axis=1, keepdims=True))

    def drain(b, carry):
        wait(copies(b))
        return carry

    lax.fori_loop(jnp.maximum(n_turns - 2, 0), n_turns, drain, 0)
    for s in stores:
        s.wait()


def kernel_a2(
    counts_ref, q_ref, k_ref, v_ref, pw, mixt_ref, normed_ref, xhat_ref, winv_ref, md_ref, pooled_ref, pa_ref,
    wg1_ref, proj_ref, wwq, wwk, wwv, wwo,
    gw_ref, keep_hbm, send_hbm, gain_ref,
    bundle, osem,
):
    phase = lax.axis_index("phase")
    wg1 = wg1_ref[...].astype(F32)[None, :]
    q, k, v, normed, pooled_low = q_ref[...], k_ref[...], v_ref[...], normed_ref[...], pooled_ref[...]
    per_count = 1.0 / row_to_column(counts_ref[phase].astype(F32))
    md = md_ref[...]
    md_low = md.astype(LOW)
    put(bundle, phase, word_order, T_O, nn(mixt_ref[...], md_low), 256, 32)
    k_t = k.T
    do = nt(md_low, wwo[...]).astype(LOW)
    dq_t, dk, dv = [], [], []
    left = iota((WORDS, 128), 1) < HEAD
    for pair in range(WORD_HEADS // 2):
        fs = slice(pair * 128, pair * 128 + 128)
        ds = []
        for t in range(2):
            ks, ql = slice(0, 128 * (t + 1)), slice(128 * t, 128 * (t + 1))
            dp = nt(v[ks, fs], two_heads_rows(do[ql, fs]))
            for i in range(2):
                pf = pw[pair * 2 + i, ks, ql].astype(F32)
                dph = dp[:, i * 128:i * 128 + 128]
                d = (pf * (dph - jnp.sum(pf * dph, axis=0, keepdims=True))).astype(LOW)
                ds.append(d if t else jnp.concatenate([d, jnp.zeros((128, 128), LOW)], axis=0))
        both = [jnp.concatenate([ds[i], ds[i + 2]], axis=1) for i in range(2)]
        for i in range(2):
            h = pair * 2 + i
            dq_t.append(nn(k_t[h * HEAD:(h + 1) * HEAD], both[i]))
        dk.append(jnp.where(left, nn(both[0], q[:, fs]), nn(both[1], q[:, fs])).astype(LOW))
        dv.append(jnp.where(left, nn(pw[pair * 2], do[:, fs]), nn(pw[pair * 2 + 1], do[:, fs])).astype(LOW))
    dq = (jnp.concatenate(dq_t, axis=0) * 0.125).astype(LOW).T
    dk = jnp.concatenate(dk, axis=1)
    dv = jnp.concatenate(dv, axis=1)
    normed_t = normed.T
    nd = nt(dq, wwq[...]) + nt(dk, wwk[...]) + nt(dv, wwv[...])
    put(bundle, phase, word_order, T_Q, nn(normed_t, dq), 256, 32)
    put(bundle, phase, word_order, T_K, nn(normed_t, dk), 256, 32)
    put(bundle, phase, word_order, T_V, nn(normed_t, dv), 256, 32)
    stores = [
        pltpu.make_async_copy(bundle.at[side, :, rows], out.at[:, rows], osem.at[i, side])
        for i, rows in enumerate((pl.ds(0, T_CDOWN), pl.ds(T_CDOWN, T_ROWS - T_CDOWN)))
        for side, out in enumerate((keep_hbm, send_hbm))
    ]
    for store in stores[:2]:
        store.start()
    vhat = xhat_ref[...]
    gain_ref[...] = jnp.broadcast_to(jnp.sum(nd * vhat, axis=0, keepdims=True), (8, WD))
    lifted = nd * wg1
    xd = md + winv_ref[:, 0:1] * (lifted - vhat * jnp.mean(lifted * vhat, axis=1, keepdims=True))
    vd = xd.astype(LOW)
    put(bundle, phase, word_order, T_PROJ, nn(pooled_low.T, vd), 256, 16)
    gw = (nt(vd, proj_ref[...]) * per_count).astype(LOW)
    gw_ref[...] = gw.T
    put(bundle, phase, word_order, T_CDOWN, nn(pa_ref[...].T, gw), 128, 64)
    for store in stores[2:]:
        store.start()
    for store in stores:
        store.wait()


def kernel_b1(
    turns_ref, gw_ref, g2_ref, up_ref, down_ref, kepts_hbm, keptm_hbm, kepti_hbm, f0_hbm, f1_hbm,
    keptd_hbm, aup_ref, gain_ref, facc_ref,
    sslope, smid, sinfo, sdelta, aup, ag2, down, f0, f1, ksem, dsem, fsem,
):
    n_turns = turns_ref[0]

    def kept_copies(b, slot):
        return (
            pltpu.make_async_copy(kepts_hbm.at[b], sslope.at[slot], ksem.at[0, slot]),
            pltpu.make_async_copy(keptm_hbm.at[b], smid.at[slot], ksem.at[1, slot]),
            pltpu.make_async_copy(kepti_hbm.at[b], sinfo.at[slot], ksem.at[2, slot]),
        )

    def delta_copy(b, slot):
        return pltpu.make_async_copy(sdelta.at[slot], keptd_hbm.at[b], dsem.at[slot])

    for c in kept_copies(0, 0):
        c.start()
    a, _, _, _ = own_bits()
    loads = [
        pltpu.make_async_copy(src.at[pl.ds(a * 8, 8)], dst, fsem.at[i])
        for i, (src, dst) in enumerate(((f0_hbm, f0), (f1_hbm, f1)))
    ]
    for load in loads:
        load.start()
    g2 = row_to_column(g2_ref[...].astype(F32)[None, :])
    down[...] = down_ref[...] * 0.5
    aup[...] = jnp.zeros_like(aup)
    ag2[...] = jnp.zeros_like(ag2)

    def turn(b, carry):
        slot = lax.rem(b, 2)

        @pl.when(b + 1 < n_turns)
        def _():
            for c in kept_copies(b + 1, 1 - slot):
                c.start()

        @pl.when(b >= 2)
        def _():
            delta_copy(b - 2, slot).wait()

        for c in kept_copies(b, slot):
            c.wait()
        inv2 = sinfo[slot, I_INV2:I_INV2 + 1]
        g_low = nn(gw_ref[...], members(sinfo[slot, I_WORD:I_WORD + 1], 0, WORDS)).astype(LOW)
        vhat = smid[slot] * inv2
        normed_two = (vhat * g2).astype(LOW)
        n2d = jnp.zeros((CD, WIDE), F32)
        for c in range(CFF // 256):
            cs = slice(c * 256, (c + 1) * 256)
            bd = (nn(down[cs, :], g_low) * sslope[slot, cs].astype(F32)).astype(LOW)
            aup[:, cs] += nt(normed_two, bd)
            n2d = n2d + nn(up_ref[:, cs], bd)
        ag2[...] += n2d * vhat
        lifted = n2d * g2
        md = g_low.astype(F32) + inv2 * (lifted - vhat * jnp.mean(lifted * vhat, axis=0, keepdims=True))
        sdelta[slot] = md.astype(LOW)
        delta_copy(b, slot).start()
        return carry

    lax.fori_loop(0, n_turns, turn, 0)
    aup_ref[...] = aup[...].astype(LOW)
    for load in loads:
        load.wait()
    add_up(facc_ref, f0, f1)
    gain_ref[...] = jnp.broadcast_to(jnp.sum(ag2[...], axis=1, keepdims=True), (CD, 8)).T

    def drain(b, carry):
        delta_copy(b, lax.rem(b, 2)).wait()
        return carry

    lax.fori_loop(jnp.maximum(n_turns - 2, 0), n_turns, drain, 0)


def kernel_b2(
    turns_ref, wgain1_ref, wgain2_ref, gain2_ref, aup_ref, g1_ref, wq_ref, wk_ref, wv_ref, wo_ref,
    keptl_hbm, keptd_hbm, kepti_hbm, facc_ref, f2_hbm, t0_hbm, t1_hbm,
    keep_ref, send_ref, fnext_ref, tacc_ref,
    slow, sinfo, sdelta, dscore, wqkv, aqkv, ao, atab, ag1, bundle, f2, t0, t1, ksem, fsem,
):
    phase = lax.axis_index("phase")
    n_turns = turns_ref[0]

    def kept_copies(b, slot):
        return (
            pltpu.make_async_copy(keptl_hbm.at[b], slow.at[slot], ksem.at[0, slot]),
            pltpu.make_async_copy(keptd_hbm.at[b], sdelta.at[slot], ksem.at[1, slot]),
            pltpu.make_async_copy(kepti_hbm.at[b], sinfo.at[slot], ksem.at[2, slot]),
        )

    for c in kept_copies(0, 0):
        c.start()
    _, _, low, _ = own_bits()
    quarter = pl.ds(own_plane() * 4, 4)
    loads = [
        pltpu.make_async_copy(src.at[at], dst, fsem.at[i])
        for i, (src, at, dst) in enumerate(((f2_hbm, pl.ds(low * 4, 4), f2), (t0_hbm, quarter, t0), (t1_hbm, quarter, t1)))
    ]
    for load in loads:
        load.start()
    g1 = row_to_column(g1_ref[...].astype(F32)[None, :])
    for i, w in enumerate((wq_ref, wk_ref, wv_ref)):
        wqkv[:, i * CD:(i + 1) * CD] = w[...]
    for acc in (aqkv, ao, atab, ag1, dscore):
        acc[...] = jnp.zeros_like(acc)

    def turn(b, carry):
        slot = lax.rem(b, 2)

        @pl.when(b + 1 < n_turns)
        def _():
            for c in kept_copies(b + 1, 1 - slot):
                c.start()

        for c in kept_copies(b, slot):
            c.wait()
        inv1 = sinfo[slot, I_INV1:I_INV1 + 1]
        ident = sinfo[slot, I_IDENT:I_IDENT + 1]
        md_low = sdelta[slot]
        ao[...] += nt(slow[slot, R_MIX:R_MIX + CD], md_low)
        do = nn(wo_ref[...], md_low).astype(LOW)
        for t in range(4):
            u, ks, ql = band(t)
            for pair in range(CHAR_HEADS // 2):
                fs = slice(u * SPAN + pair * 128, u * SPAN + pair * 128 + 128)
                dp = nn(
                    slow[slot, R_V + ks.start:R_V + ks.stop, fs], two_heads(do[pair * 128:pair * 128 + 128, ql])
                )
                for i in range(2):
                    row = (pair * 2 + i) * SPAN
                    pf = slow[slot, R_P + row + ks.start:R_P + row + ks.stop, ql].astype(F32)
                    dph = dp[:, i * 128:i * 128 + 128]
                    d = pf * (dph - jnp.sum(pf * dph, axis=0, keepdims=True))
                    dscore[row + ks.start:row + ks.stop, ql] = d.astype(LOW)
        dq, dk, dv = [], [], []
        for h in range(CHAR_HEADS):
            hs = slice(h * HEAD, (h + 1) * HEAD)
            one, two, three = [], [], []
            for u in range(2):
                us = slice(u * SPAN, (u + 1) * SPAN)
                p = slow[slot, R_P + h * SPAN:R_P + (h + 1) * SPAN, us]
                ds = dscore[h * SPAN:(h + 1) * SPAN, us]
                one.append((nn(slow[slot, R_K + h * HEAD:R_K + (h + 1) * HEAD, us], ds) * 0.125).astype(LOW))
                two.append(nt(slow[slot, R_Q + h * HEAD:R_Q + (h + 1) * HEAD, us], ds).astype(LOW))
                three.append(nt(do[hs, us], p).astype(LOW))
            for part, pair in ((dq, one), (dk, two), (dv, three)):
                part.append(jnp.concatenate(pair, axis=1))
        dqkv = jnp.concatenate(dq + dk + dv, axis=0)
        emb = slow[slot, R_EMB:R_EMB + CD].astype(F32)
        ehat = emb * inv1
        normed = (ehat * g1).astype(LOW)
        aqkv[...] += nt(normed, dqkv)
        nd = nn(wqkv[...], dqkv)
        ag1[...] += nd * ehat
        lifted = nd * g1
        ed = md_low.astype(F32) + inv1 * (lifted - ehat * jnp.mean(lifted * ehat, axis=0, keepdims=True))
        hot = jnp.where(iota((CVOC, WIDE), 0).astype(F32) == ident, 1.0, 0.0).astype(LOW)
        atab[...] += nt(hot, ed.astype(LOW))
        return carry

    lax.fori_loop(0, n_turns, turn, 0)

    for load in loads:
        load.wait()
    add_up(fnext_ref, facc_ref.at[pl.ds(low * 4, 4)], f2)
    add_up(tacc_ref, t0, t1)
    put(bundle, phase, plane_first, C_TABLE, atab[...], 128, 16)
    put(bundle, phase, plane_first, C_Q, aqkv[:, 0:CD], 128, 16)
    put(bundle, phase, plane_first, C_K, aqkv[:, CD:2 * CD], 128, 16)
    put(bundle, phase, plane_first, C_V, aqkv[:, 2 * CD:], 128, 16)
    put(bundle, phase, plane_first, C_O, ao[...], 128, 16)
    put(bundle, phase, plane_first, C_UP, aup_ref[...], 512, 16)
    cg1 = jnp.broadcast_to(jnp.sum(ag1[...], axis=1, keepdims=True), (CD, 8)).T[0:1]
    cg2 = gain2_ref[0:1]
    for d in range(SHARES):
        rows = [
            jnp.concatenate([cg1[:, d * 16:d * 16 + 16], jnp.zeros((1, 112), F32)], axis=1),
            jnp.concatenate([cg2[:, d * 16:d * 16 + 16], jnp.zeros((1, 112), F32)], axis=1),
            jnp.concatenate([wgain1_ref[0:1, d * 32:d * 32 + 32], jnp.zeros((1, 96), F32)], axis=1),
            jnp.concatenate([wgain2_ref[0:1, d * 32:d * 32 + 32], jnp.zeros((1, 96), F32)], axis=1),
            jnp.zeros((12, 128), F32),
        ]
        tile = jnp.concatenate(rows, axis=0).astype(LOW)
        bundle[0, plane_first(d), C_GAIN:C_GAIN + 16, :] = tile
        bundle[1, plane_first(d), C_GAIN:C_GAIN + 16, :] = tile
    keep_ref[...] = bundle[0]
    send_ref[...] = bundle[1]


def kernel_add_one(f0_hbm, f1_hbm, send_ref, one, two, sem):
    a, _, _, _ = own_bits()
    other = pl.ds((1 - a) * 8, 8)
    loads = [pltpu.make_async_copy(src.at[other], dst, sem.at[i]) for i, (src, dst) in enumerate(((f0_hbm, one), (f1_hbm, two)))]
    for load in loads:
        load.start()
    for load in loads:
        load.wait()
    add_up(send_ref, one, two)


def kernel_add_two(facc_ref, f2_hbm, t0_hbm, t1_hbm, fsend_ref, ts1_ref, ts2_ref, ts3_ref, f2, t0, t1, sem):
    _, _, low, _ = own_bits()
    half = pl.ds((1 - low) * 4, 4)
    loads = [pltpu.make_async_copy(f2_hbm.at[half], f2, sem.at[0])]
    for k in range(1, 4):
        at = pl.ds(lax.bitwise_xor(own_plane(), k) * 4, 4)
        for i, (src, dst) in enumerate(((t0_hbm, t0), (t1_hbm, t1))):
            loads.append(pltpu.make_async_copy(src.at[at], dst.at[k - 1], sem.at[1 + i]))
    for load in loads:
        load.start()
    loads[0].wait()
    add_up(fsend_ref, facc_ref.at[half], f2)
    for load in loads[1:]:
        load.wait()
    for k, out in enumerate((ts1_ref, ts2_ref, ts3_ref)):
        add_up(out, t0.at[k], t1.at[k])


def kernel_add_three(
    facc_ref, f3_hbm, tacc_ref, tg1_hbm, tg2_hbm, tg3_hbm, fsend_ref, fkeep_ref, tsend_ref, tkeep_ref, f3, tg, sem
):
    _, b, low, _ = own_bits()
    loads = [pltpu.make_async_copy(src, tg.at[i], sem.at[0]) for i, src in enumerate((tg1_hbm, tg2_hbm, tg3_hbm))]
    loads.append(pltpu.make_async_copy(f3_hbm, f3, sem.at[1]))
    for load in loads:
        load.start()
    for load in loads[:3]:
        load.wait()
    for out, bit in ((tsend_ref, 1 - low), (tkeep_ref, low)):
        at = pl.ds(bit * 2, 2)
        add_up(out, tacc_ref.at[at], *(tg.at[k, at] for k in range(3)))
    loads[3].wait()
    for out, bit in ((fsend_ref, 1 - b), (fkeep_ref, b)):
        add_up(out, facc_ref.at[pl.ds(bit * 2, 2)], f3.at[pl.ds(bit * 2, 2)])


def kernel_f(
    f3, f4, t2, t3, last, c0, c1, c2, c3, c4, c5, c6, c7, outk, outg,
    word_out, d_table, d_g1, d_q, d_k, d_v, d_o, d_g2, d_up, d_down, d_proj,
    e_g1, e_q, e_k, e_v, e_o, e_g2, e_up, e_down,
    fs, ts, cs, sem,
):
    phase = lax.axis_index("phase")
    dp = lax.axis_index("dp")
    _, _, low, high = own_bits()
    loads = []
    line = lax.div(dp, 4)
    place = lax.rem(dp, 4) * 4 + line
    for i, (parts, places, here) in enumerate((
        ((f3, f4, last), (high, high, pl.ds(0, F_ROWS)), fs),
        ((t2, t3, last), (high, high, pl.ds(F_ROWS, T_ROWS)), ts),
        ((c0, c1, c2, c3, c4), (place, place, line, line, line), cs),
    )):
        for j, (part, n) in enumerate(zip(parts, places)):
            loads.append(pltpu.make_async_copy(part.at[n], here.at[j], sem.at[i]))
    for j, part in enumerate((c5, c6, c7)):
        loads.append(pltpu.make_async_copy(part, cs.at[5 + j], sem.at[2]))
    for load in loads:
        load.start()
    word_out[phase, 0] = outk[...]
    word_out[1 - phase, 0] = outg[...]
    for load in loads:
        load.wait()

    def total(parts, row, n):
        t = parts[0, row:row + n].astype(F32) + parts[1, row:row + n].astype(F32)
        for j in range(2, parts.shape[0]):
            t = t + parts[j, row:row + n].astype(F32)
        return t

    f, t, c = partial(total, fs), partial(total, ts), partial(total, cs)
    d_table[...] = c(C_TABLE, 16)
    d_q[...] = c(C_Q, 16)
    d_k[...] = c(C_K, 16)
    d_v[...] = c(C_V, 16)
    d_o[...] = c(C_O, 16)
    for i in range(4):
        d_up[:, i * 128:(i + 1) * 128] = c(C_UP + i * 16, 16)
        e_up[:, i * 256:(i + 1) * 256] = f(F_UP + i * 32, 32)
    gains = c(C_GAIN, 16)
    d_g1[...] = gains[0, :16]
    d_g2[...] = gains[1, :16]
    e_g1[...] = gains[2, :32]
    e_g2[...] = gains[3, :32]
    cd = t(T_CDOWN, 32)
    d_down[0:32] = cd[:, :128]
    d_down[32:64] = cd[:, 128:]
    d_proj[...] = t(T_PROJ, 16)
    e_q[...] = t(T_Q, 32)
    e_k[...] = t(T_K, 32)
    e_v[...] = t(T_V, 32)
    e_o[...] = t(T_O, 32)
    e_down[...] = f(F_DOWN, 128)


ANYWHERE = pl.BlockSpec(memory_space=pltpu.HBM)
INSIDE = pl.BlockSpec(memory_space=pltpu.VMEM)
SCALARS = pl.BlockSpec(memory_space=pltpu.SMEM)
shape = jax.ShapeDtypeStruct


def params(mib):
    return pltpu.CompilerParams(vmem_limit_bytes=mib * 2**20)


def outside(dims, dtype):
    return pltpu.HBM(dims, dtype)


def kept_outside(*values):
    return tuple(pltpu.with_memory_space_constraint(v, pltpu.HBM) for v in values)


def call_a(char_counts, char_ids, segment_ids, out_cotangent, weights):
    v = pltpu.VMEM
    return pl.pallas_call(
        kernel_a,
        out_shape=(
            outside((TURNS, KEPT_LOW, WIDE), LOW),
            outside((TURNS, CFF, WIDE), LOW),
            outside((TURNS, CD, WIDE), F32),
            outside((TURNS, 8, WIDE), F32),
            shape((1,), jnp.int32),
            outside((SHARES, F_ROWS, 256), LOW),
            outside((SHARES, F_ROWS, 256), LOW),
            shape((WORDS, WD // 2), LOW),
            shape((WORDS, WD // 2), LOW),
            shape((8, WD), F32),
            shape((WORDS, WD), LOW), shape((WORDS, WD), LOW), shape((WORDS, WD), LOW),
            shape((WORD_HEADS, WORDS, WORDS), LOW), shape((WD, WORDS), LOW), shape((WORDS, WD), LOW),
            shape((WORDS, WD), F32), shape((WORDS, 128), F32), shape((WORDS, WD), F32),
            shape((WORDS, CD), LOW), shape((WORDS, CFF), LOW),
        ),
        in_specs=[ANYWHERE] * 22,
        out_specs=(ANYWHERE,) * 4 + (SCALARS,) + (ANYWHERE,) * 2 + (INSIDE,) * 14,
        scratch_shapes=[
            v((1, WORDS), jnp.int32), v((1, WORDS * CPW), jnp.int32), v((1, WORDS), jnp.int32),
            v((CVOC, CD), LOW), v((CD,), LOW), v((CD, CD), LOW), v((CD, CD), LOW), v((CD, CD), LOW), v((CD, CD), LOW),
            v((CD,), LOW), v((CD, CFF), LOW), v((CFF, CD), LOW), v((CD, WD), LOW), v((WD,), LOW), v((WD,), LOW),
            v((WORDS, WD), LOW),
            v((WD, WD), LOW), v((WD, WD), LOW), v((WD, WD), LOW), v((WD, WD), LOW),
            v((WD, WFF), LOW), v((WFF, WD), LOW),
            v((CD, CVOC), LOW), v((3 * CD, CD), LOW), v((CD, CD), LOW), v((CFF, CD), LOW), v((128, 32), LOW),
            v((2, KEPT_LOW, WIDE), LOW), v((2, CFF, WIDE), LOW), v((2, CD, WIDE), F32), v((2, 8, WIDE), F32),
            v((WORDS + WINDOW, CFF), F32), v((WORDS + WINDOW, CD), F32), v((16, WORDS), LOW),
            v((8, 128), jnp.int32), pltpu.SMEM((8, 128), jnp.int32),
            v((CFF, WIDE), F32), v((CFF, WIDE), LOW), v((CHAR_HEADS * SPAN, WIDE), LOW), v((8, WIDE), F32),
            v((CD, WIDE), LOW), v((CD, WIDE), LOW), v((8, WIDE), F32),
            v((2, SHARES, F_ROWS, 256), LOW),
            v((WORDS, WFF), LOW), v((WORDS, WFF), LOW),
            pltpu.SemaphoreType.DMA((15,)),
            pltpu.SemaphoreType.DMA((8,)),
            pltpu.SemaphoreType.DMA((4, 2)),
            pltpu.SemaphoreType.DMA((2,)),
        ],
        compiler_params=params(44),
        cost_estimate=pl.CostEstimate(flops=200 * 10**9, bytes_accessed=60 * 10**6, transcendentals=10**6),
        name="forward_and_words",
    )(*kept_outside(char_counts, char_ids, segment_ids, out_cotangent, *weights))


def call_a2(char_counts, kept, gain, project, weights):
    v = pltpu.VMEM
    return pl.pallas_call(
        kernel_a2,
        out_shape=(
            shape((CD, WORDS), LOW),
            outside((SHARES, T_ROWS, 256), LOW),
            outside((SHARES, T_ROWS, 256), LOW),
            shape((8, WD), F32),
        ),
        in_specs=[INSIDE] * 18,
        out_specs=(INSIDE, ANYWHERE, ANYWHERE, INSIDE),
        scratch_shapes=[
            v((2, SHARES, T_ROWS, 256), LOW),
            pltpu.SemaphoreType.DMA((2, 2)),
        ],
        compiler_params=params(20),
        cost_estimate=pl.CostEstimate(flops=200 * 10**9, bytes_accessed=10 * 10**6, transcendentals=10**6),
        name="word_attention_backward",
    )(char_counts, *kept, gain, project, *weights)


def call_b1(turns, gw, gain, up, down, kepts, keptm, kepti, f0, f1):
    v = pltpu.VMEM
    return pl.pallas_call(
        kernel_b1,
        out_shape=(outside((TURNS, CD, WIDE), LOW), shape((CD, CFF), LOW), shape((8, CD), F32), v((8, F_ROWS, 256), LOW)),
        in_specs=[SCALARS] + [INSIDE] * 4 + [ANYWHERE] * 5,
        out_specs=(ANYWHERE, INSIDE, INSIDE, INSIDE),
        scratch_shapes=[
            v((2, CFF, WIDE), LOW), v((2, CD, WIDE), F32), v((2, 8, WIDE), F32), v((2, CD, WIDE), LOW),
            v((CD, CFF), F32), v((CD, WIDE), F32), v((CFF, CD), LOW),
            v((8, F_ROWS, 256), LOW), v((8, F_ROWS, 256), LOW),
            pltpu.SemaphoreType.DMA((3, 2)),
            pltpu.SemaphoreType.DMA((2,)),
            pltpu.SemaphoreType.DMA((2,)),
        ],
        compiler_params=params(18),
        cost_estimate=pl.CostEstimate(flops=200 * 10**9, bytes_accessed=20 * 10**6, transcendentals=10**6),
        name="character_backward_one",
    )(turns, gw, gain, up, down, *kept_outside(kepts, keptm, kepti, f0, f1))


def call_b2(turns, wgain1, wgain2, gain2, aup, weights, keptl, keptd, kepti, facc, f2, t0, t1):
    v = pltpu.VMEM
    return pl.pallas_call(
        kernel_b2,
        out_shape=(
            v((SHARES, C_ROWS, 128), LOW), v((SHARES, C_ROWS, 128), LOW), v((4, F_ROWS, 256), LOW), v((4, T_ROWS, 256), LOW)
        ),
        in_specs=[SCALARS] + [INSIDE] * 9 + [ANYWHERE] * 3 + [INSIDE] + [ANYWHERE] * 3,
        out_specs=(INSIDE,) * 4,
        scratch_shapes=[
            v((2, KEPT_LOW, WIDE), LOW), v((2, 8, WIDE), F32), v((2, CD, WIDE), LOW),
            v((CHAR_HEADS * SPAN, WIDE), LOW),
            v((CD, 3 * CD), LOW),
            v((CD, 3 * CD), F32), v((CD, CD), F32), v((CVOC, CD), F32), v((CD, WIDE), F32),
            v((2, SHARES, C_ROWS, 128), LOW),
            v((4, F_ROWS, 256), LOW), v((4, T_ROWS, 256), LOW), v((4, T_ROWS, 256), LOW),
            pltpu.SemaphoreType.DMA((3, 2)),
            pltpu.SemaphoreType.DMA((3,)),
        ],
        compiler_params=params(24),
        cost_estimate=pl.CostEstimate(flops=200 * 10**9, bytes_accessed=40 * 10**6, transcendentals=10**6),
        name="character_backward_two",
    )(turns, wgain1, wgain2, gain2, aup, *weights, *kept_outside(keptl, keptd, kepti), facc, *kept_outside(f2, t0, t1))


def call_add(kernel, name, outs, parts, specs, scratch):
    v = pltpu.VMEM
    return pl.pallas_call(
        kernel,
        out_shape=tuple(v(s, LOW) for s in outs),
        in_specs=specs,
        out_specs=(INSIDE,) * len(outs),
        scratch_shapes=[v(s, LOW) for s in scratch] + [pltpu.SemaphoreType.DMA((len(scratch),))],
        compiler_params=params(12),
        name=name,
    )(*parts)


def add_one(f0, f1):
    half = (8, F_ROWS, 256)
    return call_add(kernel_add_one, "add_one", (half,), kept_outside(f0, f1), [ANYWHERE] * 2, (half, half))[0]


def add_two(facc, f2, t0, t1):
    fs, ts = (4, F_ROWS, 256), (4, T_ROWS, 256)
    return call_add(
        kernel_add_two, "add_two", (fs, ts, ts, ts), (facc, *kept_outside(f2, t0, t1)), [INSIDE] + [ANYWHERE] * 3,
        (fs, (3,) + ts, (3,) + ts),
    )


def add_three(facc, f3, tacc, tgot):
    fs, ts = (2, F_ROWS, 256), (2, T_ROWS, 256)
    return call_add(
        kernel_add_three, "add_three", (fs, fs, ts, ts), (facc, *kept_outside(f3), tacc, *kept_outside(*tgot)),
        [INSIDE, ANYWHERE] * 2 + [ANYWHERE] * 2, ((4, F_ROWS, 256), (3, 4, T_ROWS, 256)),
    )


def call_f(words, c, outk, outg):
    v = pltpu.VMEM
    outs = ((CVOC, CD), (CD,), (CD, CD), (CD, CD), (CD, CD), (CD, CD), (CD,), (CD, CFF), (CFF, CD), (CD, WD),
            (WD,), (WD, WD), (WD, WD), (WD, WD), (WD, WD), (WD,), (WD, WFF), (WFF, WD))
    outs = [(s[0] // SHARES,) + tuple(n // 2 for n in s[1:]) for s in outs]
    return pl.pallas_call(
        kernel_f,
        out_shape=(shape((2, 1, WORDS, WD // 2), LOW),) + tuple(shape(s, F32) for s in outs),
        in_specs=[pl.BlockSpec(memory_space=pl.ANY)] * 13 + [INSIDE] * 2,
        out_specs=(INSIDE,) * 19,
        scratch_shapes=[
            v((3, F_ROWS, 256), LOW), v((3, T_ROWS, 256), LOW), v((8, C_ROWS, 128), LOW), pltpu.SemaphoreType.DMA((3,)),
        ],
        compiler_params=params(8),
        name="finish",
    )(*words, *c, outk, outg)


def flip(value, axis, bits):
    count = lax.axis_size(axis)
    return lax.ppermute(value, axis, [(i, i ^ bits) for i in range(count)])


def flip_both(value, first, second):
    pairs = [(i, i ^ first) for i in range(SHARES)] + [(SHARES + i, SHARES + (i ^ second)) for i in range(SHARES)]
    return lax.ppermute(value, ("phase", "dp"), pairs)


def pick(value, index):
    return lax.dynamic_index_in_dim(value, index, 0, keepdims=False)


def plus(*parts):
    total = parts[0].astype(F32)
    for part in parts[1:]:
        total = total + part.astype(F32)
    return total.astype(LOW)


def across(value, side):
    return flip_both(value, *((1, 2), (2, 1), (4, 4), (8, 8))[side])


def half(bit, *parts):
    return plus(*(lax.dynamic_slice_in_dim(part, bit * (part.shape[0] // 2), part.shape[0] // 2, 0) for part in parts))


def after(value, *others):
    return lax.optimization_barrier((value,) + others)[0]


def together(*values):
    return lax.optimization_barrier(values)


def body(
    char_ids, char_counts, segment_ids, out_cotangent,
    char_table, char_gain_one, char_query, char_key, char_value, char_output, char_gain_two, char_up, char_down,
    char_project,
    word_gain_one, word_query, word_key, word_value, word_output, word_gain_two, word_up, word_down,
):
    keptl, kepts, keptm, kepti, turns, fkeep, fsend, outk, outs, wgain2, *words = call_a(
        char_counts, char_ids, segment_ids, out_cotangent,
        (char_table, char_gain_one, char_query, char_key, char_value, char_output, char_gain_two, char_up, char_down,
         char_project,
         word_gain_one, word_query, word_key, word_value, word_output, word_gain_two, word_up, word_down),
    )
    fgot = flip(fsend, "phase", 1)
    outg = flip(outs, "phase", 1)
    gw, tkeep, tsend, wgain1 = call_a2(
        char_counts, words, word_gain_one, char_project, (word_query, word_key, word_value, word_output)
    )
    one = (char_gain_two, char_up, char_down, kepts, keptm, kepti)
    two = (char_gain_one, char_query, char_key, char_value, char_output)
    if lax.axis_size("dp") != SHARES:
        keptd, aup, gain2, facc = call_b1(turns, gw, *one, fkeep, fgot)
        tgot = flip(tsend, "phase", 1)
        ckeep, csend, _, _ = call_b2(turns, wgain1, wgain2, gain2, aup, two, keptl, keptd, kepti, facc, facc, tkeep, tgot)
        return general_sums(outk, outg, (fkeep, fgot), (tkeep, tgot), (ckeep, flip(csend, "phase", 1)))
    gw, tsend, fgot, outg = together(gw, tsend, fgot, outg)
    gw, fsend = together(gw, add_one(fkeep, fgot))
    f2, tgot = across(fsend, 0), flip(tsend, "phase", 1)
    keptd, aup, gain2, facc = call_b1(turns, gw, *one, fkeep, fgot)
    keptd, f2, tgot = together(keptd, f2, tgot)
    sends = add_two(facc, f2, tkeep, tgot)
    keptd, fsend, *tsends = together(keptd, *sends)
    f3, *tparts = across(fsend, 2), *(flip(send, "dp", k) for k, send in enumerate(tsends, 1))
    ckeep, csend, facc, tacc = call_b2(
        turns, wgain1, wgain2, gain2, aup, two, keptl, keptd, kepti, facc, f2, tkeep, tgot
    )
    ckeep, csend, facc, f3, *tparts = together(ckeep, csend, facc, f3, *tparts)
    _, _, low, high = own_bits()
    cphase = flip(csend, "phase", 1)
    fsend, facc, tsend, tacc = add_three(facc, f3, tacc, tparts)
    f4, t3 = across(fsend, 1), across(tsend, 2)
    dp = lax.axis_index("dp")
    plane, line = lax.rem(dp, 4), lax.div(dp, 4)
    c = [ckeep.reshape(4, 4, C_ROWS, 128), cphase.reshape(4, 4, C_ROWS, 128)]
    sends = [plus(*(pick(part, lax.bitwise_xor(plane, k)) for part in c)) for k in range(1, 4)]
    cgot = [flip(send, "dp", k) for k, send in enumerate(sends, 1)]
    f4, t3 = after(f4, *sends), after(t3, *sends)
    last = jnp.concatenate([pick(half(1 - high, facc, f4), 0), pick(half(1 - high, tacc, t3), 0)], axis=0)
    last = across(last, 3)
    c = [pick(part, plane) for part in c] + cgot
    sends = [plus(*(pick(part, lax.bitwise_xor(line, k)) for part in c)) for k in range(1, 4)]
    cline = [flip(send, "dp", 4 * k) for k, send in enumerate(sends, 1)]
    return call_f((facc, f4, tacc, t3, last), (ckeep, cphase, *cgot, *cline), outk, outg)


def general_sums(outk, outg, fs, ts, cs):
    phase = lax.axis_index("phase")
    first = phase == 0
    outs = jnp.stack([jnp.where(first, outk, outg), jnp.where(first, outg, outk)])[:, None]
    def order(places):
        plain, swapped = (jnp.asarray([places(d, core) for d in range(SHARES)]) for core in range(2))
        return jnp.where(first, plain, swapped)

    def natural(pair, order):
        return jnp.take(pair[0].astype(F32) + pair[1].astype(F32), order, axis=0)

    f, t, c = natural(fs, order(feed_order)), natural(ts, order(word_order)), natural(cs, jnp.asarray([plane_first(d) for d in range(SHARES)]))

    def whole(rows):
        return rows.reshape(-1, rows.shape[-1])

    def wide(rows, pieces):
        n = rows.shape[1] // pieces
        return whole(rows.reshape(SHARES, pieces, n, rows.shape[-1]).transpose(0, 2, 1, 3).reshape(SHARES, n, -1))

    cdown = t[:, T_CDOWN:T_CDOWN + 32]
    cdown = jnp.concatenate([cdown[..., :128], cdown[..., 128:]], axis=1)
    parts = (
        whole(c[:, C_TABLE:C_TABLE + 16]), c[:, C_GAIN, :16].reshape(-1),
        whole(c[:, C_Q:C_Q + 16]), whole(c[:, C_K:C_K + 16]), whole(c[:, C_V:C_V + 16]), whole(c[:, C_O:C_O + 16]),
        c[:, C_GAIN + 1, :16].reshape(-1),
        wide(c[:, C_UP:C_UP + 64], 4), whole(cdown), whole(t[:, T_PROJ:T_PROJ + 16]),
        c[:, C_GAIN + 2, :32].reshape(-1),
        whole(t[:, T_Q:T_Q + 32]), whole(t[:, T_K:T_K + 32]), whole(t[:, T_V:T_V + 32]), whole(t[:, T_O:T_O + 32]),
        c[:, C_GAIN + 3, :32].reshape(-1),
        wide(f[:, F_UP:F_UP + 128], 4), whole(f[:, F_DOWN:F_DOWN + 128]),
    )
    return (outs,) + tuple(lax.psum_scatter(p, "dp", scatter_dimension=0, tiled=True) for p in parts)


def solution(mesh):
    rows = P(None, "dp", None)
    both = P("dp", "phase")
    one = P("dp")
    return jax.shard_map(
        body,
        mesh=mesh,
        in_specs=(rows, rows, rows, P(None, "dp", None, None)) + (P(),) * 18,
        out_specs=(
            P(None, "dp", None, "phase"),
            both, one, both, both, both, both, one, both, both, both,
            one, both, both, both, both, one, both, both,
        ),
        check_vma=False,
    )
```

```python
from functools import partial

import jax
import jax.numpy as jnp
from jax import lax
from jax.experimental import pallas as pl
from jax.experimental.pallas import tpu as pltpu
from jax.sharding import PartitionSpec as P

F32 = jnp.float32
LOW = jnp.bfloat16

CD = 256
CFF = 1024
CPW = 16
CVOC = 256
CHAR_HEADS = 4
HEAD = 64
WD = 512
WFF = 2048
WORD_HEADS = 8
WORDS = 256

SCHEDULE = "aaaafaaaaaaaaafaaaaaaaaafaaaaafa"
SPAN = 256
STEP = 241
WIDE = 2 * SPAN
TURNS = ((WORDS * CPW - 1) // STEP + 2) // 2

epsilon = 1e-06
half_root = 0.7071067811865476
density = 0.3989422804014327
floor_score = -1e30
log2_e = 1.4426950408889634

R_EMB, R_Q, R_K, R_V, R_P, R_MIX = 0, 256, 512, 768, 1024, 2048
KEPT_LOW = 2304
I_INV1, I_INV2, I_IDENT, I_WORD = 0, 1, 2, 3
BAND = 144
WINDOW = 96

F_UP, F_DOWN = 0, 128
F_ROWS = 256
T_Q, T_K, T_V, T_O, T_CDOWN, T_PROJ = 0, 32, 64, 96, 128, 160
T_ROWS = 176
C_TABLE, C_Q, C_K, C_V, C_O, C_UP, C_GAIN = 0, 16, 32, 48, 64, 80, 144
C_ROWS = 160
SHARES = 16


def nn(left, right):
    return lax.dot_general(left, right, (((1,), (0,)), ((), ())), preferred_element_type=F32)


def nt(left, right):
    return lax.dot_general(left, right, (((1,), (1,)), ((), ())), preferred_element_type=F32)


def iota(shape, axis):
    return lax.broadcasted_iota(jnp.int32, shape, axis)


def eye(n):
    return iota((n, n), 0) == iota((n, n), 1)


def row_to_column(row):
    n = row.shape[1]
    return jnp.sum(jnp.where(eye(n), row, 0.0), axis=1, keepdims=True)


def gelu_pair(v):
    e = lax.erf(v * half_root)
    half = 0.5 * v
    bell = jnp.exp2(v * v * (-0.5 * log2_e))
    return half + half * e, 0.5 + 0.5 * e + (density * v) * bell


def gelu_twice(v):
    u = v * half_root
    whole = 1.0 + lax.erf(u)
    bell = jnp.exp2(u * u * (-log2_e))
    return v * whole, whole + (2.0 * density * v) * bell


def bits(d):
    return d % 2, d // 2 % 2, d // 4 % 2, d // 8


def plane_first(d, core=0):
    return (d % 4) * 4 + d // 4


def feed_order(d, core):
    x, y, low, high = bits(d)
    return (y * 8 + x * 2 if core else x * 8 + y * 2) + low * 4 + high


def word_order(d, core=0):
    _, _, low, high = bits(d)
    return (d % 4) * 4 + low * 2 + high


def own_bits():
    phase, dp = lax.axis_index("phase"), lax.axis_index("dp")
    x, y, low, high = (lax.rem(lax.div(dp, n), 2) for n in (1, 2, 4, 8))
    return jnp.where(phase == 0, x, y), jnp.where(phase == 0, y, x), low, high


def own_plane():
    return lax.rem(lax.axis_index("dp"), 4)


def add_up(out, *parts):
    for i in range(out.shape[0]):
        if len(parts) == 2:
            out[i] = parts[0][i] + parts[1][i]
            continue
        total = parts[0][i].astype(F32)
        for part in parts[1:]:
            total = total + part[i].astype(F32)
        out[i] = total.astype(LOW)


def members(word, first, count, weight=1.0):
    return jnp.where((iota((count, WIDE), 0) + first).astype(F32) == word, weight, 0.0).astype(LOW)


def word_starts(counts_row):
    earlier = iota((WORDS, WORDS), 1) < iota((WORDS, WORDS), 0)
    return jnp.sum(jnp.where(earlier, counts_row, 0.0), axis=1, keepdims=True)


def column_to_row(column):
    return jnp.sum(jnp.where(eye(column.shape[0]), column, 0.0), axis=0, keepdims=True)


def put(keep, send, phase, order, row, halves, share_rows):
    width, lanes = halves[0].shape[1], keep.shape[-1]
    first = phase == 0
    mine, other = jnp.where(first, halves[0], halves[1]), jnp.where(first, halves[1], halves[0])
    for out, low, core in ((keep, mine, phase), (send, other, 1 - phase)):
        for i in range(low.shape[0] // share_rows):
            at, swapped = order(i, 0), order(i, 1)
            if at != swapped:
                at = at + core * (swapped - at)
            rows = low[i * share_rows:(i + 1) * share_rows]
            for piece in range(max(1, width // lanes)):
                part = rows[:, piece * lanes:piece * lanes + min(width, lanes)]
                if width < lanes:
                    part = jnp.concatenate([part[:share_rows // 2], part[share_rows // 2:]], axis=1)
                m = part.shape[0]
                out[at, row + piece * share_rows:row + piece * share_rows + m, :] = part


def column_halves(value):
    width = value.shape[1] // 2
    low = value.astype(LOW)
    return low[:, :width], low[:, width:]


def band(t):
    keys = slice(0, BAND) if t % 2 == 0 else slice(SPAN - BAND, SPAN)
    return t // 2, keys, slice(t * 128, (t + 1) * 128)


def two_heads(pair):
    zero = jnp.zeros((HEAD, pair.shape[1]), LOW)
    first = jnp.concatenate([pair[:HEAD], zero], axis=0)
    second = jnp.concatenate([zero, pair[HEAD:]], axis=0)
    return jnp.concatenate([first, second], axis=1)


def two_heads_rows(pair):
    left = iota(pair.shape, 1) < HEAD
    zero = jnp.zeros(pair.shape, LOW)
    return jnp.concatenate([jnp.where(left, pair, zero), jnp.where(left, zero, pair)], axis=0)


def softmax_keys(s):
    e = jnp.exp(s - jnp.max(s, axis=0, keepdims=True))
    return (e * (1.0 / jnp.sum(e, axis=0, keepdims=True))).astype(LOW)


def kernel_a(
    counts_hbm, ids_hbm, segs_hbm, cot_hbm,
    table_hbm, g1_hbm, wq_hbm, wk_hbm, wv_hbm, wo_hbm, g2_hbm, up_hbm, down_hbm, proj_hbm,
    wg1_hbm, wwq_hbm, wwk_hbm, wwv_hbm, wwo_hbm, wg2_hbm, wup_hbm, wdown_hbm,
    keptl_hbm, kepts_hbm, keptm_hbm, kepti_hbm, turns_ref,
    keep_ref, send_ref, outk_ref, outs_ref, gain_ref,
    q_ref, k_ref, v_ref, probs_ref, mixt_ref, normed_ref, xhat_ref, winv_ref, md_ref, pooled_ref, pa_ref,
    counts_ref, ids_ref, segs_ref,
    table_ref, g1_ref, wq_ref, wk_ref, wv_ref, wo_ref, g2_ref, up_ref, down_ref, proj_ref, wg1_ref, wg2_ref,
    cot, wwq, wwk, wwv, wwo, wup, wdown,
    tab_t, wqkv_t, wo_t, up_t, ids_t, slow, sslope, smid, sinfo, pa, pm, rowinfo, firsts_v, firsts, before_s, act_s, prob_s, found_s,
    mid_s, word_s, old_s,
    actw, slopew,
    csem, wsem, ksem,
):
    phase = lax.axis_index("phase")
    tiny = [
        pltpu.make_async_copy(src.at[phase], dst, csem.at[12 + i])
        for i, (src, dst) in enumerate(((counts_hbm, counts_ref), (ids_hbm, ids_ref), (segs_hbm, segs_ref)))
    ]
    for load in tiny:
        load.start()
    early = [
        pltpu.make_async_copy(src, dst, csem.at[i])
        for i, (src, dst) in enumerate(
            ((g1_hbm, g1_ref), (g2_hbm, g2_ref), (table_hbm, table_ref), (wq_hbm, wq_ref), (wk_hbm, wk_ref),
             (wv_hbm, wv_ref), (wo_hbm, wo_ref), (up_hbm, up_ref), (down_hbm, down_ref), (proj_hbm, proj_ref),
             (wg1_hbm, wg1_ref), (wg2_hbm, wg2_ref))
        )
    ]
    for load in early:
        load.start()
    loads = [
        pltpu.make_async_copy(src, dst, wsem.at[i])
        for i, (src, dst) in enumerate(
            ((wwq_hbm, wwq), (wwk_hbm, wwk), (wwv_hbm, wwv), (wwo_hbm, wwo),
             (wup_hbm, wup), (wdown_hbm, wdown), (cot_hbm.at[phase, 0], cot))
        )
    ]
    pa[...] = jnp.zeros_like(pa)
    pm[...] = jnp.zeros_like(pm)
    prob_s[...] = jnp.zeros_like(prob_s)
    for slot in range(2):
        slow[slot, R_P:R_P + CHAR_HEADS * SPAN] = jnp.zeros((CHAR_HEADS * SPAN, WIDE), LOW)
    for load in tiny:
        load.wait()
    counts_row = counts_ref[...].astype(F32)
    starts = word_starts(counts_row)
    counts = row_to_column(counts_row)
    blocks = jnp.floor((starts + 0.5) * (1.0 / STEP))
    places = starts + (SPAN - STEP) * blocks
    n_turns = jnp.max(places).astype(jnp.int32) // WIDE + 1
    turns_ref[0] = n_turns
    bases = (iota((1, 128), 1) * WIDE).astype(F32)
    first = jnp.sum(jnp.where(places < bases, 1.0, 0.0), axis=0, keepdims=True)
    firsts_v[...] = jnp.broadcast_to(first, (8, 128)).astype(jnp.int32)
    first_copy = pltpu.make_async_copy(firsts_v, firsts, wsem.at[7])
    first_copy.start()
    ids = ids_ref[...]
    ids_t[...] = jnp.concatenate(
        [ids[:, 128 * a:128 * a + 128] for a in range(32)], axis=0
    ).astype(F32).T.astype(LOW)
    places_row = column_to_row(places)
    none = jnp.zeros((1, 1), F32)
    rowinfo[...] = jnp.concatenate(
        [places_row - jnp.concatenate([none, places_row[:, :-1]], axis=1),
         counts_row - jnp.concatenate([none, counts_row[:, :-1]], axis=1),
         jnp.ones((1, WORDS), F32), jnp.zeros((13, WORDS), F32)], axis=0
    ).astype(LOW)
    for load in early:
        load.wait()
    for load in loads:
        load.start()
    tab_t[...] = table_ref[...].T
    wqkv_t[0:CD] = (wq_ref[...] * 0.125).T
    wqkv_t[CD:2 * CD] = wk_ref[...].T
    wqkv_t[2 * CD:] = wv_ref[...].T
    wo_t[...] = wo_ref[...].T
    up_t[...] = up_ref[...].T
    g1 = row_to_column(g1_ref[...].astype(F32)[None, :])
    g2 = row_to_column(g2_ref[...].astype(F32)[None, :])
    first_copy.wait()

    def find(turn):
        place = (iota((1, WIDE), 1) + turn * WIDE).astype(F32)
        begun = jnp.where(places <= place, 1.0, 0.0).astype(LOW)
        info = nn(rowinfo[...], begun)
        word = info[2:3] - 1.0
        slot = place - info[0:1]
        flat = (word * 16.0 + slot).astype(jnp.int32)
        chosen = jnp.where(iota((32, WIDE), 0) == (flat >> 7), 1.0, 0.0).astype(LOW)
        lanes = nn(ids_t[...], chosen)
        ident = jnp.sum(jnp.where(iota((128, WIDE), 0) == (flat & 127), lanes, 0.0), axis=0, keepdims=True)
        valid = slot < info[1:2]
        none = jnp.full((6, WIDE), -1.0, F32)
        return jnp.concatenate([jnp.where(valid, ident, -1.0), jnp.where(valid, word, -1.0), none], axis=0)

    found_s[...] = find(jnp.int32(0))

    def copies_one(b):
        slot = lax.rem(b, 2)
        return (
            pltpu.make_async_copy(slow.at[slot], keptl_hbm.at[b], ksem.at[0, slot]),
            pltpu.make_async_copy(smid.at[slot], keptm_hbm.at[b], ksem.at[2, slot]),
            pltpu.make_async_copy(sinfo.at[slot], kepti_hbm.at[b], ksem.at[3, slot]),
        )

    def copies_two(b):
        slot = lax.rem(b, 2)
        return (pltpu.make_async_copy(sslope.at[slot], kepts_hbm.at[b], ksem.at[1, slot]),)

    def start(copies):
        for c in copies:
            c.start()

    def wait(copies):
        for c in copies:
            c.wait()

    def near_words(b):
        first = (firsts[0, b] // 16) * 16
        return first, (firsts[0, b + 1] - first + WINDOW - 1) // WINDOW

    def window(first):
        return pl.ds(pl.multiple_of(first, 16), WINDOW)

    def attend(b):
        slot = lax.rem(b, 2)
        ident = found_s[0:1]
        word = found_s[1:2]
        hot = jnp.where(iota((CVOC, WIDE), 0).astype(F32) == ident, 1.0, 0.0).astype(LOW)
        emb = nn(tab_t[...], hot)
        inv1 = lax.rsqrt(jnp.mean(emb * emb, axis=0, keepdims=True) + epsilon)
        normed = (emb * inv1 * g1).astype(LOW)
        yield
        qkv = []
        for i in range(3):
            qkv.append(nn(wqkv_t[i * CD:(i + 1) * CD], normed).astype(LOW))
            yield
        query_t, key_t, value_t = qkv
        slow[slot, R_EMB:R_EMB + CD] = emb.astype(LOW)
        slow[slot, R_Q:R_Q + CD] = query_t
        slow[slot, R_K:R_K + CD] = key_t
        key_rows = [key_t[:, u * SPAN:(u + 1) * SPAN].T for u in range(2)]
        word_col = jnp.broadcast_to(jnp.where(word < 0.0, -2.0, word), (8, WIDE)).T[:, 0:1]
        yield
        scores = []
        for t in range(4):
            u, ks, ql = band(t)
            for pair in range(CHAR_HEADS // 2):
                fs = slice(pair * 128, pair * 128 + 128)
                scores.append(nn(key_rows[u][ks, fs], two_heads(query_t[fs, ql])))
                yield
        for u in range(2):
            us = slice(u * SPAN, (u + 1) * SPAN)
            slow[slot, R_V:R_V + SPAN, us] = value_t[:, us].T
        for t in range(4):
            u, ks, ql = band(t)
            bias = jnp.where(word_col[u * SPAN + ks.start:u * SPAN + ks.stop] == word[:, ql], 0.0, floor_score)
            for pair in range(CHAR_HEADS // 2):
                s = scores[t * 2 + pair]
                for i in range(2):
                    p = softmax_keys(s[:, i * 128:i * 128 + 128] + bias)
                    row = (pair * 2 + i) * SPAN
                    prob_s[row + ks.start:row + ks.stop, ql] = p
                    slow[slot, R_P + row + ks.start:R_P + row + ks.stop, ql] = p
        yield
        mixed = [[], []]
        for u in range(2):
            us = slice(u * SPAN, (u + 1) * SPAN)
            for h in range(CHAR_HEADS):
                hs = slice(h * HEAD, (h + 1) * HEAD)
                mixed[u].append(nn(value_t[hs, us], prob_s[h * SPAN:(h + 1) * SPAN, us]).astype(LOW))
                yield
        mixed = jnp.concatenate([jnp.concatenate(part, axis=0) for part in mixed], axis=1)
        slow[slot, R_MIX:R_MIX + CD] = mixed
        middle = emb + nn(wo_t[...], mixed)
        yield
        inv2 = lax.rsqrt(jnp.mean(middle * middle, axis=0, keepdims=True) + epsilon)
        smid[slot] = middle
        sinfo[slot] = jnp.concatenate([inv1, inv2, ident, word, jnp.zeros((4, WIDE), F32)], axis=0)
        normed_two = (middle * inv2 * g2).astype(LOW)
        middle_low = middle.astype(LOW)
        yield
        for c in range(CFF // 256):
            cs = slice(c * 256, (c + 1) * 256)
            before_s[cs] = nn(up_t[cs], normed_two)
            if c == 0:
                found_s[...] = find(b + 1)
            if c == 1:
                first, _ = near_words(b)
                pm[window(first), :] += nt(members(word, first, WINDOW), middle_low)
                mid_s[...] = middle_low
            if c == 3:
                old_s[0:1] = word_s[0:1]
                word_s[0:1] = word
            yield

    def feed(b):
        slot = lax.rem(b, 2)
        first, _ = near_words(b)
        near = members(word_s[0:1], first, WINDOW, 0.5)
        for c in range(CFF // 256):
            for d in range(8):
                cs = slice(c * 256 + d * 32, c * 256 + (d + 1) * 32)
                act, slope = gelu_twice(before_s[cs])
                sslope[slot, cs] = slope.astype(LOW)
                act_s[cs] = act.astype(LOW)
            cs = slice(c * 256, (c + 1) * 256)
            pa[window(first), cs] += nt(near, act_s[cs])
            yield

    def run(order, one, two):
        parts = {"a": one, "f": two}
        for step in order:
            next(parts[step])

    def more_one(b):
        first, windows = near_words(b)

        def more(i, carry):
            at = first + i * WINDOW
            pm[window(at), :] += nt(members(word_s[0:1], at, WINDOW), mid_s[...])
            return carry

        lax.fori_loop(1, windows, more, 0)

    def more_two(b, word):
        first, windows = near_words(b)

        def more(i, carry):
            at = first + i * WINDOW
            pa[window(at), :] += nt(members(word[0:1], at, WINDOW, 0.5), act_s[...])
            return carry

        lax.fori_loop(1, windows, more, 0)

    run("a" * 28, attend(jnp.int32(0)), None)
    more_one(jnp.int32(0))
    start(copies_one(jnp.int32(0)))

    def turn(b, carry):
        @pl.when(b >= 2)
        def _():
            wait(copies_one(b - 2))

        @pl.when(b >= 3)
        def _():
            wait(copies_two(b - 3))

        run(SCHEDULE, attend(b), feed(b - 1))
        more_one(b)
        more_two(b - 1, old_s)
        start(copies_one(b))
        start(copies_two(b - 1))
        return carry

    lax.fori_loop(1, n_turns, turn, 0)

    @pl.when(n_turns >= 3)
    def _():
        wait(copies_two(n_turns - 3))

    run("f" * 4, None, feed(n_turns - 1))
    more_two(n_turns - 1, word_s)
    start(copies_two(n_turns - 1))

    pa_hi = pa[0:WORDS].astype(LOW)
    per_count = 1.0 / counts
    pooled = (pm[0:WORDS] + nn(pa_hi, down_ref[...])) * per_count
    pooled_low = pooled.astype(LOW)
    pooled_ref[...] = pooled_low
    pa_ref[...] = pa_hi
    x = nn(pooled_low, proj_ref[...]).astype(LOW).astype(F32)
    for load in loads:
        load.wait()
    wg1 = wg1_ref[...].astype(F32)[None, :]
    wg2 = wg2_ref[...].astype(F32)[None, :]
    winv1 = lax.rsqrt(jnp.mean(x * x, axis=1, keepdims=True) + epsilon)
    xhat = x * winv1
    normed = (xhat * wg1).astype(LOW)
    xhat_ref[...] = xhat
    winv_ref[...] = jnp.broadcast_to(winv1, (WORDS, 128))
    normed_ref[...] = normed
    q = (nn(normed, wwq[...]) * 0.125).astype(LOW)
    k = nn(normed, wwk[...]).astype(LOW)
    v = nn(normed, wwv[...]).astype(LOW)
    seg_row = segs_ref[...].astype(F32)
    seg_col = row_to_column(seg_row)
    allowed = (seg_row == seg_col) & (iota((WORDS, WORDS), 0) <= iota((WORDS, WORDS), 1))
    bias = jnp.where(allowed, 0.0, floor_score)
    q_ref[...] = q
    k_ref[...] = k
    v_ref[...] = v
    v_t = v.T
    for h in range(WORD_HEADS):
        probs_ref[h, 128:, 0:128] = jnp.zeros((128, 128), LOW)
    halves = [(slice(0, 128 * (t + 1)), slice(128 * t, 128 * (t + 1))) for t in range(2)]
    pairs = [slice(pair * 128, pair * 128 + 128) for pair in range(WORD_HEADS // 2)]
    scores = [[nt(k[ks, fs], two_heads_rows(q[ql, fs])) for ks, ql in halves] for fs in pairs]
    mixed_t = []
    for pair in range(WORD_HEADS // 2):
        for (ks, ql), s in zip(halves, scores[pair]):
            for i in range(2):
                probs_ref[pair * 2 + i, ks, ql] = softmax_keys(s[:, i * 128:i * 128 + 128] + bias[ks, ql])
        for h in (pair * 2, pair * 2 + 1):
            mixed_t.append(nn(v_t[h * HEAD:(h + 1) * HEAD], probs_ref[h]).astype(LOW))
    mixed_t = jnp.concatenate(mixed_t, axis=0)
    mixt_ref[...] = mixed_t
    middle = x + nn(mixed_t.T, wwo[...])
    winv2 = lax.rsqrt(jnp.mean(middle * middle, axis=1, keepdims=True) + epsilon)
    normed_two = (middle * winv2 * wg2).astype(LOW)
    result = middle
    for c in range(WFF // 512):
        cs = slice(c * 512, (c + 1) * 512)
        act, slope = gelu_pair(nn(normed_two, wup[:, cs]))
        act = act.astype(LOW)
        actw[:, cs] = act
        slopew[:, cs] = slope.astype(LOW)
        result = result + nn(act, wdown[cs, :])
    result = result.astype(LOW)
    front = phase == 0
    outk_ref[...] = jnp.where(front, result[:, :256], result[:, 256:])
    outs_ref[...] = jnp.where(front, result[:, 256:], result[:, :256])

    cot_low = cot[...]
    n2d = jnp.zeros((WORDS, WD), F32)
    n2_t = normed_two.T
    held = {}
    for c in (0, 2, 1, 3):
        cs = slice(c * 512, (c + 1) * 512)
        gd = nn(actw[:, cs].T, cot_low)
        put(keep_ref, send_ref, phase, lambda i, p: feed_order(c * 4 + i, p), F_DOWN, column_halves(gd), 128)
        bd = (nt(cot_low, wdown[cs, :]) * slopew[:, cs].astype(F32)).astype(LOW)
        gu = nn(n2_t, bd).astype(LOW)
        if c < 2:
            held[c] = gu
        else:
            put(keep_ref, send_ref, phase, feed_order, F_UP + (c - 2) * 64, (held[c - 2], gu), 32)
        n2d = n2d + nt(bd, wup[:, cs])
    vhat = middle * winv2
    gain_ref[...] = jnp.broadcast_to(jnp.sum(n2d * vhat, axis=0, keepdims=True), (8, WD))
    lifted = n2d * wg2
    md_ref[...] = cot[...].astype(F32) + winv2 * (lifted - vhat * jnp.mean(lifted * vhat, axis=1, keepdims=True))

    def drain(b, carry):
        wait(copies_one(b))
        wait(copies_two(b))
        return carry

    lax.fori_loop(jnp.maximum(n_turns - 2, 0), n_turns, drain, 0)


def kernel_a2(
    counts_ref, q_ref, k_ref, v_ref, pw, mixt_ref, normed_ref, xhat_ref, winv_ref, md_ref, pooled_ref, pa_ref,
    wg1_ref, proj_ref, wwq, wwk, wwv, wwo,
    gw_ref, keep_ref, send_ref, gain_ref,
):
    phase = lax.axis_index("phase")
    wg1 = wg1_ref[...].astype(F32)[None, :]
    q, k, v, normed, pooled_low = q_ref[...], k_ref[...], v_ref[...], normed_ref[...], pooled_ref[...]
    per_count = 1.0 / row_to_column(counts_ref[phase].astype(F32))
    md = md_ref[...]
    md_low = md.astype(LOW)
    put(keep_ref, send_ref, phase, word_order, T_O, column_halves(nn(mixt_ref[...], md_low)), 32)
    k_t = k.T
    do = nt(md_low, wwo[...]).astype(LOW)
    dq_t, dk, dv = [], [], []
    left = iota((WORDS, 128), 1) < HEAD
    pairs = [slice(pair * 128, pair * 128 + 128) for pair in range(WORD_HEADS // 2)]
    halves = [(slice(0, 128 * (t + 1)), slice(128 * t, 128 * (t + 1))) for t in range(2)]
    deltas = [[nt(v[ks, fs], two_heads_rows(do[ql, fs])) for ks, ql in halves] for fs in pairs]

    def scores(pair):
        ds = []
        for (ks, ql), dp in zip(halves, deltas[pair]):
            for i in range(2):
                pf = pw[pair * 2 + i, ks, ql].astype(F32)
                dph = dp[:, i * 128:i * 128 + 128]
                d = (pf * (dph - jnp.sum(pf * dph, axis=0, keepdims=True))).astype(LOW)
                ds.append(d if ks.stop == WORDS else jnp.concatenate([d, jnp.zeros((128, 128), LOW)], axis=0))
        return [jnp.concatenate([ds[i], ds[i + 2]], axis=1) for i in range(2)]

    both = None
    for pair in range(WORD_HEADS // 2 + 1):
        ahead = scores(pair) if pair < WORD_HEADS // 2 else None
        if ahead is not None:
            fs = pairs[pair]
            dv.append(jnp.where(left, nn(pw[pair * 2], do[:, fs]), nn(pw[pair * 2 + 1], do[:, fs])).astype(LOW))
        if both is not None:
            fs = pairs[pair - 1]
            for i in range(2):
                h = (pair - 1) * 2 + i
                dq_t.append(nn(k_t[h * HEAD:(h + 1) * HEAD], both[i]))
            dk.append(jnp.where(left, nn(both[0], q[:, fs]), nn(both[1], q[:, fs])).astype(LOW))
        both = ahead
    dq = (jnp.concatenate(dq_t, axis=0) * 0.125).astype(LOW).T
    dk = jnp.concatenate(dk, axis=1)
    dv = jnp.concatenate(dv, axis=1)
    normed_t = normed.T
    nd = nt(dq, wwq[...]) + nt(dk, wwk[...]) + nt(dv, wwv[...])
    put(keep_ref, send_ref, phase, word_order, T_Q, column_halves(nn(normed_t, dq)), 32)
    put(keep_ref, send_ref, phase, word_order, T_K, column_halves(nn(normed_t, dk)), 32)
    put(keep_ref, send_ref, phase, word_order, T_V, column_halves(nn(normed_t, dv)), 32)
    vhat = xhat_ref[...]
    gain_ref[...] = jnp.broadcast_to(jnp.sum(nd * vhat, axis=0, keepdims=True), (8, WD))
    lifted = nd * wg1
    xd = md + winv_ref[:, 0:1] * (lifted - vhat * jnp.mean(lifted * vhat, axis=1, keepdims=True))
    vd = xd.astype(LOW)
    put(keep_ref, send_ref, phase, word_order, T_PROJ, column_halves(nn(pooled_low.T, vd)), 16)
    gw = (nt(vd, proj_ref[...]) * per_count).astype(LOW)
    gw_ref[...] = gw.T
    put(keep_ref, send_ref, phase, word_order, T_CDOWN, column_halves(nn(pa_ref[...].T, gw)), 64)


def kernel_b1(
    turns_ref, gw_ref, g2_ref, up_ref, down_ref, kepts_hbm, keptm_hbm, kepti_hbm, f0_ref, f1_hbm,
    keptd_hbm, aup_ref, gain_ref, facc_ref,
    sslope, smid, sinfo, sdelta, aup, ag2, down, f1, ksem, dsem, fsem,
):
    n_turns = turns_ref[0]

    def kept_copies(b, slot):
        return (
            pltpu.make_async_copy(kepts_hbm.at[b], sslope.at[slot], ksem.at[0, slot]),
            pltpu.make_async_copy(keptm_hbm.at[b], smid.at[slot], ksem.at[1, slot]),
            pltpu.make_async_copy(kepti_hbm.at[b], sinfo.at[slot], ksem.at[2, slot]),
        )

    def delta_copy(b, slot):
        return pltpu.make_async_copy(sdelta.at[slot], keptd_hbm.at[b], dsem.at[slot])

    for c in kept_copies(0, 0):
        c.start()
    a, _, _, _ = own_bits()
    load = pltpu.make_async_copy(f1_hbm.at[pl.ds(a * 8, 8)], f1, fsem.at[0])
    load.start()
    g2 = row_to_column(g2_ref[...].astype(F32)[None, :])
    down[...] = down_ref[...] * 0.5
    aup[...] = jnp.zeros_like(aup)
    ag2[...] = jnp.zeros_like(ag2)

    def turn(b, carry):
        slot = lax.rem(b, 2)

        @pl.when(b + 1 < n_turns)
        def _():
            for c in kept_copies(b + 1, 1 - slot):
                c.start()

        @pl.when(b >= 2)
        def _():
            delta_copy(b - 2, slot).wait()

        for c in kept_copies(b, slot):
            c.wait()
        inv2 = sinfo[slot, I_INV2:I_INV2 + 1]
        g_low = nn(gw_ref[...], members(sinfo[slot, I_WORD:I_WORD + 1], 0, WORDS)).astype(LOW)
        vhat = smid[slot] * inv2
        normed_two = (vhat * g2).astype(LOW)
        n2d = jnp.zeros((CD, WIDE), F32)
        for c in range(CFF // 256):
            cs = slice(c * 256, (c + 1) * 256)
            bd = (nn(down[cs, :], g_low) * sslope[slot, cs].astype(F32)).astype(LOW)
            aup[:, cs] += nt(normed_two, bd)
            n2d = n2d + nn(up_ref[:, cs], bd)
        ag2[...] += n2d * vhat
        lifted = n2d * g2
        md = g_low.astype(F32) + inv2 * (lifted - vhat * jnp.mean(lifted * vhat, axis=0, keepdims=True))
        sdelta[slot] = md.astype(LOW)
        delta_copy(b, slot).start()
        return carry

    lax.fori_loop(0, n_turns, turn, 0)
    aup_ref[...] = aup[...].astype(LOW)
    load.wait()
    add_up(facc_ref, f0_ref.at[pl.ds(a * 8, 8)], f1)
    gain_ref[...] = jnp.broadcast_to(jnp.sum(ag2[...], axis=1, keepdims=True), (CD, 8)).T

    def drain(b, carry):
        delta_copy(b, lax.rem(b, 2)).wait()
        return carry

    lax.fori_loop(jnp.maximum(n_turns - 2, 0), n_turns, drain, 0)


def kernel_b2(
    turns_ref, wgain1_ref, wgain2_ref, gain2_ref, aup_ref, g1_ref, wq_ref, wk_ref, wv_ref, wo_ref,
    keptl_hbm, keptd_hbm, kepti_hbm, facc_ref, f2_hbm, t0_ref, t1_hbm,
    keep_ref, send_ref, fnext_ref, tacc_ref,
    slow, sinfo, sdelta, dscore, wqkv, aqkv, ao, atab, ag1, f2, t1, ksem, fsem,
):
    phase = lax.axis_index("phase")
    n_turns = turns_ref[0]

    def kept_copies(b, slot):
        return (
            pltpu.make_async_copy(keptl_hbm.at[b], slow.at[slot], ksem.at[0, slot]),
            pltpu.make_async_copy(keptd_hbm.at[b], sdelta.at[slot], ksem.at[1, slot]),
            pltpu.make_async_copy(kepti_hbm.at[b], sinfo.at[slot], ksem.at[2, slot]),
        )

    for c in kept_copies(0, 0):
        c.start()
    _, _, low, _ = own_bits()
    quarter = pl.ds(own_plane() * 4, 4)
    loads = [
        pltpu.make_async_copy(src.at[at], dst, fsem.at[i])
        for i, (src, at, dst) in enumerate(((f2_hbm, pl.ds(low * 4, 4), f2), (t1_hbm, quarter, t1)))
    ]
    for load in loads:
        load.start()
    g1 = row_to_column(g1_ref[...].astype(F32)[None, :])
    for i, w in enumerate((wq_ref, wk_ref, wv_ref)):
        wqkv[:, i * CD:(i + 1) * CD] = w[...]
    for acc in (aqkv, ao, atab, ag1, dscore):
        acc[...] = jnp.zeros_like(acc)

    def turn(b, carry):
        slot = lax.rem(b, 2)

        @pl.when(b + 1 < n_turns)
        def _():
            for c in kept_copies(b + 1, 1 - slot):
                c.start()

        for c in kept_copies(b, slot):
            c.wait()
        inv1 = sinfo[slot, I_INV1:I_INV1 + 1]
        ident = sinfo[slot, I_IDENT:I_IDENT + 1]
        md_low = sdelta[slot]
        do = nn(wo_ref[...], md_low).astype(LOW)
        emb = slow[slot, R_EMB:R_EMB + CD].astype(F32)
        ehat = emb * inv1
        normed = (ehat * g1).astype(LOW)
        hot = jnp.where(iota((CVOC, WIDE), 0).astype(F32) == ident, 1.0, 0.0).astype(LOW)
        deltas = []
        for t in range(4):
            u, ks, ql = band(t)
            for pair in range(CHAR_HEADS // 2):
                fs = slice(u * SPAN + pair * 128, u * SPAN + pair * 128 + 128)
                deltas.append(nn(
                    slow[slot, R_V + ks.start:R_V + ks.stop, fs], two_heads(do[pair * 128:pair * 128 + 128, ql])
                ))
        dq, dk, dv = ([[None, None] for _ in range(CHAR_HEADS)] for _ in range(3))
        for t in range(4):
            u, ks, ql = band(t)
            for pair in range(CHAR_HEADS // 2):
                dp = deltas[t * 2 + pair]
                for i in range(2):
                    row = (pair * 2 + i) * SPAN
                    pf = slow[slot, R_P + row + ks.start:R_P + row + ks.stop, ql].astype(F32)
                    dph = dp[:, i * 128:i * 128 + 128]
                    d = pf * (dph - jnp.sum(pf * dph, axis=0, keepdims=True))
                    dscore[row + ks.start:row + ks.stop, ql] = d.astype(LOW)
                h, v = (t % 2) * 2 + pair, t // 2
                vs = slice(v * SPAN, (v + 1) * SPAN)
                dv[h][v] = nt(do[h * HEAD:(h + 1) * HEAD, vs], slow[slot, R_P + h * SPAN:R_P + (h + 1) * SPAN, vs]).astype(LOW)
        for h in range(CHAR_HEADS):
            for u in range(2):
                us = slice(u * SPAN, (u + 1) * SPAN)
                ds = dscore[h * SPAN:(h + 1) * SPAN, us]
                dq[h][u] = (nn(slow[slot, R_K + h * HEAD:R_K + (h + 1) * HEAD, us], ds) * 0.125).astype(LOW)
                dk[h][u] = nt(slow[slot, R_Q + h * HEAD:R_Q + (h + 1) * HEAD, us], ds).astype(LOW)
        dqkv = jnp.concatenate([jnp.concatenate(pair, axis=1) for part in (dq, dk, dv) for pair in part], axis=0)
        nd = nn(wqkv[...], dqkv)
        aqkv[:, 0:CD] += nt(normed, dqkv[0:CD])
        ag1[...] += nd * ehat
        lifted = nd * g1
        aqkv[:, CD:2 * CD] += nt(normed, dqkv[CD:2 * CD])
        mean = jnp.mean(lifted * ehat, axis=0, keepdims=True)
        aqkv[:, 2 * CD:] += nt(normed, dqkv[2 * CD:])
        ed = md_low.astype(F32) + inv1 * (lifted - ehat * mean)
        ao[...] += nt(slow[slot, R_MIX:R_MIX + CD], md_low)
        atab[...] += nt(hot, ed.astype(LOW))
        return carry

    lax.fori_loop(0, n_turns, turn, 0)

    for load in loads:
        load.wait()
    add_up(fnext_ref, facc_ref.at[pl.ds(low * 4, 4)], f2)
    add_up(tacc_ref, t0_ref.at[quarter], t1)
    put(keep_ref, send_ref, phase, plane_first, C_TABLE, column_halves(atab[...]), 16)
    put(keep_ref, send_ref, phase, plane_first, C_Q, column_halves(aqkv[:, 0:CD]), 16)
    put(keep_ref, send_ref, phase, plane_first, C_K, column_halves(aqkv[:, CD:2 * CD]), 16)
    put(keep_ref, send_ref, phase, plane_first, C_V, column_halves(aqkv[:, 2 * CD:]), 16)
    put(keep_ref, send_ref, phase, plane_first, C_O, column_halves(ao[...]), 16)
    put(keep_ref, send_ref, phase, plane_first, C_UP, column_halves(aup_ref[...]), 16)
    cg1 = jnp.broadcast_to(jnp.sum(ag1[...], axis=1, keepdims=True), (CD, 8)).T[0:1]
    cg2 = gain2_ref[0:1]
    for d in range(SHARES):
        rows = [
            jnp.concatenate([cg1[:, d * 16:d * 16 + 16], jnp.zeros((1, 112), F32)], axis=1),
            jnp.concatenate([cg2[:, d * 16:d * 16 + 16], jnp.zeros((1, 112), F32)], axis=1),
            jnp.concatenate([wgain1_ref[0:1, d * 32:d * 32 + 32], jnp.zeros((1, 96), F32)], axis=1),
            jnp.concatenate([wgain2_ref[0:1, d * 32:d * 32 + 32], jnp.zeros((1, 96), F32)], axis=1),
            jnp.zeros((12, 128), F32),
        ]
        tile = jnp.concatenate(rows, axis=0).astype(LOW)
        keep_ref[plane_first(d), C_GAIN:C_GAIN + 16, :] = tile
        send_ref[plane_first(d), C_GAIN:C_GAIN + 16, :] = tile


def kernel_add_one(f0_ref, f1_hbm, send_ref, f1, sem):
    a, _, _, _ = own_bits()
    loads = [
        pltpu.make_async_copy(f1_hbm.at[pl.ds((1 - a) * 8 + i, 2)], f1.at[pl.ds(i, 2)], sem.at[i // 2]) for i in range(0, 8, 2)
    ]
    for load in loads:
        load.start()
    for i, load in enumerate(loads):
        load.wait()
        at = pl.ds(i * 2, 2)
        add_up(send_ref.at[at], f0_ref.at[pl.ds((1 - a) * 8 + i * 2, 2)], f1.at[at])


def kernel_add_two(facc_ref, f2_hbm, t0_ref, t1_hbm, fsend_ref, ts1_ref, ts2_ref, ts3_ref, f2, t1, sem):
    _, _, low, _ = own_bits()
    half = pl.ds((1 - low) * 4, 4)
    loads = [pltpu.make_async_copy(f2_hbm.at[half], f2, sem.at[0])]
    places = [pl.ds(lax.bitwise_xor(own_plane(), k) * 4, 4) for k in range(1, 4)]
    for k, at in enumerate(places):
        loads.append(pltpu.make_async_copy(t1_hbm.at[at], t1.at[k], sem.at[1 + k]))
    for load in loads:
        load.start()
    loads[0].wait()
    add_up(fsend_ref, facc_ref.at[half], f2)
    for k, out in enumerate((ts1_ref, ts2_ref, ts3_ref)):
        loads[1 + k].wait()
        add_up(out, t0_ref.at[places[k]], t1.at[k])


def kernel_add_three(
    facc_ref, f3_hbm, tacc_ref, tg1_hbm, tg2_hbm, tg3_hbm, fsend_ref, fkeep_ref, tsend_ref, tkeep_ref, f3, tg, sem
):
    _, b, low, _ = own_bits()
    loads = [pltpu.make_async_copy(src, tg.at[i], sem.at[0]) for i, src in enumerate((tg1_hbm, tg2_hbm, tg3_hbm))]
    loads.append(pltpu.make_async_copy(f3_hbm, f3, sem.at[1]))
    for load in loads:
        load.start()
    for load in loads[:3]:
        load.wait()
    for out, bit in ((tsend_ref, 1 - low), (tkeep_ref, low)):
        at = pl.ds(bit * 2, 2)
        add_up(out, tacc_ref.at[at], *(tg.at[k, at] for k in range(3)))
    loads[3].wait()
    for out, bit in ((fsend_ref, 1 - b), (fkeep_ref, b)):
        add_up(out, facc_ref.at[pl.ds(bit * 2, 2)], f3.at[pl.ds(bit * 2, 2)])


def kernel_f(
    f3, f4, t2, t3, last, c0, c1, c2, c3, c4, c5, c6, c7, outk, outg,
    word_out, d_table, d_g1, d_q, d_k, d_v, d_o, d_g2, d_up, d_down, d_proj,
    e_g1, e_q, e_k, e_v, e_o, e_g2, e_up, e_down,
):
    phase = lax.axis_index("phase")
    dp = lax.axis_index("dp")
    _, _, low, high = own_bits()
    line = lax.div(dp, 4)
    place = lax.rem(dp, 4) * 4 + line
    fs = ((f3, high), (f4, high), (last, 0))
    ts = ((t2, high), (t3, high), (last, F_ROWS))
    cs = ((c0, place), (c1, place), (c2, line), (c3, line), (c4, line), (c5, None), (c6, None), (c7, None))
    word_out[phase, 0] = outk[...]
    word_out[1 - phase, 0] = outg[...]

    def total(parts, row, n):
        t = None
        for part, at in parts:
            if part is last:
                piece = part[at + row:at + row + n]
            else:
                piece = part[row:row + n] if at is None else part[at, row:row + n]
            t = piece.astype(F32) if t is None else t + piece.astype(F32)
        return t

    f, t, c = partial(total, fs), partial(total, ts), partial(total, cs)
    d_table[...] = c(C_TABLE, 16)
    d_q[...] = c(C_Q, 16)
    d_k[...] = c(C_K, 16)
    d_v[...] = c(C_V, 16)
    d_o[...] = c(C_O, 16)
    for i in range(4):
        d_up[:, i * 128:(i + 1) * 128] = c(C_UP + i * 16, 16)
        e_up[:, i * 256:(i + 1) * 256] = f(F_UP + i * 32, 32)
    gains = c(C_GAIN, 16)
    d_g1[...] = gains[0, :16]
    d_g2[...] = gains[1, :16]
    e_g1[...] = gains[2, :32]
    e_g2[...] = gains[3, :32]
    cd = t(T_CDOWN, 32)
    d_down[0:32] = cd[:, :128]
    d_down[32:64] = cd[:, 128:]
    d_proj[...] = t(T_PROJ, 16)
    e_q[...] = t(T_Q, 32)
    e_k[...] = t(T_K, 32)
    e_v[...] = t(T_V, 32)
    e_o[...] = t(T_O, 32)
    e_down[...] = f(F_DOWN, 128)


ANYWHERE = pl.BlockSpec(memory_space=pltpu.HBM)
INSIDE = pl.BlockSpec(memory_space=pltpu.VMEM)
SCALARS = pl.BlockSpec(memory_space=pltpu.SMEM)
shape = jax.ShapeDtypeStruct


def params(mib):
    return pltpu.CompilerParams(vmem_limit_bytes=mib * 2**20)


def outside(dims, dtype):
    return pltpu.HBM(dims, dtype)


def kept_outside(*values):
    return tuple(pltpu.with_memory_space_constraint(v, pltpu.HBM) for v in values)


def call_a(char_counts, char_ids, segment_ids, out_cotangent, weights):
    v = pltpu.VMEM
    return pl.pallas_call(
        kernel_a,
        out_shape=(
            outside((TURNS, KEPT_LOW, WIDE), LOW),
            outside((TURNS, CFF, WIDE), LOW),
            outside((TURNS, CD, WIDE), F32),
            outside((TURNS, 8, WIDE), F32),
            shape((1,), jnp.int32),
            v((SHARES, F_ROWS, 256), LOW),
            v((SHARES, F_ROWS, 256), LOW),
            shape((WORDS, WD // 2), LOW),
            shape((WORDS, WD // 2), LOW),
            shape((8, WD), F32),
            shape((WORDS, WD), LOW), shape((WORDS, WD), LOW), shape((WORDS, WD), LOW),
            shape((WORD_HEADS, WORDS, WORDS), LOW), shape((WD, WORDS), LOW), shape((WORDS, WD), LOW),
            shape((WORDS, WD), F32), shape((WORDS, 128), F32), shape((WORDS, WD), F32),
            shape((WORDS, CD), LOW), shape((WORDS, CFF), LOW),
        ),
        in_specs=[ANYWHERE] * 22,
        out_specs=(ANYWHERE,) * 4 + (SCALARS,) + (INSIDE,) * 16,
        scratch_shapes=[
            v((1, WORDS), jnp.int32), v((1, WORDS * CPW), jnp.int32), v((1, WORDS), jnp.int32),
            v((CVOC, CD), LOW), v((CD,), LOW), v((CD, CD), LOW), v((CD, CD), LOW), v((CD, CD), LOW), v((CD, CD), LOW),
            v((CD,), LOW), v((CD, CFF), LOW), v((CFF, CD), LOW), v((CD, WD), LOW), v((WD,), LOW), v((WD,), LOW),
            v((WORDS, WD), LOW),
            v((WD, WD), LOW), v((WD, WD), LOW), v((WD, WD), LOW), v((WD, WD), LOW),
            v((WD, WFF), LOW), v((WFF, WD), LOW),
            v((CD, CVOC), LOW), v((3 * CD, CD), LOW), v((CD, CD), LOW), v((CFF, CD), LOW), v((128, 32), LOW),
            v((2, KEPT_LOW, WIDE), LOW), v((2, CFF, WIDE), LOW), v((2, CD, WIDE), F32), v((2, 8, WIDE), F32),
            v((WORDS + WINDOW, CFF), F32), v((WORDS + WINDOW, CD), F32), v((16, WORDS), LOW),
            v((8, 128), jnp.int32), pltpu.SMEM((8, 128), jnp.int32),
            v((CFF, WIDE), F32), v((CFF, WIDE), LOW), v((CHAR_HEADS * SPAN, WIDE), LOW), v((8, WIDE), F32),
            v((CD, WIDE), LOW), v((8, WIDE), F32), v((8, WIDE), F32),
            v((WORDS, WFF), LOW), v((WORDS, WFF), LOW),
            pltpu.SemaphoreType.DMA((15,)),
            pltpu.SemaphoreType.DMA((8,)),
            pltpu.SemaphoreType.DMA((4, 2)),
        ],
        compiler_params=params(44),
        cost_estimate=pl.CostEstimate(flops=200 * 10**9, bytes_accessed=60 * 10**6, transcendentals=10**6),
        name="forward_and_words",
    )(*kept_outside(char_counts, char_ids, segment_ids, out_cotangent, *weights))


def call_a2(char_counts, kept, gain, project, weights):
    v = pltpu.VMEM
    return pl.pallas_call(
        kernel_a2,
        out_shape=(
            shape((CD, WORDS), LOW),
            v((SHARES, T_ROWS, 256), LOW),
            v((SHARES, T_ROWS, 256), LOW),
            shape((8, WD), F32),
        ),
        in_specs=[INSIDE] * 18,
        out_specs=(INSIDE,) * 4,
        compiler_params=params(20),
        cost_estimate=pl.CostEstimate(flops=200 * 10**9, bytes_accessed=10 * 10**6, transcendentals=10**6),
        name="word_attention_backward",
    )(char_counts, *kept, gain, project, *weights)


def call_b1(turns, gw, gain, up, down, kepts, keptm, kepti, f0, f1):
    v = pltpu.VMEM
    return pl.pallas_call(
        kernel_b1,
        out_shape=(outside((TURNS, CD, WIDE), LOW), shape((CD, CFF), LOW), shape((8, CD), F32), v((8, F_ROWS, 256), LOW)),
        in_specs=[SCALARS] + [INSIDE] * 4 + [ANYWHERE] * 3 + [INSIDE, ANYWHERE],
        out_specs=(ANYWHERE, INSIDE, INSIDE, INSIDE),
        scratch_shapes=[
            v((2, CFF, WIDE), LOW), v((2, CD, WIDE), F32), v((2, 8, WIDE), F32), v((2, CD, WIDE), LOW),
            v((CD, CFF), F32), v((CD, WIDE), F32), v((CFF, CD), LOW),
            v((8, F_ROWS, 256), LOW),
            pltpu.SemaphoreType.DMA((3, 2)),
            pltpu.SemaphoreType.DMA((2,)),
            pltpu.SemaphoreType.DMA((1,)),
        ],
        compiler_params=params(18),
        cost_estimate=pl.CostEstimate(flops=200 * 10**9, bytes_accessed=20 * 10**6, transcendentals=10**6),
        name="character_backward_one",
    )(turns, gw, gain, up, down, *kept_outside(kepts, keptm, kepti), f0, *kept_outside(f1))


def call_b2(turns, wgain1, wgain2, gain2, aup, weights, keptl, keptd, kepti, facc, f2, t0, t1):
    v = pltpu.VMEM
    return pl.pallas_call(
        kernel_b2,
        out_shape=(
            v((SHARES, C_ROWS, 128), LOW), v((SHARES, C_ROWS, 128), LOW), v((4, F_ROWS, 256), LOW), v((4, T_ROWS, 256), LOW)
        ),
        in_specs=[SCALARS] + [INSIDE] * 9 + [ANYWHERE] * 3 + [INSIDE, ANYWHERE] * 2,
        out_specs=(INSIDE,) * 4,
        scratch_shapes=[
            v((2, KEPT_LOW, WIDE), LOW), v((2, 8, WIDE), F32), v((2, CD, WIDE), LOW),
            v((CHAR_HEADS * SPAN, WIDE), LOW),
            v((CD, 3 * CD), LOW),
            v((CD, 3 * CD), F32), v((CD, CD), F32), v((CVOC, CD), F32), v((CD, WIDE), F32),
            v((4, F_ROWS, 256), LOW), v((4, T_ROWS, 256), LOW),
            pltpu.SemaphoreType.DMA((3, 2)),
            pltpu.SemaphoreType.DMA((2,)),
        ],
        compiler_params=params(24),
        cost_estimate=pl.CostEstimate(flops=200 * 10**9, bytes_accessed=40 * 10**6, transcendentals=10**6),
        name="character_backward_two",
    )(turns, wgain1, wgain2, gain2, aup, *weights, *kept_outside(keptl, keptd, kepti), facc, *kept_outside(f2), t0, *kept_outside(t1))


def call_add(kernel, name, outs, parts, specs, scratch):
    v = pltpu.VMEM
    return pl.pallas_call(
        kernel,
        out_shape=tuple(v(s, LOW) for s in outs),
        in_specs=specs,
        out_specs=(INSIDE,) * len(outs),
        scratch_shapes=[v(s, LOW) for s in scratch] + [pltpu.SemaphoreType.DMA((4,))],
        compiler_params=params(12),
        name=name,
    )(*parts)


def add_one(f0, f1):
    half = (8, F_ROWS, 256)
    return call_add(kernel_add_one, "add_one", (half,), (f0, *kept_outside(f1)), [INSIDE, ANYWHERE], (half,))[0]


def add_two(facc, f2, t0, t1):
    fs, ts = (4, F_ROWS, 256), (4, T_ROWS, 256)
    return call_add(
        kernel_add_two, "add_two", (fs, ts, ts, ts), (facc, *kept_outside(f2), t0, *kept_outside(t1)),
        [INSIDE, ANYWHERE] * 2, (fs, (3,) + ts),
    )


def add_three(facc, f3, tacc, tgot):
    fs, ts = (2, F_ROWS, 256), (2, T_ROWS, 256)
    return call_add(
        kernel_add_three, "add_three", (fs, fs, ts, ts), (facc, *kept_outside(f3), tacc, *kept_outside(*tgot)),
        [INSIDE, ANYWHERE] * 2 + [ANYWHERE] * 2, ((4, F_ROWS, 256), (3, 4, T_ROWS, 256)),
    )


def call_f(words, c, outk, outg):
    v = pltpu.VMEM
    outs = ((CVOC, CD), (CD,), (CD, CD), (CD, CD), (CD, CD), (CD, CD), (CD,), (CD, CFF), (CFF, CD), (CD, WD),
            (WD,), (WD, WD), (WD, WD), (WD, WD), (WD, WD), (WD,), (WD, WFF), (WFF, WD))
    outs = [(s[0] // SHARES,) + tuple(n // 2 for n in s[1:]) for s in outs]
    return pl.pallas_call(
        kernel_f,
        out_shape=(shape((2, 1, WORDS, WD // 2), LOW),) + tuple(shape(s, F32) for s in outs),
        in_specs=[INSIDE] * 15,
        out_specs=(INSIDE,) * 19,
        compiler_params=params(8),
        name="finish",
    )(*words, *c, outk, outg)


def flip(value, axis, bits):
    count = lax.axis_size(axis)
    return lax.ppermute(value, axis, [(i, i ^ bits) for i in range(count)])


def flip_both(value, first, second):
    pairs = [(i, i ^ first) for i in range(SHARES)] + [(SHARES + i, SHARES + (i ^ second)) for i in range(SHARES)]
    return lax.ppermute(value, ("phase", "dp"), pairs)


def pick(value, index):
    return lax.dynamic_index_in_dim(value, index, 0, keepdims=False)


def plus(*parts):
    total = parts[0].astype(F32)
    for part in parts[1:]:
        total = total + part.astype(F32)
    return total.astype(LOW)


def across(value, side):
    return flip_both(value, *((1, 2), (2, 1), (4, 4), (8, 8))[side])


def half(bit, *parts):
    return plus(*(lax.dynamic_slice_in_dim(part, bit * (part.shape[0] // 2), part.shape[0] // 2, 0) for part in parts))


def after(value, *others):
    return lax.optimization_barrier((value,) + others)[0]


def together(*values):
    return lax.optimization_barrier(values)


def body(
    char_ids, char_counts, segment_ids, out_cotangent,
    char_table, char_gain_one, char_query, char_key, char_value, char_output, char_gain_two, char_up, char_down,
    char_project,
    word_gain_one, word_query, word_key, word_value, word_output, word_gain_two, word_up, word_down,
):
    keptl, kepts, keptm, kepti, turns, fkeep, fsend, outk, outs, wgain2, *words = call_a(
        char_counts, char_ids, segment_ids, out_cotangent,
        (char_table, char_gain_one, char_query, char_key, char_value, char_output, char_gain_two, char_up, char_down,
         char_project,
         word_gain_one, word_query, word_key, word_value, word_output, word_gain_two, word_up, word_down),
    )
    fgot = flip(fsend, "phase", 1)
    outg = flip(outs, "phase", 1)
    gw, tkeep, tsend, wgain1 = call_a2(
        char_counts, words, word_gain_one, char_project, (word_query, word_key, word_value, word_output)
    )
    one = (char_gain_two, char_up, char_down, kepts, keptm, kepti)
    two = (char_gain_one, char_query, char_key, char_value, char_output)
    if lax.axis_size("dp") != SHARES:
        keptd, aup, gain2, facc = call_b1(turns, gw, *one, fkeep, fgot)
        tgot = flip(tsend, "phase", 1)
        ckeep, csend, _, _ = call_b2(turns, wgain1, wgain2, gain2, aup, two, keptl, keptd, kepti, facc, facc, tkeep, tgot)
        return general_sums(outk, outg, (fkeep, fgot), (tkeep, tgot), (ckeep, flip(csend, "phase", 1)))
    gw, tsend, fgot, outg = together(gw, tsend, fgot, outg)
    gw, fsend = together(gw, add_one(fkeep, fgot))
    f2, tgot = across(fsend, 0), flip(tsend, "phase", 1)
    keptd, aup, gain2, facc = call_b1(turns, gw, *one, fkeep, fgot)
    keptd, f2, tgot = together(keptd, f2, tgot)
    sends = add_two(facc, f2, tkeep, tgot)
    keptd, fsend, *tsends = together(keptd, *sends)
    f3, *tparts = across(fsend, 2), *(flip(send, "dp", k) for k, send in enumerate(tsends, 1))
    ckeep, csend, facc, tacc = call_b2(
        turns, wgain1, wgain2, gain2, aup, two, keptl, keptd, kepti, facc, f2, tkeep, tgot
    )
    ckeep, csend, facc, f3, *tparts = together(ckeep, csend, facc, f3, *tparts)
    _, _, low, high = own_bits()
    cphase = flip(csend, "phase", 1)
    fsend, facc, tsend, tacc = add_three(facc, f3, tacc, tparts)
    f4, t3 = across(fsend, 1), across(tsend, 2)
    dp = lax.axis_index("dp")
    plane, line = lax.rem(dp, 4), lax.div(dp, 4)
    c = [ckeep.reshape(4, 4, C_ROWS, 128), cphase.reshape(4, 4, C_ROWS, 128)]
    sends = [plus(*(pick(part, lax.bitwise_xor(plane, k)) for part in c)) for k in range(1, 4)]
    cgot = [flip(send, "dp", k) for k, send in enumerate(sends, 1)]
    f4, t3 = after(f4, *sends), after(t3, *sends)
    last = jnp.concatenate([pick(half(1 - high, facc, f4), 0), pick(half(1 - high, tacc, t3), 0)], axis=0)
    last = across(last, 3)
    c = [pick(part, plane) for part in c] + cgot
    sends = [plus(*(pick(part, lax.bitwise_xor(line, k)) for part in c)) for k in range(1, 4)]
    cline = [flip(send, "dp", 4 * k) for k, send in enumerate(sends, 1)]
    return call_f((facc, f4, tacc, t3, last), (ckeep, cphase, *cgot, *cline), outk, outg)


def general_sums(outk, outg, fs, ts, cs):
    phase = lax.axis_index("phase")
    first = phase == 0
    outs = jnp.stack([jnp.where(first, outk, outg), jnp.where(first, outg, outk)])[:, None]
    def order(places):
        plain, swapped = (jnp.asarray([places(d, core) for d in range(SHARES)]) for core in range(2))
        return jnp.where(first, plain, swapped)

    def natural(pair, order):
        return jnp.take(pair[0].astype(F32) + pair[1].astype(F32), order, axis=0)

    f, t, c = natural(fs, order(feed_order)), natural(ts, order(word_order)), natural(cs, jnp.asarray([plane_first(d) for d in range(SHARES)]))

    def whole(rows):
        return rows.reshape(-1, rows.shape[-1])

    def wide(rows, pieces):
        n = rows.shape[1] // pieces
        return whole(rows.reshape(SHARES, pieces, n, rows.shape[-1]).transpose(0, 2, 1, 3).reshape(SHARES, n, -1))

    cdown = t[:, T_CDOWN:T_CDOWN + 32]
    cdown = jnp.concatenate([cdown[..., :128], cdown[..., 128:]], axis=1)
    parts = (
        whole(c[:, C_TABLE:C_TABLE + 16]), c[:, C_GAIN, :16].reshape(-1),
        whole(c[:, C_Q:C_Q + 16]), whole(c[:, C_K:C_K + 16]), whole(c[:, C_V:C_V + 16]), whole(c[:, C_O:C_O + 16]),
        c[:, C_GAIN + 1, :16].reshape(-1),
        wide(c[:, C_UP:C_UP + 64], 4), whole(cdown), whole(t[:, T_PROJ:T_PROJ + 16]),
        c[:, C_GAIN + 2, :32].reshape(-1),
        whole(t[:, T_Q:T_Q + 32]), whole(t[:, T_K:T_K + 32]), whole(t[:, T_V:T_V + 32]), whole(t[:, T_O:T_O + 32]),
        c[:, C_GAIN + 3, :32].reshape(-1),
        wide(f[:, F_UP:F_UP + 128], 4), whole(f[:, F_DOWN:F_DOWN + 128]),
    )
    return (outs,) + tuple(lax.psum_scatter(p, "dp", scatter_dimension=0, tiled=True) for p in parts)


def solution(mesh):
    rows = P(None, "dp", None)
    both = P("dp", "phase")
    one = P("dp")
    return jax.shard_map(
        body,
        mesh=mesh,
        in_specs=(rows, rows, rows, P(None, "dp", None, None)) + (P(),) * 18,
        out_specs=(
            P(None, "dp", None, "phase"),
            both, one, both, both, both, both, one, both, both, both,
            one, both, both, both, both, one, both, both,
        ),
        check_vma=False,
    )
```

```python
from functools import partial

import jax
import jax.numpy as jnp
from jax import lax
from jax.experimental import pallas as pl
from jax.experimental.pallas import tpu as pltpu
from jax.sharding import PartitionSpec as P

F32 = jnp.float32
LOW = jnp.bfloat16

CD = 256
CFF = 1024
CPW = 16
CVOC = 256
CHAR_HEADS = 4
HEAD = 64
WD = 512
WFF = 2048
WORD_HEADS = 8
WORDS = 256

SCHEDULE = "aaaafaaaaaaaaafaaaaaaaaafaaaaafa"
SPAN = 256
STEP = 241
WIDE = 2 * SPAN
TURNS = ((WORDS * CPW - 1) // STEP + 2) // 2

epsilon = 1e-06
half_root = 0.7071067811865476
density = 0.3989422804014327
floor_score = -1e30
log2_e = 1.4426950408889634

R_V, R_P, R_EMB, R_Q, R_K, R_MIX = 0, 256, 1280, 1536, 1792, 2048
KEPT_FIRST = 1280
KEPT_LOW = 2304
I_INV1, I_INV2, I_IDENT, I_WORD = 0, 1, 2, 3
BAND = 144
WINDOW = 96

F_UP, F_DOWN = 0, 128
F_ROWS = 256
T_Q, T_K, T_V, T_O, T_CDOWN, T_PROJ = 0, 32, 64, 96, 128, 160
T_ROWS = 176
C_TABLE, C_Q, C_K, C_V, C_O, C_UP, C_GAIN = 0, 16, 32, 48, 64, 80, 144
C_ROWS = 160
SHARES = 16


def nn(left, right):
    return lax.dot_general(left, right, (((1,), (0,)), ((), ())), preferred_element_type=F32)


def nt(left, right):
    return lax.dot_general(left, right, (((1,), (1,)), ((), ())), preferred_element_type=F32)


def iota(shape, axis):
    return lax.broadcasted_iota(jnp.int32, shape, axis)


def eye(n):
    return iota((n, n), 0) == iota((n, n), 1)


def row_to_column(row):
    n = row.shape[1]
    return jnp.sum(jnp.where(eye(n), row, 0.0), axis=1, keepdims=True)


def gelu_pair(v):
    e = lax.erf(v * half_root)
    half = 0.5 * v
    bell = jnp.exp2(v * v * (-0.5 * log2_e))
    return half + half * e, 0.5 + 0.5 * e + (density * v) * bell


def gelu_twice(v):
    u = v * half_root
    whole = 1.0 + lax.erf(u)
    bell = jnp.exp2(u * u * (-log2_e))
    return v * whole, whole + (2.0 * density * v) * bell


def bits(d):
    return d % 2, d // 2 % 2, d // 4 % 2, d // 8


def plane_first(d, core=0):
    return (d % 4) * 4 + d // 4


def feed_order(d, core):
    x, y, low, high = bits(d)
    return (y * 8 + x * 2 if core else x * 8 + y * 2) + low * 4 + high


def word_order(d, core=0):
    _, _, low, high = bits(d)
    return (d % 4) * 4 + low * 2 + high


def own_bits():
    phase, dp = lax.axis_index("phase"), lax.axis_index("dp")
    x, y, low, high = (lax.rem(lax.div(dp, n), 2) for n in (1, 2, 4, 8))
    return jnp.where(phase == 0, x, y), jnp.where(phase == 0, y, x), low, high


def own_plane():
    return lax.rem(lax.axis_index("dp"), 4)


def add_up(out, *parts):
    for i in range(out.shape[0]):
        if len(parts) == 2:
            out[i] = parts[0][i] + parts[1][i]
            continue
        total = parts[0][i].astype(F32)
        for part in parts[1:]:
            total = total + part[i].astype(F32)
        out[i] = total.astype(LOW)


def members(word, first, count, weight=1.0):
    return jnp.where((iota((count, WIDE), 0) + first).astype(F32) == word, weight, 0.0).astype(LOW)


def word_starts(counts_row):
    earlier = iota((WORDS, WORDS), 1) < iota((WORDS, WORDS), 0)
    return jnp.sum(jnp.where(earlier, counts_row, 0.0), axis=1, keepdims=True)


def column_to_row(column):
    return jnp.sum(jnp.where(eye(column.shape[0]), column, 0.0), axis=0, keepdims=True)


def put(keep, send, phase, order, row, halves, share_rows):
    width, lanes = halves[0].shape[1], keep.shape[-1]
    first = phase == 0
    mine, other = jnp.where(first, halves[0], halves[1]), jnp.where(first, halves[1], halves[0])
    for out, low, core in ((keep, mine, phase), (send, other, 1 - phase)):
        for i in range(low.shape[0] // share_rows):
            at, swapped = order(i, 0), order(i, 1)
            if at != swapped:
                at = at + core * (swapped - at)
            rows = low[i * share_rows:(i + 1) * share_rows]
            for piece in range(max(1, width // lanes)):
                part = rows[:, piece * lanes:piece * lanes + min(width, lanes)]
                if width < lanes:
                    part = jnp.concatenate([part[:share_rows // 2], part[share_rows // 2:]], axis=1)
                m = part.shape[0]
                out[at, row + piece * share_rows:row + piece * share_rows + m, :] = part


def column_halves(value):
    width = value.shape[1] // 2
    low = value.astype(LOW)
    return low[:, :width], low[:, width:]


def band(t):
    keys = slice(0, BAND) if t % 2 == 0 else slice(SPAN - BAND, SPAN)
    return t // 2, keys, slice(t * 128, (t + 1) * 128)


def two_heads(pair):
    zero = jnp.zeros((HEAD, pair.shape[1]), LOW)
    first = jnp.concatenate([pair[:HEAD], zero], axis=0)
    second = jnp.concatenate([zero, pair[HEAD:]], axis=0)
    return jnp.concatenate([first, second], axis=1)


def two_heads_rows(pair):
    left = iota(pair.shape, 1) < HEAD
    zero = jnp.zeros(pair.shape, LOW)
    return jnp.concatenate([jnp.where(left, pair, zero), jnp.where(left, zero, pair)], axis=0)


def softmax_keys(s):
    e = jnp.exp(s - jnp.max(s, axis=0, keepdims=True))
    return (e * (1.0 / jnp.sum(e, axis=0, keepdims=True))).astype(LOW)


def kernel_a(
    counts_hbm, ids_hbm, segs_hbm, cot_hbm,
    table_hbm, g1_hbm, wq_hbm, wk_hbm, wv_hbm, wo_hbm, g2_hbm, up_hbm, down_hbm, proj_hbm,
    wg1_hbm, wwq_hbm, wwk_hbm, wwv_hbm, wwo_hbm, wg2_hbm, wup_hbm, wdown_hbm,
    keptl_hbm, kepts_hbm, keptm_hbm, kepti_hbm, turns_ref,
    keep_ref, send_ref, outk_ref, outs_ref, gain_ref,
    q_ref, k_ref, v_ref, probs_ref, mixt_ref, normed_ref, xhat_ref, winv_ref, md_ref, pooled_ref, pa_ref,
    counts_ref, ids_ref, segs_ref,
    table_ref, g1_ref, wq_ref, wk_ref, wv_ref, wo_ref, g2_ref, up_ref, down_ref, proj_ref, wg1_ref, wg2_ref,
    cot, wwq, wwk, wwv, wwo, wup, wdown,
    tab_t, wqkv_t, wo_t, up_t, ids_t, slow, sslope, smid, sinfo, pa, pm, rowinfo, firsts_v, firsts, before_s, act_s, prob_s, found_s,
    mid_s, word_s, old_s,
    csem, wsem, ksem,
):
    phase = lax.axis_index("phase")
    tiny = [
        pltpu.make_async_copy(src.at[phase], dst, csem.at[12 + i])
        for i, (src, dst) in enumerate(((counts_hbm, counts_ref), (ids_hbm, ids_ref), (segs_hbm, segs_ref)))
    ]
    for load in tiny:
        load.start()
    early = [
        pltpu.make_async_copy(src, dst, csem.at[i])
        for i, (src, dst) in enumerate(
            ((g1_hbm, g1_ref), (g2_hbm, g2_ref), (table_hbm, table_ref), (wq_hbm, wq_ref), (wk_hbm, wk_ref),
             (wv_hbm, wv_ref), (wo_hbm, wo_ref), (up_hbm, up_ref), (down_hbm, down_ref), (proj_hbm, proj_ref),
             (wg1_hbm, wg1_ref), (wg2_hbm, wg2_ref))
        )
    ]
    for load in early:
        load.start()
    loads = [
        pltpu.make_async_copy(src, dst, wsem.at[i])
        for i, (src, dst) in enumerate(
            ((wwq_hbm, wwq), (wwk_hbm, wwk), (wwv_hbm, wwv), (wwo_hbm, wwo),
             (wup_hbm, wup), (wdown_hbm, wdown), (cot_hbm.at[phase, 0], cot))
        )
    ]
    pa[...] = jnp.zeros_like(pa)
    pm[...] = jnp.zeros_like(pm)
    prob_s[...] = jnp.zeros_like(prob_s)
    for slot in range(2):
        slow[slot, R_P:R_P + CHAR_HEADS * SPAN] = jnp.zeros((CHAR_HEADS * SPAN, WIDE), LOW)
    for load in tiny:
        load.wait()
    counts_row = counts_ref[...].astype(F32)
    starts = word_starts(counts_row)
    counts = row_to_column(counts_row)
    blocks = jnp.floor((starts + 0.5) * (1.0 / STEP))
    places = starts + (SPAN - STEP) * blocks
    n_turns = jnp.max(places).astype(jnp.int32) // WIDE + 1
    turns_ref[0] = n_turns
    bases = (iota((1, 128), 1) * WIDE).astype(F32)
    first = jnp.sum(jnp.where(places < bases, 1.0, 0.0), axis=0, keepdims=True)
    firsts_v[...] = jnp.broadcast_to(first, (8, 128)).astype(jnp.int32)
    first_copy = pltpu.make_async_copy(firsts_v, firsts, wsem.at[7])
    first_copy.start()
    ids = ids_ref[...]
    ids_t[...] = jnp.concatenate(
        [ids[:, 128 * a:128 * a + 128] for a in range(32)], axis=0
    ).astype(F32).T.astype(LOW)
    places_row = column_to_row(places)
    none = jnp.zeros((1, 1), F32)
    rowinfo[...] = jnp.concatenate(
        [places_row - jnp.concatenate([none, places_row[:, :-1]], axis=1),
         counts_row - jnp.concatenate([none, counts_row[:, :-1]], axis=1),
         jnp.ones((1, WORDS), F32), jnp.zeros((13, WORDS), F32)], axis=0
    ).astype(LOW)
    for load in early:
        load.wait()
    for load in loads:
        load.start()
    tab_t[...] = table_ref[...].T
    wqkv_t[0:CD] = (wq_ref[...] * 0.125).T
    wqkv_t[CD:2 * CD] = wk_ref[...].T
    wqkv_t[2 * CD:] = wv_ref[...].T
    wo_t[...] = wo_ref[...].T
    up_t[...] = up_ref[...].T
    g1 = row_to_column(g1_ref[...].astype(F32)[None, :])
    g2 = row_to_column(g2_ref[...].astype(F32)[None, :])
    first_copy.wait()

    def find(turn):
        place = (iota((1, WIDE), 1) + turn * WIDE).astype(F32)
        begun = jnp.where(places <= place, 1.0, 0.0).astype(LOW)
        info = nn(rowinfo[...], begun)
        word = info[2:3] - 1.0
        slot = place - info[0:1]
        flat = (word * 16.0 + slot).astype(jnp.int32)
        chosen = jnp.where(iota((32, WIDE), 0) == (flat >> 7), 1.0, 0.0).astype(LOW)
        lanes = nn(ids_t[...], chosen)
        ident = jnp.sum(jnp.where(iota((128, WIDE), 0) == (flat & 127), lanes, 0.0), axis=0, keepdims=True)
        valid = slot < info[1:2]
        none = jnp.full((6, WIDE), -1.0, F32)
        return jnp.concatenate([jnp.where(valid, ident, -1.0), jnp.where(valid, word, -1.0), none], axis=0)

    found_s[...] = find(jnp.int32(0))

    def copies_one(b):
        slot = lax.rem(b, 2)
        return (
            pltpu.make_async_copy(slow.at[slot], keptl_hbm.at[b], ksem.at[0, slot]),
            pltpu.make_async_copy(smid.at[slot], keptm_hbm.at[b], ksem.at[2, slot]),
            pltpu.make_async_copy(sinfo.at[slot], kepti_hbm.at[b], ksem.at[3, slot]),
        )

    def copies_two(b):
        slot = lax.rem(b, 2)
        return (pltpu.make_async_copy(sslope.at[slot], kepts_hbm.at[b], ksem.at[1, slot]),)

    def start(copies):
        for c in copies:
            c.start()

    def wait(copies):
        for c in copies:
            c.wait()

    def near_words(b):
        first = (firsts[0, b] // 16) * 16
        return first, (firsts[0, b + 1] - first + WINDOW - 1) // WINDOW

    def window(first):
        return pl.ds(pl.multiple_of(first, 16), WINDOW)

    def attend(b):
        slot = lax.rem(b, 2)
        ident = found_s[0:1]
        word = found_s[1:2]
        hot = jnp.where(iota((CVOC, WIDE), 0).astype(F32) == ident, 1.0, 0.0).astype(LOW)
        emb = nn(tab_t[...], hot)
        inv1 = lax.rsqrt(jnp.mean(emb * emb, axis=0, keepdims=True) + epsilon)
        normed = (emb * inv1 * g1).astype(LOW)
        yield
        qkv = []
        for i in range(3):
            qkv.append(nn(wqkv_t[i * CD:(i + 1) * CD], normed).astype(LOW))
            yield
        query_t, key_t, value_t = qkv
        slow[slot, R_EMB:R_EMB + CD] = emb.astype(LOW)
        slow[slot, R_Q:R_Q + CD] = query_t
        slow[slot, R_K:R_K + CD] = key_t
        key_rows = [key_t[:, u * SPAN:(u + 1) * SPAN].T for u in range(2)]
        word_col = jnp.broadcast_to(jnp.where(word < 0.0, -2.0, word), (8, WIDE)).T[:, 0:1]
        yield
        scores = []
        for t in range(4):
            u, ks, ql = band(t)
            for pair in range(CHAR_HEADS // 2):
                fs = slice(pair * 128, pair * 128 + 128)
                scores.append(nn(key_rows[u][ks, fs], two_heads(query_t[fs, ql])))
                yield
        for u in range(2):
            us = slice(u * SPAN, (u + 1) * SPAN)
            slow[slot, R_V:R_V + SPAN, us] = value_t[:, us].T
        for t in range(4):
            u, ks, ql = band(t)
            bias = jnp.where(word_col[u * SPAN + ks.start:u * SPAN + ks.stop] == word[:, ql], 0.0, floor_score)
            for pair in range(CHAR_HEADS // 2):
                s = scores[t * 2 + pair]
                for i in range(2):
                    p = softmax_keys(s[:, i * 128:i * 128 + 128] + bias)
                    row = (pair * 2 + i) * SPAN
                    prob_s[row + ks.start:row + ks.stop, ql] = p
                    slow[slot, R_P + row + ks.start:R_P + row + ks.stop, ql] = p
        yield
        mixed = [[], []]
        for u in range(2):
            us = slice(u * SPAN, (u + 1) * SPAN)
            for h in range(CHAR_HEADS):
                hs = slice(h * HEAD, (h + 1) * HEAD)
                mixed[u].append(nn(value_t[hs, us], prob_s[h * SPAN:(h + 1) * SPAN, us]).astype(LOW))
                yield
        mixed = jnp.concatenate([jnp.concatenate(part, axis=0) for part in mixed], axis=1)
        slow[slot, R_MIX:R_MIX + CD] = mixed
        middle = emb + nn(wo_t[...], mixed)
        yield
        inv2 = lax.rsqrt(jnp.mean(middle * middle, axis=0, keepdims=True) + epsilon)
        smid[slot] = middle
        sinfo[slot] = jnp.concatenate([inv1, inv2, ident, word, jnp.zeros((4, WIDE), F32)], axis=0)
        normed_two = (middle * inv2 * g2).astype(LOW)
        middle_low = middle.astype(LOW)
        yield
        for c in range(CFF // 256):
            cs = slice(c * 256, (c + 1) * 256)
            before_s[cs] = nn(up_t[cs], normed_two)
            if c == 0:
                found_s[...] = find(b + 1)
            if c == 1:
                first, _ = near_words(b)
                pm[window(first), :] += nt(members(word, first, WINDOW), middle_low)
                mid_s[...] = middle_low
            if c == 3:
                old_s[0:1] = word_s[0:1]
                word_s[0:1] = word
            yield

    def feed(b):
        slot = lax.rem(b, 2)
        first, _ = near_words(b)
        near = members(word_s[0:1], first, WINDOW, 0.5)
        for c in range(CFF // 256):
            for d in range(8):
                cs = slice(c * 256 + d * 32, c * 256 + (d + 1) * 32)
                act, slope = gelu_twice(before_s[cs])
                sslope[slot, cs] = slope.astype(LOW)
                act_s[cs] = act.astype(LOW)
            cs = slice(c * 256, (c + 1) * 256)
            pa[window(first), cs] += nt(near, act_s[cs])
            yield

    def run(order, one, two):
        parts = {"a": one, "f": two}
        for step in order:
            next(parts[step])

    def more_one(b):
        first, windows = near_words(b)

        def more(i, carry):
            at = first + i * WINDOW
            pm[window(at), :] += nt(members(word_s[0:1], at, WINDOW), mid_s[...])
            return carry

        lax.fori_loop(1, windows, more, 0)

    def more_two(b, word):
        first, windows = near_words(b)

        def more(i, carry):
            at = first + i * WINDOW
            pa[window(at), :] += nt(members(word[0:1], at, WINDOW, 0.5), act_s[...])
            return carry

        lax.fori_loop(1, windows, more, 0)

    run("a" * 28, attend(jnp.int32(0)), None)
    more_one(jnp.int32(0))
    start(copies_one(jnp.int32(0)))

    def turn(b, carry):
        @pl.when(b >= 2)
        def _():
            wait(copies_one(b - 2))

        @pl.when(b >= 3)
        def _():
            wait(copies_two(b - 3))

        run(SCHEDULE, attend(b), feed(b - 1))
        more_one(b)
        more_two(b - 1, old_s)
        start(copies_one(b))
        start(copies_two(b - 1))
        return carry

    lax.fori_loop(1, n_turns, turn, 0)

    @pl.when(n_turns >= 3)
    def _():
        wait(copies_two(n_turns - 3))

    run("f" * 4, None, feed(n_turns - 1))
    more_two(n_turns - 1, word_s)
    start(copies_two(n_turns - 1))

    pa_hi = pa[0:WORDS].astype(LOW)
    per_count = 1.0 / counts
    pooled = (pm[0:WORDS] + nn(pa_hi, down_ref[...])) * per_count
    pooled_low = pooled.astype(LOW)
    pooled_ref[...] = pooled_low
    pa_ref[...] = pa_hi
    x = nn(pooled_low, proj_ref[...]).astype(LOW).astype(F32)
    for load in loads:
        load.wait()
    wg1 = wg1_ref[...].astype(F32)[None, :]
    wg2 = wg2_ref[...].astype(F32)[None, :]
    winv1 = lax.rsqrt(jnp.mean(x * x, axis=1, keepdims=True) + epsilon)
    xhat = x * winv1
    normed = (xhat * wg1).astype(LOW)
    xhat_ref[...] = xhat
    winv_ref[...] = jnp.broadcast_to(winv1, (WORDS, 128))
    normed_ref[...] = normed
    q = (nn(normed, wwq[...]) * 0.125).astype(LOW)
    k = nn(normed, wwk[...]).astype(LOW)
    v = nn(normed, wwv[...]).astype(LOW)
    seg_row = segs_ref[...].astype(F32)
    seg_col = row_to_column(seg_row)
    allowed = (seg_row == seg_col) & (iota((WORDS, WORDS), 0) <= iota((WORDS, WORDS), 1))
    bias = jnp.where(allowed, 0.0, floor_score)
    q_ref[...] = q
    k_ref[...] = k
    v_ref[...] = v
    v_t = v.T
    for h in range(WORD_HEADS):
        probs_ref[h, 128:, 0:128] = jnp.zeros((128, 128), LOW)
    halves = [(slice(0, 128 * (t + 1)), slice(128 * t, 128 * (t + 1))) for t in range(2)]
    pairs = [slice(pair * 128, pair * 128 + 128) for pair in range(WORD_HEADS // 2)]
    scores = [[nt(k[ks, fs], two_heads_rows(q[ql, fs])) for ks, ql in halves] for fs in pairs]
    mixed_t = []
    for pair in range(WORD_HEADS // 2):
        for (ks, ql), s in zip(halves, scores[pair]):
            for i in range(2):
                probs_ref[pair * 2 + i, ks, ql] = softmax_keys(s[:, i * 128:i * 128 + 128] + bias[ks, ql])
        for h in (pair * 2, pair * 2 + 1):
            mixed_t.append(nn(v_t[h * HEAD:(h + 1) * HEAD], probs_ref[h]).astype(LOW))
    mixed_t = jnp.concatenate(mixed_t, axis=0)
    mixt_ref[...] = mixed_t
    middle = x + nn(mixed_t.T, wwo[...])
    winv2 = lax.rsqrt(jnp.mean(middle * middle, axis=1, keepdims=True) + epsilon)
    normed_two = (middle * winv2 * wg2).astype(LOW)
    cot_low = cot[...]
    result = middle
    n2d = jnp.zeros((WORDS, WD), F32)
    n2_t = normed_two.T
    held = {}
    turns = (0, 2, 1, 3)
    quarter = [slice(c * 512, (c + 1) * 512) for c in range(4)]
    act, slope = gelu_pair(nn(normed_two, wup[:, quarter[0]]))
    for i, c in enumerate(turns):
        cs = quarter[c]
        act = act.astype(LOW)
        bd = (nt(cot_low, wdown[cs, :]) * slope).astype(LOW)
        if i < 3:
            ahead = nn(normed_two, wup[:, quarter[turns[i + 1]]])
        result = result + nn(act, wdown[cs, :])
        gd = nn(act.T, cot_low)
        gu = nn(n2_t, bd).astype(LOW)
        n2d = n2d + nt(bd, wup[:, cs])
        if i < 3:
            act, slope = gelu_pair(ahead)
        put(keep_ref, send_ref, phase, lambda i, p: feed_order(c * 4 + i, p), F_DOWN, column_halves(gd), 128)
        if c < 2:
            held[c] = gu
        else:
            put(keep_ref, send_ref, phase, feed_order, F_UP + (c - 2) * 64, (held[c - 2], gu), 32)
    result = result.astype(LOW)
    front = phase == 0
    outk_ref[...] = jnp.where(front, result[:, :256], result[:, 256:])
    outs_ref[...] = jnp.where(front, result[:, 256:], result[:, :256])
    vhat = middle * winv2
    gain_ref[...] = jnp.broadcast_to(jnp.sum(n2d * vhat, axis=0, keepdims=True), (8, WD))
    lifted = n2d * wg2
    md_ref[...] = cot[...].astype(F32) + winv2 * (lifted - vhat * jnp.mean(lifted * vhat, axis=1, keepdims=True))

    def drain(b, carry):
        wait(copies_one(b))
        wait(copies_two(b))
        return carry

    lax.fori_loop(jnp.maximum(n_turns - 2, 0), n_turns, drain, 0)


def kernel_a2(
    counts_ref, q_ref, k_ref, v_ref, pw, mixt_ref, normed_ref, xhat_ref, winv_ref, md_ref, pooled_ref, pa_ref,
    wg1_ref, proj_ref, wwq, wwk, wwv, wwo,
    gw_ref, keep_ref, send_ref, gain_ref,
):
    phase = lax.axis_index("phase")
    wg1 = wg1_ref[...].astype(F32)[None, :]
    q, k, v, normed, pooled_low = q_ref[...], k_ref[...], v_ref[...], normed_ref[...], pooled_ref[...]
    per_count = 1.0 / row_to_column(counts_ref[phase].astype(F32))
    md = md_ref[...]
    md_low = md.astype(LOW)
    put(keep_ref, send_ref, phase, word_order, T_O, column_halves(nn(mixt_ref[...], md_low)), 32)
    k_t = k.T
    do = nt(md_low, wwo[...]).astype(LOW)
    dq_t, dk, dv = [], [], []
    left = iota((WORDS, 128), 1) < HEAD
    pairs = [slice(pair * 128, pair * 128 + 128) for pair in range(WORD_HEADS // 2)]
    halves = [(slice(0, 128 * (t + 1)), slice(128 * t, 128 * (t + 1))) for t in range(2)]
    deltas = [[nt(v[ks, fs], two_heads_rows(do[ql, fs])) for ks, ql in halves] for fs in pairs]

    def scores(pair):
        ds = []
        for (ks, ql), dp in zip(halves, deltas[pair]):
            for i in range(2):
                pf = pw[pair * 2 + i, ks, ql].astype(F32)
                dph = dp[:, i * 128:i * 128 + 128]
                d = (pf * (dph - jnp.sum(pf * dph, axis=0, keepdims=True))).astype(LOW)
                ds.append(d if ks.stop == WORDS else jnp.concatenate([d, jnp.zeros((128, 128), LOW)], axis=0))
        return [jnp.concatenate([ds[i], ds[i + 2]], axis=1) for i in range(2)]

    both = None
    for pair in range(WORD_HEADS // 2 + 1):
        ahead = scores(pair) if pair < WORD_HEADS // 2 else None
        if ahead is not None:
            fs = pairs[pair]
            dv.append(jnp.where(left, nn(pw[pair * 2], do[:, fs]), nn(pw[pair * 2 + 1], do[:, fs])).astype(LOW))
        if both is not None:
            fs = pairs[pair - 1]
            for i in range(2):
                h = (pair - 1) * 2 + i
                dq_t.append(nn(k_t[h * HEAD:(h + 1) * HEAD], both[i]))
            dk.append(jnp.where(left, nn(both[0], q[:, fs]), nn(both[1], q[:, fs])).astype(LOW))
        both = ahead
    dq = (jnp.concatenate(dq_t, axis=0) * 0.125).astype(LOW).T
    dk = jnp.concatenate(dk, axis=1)
    dv = jnp.concatenate(dv, axis=1)
    normed_t = normed.T
    nd = nt(dq, wwq[...]) + nt(dk, wwk[...]) + nt(dv, wwv[...])
    put(keep_ref, send_ref, phase, word_order, T_Q, column_halves(nn(normed_t, dq)), 32)
    put(keep_ref, send_ref, phase, word_order, T_K, column_halves(nn(normed_t, dk)), 32)
    put(keep_ref, send_ref, phase, word_order, T_V, column_halves(nn(normed_t, dv)), 32)
    vhat = xhat_ref[...]
    gain_ref[...] = jnp.broadcast_to(jnp.sum(nd * vhat, axis=0, keepdims=True), (8, WD))
    lifted = nd * wg1
    xd = md + winv_ref[:, 0:1] * (lifted - vhat * jnp.mean(lifted * vhat, axis=1, keepdims=True))
    vd = xd.astype(LOW)
    put(keep_ref, send_ref, phase, word_order, T_PROJ, column_halves(nn(pooled_low.T, vd)), 16)
    gw = (nt(vd, proj_ref[...]) * per_count).astype(LOW)
    gw_ref[...] = gw.T
    put(keep_ref, send_ref, phase, word_order, T_CDOWN, column_halves(nn(pa_ref[...].T, gw)), 64)


def kernel_b1(
    turns_ref, gw_ref, g2_ref, up_ref, down_ref, kepts_hbm, keptm_hbm, info_ref, f0_ref, f1_hbm,
    delta_ref, aup_ref, gain_ref, facc_ref,
    sslope, smid, given, aup, ag2, down, f1, ksem, fsem,
):
    n_turns = turns_ref[0]

    def kept_copies(b, slot):
        return (
            pltpu.make_async_copy(kepts_hbm.at[b], sslope.at[slot], ksem.at[0, slot]),
            pltpu.make_async_copy(keptm_hbm.at[b], smid.at[slot], ksem.at[1, slot]),
        )

    for c in kept_copies(0, 0):
        c.start()
    a, _, _, _ = own_bits()
    load = pltpu.make_async_copy(f1_hbm.at[pl.ds(a * 8, 8)], f1, fsem.at[0])
    load.start()
    g2 = row_to_column(g2_ref[...].astype(F32)[None, :])
    down[...] = down_ref[...] * 0.5
    aup[...] = jnp.zeros_like(aup)
    ag2[...] = jnp.zeros_like(ag2)

    def give(b):
        given[...] = nn(gw_ref[...], members(info_ref[b, I_WORD:I_WORD + 1], 0, WORDS)).astype(LOW)

    give(0)

    def turn(b, carry):
        slot = lax.rem(b, 2)

        @pl.when(b + 1 < n_turns)
        def _():
            for c in kept_copies(b + 1, 1 - slot):
                c.start()

        for c in kept_copies(b, slot):
            c.wait()
        cuts = [slice(c * 256, (c + 1) * 256) for c in range(CFF // 256)]
        inv2 = info_ref[b, I_INV2:I_INV2 + 1]
        g_low = given[...]
        vhat = smid[slot] * inv2
        normed_two = (vhat * g2).astype(LOW)
        n2d = jnp.zeros((CD, WIDE), F32)
        ahead = nn(down[cuts[0], :], g_low)
        bds = []
        for c, cs in enumerate(cuts):
            bds.append((ahead * sslope[slot, cs].astype(F32)).astype(LOW))
            if c + 1 < len(cuts):
                ahead = nn(down[cuts[c + 1], :], g_low)
            n2d = n2d + nn(up_ref[:, cs], bds[c])
        aup[:, cuts[0]] += nt(normed_two, bds[0])
        ag2[...] += n2d * vhat
        lifted = n2d * g2
        aup[:, cuts[1]] += nt(normed_two, bds[1])
        mean = jnp.mean(lifted * vhat, axis=0, keepdims=True)
        aup[:, cuts[2]] += nt(normed_two, bds[2])
        md = g_low.astype(F32) + inv2 * (lifted - vhat * mean)
        delta_ref[b] = md.astype(LOW)
        aup[:, cuts[3]] += nt(normed_two, bds[3])
        give(jnp.minimum(b + 1, TURNS - 1))
        return carry

    lax.fori_loop(0, n_turns, turn, 0)
    aup_ref[...] = aup[...].astype(LOW)
    load.wait()
    add_up(facc_ref, f0_ref.at[pl.ds(a * 8, 8)], f1)
    gain_ref[...] = jnp.broadcast_to(jnp.sum(ag2[...], axis=1, keepdims=True), (CD, 8)).T


def kernel_b2(
    turns_ref, wgain1_ref, wgain2_ref, gain2_ref, aup_ref, g1_ref, wq_ref, wk_ref, wv_ref, wo_ref,
    keptl_hbm, delta_ref, info_ref, facc_ref, f2_hbm, t0_ref, t1_hbm,
    keep_ref, send_ref, fnext_ref, tacc_ref,
    slow, up_next, dscore, wqkv, aqkv, ao, atab, ag1, f2, t1, ksem, fsem,
):
    phase = lax.axis_index("phase")
    n_turns = turns_ref[0]

    def kept_copies(b, slot):
        return [
            pltpu.make_async_copy(keptl_hbm.at[b, rows], slow.at[slot, rows], ksem.at[i, slot])
            for i, rows in enumerate((pl.ds(0, KEPT_FIRST), pl.ds(KEPT_FIRST, KEPT_LOW - KEPT_FIRST)))
        ]

    for c in kept_copies(0, 0):
        c.start()
    _, _, low, _ = own_bits()
    quarter = pl.ds(own_plane() * 4, 4)
    loads = [
        pltpu.make_async_copy(src.at[at], dst, fsem.at[i])
        for i, (src, at, dst) in enumerate(((f2_hbm, pl.ds(low * 4, 4), f2), (t1_hbm, quarter, t1)))
    ]
    for load in loads:
        load.start()
    g1 = row_to_column(g1_ref[...].astype(F32)[None, :])
    for i, w in enumerate((wq_ref, wk_ref, wv_ref)):
        wqkv[:, i * CD:(i + 1) * CD] = w[...]
    for acc in (aqkv, ao, atab, ag1, dscore):
        acc[...] = jnp.zeros_like(acc)

    def step(b):
        up_next[...] = nn(wo_ref[...], delta_ref[b]).astype(LOW)

    step(0)

    def turn(b, carry):
        slot = lax.rem(b, 2)

        @pl.when(b + 1 < n_turns)
        def _():
            for c in kept_copies(b + 1, 1 - slot):
                c.start()

        for c in kept_copies(b, slot):
            c.wait()
        do = up_next[...]
        deltas = []
        for t in range(4):
            u, ks, ql = band(t)
            for pair in range(CHAR_HEADS // 2):
                fs = slice(u * SPAN + pair * 128, u * SPAN + pair * 128 + 128)
                deltas.append(nn(
                    slow[slot, R_V + ks.start:R_V + ks.stop, fs], two_heads(do[pair * 128:pair * 128 + 128, ql])
                ))
        dq, dk, dv = ([[None, None] for _ in range(CHAR_HEADS)] for _ in range(3))
        for t in range(4):
            u, ks, ql = band(t)
            for pair in range(CHAR_HEADS // 2):
                dp = deltas[t * 2 + pair]
                for i in range(2):
                    row = (pair * 2 + i) * SPAN
                    pf = slow[slot, R_P + row + ks.start:R_P + row + ks.stop, ql].astype(F32)
                    dph = dp[:, i * 128:i * 128 + 128]
                    d = pf * (dph - jnp.sum(pf * dph, axis=0, keepdims=True))
                    dscore[row + ks.start:row + ks.stop, ql] = d.astype(LOW)
                h, v = (t % 2) * 2 + pair, t // 2
                vs = slice(v * SPAN, (v + 1) * SPAN)
                dv[h][v] = nt(do[h * HEAD:(h + 1) * HEAD, vs], slow[slot, R_P + h * SPAN:R_P + (h + 1) * SPAN, vs]).astype(LOW)
        inv1 = info_ref[b, I_INV1:I_INV1 + 1]
        ident = info_ref[b, I_IDENT:I_IDENT + 1]
        md_low = delta_ref[b]
        emb = slow[slot, R_EMB:R_EMB + CD].astype(F32)
        ehat = emb * inv1
        normed = (ehat * g1).astype(LOW)
        hot = jnp.where(iota((CVOC, WIDE), 0).astype(F32) == ident, 1.0, 0.0).astype(LOW)
        for h in range(CHAR_HEADS):
            for u in range(2):
                us = slice(u * SPAN, (u + 1) * SPAN)
                ds = dscore[h * SPAN:(h + 1) * SPAN, us]
                dq[h][u] = (nn(slow[slot, R_K + h * HEAD:R_K + (h + 1) * HEAD, us], ds) * 0.125).astype(LOW)
                dk[h][u] = nt(slow[slot, R_Q + h * HEAD:R_Q + (h + 1) * HEAD, us], ds).astype(LOW)
        dqkv = jnp.concatenate([jnp.concatenate(pair, axis=1) for part in (dq, dk, dv) for pair in part], axis=0)
        nd = nn(wqkv[...], dqkv)
        aqkv[:, 0:CD] += nt(normed, dqkv[0:CD])
        ag1[...] += nd * ehat
        lifted = nd * g1
        aqkv[:, CD:2 * CD] += nt(normed, dqkv[CD:2 * CD])
        mean = jnp.mean(lifted * ehat, axis=0, keepdims=True)
        aqkv[:, 2 * CD:] += nt(normed, dqkv[2 * CD:])
        ed = md_low.astype(F32) + inv1 * (lifted - ehat * mean)
        step(jnp.minimum(b + 1, TURNS - 1))
        ao[...] += nt(slow[slot, R_MIX:R_MIX + CD], md_low)
        atab[...] += nt(hot, ed.astype(LOW))
        return carry

    lax.fori_loop(0, n_turns, turn, 0)

    for load in loads:
        load.wait()
    add_up(fnext_ref, facc_ref.at[pl.ds(low * 4, 4)], f2)
    add_up(tacc_ref, t0_ref.at[quarter], t1)
    put(keep_ref, send_ref, phase, plane_first, C_TABLE, column_halves(atab[...]), 16)
    put(keep_ref, send_ref, phase, plane_first, C_Q, column_halves(aqkv[:, 0:CD]), 16)
    put(keep_ref, send_ref, phase, plane_first, C_K, column_halves(aqkv[:, CD:2 * CD]), 16)
    put(keep_ref, send_ref, phase, plane_first, C_V, column_halves(aqkv[:, 2 * CD:]), 16)
    put(keep_ref, send_ref, phase, plane_first, C_O, column_halves(ao[...]), 16)
    put(keep_ref, send_ref, phase, plane_first, C_UP, column_halves(aup_ref[...]), 16)
    cg1 = jnp.broadcast_to(jnp.sum(ag1[...], axis=1, keepdims=True), (CD, 8)).T[0:1]
    cg2 = gain2_ref[0:1]
    for d in range(SHARES):
        rows = [
            jnp.concatenate([cg1[:, d * 16:d * 16 + 16], jnp.zeros((1, 112), F32)], axis=1),
            jnp.concatenate([cg2[:, d * 16:d * 16 + 16], jnp.zeros((1, 112), F32)], axis=1),
            jnp.concatenate([wgain1_ref[0:1, d * 32:d * 32 + 32], jnp.zeros((1, 96), F32)], axis=1),
            jnp.concatenate([wgain2_ref[0:1, d * 32:d * 32 + 32], jnp.zeros((1, 96), F32)], axis=1),
            jnp.zeros((12, 128), F32),
        ]
        tile = jnp.concatenate(rows, axis=0).astype(LOW)
        keep_ref[plane_first(d), C_GAIN:C_GAIN + 16, :] = tile
        send_ref[plane_first(d), C_GAIN:C_GAIN + 16, :] = tile


def kernel_add_one(f0_ref, f1_hbm, send_ref, f1, sem):
    a, _, _, _ = own_bits()
    loads = [
        pltpu.make_async_copy(f1_hbm.at[pl.ds((1 - a) * 8 + i, 2)], f1.at[pl.ds(i, 2)], sem.at[i // 2]) for i in range(0, 8, 2)
    ]
    for load in loads:
        load.start()
    for i, load in enumerate(loads):
        load.wait()
        at = pl.ds(i * 2, 2)
        add_up(send_ref.at[at], f0_ref.at[pl.ds((1 - a) * 8 + i * 2, 2)], f1.at[at])


def kernel_add_words(t0_ref, t1_hbm, ts1_ref, ts2_ref, ts3_ref, t1, sem):
    places = [pl.ds(lax.bitwise_xor(own_plane(), k) * 4, 4) for k in range(1, 4)]
    loads = [pltpu.make_async_copy(t1_hbm.at[at], t1.at[k], sem.at[k]) for k, at in enumerate(places)]
    for load in loads:
        load.start()
    for k, out in enumerate((ts1_ref, ts2_ref, ts3_ref)):
        loads[k].wait()
        add_up(out, t0_ref.at[places[k]], t1.at[k])


def kernel_add_two(facc_ref, f2_hbm, fsend_ref, f2, sem):
    _, _, low, _ = own_bits()
    half = pl.ds((1 - low) * 4, 4)
    load = pltpu.make_async_copy(f2_hbm.at[half], f2, sem.at[0])
    load.start()
    load.wait()
    add_up(fsend_ref, facc_ref.at[half], f2)


def kernel_add_three(
    facc_ref, f3_hbm, tacc_ref, tg1_hbm, tg2_hbm, tg3_hbm, fsend_ref, fkeep_ref, tsend_ref, tkeep_ref, f3, tg, sem
):
    _, b, low, _ = own_bits()
    loads = [pltpu.make_async_copy(src, tg.at[i], sem.at[0]) for i, src in enumerate((tg1_hbm, tg2_hbm, tg3_hbm))]
    loads.append(pltpu.make_async_copy(f3_hbm, f3, sem.at[1]))
    for load in loads:
        load.start()
    for load in loads[:3]:
        load.wait()
    for out, bit in ((tsend_ref, 1 - low), (tkeep_ref, low)):
        at = pl.ds(bit * 2, 2)
        add_up(out, tacc_ref.at[at], *(tg.at[k, at] for k in range(3)))
    loads[3].wait()
    for out, bit in ((fsend_ref, 1 - b), (fkeep_ref, b)):
        add_up(out, facc_ref.at[pl.ds(bit * 2, 2)], f3.at[pl.ds(bit * 2, 2)])


def kernel_f(
    f3, f4, t2, t3, last, c0, c1, c2, c3, c4, c5, c6, c7, outk, outg,
    word_out, d_table, d_g1, d_q, d_k, d_v, d_o, d_g2, d_up, d_down, d_proj,
    e_g1, e_q, e_k, e_v, e_o, e_g2, e_up, e_down,
):
    phase = lax.axis_index("phase")
    dp = lax.axis_index("dp")
    _, _, low, high = own_bits()
    line = lax.div(dp, 4)
    place = lax.rem(dp, 4) * 4 + line
    fs = ((f3, high), (f4, high), (last, 0))
    ts = ((t2, high), (t3, high), (last, F_ROWS))
    cs = ((c0, place), (c1, place), (c2, line), (c3, line), (c4, line), (c5, None), (c6, None), (c7, None))
    word_out[phase, 0] = outk[...]
    word_out[1 - phase, 0] = outg[...]

    def total(parts, row, n):
        t = None
        for part, at in parts:
            if part is last:
                piece = part[at + row:at + row + n]
            else:
                piece = part[row:row + n] if at is None else part[at, row:row + n]
            t = piece.astype(F32) if t is None else t + piece.astype(F32)
        return t

    f, t, c = partial(total, fs), partial(total, ts), partial(total, cs)
    d_table[...] = c(C_TABLE, 16)
    d_q[...] = c(C_Q, 16)
    d_k[...] = c(C_K, 16)
    d_v[...] = c(C_V, 16)
    d_o[...] = c(C_O, 16)
    for i in range(4):
        d_up[:, i * 128:(i + 1) * 128] = c(C_UP + i * 16, 16)
        e_up[:, i * 256:(i + 1) * 256] = f(F_UP + i * 32, 32)
    gains = c(C_GAIN, 16)
    d_g1[...] = gains[0, :16]
    d_g2[...] = gains[1, :16]
    e_g1[...] = gains[2, :32]
    e_g2[...] = gains[3, :32]
    cd = t(T_CDOWN, 32)
    d_down[0:32] = cd[:, :128]
    d_down[32:64] = cd[:, 128:]
    d_proj[...] = t(T_PROJ, 16)
    e_q[...] = t(T_Q, 32)
    e_k[...] = t(T_K, 32)
    e_v[...] = t(T_V, 32)
    e_o[...] = t(T_O, 32)
    e_down[...] = f(F_DOWN, 128)


ANYWHERE = pl.BlockSpec(memory_space=pltpu.HBM)
INSIDE = pl.BlockSpec(memory_space=pltpu.VMEM)
SCALARS = pl.BlockSpec(memory_space=pltpu.SMEM)
shape = jax.ShapeDtypeStruct


def params(mib):
    return pltpu.CompilerParams(vmem_limit_bytes=mib * 2**20)


def outside(dims, dtype):
    return pltpu.HBM(dims, dtype)


def kept_outside(*values):
    return tuple(pltpu.with_memory_space_constraint(v, pltpu.HBM) for v in values)


def call_a(char_counts, char_ids, segment_ids, out_cotangent, weights):
    v = pltpu.VMEM
    return pl.pallas_call(
        kernel_a,
        out_shape=(
            outside((TURNS, KEPT_LOW, WIDE), LOW),
            outside((TURNS, CFF, WIDE), LOW),
            outside((TURNS, CD, WIDE), F32),
            outside((TURNS, 8, WIDE), F32),
            shape((1,), jnp.int32),
            v((SHARES, F_ROWS, 256), LOW),
            v((SHARES, F_ROWS, 256), LOW),
            shape((WORDS, WD // 2), LOW),
            shape((WORDS, WD // 2), LOW),
            shape((8, WD), F32),
            shape((WORDS, WD), LOW), shape((WORDS, WD), LOW), shape((WORDS, WD), LOW),
            shape((WORD_HEADS, WORDS, WORDS), LOW), shape((WD, WORDS), LOW), shape((WORDS, WD), LOW),
            shape((WORDS, WD), F32), shape((WORDS, 128), F32), shape((WORDS, WD), F32),
            shape((WORDS, CD), LOW), shape((WORDS, CFF), LOW),
        ),
        in_specs=[ANYWHERE] * 22,
        out_specs=(ANYWHERE,) * 4 + (SCALARS,) + (INSIDE,) * 16,
        scratch_shapes=[
            v((1, WORDS), jnp.int32), v((1, WORDS * CPW), jnp.int32), v((1, WORDS), jnp.int32),
            v((CVOC, CD), LOW), v((CD,), LOW), v((CD, CD), LOW), v((CD, CD), LOW), v((CD, CD), LOW), v((CD, CD), LOW),
            v((CD,), LOW), v((CD, CFF), LOW), v((CFF, CD), LOW), v((CD, WD), LOW), v((WD,), LOW), v((WD,), LOW),
            v((WORDS, WD), LOW),
            v((WD, WD), LOW), v((WD, WD), LOW), v((WD, WD), LOW), v((WD, WD), LOW),
            v((WD, WFF), LOW), v((WFF, WD), LOW),
            v((CD, CVOC), LOW), v((3 * CD, CD), LOW), v((CD, CD), LOW), v((CFF, CD), LOW), v((128, 32), LOW),
            v((2, KEPT_LOW, WIDE), LOW), v((2, CFF, WIDE), LOW), v((2, CD, WIDE), F32), v((2, 8, WIDE), F32),
            v((WORDS + WINDOW, CFF), F32), v((WORDS + WINDOW, CD), F32), v((16, WORDS), LOW),
            v((8, 128), jnp.int32), pltpu.SMEM((8, 128), jnp.int32),
            v((CFF, WIDE), F32), v((CFF, WIDE), LOW), v((CHAR_HEADS * SPAN, WIDE), LOW), v((8, WIDE), F32),
            v((CD, WIDE), LOW), v((8, WIDE), F32), v((8, WIDE), F32),
            pltpu.SemaphoreType.DMA((15,)),
            pltpu.SemaphoreType.DMA((8,)),
            pltpu.SemaphoreType.DMA((4, 2)),
        ],
        compiler_params=params(44),
        cost_estimate=pl.CostEstimate(flops=200 * 10**9, bytes_accessed=60 * 10**6, transcendentals=10**6),
        name="forward_and_words",
    )(*kept_outside(char_counts, char_ids, segment_ids, out_cotangent, *weights))


def call_a2(char_counts, kept, gain, project, weights):
    v = pltpu.VMEM
    return pl.pallas_call(
        kernel_a2,
        out_shape=(
            shape((CD, WORDS), LOW),
            v((SHARES, T_ROWS, 256), LOW),
            v((SHARES, T_ROWS, 256), LOW),
            shape((8, WD), F32),
        ),
        in_specs=[INSIDE] * 18,
        out_specs=(INSIDE,) * 4,
        compiler_params=params(20),
        cost_estimate=pl.CostEstimate(flops=200 * 10**9, bytes_accessed=10 * 10**6, transcendentals=10**6),
        name="word_attention_backward",
    )(char_counts, *kept, gain, project, *weights)


def call_b1(turns, gw, gain, up, down, kepts, keptm, kepti, f0, f1):
    v = pltpu.VMEM
    return pl.pallas_call(
        kernel_b1,
        out_shape=(v((TURNS, CD, WIDE), LOW), shape((CD, CFF), LOW), shape((8, CD), F32), v((8, F_ROWS, 256), LOW)),
        in_specs=[SCALARS] + [INSIDE] * 4 + [ANYWHERE] * 2 + [INSIDE] * 2 + [ANYWHERE],
        out_specs=(INSIDE,) * 4,
        scratch_shapes=[
            v((2, CFF, WIDE), LOW), v((2, CD, WIDE), F32), v((CD, WIDE), LOW),
            v((CD, CFF), F32), v((CD, WIDE), F32), v((CFF, CD), LOW),
            v((8, F_ROWS, 256), LOW),
            pltpu.SemaphoreType.DMA((2, 2)),
            pltpu.SemaphoreType.DMA((1,)),
        ],
        compiler_params=params(18),
        cost_estimate=pl.CostEstimate(flops=200 * 10**9, bytes_accessed=20 * 10**6, transcendentals=10**6),
        name="character_backward_one",
    )(turns, gw, gain, up, down, *kept_outside(kepts, keptm), kepti, f0, *kept_outside(f1))


def call_b2(turns, wgain1, wgain2, gain2, aup, weights, keptl, keptd, kepti, facc, f2, t0, t1):
    v = pltpu.VMEM
    return pl.pallas_call(
        kernel_b2,
        out_shape=(
            v((SHARES, C_ROWS, 128), LOW), v((SHARES, C_ROWS, 128), LOW), v((4, F_ROWS, 256), LOW), v((4, T_ROWS, 256), LOW)
        ),
        in_specs=[SCALARS] + [INSIDE] * 9 + [ANYWHERE] + [INSIDE] * 3 + [ANYWHERE, INSIDE, ANYWHERE],
        out_specs=(INSIDE,) * 4,
        scratch_shapes=[
            v((2, KEPT_LOW, WIDE), LOW), v((CD, WIDE), LOW),
            v((CHAR_HEADS * SPAN, WIDE), LOW),
            v((CD, 3 * CD), LOW),
            v((CD, 3 * CD), F32), v((CD, CD), F32), v((CVOC, CD), F32), v((CD, WIDE), F32),
            v((4, F_ROWS, 256), LOW), v((4, T_ROWS, 256), LOW),
            pltpu.SemaphoreType.DMA((3, 2)),
            pltpu.SemaphoreType.DMA((2,)),
        ],
        compiler_params=params(24),
        cost_estimate=pl.CostEstimate(flops=200 * 10**9, bytes_accessed=40 * 10**6, transcendentals=10**6),
        name="character_backward_two",
    )(turns, wgain1, wgain2, gain2, aup, *weights, *kept_outside(keptl), keptd, kepti, facc, *kept_outside(f2), t0, *kept_outside(t1))


def call_add(kernel, name, outs, parts, specs, scratch):
    v = pltpu.VMEM
    return pl.pallas_call(
        kernel,
        out_shape=tuple(v(s, LOW) for s in outs),
        in_specs=specs,
        out_specs=(INSIDE,) * len(outs),
        scratch_shapes=[v(s, LOW) for s in scratch] + [pltpu.SemaphoreType.DMA((4,))],
        compiler_params=params(12),
        name=name,
    )(*parts)


def add_one(f0, f1):
    half = (8, F_ROWS, 256)
    return call_add(kernel_add_one, "add_one", (half,), (f0, *kept_outside(f1)), [INSIDE, ANYWHERE], (half,))[0]


def add_words(t0, t1):
    ts = (4, T_ROWS, 256)
    return call_add(
        kernel_add_words, "add_words", (ts, ts, ts), (t0, *kept_outside(t1)), [INSIDE, ANYWHERE], ((3,) + ts,)
    )


def add_two(facc, f2):
    fs = (4, F_ROWS, 256)
    return call_add(kernel_add_two, "add_two", (fs,), (facc, *kept_outside(f2)), [INSIDE, ANYWHERE], (fs,))[0]


def add_three(facc, f3, tacc, tgot):
    fs, ts = (2, F_ROWS, 256), (2, T_ROWS, 256)
    return call_add(
        kernel_add_three, "add_three", (fs, fs, ts, ts), (facc, *kept_outside(f3), tacc, *kept_outside(*tgot)),
        [INSIDE, ANYWHERE] * 2 + [ANYWHERE] * 2, ((4, F_ROWS, 256), (3, 4, T_ROWS, 256)),
    )


def call_f(words, c, outk, outg):
    v = pltpu.VMEM
    outs = ((CVOC, CD), (CD,), (CD, CD), (CD, CD), (CD, CD), (CD, CD), (CD,), (CD, CFF), (CFF, CD), (CD, WD),
            (WD,), (WD, WD), (WD, WD), (WD, WD), (WD, WD), (WD,), (WD, WFF), (WFF, WD))
    outs = [(s[0] // SHARES,) + tuple(n // 2 for n in s[1:]) for s in outs]
    return pl.pallas_call(
        kernel_f,
        out_shape=(shape((2, 1, WORDS, WD // 2), LOW),) + tuple(shape(s, F32) for s in outs),
        in_specs=[INSIDE] * 15,
        out_specs=(INSIDE,) * 19,
        compiler_params=params(8),
        name="finish",
    )(*words, *c, outk, outg)


def flip(value, axis, bits):
    count = lax.axis_size(axis)
    return lax.ppermute(value, axis, [(i, i ^ bits) for i in range(count)])


def flip_both(value, first, second):
    pairs = [(i, i ^ first) for i in range(SHARES)] + [(SHARES + i, SHARES + (i ^ second)) for i in range(SHARES)]
    return lax.ppermute(value, ("phase", "dp"), pairs)


def pick(value, index):
    return lax.dynamic_index_in_dim(value, index, 0, keepdims=False)


def plus(*parts):
    total = parts[0].astype(F32)
    for part in parts[1:]:
        total = total + part.astype(F32)
    return total.astype(LOW)


def across(value, side):
    return flip_both(value, *((1, 2), (2, 1), (4, 4), (8, 8))[side])


def half(bit, *parts):
    return plus(*(lax.dynamic_slice_in_dim(part, bit * (part.shape[0] // 2), part.shape[0] // 2, 0) for part in parts))


def after(value, *others):
    return lax.optimization_barrier((value,) + others)[0]


def together(*values):
    return lax.optimization_barrier(values)


def body(
    char_ids, char_counts, segment_ids, out_cotangent,
    char_table, char_gain_one, char_query, char_key, char_value, char_output, char_gain_two, char_up, char_down,
    char_project,
    word_gain_one, word_query, word_key, word_value, word_output, word_gain_two, word_up, word_down,
):
    keptl, kepts, keptm, kepti, turns, fkeep, fsend, outk, outs, wgain2, *words = call_a(
        char_counts, char_ids, segment_ids, out_cotangent,
        (char_table, char_gain_one, char_query, char_key, char_value, char_output, char_gain_two, char_up, char_down,
         char_project,
         word_gain_one, word_query, word_key, word_value, word_output, word_gain_two, word_up, word_down),
    )
    fgot = flip(fsend, "phase", 1)
    outg = flip(outs, "phase", 1)
    gw, tkeep, tsend, wgain1 = call_a2(
        char_counts, words, word_gain_one, char_project, (word_query, word_key, word_value, word_output)
    )
    one = (char_gain_two, char_up, char_down, kepts, keptm, kepti)
    two = (char_gain_one, char_query, char_key, char_value, char_output)
    if lax.axis_size("dp") != SHARES:
        keptd, aup, gain2, facc = call_b1(turns, gw, *one, fkeep, fgot)
        tgot = flip(tsend, "phase", 1)
        ckeep, csend, _, _ = call_b2(turns, wgain1, wgain2, gain2, aup, two, keptl, keptd, kepti, facc, facc, tkeep, tgot)
        return general_sums(outk, outg, (fkeep, fgot), (tkeep, tgot), (ckeep, flip(csend, "phase", 1)))
    gw, tsend, fgot, outg = together(gw, tsend, fgot, outg)
    gw, fsend = together(gw, add_one(fkeep, fgot))
    f2, tgot = across(fsend, 0), flip(tsend, "phase", 1)
    keptd, aup, gain2, facc = call_b1(turns, gw, *one, fkeep, fgot)
    keptd, tgot = together(keptd, tgot)
    tsends = add_words(tkeep, tgot)
    tparts = [flip(send, "dp", k) for k, send in enumerate(tsends, 1)]
    f2 = after(f2, *tsends)
    fsend = add_two(facc, f2)
    keptd, fsend = together(keptd, fsend)
    f3 = across(fsend, 2)
    ckeep, csend, facc, tacc = call_b2(
        turns, wgain1, wgain2, gain2, aup, two, keptl, keptd, kepti, facc, f2, tkeep, tgot
    )
    ckeep, csend, facc, f3, *tparts = together(ckeep, csend, facc, f3, *tparts)
    _, _, low, high = own_bits()
    cphase = flip(csend, "phase", 1)
    fsend, facc, tsend, tacc = add_three(facc, f3, tacc, tparts)
    f4, t3 = across(fsend, 1), across(tsend, 2)
    dp = lax.axis_index("dp")
    plane, line = lax.rem(dp, 4), lax.div(dp, 4)
    c = [ckeep.reshape(4, 4, C_ROWS, 128), cphase.reshape(4, 4, C_ROWS, 128)]
    sends = [plus(*(pick(part, lax.bitwise_xor(plane, k)) for part in c)) for k in range(1, 4)]
    cgot = [flip(send, "dp", k) for k, send in enumerate(sends, 1)]
    f4, t3 = after(f4, *sends), after(t3, *sends)
    last = jnp.concatenate([pick(half(1 - high, facc, f4), 0), pick(half(1 - high, tacc, t3), 0)], axis=0)
    last = across(last, 3)
    c = [pick(part, plane) for part in c] + cgot
    sends = [plus(*(pick(part, lax.bitwise_xor(line, k)) for part in c)) for k in range(1, 4)]
    cline = [flip(send, "dp", 4 * k) for k, send in enumerate(sends, 1)]
    return call_f((facc, f4, tacc, t3, last), (ckeep, cphase, *cgot, *cline), outk, outg)


def general_sums(outk, outg, fs, ts, cs):
    phase = lax.axis_index("phase")
    first = phase == 0
    outs = jnp.stack([jnp.where(first, outk, outg), jnp.where(first, outg, outk)])[:, None]
    def order(places):
        plain, swapped = (jnp.asarray([places(d, core) for d in range(SHARES)]) for core in range(2))
        return jnp.where(first, plain, swapped)

    def natural(pair, order):
        return jnp.take(pair[0].astype(F32) + pair[1].astype(F32), order, axis=0)

    f, t, c = natural(fs, order(feed_order)), natural(ts, order(word_order)), natural(cs, jnp.asarray([plane_first(d) for d in range(SHARES)]))

    def whole(rows):
        return rows.reshape(-1, rows.shape[-1])

    def wide(rows, pieces):
        n = rows.shape[1] // pieces
        return whole(rows.reshape(SHARES, pieces, n, rows.shape[-1]).transpose(0, 2, 1, 3).reshape(SHARES, n, -1))

    cdown = t[:, T_CDOWN:T_CDOWN + 32]
    cdown = jnp.concatenate([cdown[..., :128], cdown[..., 128:]], axis=1)
    parts = (
        whole(c[:, C_TABLE:C_TABLE + 16]), c[:, C_GAIN, :16].reshape(-1),
        whole(c[:, C_Q:C_Q + 16]), whole(c[:, C_K:C_K + 16]), whole(c[:, C_V:C_V + 16]), whole(c[:, C_O:C_O + 16]),
        c[:, C_GAIN + 1, :16].reshape(-1),
        wide(c[:, C_UP:C_UP + 64], 4), whole(cdown), whole(t[:, T_PROJ:T_PROJ + 16]),
        c[:, C_GAIN + 2, :32].reshape(-1),
        whole(t[:, T_Q:T_Q + 32]), whole(t[:, T_K:T_K + 32]), whole(t[:, T_V:T_V + 32]), whole(t[:, T_O:T_O + 32]),
        c[:, C_GAIN + 3, :32].reshape(-1),
        wide(f[:, F_UP:F_UP + 128], 4), whole(f[:, F_DOWN:F_DOWN + 128]),
    )
    return (outs,) + tuple(lax.psum_scatter(p, "dp", scatter_dimension=0, tiled=True) for p in parts)


def solution(mesh):
    rows = P(None, "dp", None)
    both = P("dp", "phase")
    one = P("dp")
    return jax.shard_map(
        body,
        mesh=mesh,
        in_specs=(rows, rows, rows, P(None, "dp", None, None)) + (P(),) * 18,
        out_specs=(
            P(None, "dp", None, "phase"),
            both, one, both, both, both, both, one, both, both, both,
            one, both, both, both, both, one, both, both,
        ),
        check_vma=False,
    )
```

```python
from functools import partial

import jax
import jax.numpy as jnp
from jax import lax
from jax.experimental import pallas as pl
from jax.experimental.pallas import tpu as pltpu
from jax.sharding import PartitionSpec as P

F32 = jnp.float32
LOW = jnp.bfloat16

CD = 256
CFF = 1024
CPW = 16
CVOC = 256
CHAR_HEADS = 4
HEAD = 64
WD = 512
WFF = 2048
WORD_HEADS = 8
WORDS = 256

SCHEDULE = "aaaafaaaaaaaaafaaaaaaaaafaaaaafa"
SPAN = 256
STEP = 241
WIDE = 2 * SPAN
TURNS = ((WORDS * CPW - 1) // STEP + 2) // 2

epsilon = 1e-06
half_root = 0.7071067811865476
density = 0.3989422804014327
floor_score = -1e30
log2_e = 1.4426950408889634

R_V, R_P, R_EMB, R_Q, R_K, R_MIX = 0, 256, 1280, 1536, 1792, 2048
KEPT_FIRST = 1280
KEPT_LOW = 2304
I_INV1, I_INV2, I_IDENT, I_WORD = 0, 1, 2, 3
BAND = 144
WINDOW = 96

F_UP, F_DOWN = 0, 128
F_ROWS = 256
T_Q, T_K, T_V, T_O, T_CDOWN, T_PROJ = 0, 32, 64, 96, 128, 160
T_ROWS = 176
C_TABLE, C_Q, C_K, C_V, C_O, C_UP, C_GAIN = 0, 16, 32, 48, 64, 80, 144
C_ROWS = 160
SHARES = 16


def nn(left, right):
    return lax.dot_general(left, right, (((1,), (0,)), ((), ())), preferred_element_type=F32)


def nt(left, right):
    return lax.dot_general(left, right, (((1,), (1,)), ((), ())), preferred_element_type=F32)


def iota(shape, axis):
    return lax.broadcasted_iota(jnp.int32, shape, axis)


def eye(n):
    return iota((n, n), 0) == iota((n, n), 1)


def row_to_column(row):
    n = row.shape[1]
    return jnp.sum(jnp.where(eye(n), row, 0.0), axis=1, keepdims=True)


def gelu_pair(v):
    e = lax.erf(v * half_root)
    half = 0.5 * v
    bell = jnp.exp2(v * v * (-0.5 * log2_e))
    return half + half * e, 0.5 + 0.5 * e + (density * v) * bell


def gelu_twice(v):
    u = v * half_root
    whole = 1.0 + lax.erf(u)
    bell = jnp.exp2(u * u * (-log2_e))
    return v * whole, whole + (2.0 * density * v) * bell


def bits(d):
    return d % 2, d // 2 % 2, d // 4 % 2, d // 8


def plane_first(d, core=0):
    return (d % 4) * 4 + d // 4


def feed_order(d, core):
    x, y, low, high = bits(d)
    return (y * 8 + x * 2 if core else x * 8 + y * 2) + low * 4 + high


def word_order(d, core=0):
    _, _, low, high = bits(d)
    return (d % 4) * 4 + low * 2 + high


def own_bits():
    phase, dp = lax.axis_index("phase"), lax.axis_index("dp")
    x, y, low, high = (lax.rem(lax.div(dp, n), 2) for n in (1, 2, 4, 8))
    return jnp.where(phase == 0, x, y), jnp.where(phase == 0, y, x), low, high


def own_plane():
    return lax.rem(lax.axis_index("dp"), 4)


def add_up(out, *parts):
    for i in range(out.shape[0]):
        if len(parts) == 2:
            out[i] = parts[0][i] + parts[1][i]
            continue
        total = parts[0][i].astype(F32)
        for part in parts[1:]:
            total = total + part[i].astype(F32)
        out[i] = total.astype(LOW)


def members(word, first, count, weight=1.0):
    return jnp.where((iota((count, WIDE), 0) + first).astype(F32) == word, weight, 0.0).astype(LOW)


def word_starts(counts_row):
    earlier = iota((WORDS, WORDS), 1) < iota((WORDS, WORDS), 0)
    return jnp.sum(jnp.where(earlier, counts_row, 0.0), axis=1, keepdims=True)


def column_to_row(column):
    return jnp.sum(jnp.where(eye(column.shape[0]), column, 0.0), axis=0, keepdims=True)


def put(keep, send, phase, order, row, halves, share_rows):
    width, lanes = halves[0].shape[1], keep.shape[-1]
    first = phase == 0
    mine, other = jnp.where(first, halves[0], halves[1]), jnp.where(first, halves[1], halves[0])
    for out, low, core in ((keep, mine, phase), (send, other, 1 - phase)):
        for i in range(low.shape[0] // share_rows):
            at, swapped = order(i, 0), order(i, 1)
            if at != swapped:
                at = at + core * (swapped - at)
            rows = low[i * share_rows:(i + 1) * share_rows]
            for piece in range(max(1, width // lanes)):
                part = rows[:, piece * lanes:piece * lanes + min(width, lanes)]
                if width < lanes:
                    part = jnp.concatenate([part[:share_rows // 2], part[share_rows // 2:]], axis=1)
                m = part.shape[0]
                out[at, row + piece * share_rows:row + piece * share_rows + m, :] = part


def column_halves(value):
    width = value.shape[1] // 2
    low = value.astype(LOW)
    return low[:, :width], low[:, width:]


def band(t):
    keys = slice(0, BAND) if t % 2 == 0 else slice(SPAN - BAND, SPAN)
    return t // 2, keys, slice(t * 128, (t + 1) * 128)


def two_heads(pair):
    zero = jnp.zeros((HEAD, pair.shape[1]), LOW)
    first = jnp.concatenate([pair[:HEAD], zero], axis=0)
    second = jnp.concatenate([zero, pair[HEAD:]], axis=0)
    return jnp.concatenate([first, second], axis=1)


def two_heads_rows(pair):
    left = iota(pair.shape, 1) < HEAD
    zero = jnp.zeros(pair.shape, LOW)
    return jnp.concatenate([jnp.where(left, pair, zero), jnp.where(left, zero, pair)], axis=0)


def softmax_keys(s):
    e = jnp.exp(s - jnp.max(s, axis=0, keepdims=True))
    return (e * (1.0 / jnp.sum(e, axis=0, keepdims=True))).astype(LOW)


def kernel_a(
    counts_hbm, ids_hbm, segs_hbm, cot_hbm,
    table_hbm, g1_hbm, wq_hbm, wk_hbm, wv_hbm, wo_hbm, g2_hbm, up_hbm, down_hbm, proj_hbm,
    wg1_hbm, wwq_hbm, wwk_hbm, wwv_hbm, wwo_hbm, wg2_hbm, wup_hbm, wdown_hbm,
    keptl_hbm, kepts_hbm, keptm_hbm, kepti_hbm, turns_ref,
    keep_ref, send_ref, outk_ref, outs_ref, gain_ref,
    first_low_ref, first_slope_ref, first_mid_ref,
    q_ref, k_ref, v_ref, probs_ref, mixt_ref, normed_ref, xhat_ref, winv_ref, md_ref, pooled_ref, pa_ref,
    counts_ref, ids_ref, segs_ref,
    table_ref, g1_ref, wq_ref, wk_ref, wv_ref, wo_ref, g2_ref, up_ref, down_ref, proj_ref, wg1_ref, wg2_ref,
    cot, wwq, wwk, wwv, wwo, wup, wdown,
    tab_t, wqkv_t, wo_t, up_t, ids_t, slow, sslope, smid, sinfo, pa, pm, rowinfo, firsts_v, firsts, before_s, act_s, prob_s, found_s,
    mid_s, word_s, old_s, back_s,
    csem, wsem, ksem,
):
    phase = lax.axis_index("phase")
    tiny = [
        pltpu.make_async_copy(src.at[phase], dst, csem.at[12 + i])
        for i, (src, dst) in enumerate(((counts_hbm, counts_ref), (ids_hbm, ids_ref), (segs_hbm, segs_ref)))
    ]
    for load in tiny:
        load.start()
    early = [
        pltpu.make_async_copy(src, dst, csem.at[i])
        for i, (src, dst) in enumerate(
            ((g1_hbm, g1_ref), (g2_hbm, g2_ref), (table_hbm, table_ref), (wq_hbm, wq_ref), (wk_hbm, wk_ref),
             (wv_hbm, wv_ref), (wo_hbm, wo_ref), (up_hbm, up_ref), (down_hbm, down_ref), (proj_hbm, proj_ref),
             (wg1_hbm, wg1_ref), (wg2_hbm, wg2_ref))
        )
    ]
    for load in early:
        load.start()
    loads = [
        pltpu.make_async_copy(src, dst, wsem.at[i])
        for i, (src, dst) in enumerate(
            ((wwq_hbm, wwq), (wwk_hbm, wwk), (wwv_hbm, wwv), (wwo_hbm, wwo),
             (wup_hbm, wup), (wdown_hbm, wdown), (cot_hbm.at[phase, 0], cot))
        )
    ]
    pa[...] = jnp.zeros_like(pa)
    pm[...] = jnp.zeros_like(pm)
    prob_s[...] = jnp.zeros_like(prob_s)
    for slot in range(2):
        slow[slot, R_P:R_P + CHAR_HEADS * SPAN] = jnp.zeros((CHAR_HEADS * SPAN, WIDE), LOW)
    for load in tiny:
        load.wait()
    counts_row = counts_ref[...].astype(F32)
    starts = word_starts(counts_row)
    counts = row_to_column(counts_row)
    blocks = jnp.floor((starts + 0.5) * (1.0 / STEP))
    places = starts + (SPAN - STEP) * blocks
    n_turns = jnp.max(places).astype(jnp.int32) // WIDE + 1
    turns_ref[0] = n_turns
    bases = (iota((1, 128), 1) * WIDE).astype(F32)
    first = jnp.sum(jnp.where(places < bases, 1.0, 0.0), axis=0, keepdims=True)
    firsts_v[...] = jnp.broadcast_to(first, (8, 128)).astype(jnp.int32)
    first_copy = pltpu.make_async_copy(firsts_v, firsts, wsem.at[7])
    first_copy.start()
    ids = ids_ref[...]
    ids_t[...] = jnp.concatenate(
        [ids[:, 128 * a:128 * a + 128] for a in range(32)], axis=0
    ).astype(F32).T.astype(LOW)
    places_row = column_to_row(places)
    none = jnp.zeros((1, 1), F32)
    rowinfo[...] = jnp.concatenate(
        [places_row - jnp.concatenate([none, places_row[:, :-1]], axis=1),
         counts_row - jnp.concatenate([none, counts_row[:, :-1]], axis=1),
         jnp.ones((1, WORDS), F32), jnp.zeros((13, WORDS), F32)], axis=0
    ).astype(LOW)
    for load in early:
        load.wait()
    for load in loads:
        load.start()
    tab_t[...] = table_ref[...].T
    wqkv_t[0:CD] = (wq_ref[...] * 0.125).T
    wqkv_t[CD:2 * CD] = wk_ref[...].T
    wqkv_t[2 * CD:] = wv_ref[...].T
    wo_t[...] = wo_ref[...].T
    up_t[...] = up_ref[...].T
    g1 = row_to_column(g1_ref[...].astype(F32)[None, :])
    g2 = row_to_column(g2_ref[...].astype(F32)[None, :])
    first_copy.wait()

    def find(turn):
        place = (iota((1, WIDE), 1) + turn * WIDE).astype(F32)
        begun = jnp.where(places <= place, 1.0, 0.0).astype(LOW)
        info = nn(rowinfo[...], begun)
        word = info[2:3] - 1.0
        slot = place - info[0:1]
        flat = (word * 16.0 + slot).astype(jnp.int32)
        chosen = jnp.where(iota((32, WIDE), 0) == (flat >> 7), 1.0, 0.0).astype(LOW)
        lanes = nn(ids_t[...], chosen)
        ident = jnp.sum(jnp.where(iota((128, WIDE), 0) == (flat & 127), lanes, 0.0), axis=0, keepdims=True)
        valid = slot < info[1:2]
        none = jnp.full((6, WIDE), -1.0, F32)
        return jnp.concatenate([jnp.where(valid, ident, -1.0), jnp.where(valid, word, -1.0), none], axis=0)

    found_s[...] = find(jnp.int32(0))

    def copies_one(b):
        slot = lax.rem(b, 2)
        return (
            pltpu.make_async_copy(slow.at[slot], keptl_hbm.at[b], ksem.at[0, slot]),
            pltpu.make_async_copy(smid.at[slot], keptm_hbm.at[b], ksem.at[2, slot]),
            pltpu.make_async_copy(sinfo.at[slot], kepti_hbm.at[b], ksem.at[3, slot]),
        )

    def copies_two(b):
        slot = lax.rem(b, 2)
        return (pltpu.make_async_copy(sslope.at[slot], kepts_hbm.at[b], ksem.at[1, slot]),)

    def start(copies):
        for c in copies:
            c.start()

    def wait(copies):
        for c in copies:
            c.wait()

    def near_words(b):
        first = (firsts[0, b] // 16) * 16
        return first, (firsts[0, b + 1] - first + WINDOW - 1) // WINDOW

    def window(first):
        return pl.ds(pl.multiple_of(first, 16), WINDOW)

    def attend(b):
        slot = lax.rem(b, 2)
        ident = found_s[0:1]
        word = found_s[1:2]
        hot = jnp.where(iota((CVOC, WIDE), 0).astype(F32) == ident, 1.0, 0.0).astype(LOW)
        emb = nn(tab_t[...], hot)
        inv1 = lax.rsqrt(jnp.mean(emb * emb, axis=0, keepdims=True) + epsilon)
        normed = (emb * inv1 * g1).astype(LOW)
        yield
        qkv = []
        for i in range(3):
            qkv.append(nn(wqkv_t[i * CD:(i + 1) * CD], normed).astype(LOW))
            yield
        query_t, key_t, value_t = qkv
        slow[slot, R_EMB:R_EMB + CD] = emb.astype(LOW)
        slow[slot, R_Q:R_Q + CD] = query_t
        slow[slot, R_K:R_K + CD] = key_t
        key_rows = [key_t[:, u * SPAN:(u + 1) * SPAN].T for u in range(2)]
        word_col = jnp.broadcast_to(jnp.where(word < 0.0, -2.0, word), (8, WIDE)).T[:, 0:1]
        yield
        scores = []
        for t in range(4):
            u, ks, ql = band(t)
            for pair in range(CHAR_HEADS // 2):
                fs = slice(pair * 128, pair * 128 + 128)
                scores.append(nn(key_rows[u][ks, fs], two_heads(query_t[fs, ql])))
                yield
        for u in range(2):
            us = slice(u * SPAN, (u + 1) * SPAN)
            slow[slot, R_V:R_V + SPAN, us] = value_t[:, us].T
        for t in range(4):
            u, ks, ql = band(t)
            bias = jnp.where(word_col[u * SPAN + ks.start:u * SPAN + ks.stop] == word[:, ql], 0.0, floor_score)
            for pair in range(CHAR_HEADS // 2):
                s = scores[t * 2 + pair]
                for i in range(2):
                    p = softmax_keys(s[:, i * 128:i * 128 + 128] + bias)
                    row = (pair * 2 + i) * SPAN
                    prob_s[row + ks.start:row + ks.stop, ql] = p
                    slow[slot, R_P + row + ks.start:R_P + row + ks.stop, ql] = p
        yield
        mixed = [[], []]
        for u in range(2):
            us = slice(u * SPAN, (u + 1) * SPAN)
            for h in range(CHAR_HEADS):
                hs = slice(h * HEAD, (h + 1) * HEAD)
                mixed[u].append(nn(value_t[hs, us], prob_s[h * SPAN:(h + 1) * SPAN, us]).astype(LOW))
                yield
        mixed = jnp.concatenate([jnp.concatenate(part, axis=0) for part in mixed], axis=1)
        slow[slot, R_MIX:R_MIX + CD] = mixed
        middle = emb + nn(wo_t[...], mixed)
        yield
        inv2 = lax.rsqrt(jnp.mean(middle * middle, axis=0, keepdims=True) + epsilon)
        smid[slot] = middle
        sinfo[slot] = jnp.concatenate([inv1, inv2, ident, word, jnp.zeros((4, WIDE), F32)], axis=0)
        normed_two = (middle * inv2 * g2).astype(LOW)
        middle_low = middle.astype(LOW)
        yield
        for c in range(CFF // 256):
            cs = slice(c * 256, (c + 1) * 256)
            before_s[cs] = nn(up_t[cs], normed_two)
            if c == 0:
                found_s[...] = find(b + 1)
            if c == 1:
                first, _ = near_words(b)
                pm[window(first), :] += nt(members(word, first, WINDOW), middle_low)
                mid_s[...] = middle_low
            if c == 3:
                old_s[0:1] = word_s[0:1]
                word_s[0:1] = word
            yield

    def feed(b):
        slot = lax.rem(b, 2)
        first, _ = near_words(b)
        near = members(word_s[0:1], first, WINDOW, 0.5)
        for c in range(CFF // 256):
            for d in range(8):
                cs = slice(c * 256 + d * 32, c * 256 + (d + 1) * 32)
                act, slope = gelu_twice(before_s[cs])
                sslope[slot, cs] = slope.astype(LOW)
                act_s[cs] = act.astype(LOW)
            cs = slice(c * 256, (c + 1) * 256)
            pa[window(first), cs] += nt(near, act_s[cs])
            yield

    def run(order, one, two):
        parts = {"a": one, "f": two}
        for step in order:
            next(parts[step])

    def more_one(b):
        first, windows = near_words(b)

        def more(i, carry):
            at = first + i * WINDOW
            pm[window(at), :] += nt(members(word_s[0:1], at, WINDOW), mid_s[...])
            return carry

        lax.fori_loop(1, windows, more, 0)

    def more_two(b, word):
        first, windows = near_words(b)

        def more(i, carry):
            at = first + i * WINDOW
            pa[window(at), :] += nt(members(word[0:1], at, WINDOW, 0.5), act_s[...])
            return carry

        lax.fori_loop(1, windows, more, 0)

    run("a" * 28, attend(jnp.int32(0)), None)
    more_one(jnp.int32(0))
    start(copies_one(jnp.int32(0)))
    first_low_ref[...] = slow[0]
    first_mid_ref[...] = smid[0]

    def turn(b, carry):
        @pl.when(b >= 2)
        def _():
            wait(copies_one(b - 2))

        @pl.when(b >= 3)
        def _():
            wait(copies_two(b - 3))

        run(SCHEDULE, attend(b), feed(b - 1))
        more_one(b)
        more_two(b - 1, old_s)

        @pl.when(b == 1)
        def _():
            first_slope_ref[...] = sslope[0]

        start(copies_one(b))
        start(copies_two(b - 1))
        return carry

    lax.fori_loop(1, n_turns, turn, 0)

    @pl.when(n_turns >= 3)
    def _():
        wait(copies_two(n_turns - 3))

    for load in loads:
        load.wait()
    cot_low = cot[...]
    last = feed(n_turns - 1)
    for c in range(4):
        cs = slice(c * 512, (c + 1) * 512)
        back_s[:, cs] = nt(cot_low, wdown[cs, :])
        next(last)
    more_two(n_turns - 1, word_s)

    @pl.when(n_turns == 1)
    def _():
        first_slope_ref[...] = sslope[0]

    start(copies_two(n_turns - 1))

    pa_hi = pa[0:WORDS].astype(LOW)
    per_count = 1.0 / counts
    pooled = (pm[0:WORDS] + nn(pa_hi, down_ref[...])) * per_count
    pooled_low = pooled.astype(LOW)
    pooled_ref[...] = pooled_low
    pa_ref[...] = pa_hi
    x = nn(pooled_low, proj_ref[...]).astype(LOW).astype(F32)
    wg1 = wg1_ref[...].astype(F32)[None, :]
    wg2 = wg2_ref[...].astype(F32)[None, :]
    winv1 = lax.rsqrt(jnp.mean(x * x, axis=1, keepdims=True) + epsilon)
    xhat = x * winv1
    normed = (xhat * wg1).astype(LOW)
    xhat_ref[...] = xhat
    winv_ref[...] = jnp.broadcast_to(winv1, (WORDS, 128))
    normed_ref[...] = normed
    q = (nn(normed, wwq[...]) * 0.125).astype(LOW)
    k = nn(normed, wwk[...]).astype(LOW)
    v = nn(normed, wwv[...]).astype(LOW)
    seg_row = segs_ref[...].astype(F32)
    seg_col = row_to_column(seg_row)
    allowed = (seg_row == seg_col) & (iota((WORDS, WORDS), 0) <= iota((WORDS, WORDS), 1))
    bias = jnp.where(allowed, 0.0, floor_score)
    q_ref[...] = q
    k_ref[...] = k
    v_ref[...] = v
    v_t = v.T
    for h in range(WORD_HEADS):
        probs_ref[h, 128:, 0:128] = jnp.zeros((128, 128), LOW)
    halves = [(slice(0, 128 * (t + 1)), slice(128 * t, 128 * (t + 1))) for t in range(2)]
    pairs = [slice(pair * 128, pair * 128 + 128) for pair in range(WORD_HEADS // 2)]
    scores = [[nt(k[ks, fs], two_heads_rows(q[ql, fs])) for ks, ql in halves] for fs in pairs]
    mixed_t = []
    for pair in range(WORD_HEADS // 2):
        for (ks, ql), s in zip(halves, scores[pair]):
            for i in range(2):
                probs_ref[pair * 2 + i, ks, ql] = softmax_keys(s[:, i * 128:i * 128 + 128] + bias[ks, ql])
        for h in (pair * 2, pair * 2 + 1):
            mixed_t.append(nn(v_t[h * HEAD:(h + 1) * HEAD], probs_ref[h]).astype(LOW))
    mixed_t = jnp.concatenate(mixed_t, axis=0)
    mixt_ref[...] = mixed_t
    middle = x + nn(mixed_t.T, wwo[...])
    winv2 = lax.rsqrt(jnp.mean(middle * middle, axis=1, keepdims=True) + epsilon)
    normed_two = (middle * winv2 * wg2).astype(LOW)
    result = middle
    n2d = jnp.zeros((WORDS, WD), F32)
    n2_t = normed_two.T
    held = {}
    turns = (0, 2, 1, 3)
    quarter = [slice(c * 512, (c + 1) * 512) for c in range(4)]
    act, slope = gelu_pair(nn(normed_two, wup[:, quarter[0]]))
    for i, c in enumerate(turns):
        cs = quarter[c]
        act = act.astype(LOW)
        bd = (back_s[:, cs] * slope).astype(LOW)
        if i < 3:
            ahead = nn(normed_two, wup[:, quarter[turns[i + 1]]])
        result = result + nn(act, wdown[cs, :])
        gd = nn(act.T, cot_low)
        gu = nn(n2_t, bd).astype(LOW)
        n2d = n2d + nt(bd, wup[:, cs])
        if i < 3:
            act, slope = gelu_pair(ahead)
        put(keep_ref, send_ref, phase, lambda i, p: feed_order(c * 4 + i, p), F_DOWN, column_halves(gd), 128)
        if c < 2:
            held[c] = gu
        else:
            put(keep_ref, send_ref, phase, feed_order, F_UP + (c - 2) * 64, (held[c - 2], gu), 32)
    result = result.astype(LOW)
    front = phase == 0
    outk_ref[...] = jnp.where(front, result[:, :256], result[:, 256:])
    outs_ref[...] = jnp.where(front, result[:, 256:], result[:, :256])
    vhat = middle * winv2
    gain_ref[...] = jnp.broadcast_to(jnp.sum(n2d * vhat, axis=0, keepdims=True), (8, WD))
    lifted = n2d * wg2
    md_ref[...] = cot[...].astype(F32) + winv2 * (lifted - vhat * jnp.mean(lifted * vhat, axis=1, keepdims=True))

    def drain(b, carry):
        wait(copies_one(b))
        wait(copies_two(b))
        return carry

    lax.fori_loop(jnp.maximum(n_turns - 2, 0), n_turns, drain, 0)


def kernel_a2(
    counts_ref, q_ref, k_ref, v_ref, pw, mixt_ref, normed_ref, xhat_ref, winv_ref, md_ref, pooled_ref, pa_ref,
    wg1_ref, proj_ref, wwq, wwk, wwv, wwo,
    gw_ref, keep_ref, send_ref, gain_ref,
):
    phase = lax.axis_index("phase")
    wg1 = wg1_ref[...].astype(F32)[None, :]
    q, k, v, normed, pooled_low = q_ref[...], k_ref[...], v_ref[...], normed_ref[...], pooled_ref[...]
    per_count = 1.0 / row_to_column(counts_ref[phase].astype(F32))
    md = md_ref[...]
    md_low = md.astype(LOW)
    put(keep_ref, send_ref, phase, word_order, T_O, column_halves(nn(mixt_ref[...], md_low)), 32)
    k_t = k.T
    do = nt(md_low, wwo[...]).astype(LOW)
    dq_t, dk, dv = [], [], []
    left = iota((WORDS, 128), 1) < HEAD
    pairs = [slice(pair * 128, pair * 128 + 128) for pair in range(WORD_HEADS // 2)]
    halves = [(slice(0, 128 * (t + 1)), slice(128 * t, 128 * (t + 1))) for t in range(2)]
    deltas = [[nt(v[ks, fs], two_heads_rows(do[ql, fs])) for ks, ql in halves] for fs in pairs]

    def scores(pair):
        ds = []
        for (ks, ql), dp in zip(halves, deltas[pair]):
            for i in range(2):
                pf = pw[pair * 2 + i, ks, ql].astype(F32)
                dph = dp[:, i * 128:i * 128 + 128]
                d = (pf * (dph - jnp.sum(pf * dph, axis=0, keepdims=True))).astype(LOW)
                ds.append(d if ks.stop == WORDS else jnp.concatenate([d, jnp.zeros((128, 128), LOW)], axis=0))
        return [jnp.concatenate([ds[i], ds[i + 2]], axis=1) for i in range(2)]

    both = None
    for pair in range(WORD_HEADS // 2 + 1):
        ahead = scores(pair) if pair < WORD_HEADS // 2 else None
        if ahead is not None:
            fs = pairs[pair]
            dv.append(jnp.where(left, nn(pw[pair * 2], do[:, fs]), nn(pw[pair * 2 + 1], do[:, fs])).astype(LOW))
        if both is not None:
            fs = pairs[pair - 1]
            for i in range(2):
                h = (pair - 1) * 2 + i
                dq_t.append(nn(k_t[h * HEAD:(h + 1) * HEAD], both[i]))
            dk.append(jnp.where(left, nn(both[0], q[:, fs]), nn(both[1], q[:, fs])).astype(LOW))
        both = ahead
    dq = (jnp.concatenate(dq_t, axis=0) * 0.125).astype(LOW).T
    dk = jnp.concatenate(dk, axis=1)
    dv = jnp.concatenate(dv, axis=1)
    normed_t = normed.T
    nd = nt(dq, wwq[...]) + nt(dk, wwk[...]) + nt(dv, wwv[...])
    put(keep_ref, send_ref, phase, word_order, T_Q, column_halves(nn(normed_t, dq)), 32)
    put(keep_ref, send_ref, phase, word_order, T_K, column_halves(nn(normed_t, dk)), 32)
    put(keep_ref, send_ref, phase, word_order, T_V, column_halves(nn(normed_t, dv)), 32)
    vhat = xhat_ref[...]
    gain_ref[...] = jnp.broadcast_to(jnp.sum(nd * vhat, axis=0, keepdims=True), (8, WD))
    lifted = nd * wg1
    xd = md + winv_ref[:, 0:1] * (lifted - vhat * jnp.mean(lifted * vhat, axis=1, keepdims=True))
    vd = xd.astype(LOW)
    put(keep_ref, send_ref, phase, word_order, T_PROJ, column_halves(nn(pooled_low.T, vd)), 16)
    gw = (nt(vd, proj_ref[...]) * per_count).astype(LOW)
    gw_ref[...] = gw.T
    put(keep_ref, send_ref, phase, word_order, T_CDOWN, column_halves(nn(pa_ref[...].T, gw)), 64)


def kernel_b1(
    turns_ref, gw_ref, g2_ref, up_ref, down_ref, kepts_hbm, keptm_hbm, info_ref, f0_ref, f1_hbm, first_slope_ref, first_mid_ref,
    delta_ref, aup_ref, gain_ref, facc_ref,
    sslope, smid, given, aup, ag2, down, f1, ksem, fsem,
):
    n_turns = turns_ref[0]

    def kept_copies(b, slot):
        return (
            pltpu.make_async_copy(kepts_hbm.at[b], sslope.at[slot], ksem.at[0, slot]),
            pltpu.make_async_copy(keptm_hbm.at[b], smid.at[slot], ksem.at[1, slot]),
        )

    sslope[0] = first_slope_ref[...]
    smid[0] = first_mid_ref[...]
    a, _, _, _ = own_bits()
    load = pltpu.make_async_copy(f1_hbm.at[pl.ds(a * 8, 8)], f1, fsem.at[0])
    load.start()
    g2 = row_to_column(g2_ref[...].astype(F32)[None, :])
    down[...] = down_ref[...] * 0.5
    aup[...] = jnp.zeros_like(aup)
    ag2[...] = jnp.zeros_like(ag2)

    def give(b):
        given[...] = nn(gw_ref[...], members(info_ref[b, I_WORD:I_WORD + 1], 0, WORDS)).astype(LOW)

    give(0)

    def turn(b, carry):
        slot = lax.rem(b, 2)

        @pl.when(b + 1 < n_turns)
        def _():
            for c in kept_copies(b + 1, 1 - slot):
                c.start()

        @pl.when(b > 0)
        def _():
            for c in kept_copies(b, slot):
                c.wait()

        cuts = [slice(c * 256, (c + 1) * 256) for c in range(CFF // 256)]
        inv2 = info_ref[b, I_INV2:I_INV2 + 1]
        g_low = given[...]
        vhat = smid[slot] * inv2
        normed_two = (vhat * g2).astype(LOW)
        n2d = jnp.zeros((CD, WIDE), F32)
        ahead = nn(down[cuts[0], :], g_low)
        bds = []
        for c, cs in enumerate(cuts):
            bds.append((ahead * sslope[slot, cs].astype(F32)).astype(LOW))
            if c + 1 < len(cuts):
                ahead = nn(down[cuts[c + 1], :], g_low)
            n2d = n2d + nn(up_ref[:, cs], bds[c])
        aup[:, cuts[0]] += nt(normed_two, bds[0])
        ag2[...] += n2d * vhat
        lifted = n2d * g2
        aup[:, cuts[1]] += nt(normed_two, bds[1])
        mean = jnp.mean(lifted * vhat, axis=0, keepdims=True)
        aup[:, cuts[2]] += nt(normed_two, bds[2])
        md = g_low.astype(F32) + inv2 * (lifted - vhat * mean)
        delta_ref[b] = md.astype(LOW)
        aup[:, cuts[3]] += nt(normed_two, bds[3])
        give(jnp.minimum(b + 1, TURNS - 1))
        return carry

    lax.fori_loop(0, n_turns, turn, 0)
    aup_ref[...] = aup[...].astype(LOW)
    load.wait()
    add_up(facc_ref, f0_ref.at[pl.ds(a * 8, 8)], f1)
    gain_ref[...] = jnp.broadcast_to(jnp.sum(ag2[...], axis=1, keepdims=True), (CD, 8)).T


def kernel_b2(
    turns_ref, wgain1_ref, wgain2_ref, gain2_ref, aup_ref, g1_ref, wq_ref, wk_ref, wv_ref, wo_ref,
    keptl_hbm, first_low_ref, delta_ref, info_ref, facc_ref, f2_hbm, t0_ref, t1_hbm,
    keep_ref, send_ref, fnext_ref, tacc_ref,
    slow, up_next, dscore, wqkv, aqkv, ao, atab, ag1, f2, t1, ksem, fsem,
):
    phase = lax.axis_index("phase")
    n_turns = turns_ref[0]

    def kept_copies(b, slot):
        return [
            pltpu.make_async_copy(keptl_hbm.at[b, rows], slow.at[slot, rows], ksem.at[i, slot])
            for i, rows in enumerate((pl.ds(0, KEPT_FIRST), pl.ds(KEPT_FIRST, KEPT_LOW - KEPT_FIRST)))
        ]

    slow[0] = first_low_ref[...]
    _, _, low, _ = own_bits()
    quarter = pl.ds(own_plane() * 4, 4)
    loads = [
        pltpu.make_async_copy(src.at[at], dst, fsem.at[i])
        for i, (src, at, dst) in enumerate(((f2_hbm, pl.ds(low * 4, 4), f2), (t1_hbm, quarter, t1)))
    ]
    for load in loads:
        load.start()
    g1 = row_to_column(g1_ref[...].astype(F32)[None, :])
    for i, w in enumerate((wq_ref, wk_ref, wv_ref)):
        wqkv[:, i * CD:(i + 1) * CD] = w[...]
    for acc in (aqkv, ao, atab, ag1, dscore):
        acc[...] = jnp.zeros_like(acc)

    def step(b):
        up_next[...] = nn(wo_ref[...], delta_ref[b]).astype(LOW)

    step(0)

    def turn(b, carry):
        slot = lax.rem(b, 2)

        @pl.when(b + 1 < n_turns)
        def _():
            for c in kept_copies(b + 1, 1 - slot):
                c.start()

        @pl.when(b > 0)
        def _():
            for c in kept_copies(b, slot):
                c.wait()

        do = up_next[...]
        deltas = []
        for t in range(4):
            u, ks, ql = band(t)
            for pair in range(CHAR_HEADS // 2):
                fs = slice(u * SPAN + pair * 128, u * SPAN + pair * 128 + 128)
                deltas.append(nn(
                    slow[slot, R_V + ks.start:R_V + ks.stop, fs], two_heads(do[pair * 128:pair * 128 + 128, ql])
                ))
        dq, dk, dv = ([[None, None] for _ in range(CHAR_HEADS)] for _ in range(3))
        for t in range(4):
            u, ks, ql = band(t)
            for pair in range(CHAR_HEADS // 2):
                dp = deltas[t * 2 + pair]
                for i in range(2):
                    row = (pair * 2 + i) * SPAN
                    pf = slow[slot, R_P + row + ks.start:R_P + row + ks.stop, ql].astype(F32)
                    dph = dp[:, i * 128:i * 128 + 128]
                    d = pf * (dph - jnp.sum(pf * dph, axis=0, keepdims=True))
                    dscore[row + ks.start:row + ks.stop, ql] = d.astype(LOW)
                h, v = (t % 2) * 2 + pair, t // 2
                vs = slice(v * SPAN, (v + 1) * SPAN)
                dv[h][v] = nt(do[h * HEAD:(h + 1) * HEAD, vs], slow[slot, R_P + h * SPAN:R_P + (h + 1) * SPAN, vs]).astype(LOW)
        inv1 = info_ref[b, I_INV1:I_INV1 + 1]
        ident = info_ref[b, I_IDENT:I_IDENT + 1]
        md_low = delta_ref[b]
        emb = slow[slot, R_EMB:R_EMB + CD].astype(F32)
        ehat = emb * inv1
        normed = (ehat * g1).astype(LOW)
        hot = jnp.where(iota((CVOC, WIDE), 0).astype(F32) == ident, 1.0, 0.0).astype(LOW)
        for h in range(CHAR_HEADS):
            for u in range(2):
                us = slice(u * SPAN, (u + 1) * SPAN)
                ds = dscore[h * SPAN:(h + 1) * SPAN, us]
                dq[h][u] = (nn(slow[slot, R_K + h * HEAD:R_K + (h + 1) * HEAD, us], ds) * 0.125).astype(LOW)
                dk[h][u] = nt(slow[slot, R_Q + h * HEAD:R_Q + (h + 1) * HEAD, us], ds).astype(LOW)
        dqkv = jnp.concatenate([jnp.concatenate(pair, axis=1) for part in (dq, dk, dv) for pair in part], axis=0)
        nd = nn(wqkv[...], dqkv)
        aqkv[:, 0:CD] += nt(normed, dqkv[0:CD])
        ag1[...] += nd * ehat
        lifted = nd * g1
        aqkv[:, CD:2 * CD] += nt(normed, dqkv[CD:2 * CD])
        mean = jnp.mean(lifted * ehat, axis=0, keepdims=True)
        aqkv[:, 2 * CD:] += nt(normed, dqkv[2 * CD:])
        ed = md_low.astype(F32) + inv1 * (lifted - ehat * mean)
        step(jnp.minimum(b + 1, TURNS - 1))
        ao[...] += nt(slow[slot, R_MIX:R_MIX + CD], md_low)
        atab[...] += nt(hot, ed.astype(LOW))
        return carry

    lax.fori_loop(0, n_turns, turn, 0)

    for load in loads:
        load.wait()
    add_up(fnext_ref, facc_ref.at[pl.ds(low * 4, 4)], f2)
    add_up(tacc_ref, t0_ref.at[quarter], t1)
    put(keep_ref, send_ref, phase, plane_first, C_TABLE, column_halves(atab[...]), 16)
    put(keep_ref, send_ref, phase, plane_first, C_Q, column_halves(aqkv[:, 0:CD]), 16)
    put(keep_ref, send_ref, phase, plane_first, C_K, column_halves(aqkv[:, CD:2 * CD]), 16)
    put(keep_ref, send_ref, phase, plane_first, C_V, column_halves(aqkv[:, 2 * CD:]), 16)
    put(keep_ref, send_ref, phase, plane_first, C_O, column_halves(ao[...]), 16)
    put(keep_ref, send_ref, phase, plane_first, C_UP, column_halves(aup_ref[...]), 16)
    cg1 = jnp.broadcast_to(jnp.sum(ag1[...], axis=1, keepdims=True), (CD, 8)).T[0:1]
    cg2 = gain2_ref[0:1]
    for d in range(SHARES):
        rows = [
            jnp.concatenate([cg1[:, d * 16:d * 16 + 16], jnp.zeros((1, 112), F32)], axis=1),
            jnp.concatenate([cg2[:, d * 16:d * 16 + 16], jnp.zeros((1, 112), F32)], axis=1),
            jnp.concatenate([wgain1_ref[0:1, d * 32:d * 32 + 32], jnp.zeros((1, 96), F32)], axis=1),
            jnp.concatenate([wgain2_ref[0:1, d * 32:d * 32 + 32], jnp.zeros((1, 96), F32)], axis=1),
            jnp.zeros((12, 128), F32),
        ]
        tile = jnp.concatenate(rows, axis=0).astype(LOW)
        keep_ref[plane_first(d), C_GAIN:C_GAIN + 16, :] = tile
        send_ref[plane_first(d), C_GAIN:C_GAIN + 16, :] = tile


def kernel_add_one(f0_ref, f1_hbm, send_ref, f1, sem):
    a, _, _, _ = own_bits()
    loads = [
        pltpu.make_async_copy(f1_hbm.at[pl.ds((1 - a) * 8 + i, 2)], f1.at[pl.ds(i, 2)], sem.at[i // 2]) for i in range(0, 8, 2)
    ]
    for load in loads:
        load.start()
    for i, load in enumerate(loads):
        load.wait()
        at = pl.ds(i * 2, 2)
        add_up(send_ref.at[at], f0_ref.at[pl.ds((1 - a) * 8 + i * 2, 2)], f1.at[at])


def kernel_add_words(t0_ref, t1_hbm, ts1_ref, ts2_ref, ts3_ref, t1, sem):
    places = [pl.ds(lax.bitwise_xor(own_plane(), k) * 4, 4) for k in range(1, 4)]
    loads = [pltpu.make_async_copy(t1_hbm.at[at], t1.at[k], sem.at[k]) for k, at in enumerate(places)]
    for load in loads:
        load.start()
    for k, out in enumerate((ts1_ref, ts2_ref, ts3_ref)):
        loads[k].wait()
        add_up(out, t0_ref.at[places[k]], t1.at[k])


def kernel_add_two(facc_ref, f2_hbm, fsend_ref, f2, sem):
    _, _, low, _ = own_bits()
    half = pl.ds((1 - low) * 4, 4)
    load = pltpu.make_async_copy(f2_hbm.at[half], f2, sem.at[0])
    load.start()
    load.wait()
    add_up(fsend_ref, facc_ref.at[half], f2)


def kernel_add_three(
    facc_ref, f3_hbm, tacc_ref, tg1_hbm, tg2_hbm, tg3_hbm, fsend_ref, fkeep_ref, tsend_ref, tkeep_ref, f3, tg, sem
):
    _, b, low, _ = own_bits()
    loads = [pltpu.make_async_copy(src, tg.at[i], sem.at[0]) for i, src in enumerate((tg1_hbm, tg2_hbm, tg3_hbm))]
    loads.append(pltpu.make_async_copy(f3_hbm, f3, sem.at[1]))
    for load in loads:
        load.start()
    for load in loads[:3]:
        load.wait()
    for out, bit in ((tsend_ref, 1 - low), (tkeep_ref, low)):
        at = pl.ds(bit * 2, 2)
        add_up(out, tacc_ref.at[at], *(tg.at[k, at] for k in range(3)))
    loads[3].wait()
    for out, bit in ((fsend_ref, 1 - b), (fkeep_ref, b)):
        add_up(out, facc_ref.at[pl.ds(bit * 2, 2)], f3.at[pl.ds(bit * 2, 2)])


def kernel_f(
    f3, f4, t2, t3, last, c0, c1, c2, c3, c4, c5, c6, c7, outk, outg,
    word_out, d_table, d_g1, d_q, d_k, d_v, d_o, d_g2, d_up, d_down, d_proj,
    e_g1, e_q, e_k, e_v, e_o, e_g2, e_up, e_down,
):
    phase = lax.axis_index("phase")
    dp = lax.axis_index("dp")
    _, _, low, high = own_bits()
    line = lax.div(dp, 4)
    place = lax.rem(dp, 4) * 4 + line
    fs = ((f3, high), (f4, high), (last, 0))
    ts = ((t2, high), (t3, high), (last, F_ROWS))
    cs = ((c0, place), (c1, place), (c2, line), (c3, line), (c4, line), (c5, None), (c6, None), (c7, None))
    word_out[phase, 0] = outk[...]
    word_out[1 - phase, 0] = outg[...]

    def total(parts, row, n):
        t = None
        for part, at in parts:
            if part is last:
                piece = part[at + row:at + row + n]
            else:
                piece = part[row:row + n] if at is None else part[at, row:row + n]
            t = piece.astype(F32) if t is None else t + piece.astype(F32)
        return t

    f, t, c = partial(total, fs), partial(total, ts), partial(total, cs)
    d_table[...] = c(C_TABLE, 16)
    d_q[...] = c(C_Q, 16)
    d_k[...] = c(C_K, 16)
    d_v[...] = c(C_V, 16)
    d_o[...] = c(C_O, 16)
    for i in range(4):
        d_up[:, i * 128:(i + 1) * 128] = c(C_UP + i * 16, 16)
        e_up[:, i * 256:(i + 1) * 256] = f(F_UP + i * 32, 32)
    gains = c(C_GAIN, 16)
    d_g1[...] = gains[0, :16]
    d_g2[...] = gains[1, :16]
    e_g1[...] = gains[2, :32]
    e_g2[...] = gains[3, :32]
    cd = t(T_CDOWN, 32)
    d_down[0:32] = cd[:, :128]
    d_down[32:64] = cd[:, 128:]
    d_proj[...] = t(T_PROJ, 16)
    e_q[...] = t(T_Q, 32)
    e_k[...] = t(T_K, 32)
    e_v[...] = t(T_V, 32)
    e_o[...] = t(T_O, 32)
    e_down[...] = f(F_DOWN, 128)


ANYWHERE = pl.BlockSpec(memory_space=pltpu.HBM)
INSIDE = pl.BlockSpec(memory_space=pltpu.VMEM)
SCALARS = pl.BlockSpec(memory_space=pltpu.SMEM)
shape = jax.ShapeDtypeStruct


def params(mib):
    return pltpu.CompilerParams(vmem_limit_bytes=mib * 2**20)


def outside(dims, dtype):
    return pltpu.HBM(dims, dtype)


def kept_outside(*values):
    return tuple(pltpu.with_memory_space_constraint(v, pltpu.HBM) for v in values)


def call_a(char_counts, char_ids, segment_ids, out_cotangent, weights):
    v = pltpu.VMEM
    return pl.pallas_call(
        kernel_a,
        out_shape=(
            outside((TURNS, KEPT_LOW, WIDE), LOW),
            outside((TURNS, CFF, WIDE), LOW),
            outside((TURNS, CD, WIDE), F32),
            outside((TURNS, 8, WIDE), F32),
            shape((1,), jnp.int32),
            v((SHARES, F_ROWS, 256), LOW),
            v((SHARES, F_ROWS, 256), LOW),
            shape((WORDS, WD // 2), LOW),
            shape((WORDS, WD // 2), LOW),
            shape((8, WD), F32),
            v((KEPT_LOW, WIDE), LOW), v((CFF, WIDE), LOW), v((CD, WIDE), F32),
            shape((WORDS, WD), LOW), shape((WORDS, WD), LOW), shape((WORDS, WD), LOW),
            shape((WORD_HEADS, WORDS, WORDS), LOW), shape((WD, WORDS), LOW), shape((WORDS, WD), LOW),
            shape((WORDS, WD), F32), shape((WORDS, 128), F32), shape((WORDS, WD), F32),
            shape((WORDS, CD), LOW), shape((WORDS, CFF), LOW),
        ),
        in_specs=[ANYWHERE] * 22,
        out_specs=(ANYWHERE,) * 4 + (SCALARS,) + (INSIDE,) * 19,
        scratch_shapes=[
            v((1, WORDS), jnp.int32), v((1, WORDS * CPW), jnp.int32), v((1, WORDS), jnp.int32),
            v((CVOC, CD), LOW), v((CD,), LOW), v((CD, CD), LOW), v((CD, CD), LOW), v((CD, CD), LOW), v((CD, CD), LOW),
            v((CD,), LOW), v((CD, CFF), LOW), v((CFF, CD), LOW), v((CD, WD), LOW), v((WD,), LOW), v((WD,), LOW),
            v((WORDS, WD), LOW),
            v((WD, WD), LOW), v((WD, WD), LOW), v((WD, WD), LOW), v((WD, WD), LOW),
            v((WD, WFF), LOW), v((WFF, WD), LOW),
            v((CD, CVOC), LOW), v((3 * CD, CD), LOW), v((CD, CD), LOW), v((CFF, CD), LOW), v((128, 32), LOW),
            v((2, KEPT_LOW, WIDE), LOW), v((2, CFF, WIDE), LOW), v((2, CD, WIDE), F32), v((2, 8, WIDE), F32),
            v((WORDS + WINDOW, CFF), F32), v((WORDS + WINDOW, CD), F32), v((16, WORDS), LOW),
            v((8, 128), jnp.int32), pltpu.SMEM((8, 128), jnp.int32),
            v((CFF, WIDE), F32), v((CFF, WIDE), LOW), v((CHAR_HEADS * SPAN, WIDE), LOW), v((8, WIDE), F32),
            v((CD, WIDE), LOW), v((8, WIDE), F32), v((8, WIDE), F32), v((WORDS, WFF), F32),
            pltpu.SemaphoreType.DMA((15,)),
            pltpu.SemaphoreType.DMA((8,)),
            pltpu.SemaphoreType.DMA((4, 2)),
        ],
        compiler_params=params(38),
        cost_estimate=pl.CostEstimate(flops=200 * 10**9, bytes_accessed=60 * 10**6, transcendentals=10**6),
        name="forward_and_words",
    )(*kept_outside(char_counts, char_ids, segment_ids, out_cotangent, *weights))


def call_a2(char_counts, kept, gain, project, weights):
    v = pltpu.VMEM
    return pl.pallas_call(
        kernel_a2,
        out_shape=(
            shape((CD, WORDS), LOW),
            v((SHARES, T_ROWS, 256), LOW),
            v((SHARES, T_ROWS, 256), LOW),
            shape((8, WD), F32),
        ),
        in_specs=[INSIDE] * 18,
        out_specs=(INSIDE,) * 4,
        compiler_params=params(20),
        cost_estimate=pl.CostEstimate(flops=200 * 10**9, bytes_accessed=10 * 10**6, transcendentals=10**6),
        name="word_attention_backward",
    )(char_counts, *kept, gain, project, *weights)


def call_b1(turns, gw, gain, up, down, kepts, keptm, kepti, f0, f1, first):
    v = pltpu.VMEM
    return pl.pallas_call(
        kernel_b1,
        out_shape=(v((TURNS, CD, WIDE), LOW), shape((CD, CFF), LOW), shape((8, CD), F32), v((8, F_ROWS, 256), LOW)),
        in_specs=[SCALARS] + [INSIDE] * 4 + [ANYWHERE] * 2 + [INSIDE] * 2 + [ANYWHERE] + [INSIDE] * 2,
        out_specs=(INSIDE,) * 4,
        scratch_shapes=[
            v((2, CFF, WIDE), LOW), v((2, CD, WIDE), F32), v((CD, WIDE), LOW),
            v((CD, CFF), F32), v((CD, WIDE), F32), v((CFF, CD), LOW),
            v((8, F_ROWS, 256), LOW),
            pltpu.SemaphoreType.DMA((2, 2)),
            pltpu.SemaphoreType.DMA((1,)),
        ],
        compiler_params=params(18),
        cost_estimate=pl.CostEstimate(flops=200 * 10**9, bytes_accessed=20 * 10**6, transcendentals=10**6),
        name="character_backward_one",
    )(turns, gw, gain, up, down, *kept_outside(kepts, keptm), kepti, f0, *kept_outside(f1), *first)


def call_b2(turns, wgain1, wgain2, gain2, aup, weights, keptl, first, keptd, kepti, facc, f2, t0, t1):
    v = pltpu.VMEM
    return pl.pallas_call(
        kernel_b2,
        out_shape=(
            v((SHARES, C_ROWS, 128), LOW), v((SHARES, C_ROWS, 128), LOW), v((4, F_ROWS, 256), LOW), v((4, T_ROWS, 256), LOW)
        ),
        in_specs=[SCALARS] + [INSIDE] * 9 + [ANYWHERE] + [INSIDE] * 4 + [ANYWHERE, INSIDE, ANYWHERE],
        out_specs=(INSIDE,) * 4,
        scratch_shapes=[
            v((2, KEPT_LOW, WIDE), LOW), v((CD, WIDE), LOW),
            v((CHAR_HEADS * SPAN, WIDE), LOW),
            v((CD, 3 * CD), LOW),
            v((CD, 3 * CD), F32), v((CD, CD), F32), v((CVOC, CD), F32), v((CD, WIDE), F32),
            v((4, F_ROWS, 256), LOW), v((4, T_ROWS, 256), LOW),
            pltpu.SemaphoreType.DMA((3, 2)),
            pltpu.SemaphoreType.DMA((2,)),
        ],
        compiler_params=params(24),
        cost_estimate=pl.CostEstimate(flops=200 * 10**9, bytes_accessed=40 * 10**6, transcendentals=10**6),
        name="character_backward_two",
    )(turns, wgain1, wgain2, gain2, aup, *weights, *kept_outside(keptl), first, keptd, kepti, facc, *kept_outside(f2), t0, *kept_outside(t1))


def call_add(kernel, name, outs, parts, specs, scratch):
    v = pltpu.VMEM
    return pl.pallas_call(
        kernel,
        out_shape=tuple(v(s, LOW) for s in outs),
        in_specs=specs,
        out_specs=(INSIDE,) * len(outs),
        scratch_shapes=[v(s, LOW) for s in scratch] + [pltpu.SemaphoreType.DMA((4,))],
        compiler_params=params(12),
        name=name,
    )(*parts)


def add_one(f0, f1):
    half = (8, F_ROWS, 256)
    return call_add(kernel_add_one, "add_one", (half,), (f0, *kept_outside(f1)), [INSIDE, ANYWHERE], (half,))[0]


def add_words(t0, t1):
    ts = (4, T_ROWS, 256)
    return call_add(
        kernel_add_words, "add_words", (ts, ts, ts), (t0, *kept_outside(t1)), [INSIDE, ANYWHERE], ((3,) + ts,)
    )


def add_two(facc, f2):
    fs = (4, F_ROWS, 256)
    return call_add(kernel_add_two, "add_two", (fs,), (facc, *kept_outside(f2)), [INSIDE, ANYWHERE], (fs,))[0]


def add_three(facc, f3, tacc, tgot):
    fs, ts = (2, F_ROWS, 256), (2, T_ROWS, 256)
    return call_add(
        kernel_add_three, "add_three", (fs, fs, ts, ts), (facc, *kept_outside(f3), tacc, *kept_outside(*tgot)),
        [INSIDE, ANYWHERE] * 2 + [ANYWHERE] * 2, ((4, F_ROWS, 256), (3, 4, T_ROWS, 256)),
    )


def call_f(words, c, outk, outg):
    v = pltpu.VMEM
    outs = ((CVOC, CD), (CD,), (CD, CD), (CD, CD), (CD, CD), (CD, CD), (CD,), (CD, CFF), (CFF, CD), (CD, WD),
            (WD,), (WD, WD), (WD, WD), (WD, WD), (WD, WD), (WD,), (WD, WFF), (WFF, WD))
    outs = [(s[0] // SHARES,) + tuple(n // 2 for n in s[1:]) for s in outs]
    return pl.pallas_call(
        kernel_f,
        out_shape=(shape((2, 1, WORDS, WD // 2), LOW),) + tuple(shape(s, F32) for s in outs),
        in_specs=[INSIDE] * 15,
        out_specs=(INSIDE,) * 19,
        compiler_params=params(8),
        name="finish",
    )(*words, *c, outk, outg)


def flip(value, axis, bits):
    count = lax.axis_size(axis)
    return lax.ppermute(value, axis, [(i, i ^ bits) for i in range(count)])


def flip_both(value, first, second):
    pairs = [(i, i ^ first) for i in range(SHARES)] + [(SHARES + i, SHARES + (i ^ second)) for i in range(SHARES)]
    return lax.ppermute(value, ("phase", "dp"), pairs)


def pick(value, index):
    return lax.dynamic_index_in_dim(value, index, 0, keepdims=False)


def plus(*parts):
    total = parts[0].astype(F32)
    for part in parts[1:]:
        total = total + part.astype(F32)
    return total.astype(LOW)


def across(value, side):
    return flip_both(value, *((1, 2), (2, 1), (4, 4), (8, 8))[side])


def half(bit, *parts):
    return plus(*(lax.dynamic_slice_in_dim(part, bit * (part.shape[0] // 2), part.shape[0] // 2, 0) for part in parts))


def after(value, *others):
    return lax.optimization_barrier((value,) + others)[0]


def together(*values):
    return lax.optimization_barrier(values)


def body(
    char_ids, char_counts, segment_ids, out_cotangent,
    char_table, char_gain_one, char_query, char_key, char_value, char_output, char_gain_two, char_up, char_down,
    char_project,
    word_gain_one, word_query, word_key, word_value, word_output, word_gain_two, word_up, word_down,
):
    keptl, kepts, keptm, kepti, turns, fkeep, fsend, outk, outs, wgain2, flow, fslope, fmid, *words = call_a(
        char_counts, char_ids, segment_ids, out_cotangent,
        (char_table, char_gain_one, char_query, char_key, char_value, char_output, char_gain_two, char_up, char_down,
         char_project,
         word_gain_one, word_query, word_key, word_value, word_output, word_gain_two, word_up, word_down),
    )
    fgot = flip(fsend, "phase", 1)
    outg = flip(outs, "phase", 1)
    gw, tkeep, tsend, wgain1 = call_a2(
        char_counts, words, word_gain_one, char_project, (word_query, word_key, word_value, word_output)
    )
    one = (char_gain_two, char_up, char_down, kepts, keptm, kepti)
    two = (char_gain_one, char_query, char_key, char_value, char_output)
    if lax.axis_size("dp") != SHARES:
        keptd, aup, gain2, facc = call_b1(turns, gw, *one, fkeep, fgot, (fslope, fmid))
        tgot = flip(tsend, "phase", 1)
        ckeep, csend, _, _ = call_b2(turns, wgain1, wgain2, gain2, aup, two, keptl, flow, keptd, kepti, facc, facc, tkeep, tgot)
        return general_sums(outk, outg, (fkeep, fgot), (tkeep, tgot), (ckeep, flip(csend, "phase", 1)))
    gw, tsend, fgot, outg = together(gw, tsend, fgot, outg)
    gw, fsend = together(gw, add_one(fkeep, fgot))
    f2, tgot = across(fsend, 0), flip(tsend, "phase", 1)
    keptd, aup, gain2, facc = call_b1(turns, gw, *one, fkeep, fgot, (fslope, fmid))
    keptd, tgot = together(keptd, tgot)
    tsends = add_words(tkeep, tgot)
    tparts = [flip(send, "dp", k) for k, send in enumerate(tsends, 1)]
    f2 = after(f2, *tsends)
    fsend = add_two(facc, f2)
    keptd, fsend = together(keptd, fsend)
    f3 = across(fsend, 2)
    ckeep, csend, facc, tacc = call_b2(
        turns, wgain1, wgain2, gain2, aup, two, keptl, flow, keptd, kepti, facc, f2, tkeep, tgot
    )
    ckeep, csend, facc, f3, *tparts = together(ckeep, csend, facc, f3, *tparts)
    _, _, low, high = own_bits()
    cphase = flip(csend, "phase", 1)
    fsend, facc, tsend, tacc = add_three(facc, f3, tacc, tparts)
    f4, t3 = across(fsend, 1), across(tsend, 2)
    dp = lax.axis_index("dp")
    plane, line = lax.rem(dp, 4), lax.div(dp, 4)
    c = [ckeep.reshape(4, 4, C_ROWS, 128), cphase.reshape(4, 4, C_ROWS, 128)]
    sends = [plus(*(pick(part, lax.bitwise_xor(plane, k)) for part in c)) for k in range(1, 4)]
    cgot = [flip(send, "dp", k) for k, send in enumerate(sends, 1)]
    f4, t3 = after(f4, *sends), after(t3, *sends)
    last = jnp.concatenate([pick(half(1 - high, facc, f4), 0), pick(half(1 - high, tacc, t3), 0)], axis=0)
    last = across(last, 3)
    c = [pick(part, plane) for part in c] + cgot
    sends = [plus(*(pick(part, lax.bitwise_xor(line, k)) for part in c)) for k in range(1, 4)]
    cline = [flip(send, "dp", 4 * k) for k, send in enumerate(sends, 1)]
    return call_f((facc, f4, tacc, t3, last), (ckeep, cphase, *cgot, *cline), outk, outg)


def general_sums(outk, outg, fs, ts, cs):
    phase = lax.axis_index("phase")
    first = phase == 0
    outs = jnp.stack([jnp.where(first, outk, outg), jnp.where(first, outg, outk)])[:, None]
    def order(places):
        plain, swapped = (jnp.asarray([places(d, core) for d in range(SHARES)]) for core in range(2))
        return jnp.where(first, plain, swapped)

    def natural(pair, order):
        return jnp.take(pair[0].astype(F32) + pair[1].astype(F32), order, axis=0)

    f, t, c = natural(fs, order(feed_order)), natural(ts, order(word_order)), natural(cs, jnp.asarray([plane_first(d) for d in range(SHARES)]))

    def whole(rows):
        return rows.reshape(-1, rows.shape[-1])

    def wide(rows, pieces):
        n = rows.shape[1] // pieces
        return whole(rows.reshape(SHARES, pieces, n, rows.shape[-1]).transpose(0, 2, 1, 3).reshape(SHARES, n, -1))

    cdown = t[:, T_CDOWN:T_CDOWN + 32]
    cdown = jnp.concatenate([cdown[..., :128], cdown[..., 128:]], axis=1)
    parts = (
        whole(c[:, C_TABLE:C_TABLE + 16]), c[:, C_GAIN, :16].reshape(-1),
        whole(c[:, C_Q:C_Q + 16]), whole(c[:, C_K:C_K + 16]), whole(c[:, C_V:C_V + 16]), whole(c[:, C_O:C_O + 16]),
        c[:, C_GAIN + 1, :16].reshape(-1),
        wide(c[:, C_UP:C_UP + 64], 4), whole(cdown), whole(t[:, T_PROJ:T_PROJ + 16]),
        c[:, C_GAIN + 2, :32].reshape(-1),
        whole(t[:, T_Q:T_Q + 32]), whole(t[:, T_K:T_K + 32]), whole(t[:, T_V:T_V + 32]), whole(t[:, T_O:T_O + 32]),
        c[:, C_GAIN + 3, :32].reshape(-1),
        wide(f[:, F_UP:F_UP + 128], 4), whole(f[:, F_DOWN:F_DOWN + 128]),
    )
    return (outs,) + tuple(lax.psum_scatter(p, "dp", scatter_dimension=0, tiled=True) for p in parts)


def solution(mesh):
    rows = P(None, "dp", None)
    both = P("dp", "phase")
    one = P("dp")
    return jax.shard_map(
        body,
        mesh=mesh,
        in_specs=(rows, rows, rows, P(None, "dp", None, None)) + (P(),) * 18,
        out_specs=(
            P(None, "dp", None, "phase"),
            both, one, both, both, both, both, one, both, both, both,
            one, both, both, both, both, one, both, both,
        ),
        check_vma=False,
    )
```

```python
from functools import partial

import jax
import jax.numpy as jnp
from jax import lax
from jax.experimental import pallas as pl
from jax.experimental.pallas import tpu as pltpu
from jax.sharding import PartitionSpec as P

F32 = jnp.float32
LOW = jnp.bfloat16

CD = 256
CFF = 1024
CPW = 16
CVOC = 256
CHAR_HEADS = 4
HEAD = 64
WD = 512
WFF = 2048
WORD_HEADS = 8
WORDS = 256

SCHEDULE = "aaafaaaaaaaaaafaaaaaaaaafaaaaafa"
SPAN = 256
STEP = 241
WIDE = 2 * SPAN
TURNS = ((WORDS * CPW - 1) // STEP + 2) // 2

epsilon = 1e-06
half_root = 0.7071067811865476
density = 0.3989422804014327
floor_score = -1e30
log2_e = 1.4426950408889634

R_V, R_P, R_EMB, R_Q, R_K, R_MIX = 0, 256, 1280, 1536, 1792, 2048
KEPT_FIRST = 1280
KEPT_LOW = 2304
I_INV1, I_INV2, I_IDENT, I_WORD = 0, 1, 2, 3
BAND = 144
WINDOW = 96

F_UP, F_DOWN = 0, 128
F_ROWS = 256
T_Q, T_K, T_V, T_O, T_CDOWN, T_PROJ = 0, 32, 64, 96, 128, 160
T_ROWS = 176
C_TABLE, C_Q, C_K, C_V, C_O, C_UP, C_GAIN = 0, 16, 32, 48, 64, 80, 144
C_ROWS = 160
SHARES = 16


def nn(left, right):
    return lax.dot_general(left, right, (((1,), (0,)), ((), ())), preferred_element_type=F32)


def nt(left, right):
    return lax.dot_general(left, right, (((1,), (1,)), ((), ())), preferred_element_type=F32)


def iota(shape, axis):
    return lax.broadcasted_iota(jnp.int32, shape, axis)


def eye(n):
    return iota((n, n), 0) == iota((n, n), 1)


def row_to_column(row):
    n = row.shape[1]
    return jnp.sum(jnp.where(eye(n), row, 0.0), axis=1, keepdims=True)


def gelu_pair(v):
    e = lax.erf(v * half_root)
    half = 0.5 * v
    bell = jnp.exp2(v * v * (-0.5 * log2_e))
    return half + half * e, 0.5 + 0.5 * e + (density * v) * bell


def gelu_twice(v):
    u = v * half_root
    whole = 1.0 + lax.erf(u)
    bell = jnp.exp2(u * u * (-log2_e))
    return v * whole, whole + (2.0 * density * v) * bell


def bits(d):
    return d % 2, d // 2 % 2, d // 4 % 2, d // 8


def plane_first(d, core=0):
    return (d % 4) * 4 + d // 4


def feed_order(d, core):
    x, y, low, high = bits(d)
    return (y * 8 + x * 2 if core else x * 8 + y * 2) + low * 4 + high


def word_order(d, core=0):
    _, _, low, high = bits(d)
    return (d % 4) * 4 + low * 2 + high


def own_bits():
    phase, dp = lax.axis_index("phase"), lax.axis_index("dp")
    x, y, low, high = (lax.rem(lax.div(dp, n), 2) for n in (1, 2, 4, 8))
    return jnp.where(phase == 0, x, y), jnp.where(phase == 0, y, x), low, high


def own_plane():
    return lax.rem(lax.axis_index("dp"), 4)


def add_up(out, *parts):
    for i in range(out.shape[0]):
        if len(parts) == 2:
            out[i] = parts[0][i] + parts[1][i]
            continue
        total = parts[0][i].astype(F32)
        for part in parts[1:]:
            total = total + part[i].astype(F32)
        out[i] = total.astype(LOW)


def members(word, first, count, weight=1.0):
    return jnp.where((iota((count, WIDE), 0) + first).astype(F32) == word, weight, 0.0).astype(LOW)


def word_starts(counts_row):
    earlier = iota((WORDS, WORDS), 1) < iota((WORDS, WORDS), 0)
    return jnp.sum(jnp.where(earlier, counts_row, 0.0), axis=1, keepdims=True)


def column_to_row(column):
    return jnp.sum(jnp.where(eye(column.shape[0]), column, 0.0), axis=0, keepdims=True)


def put(keep, send, phase, order, row, halves, share_rows):
    width, lanes = halves[0].shape[1], keep.shape[-1]
    first = phase == 0
    mine, other = jnp.where(first, halves[0], halves[1]), jnp.where(first, halves[1], halves[0])
    for out, low, core in ((keep, mine, phase), (send, other, 1 - phase)):
        for i in range(low.shape[0] // share_rows):
            at, swapped = order(i, 0), order(i, 1)
            if at != swapped:
                at = at + core * (swapped - at)
            rows = low[i * share_rows:(i + 1) * share_rows]
            for piece in range(max(1, width // lanes)):
                part = rows[:, piece * lanes:piece * lanes + min(width, lanes)]
                if width < lanes:
                    part = jnp.concatenate([part[:share_rows // 2], part[share_rows // 2:]], axis=1)
                m = part.shape[0]
                out[at, row + piece * share_rows:row + piece * share_rows + m, :] = part


def column_halves(value):
    width = value.shape[1] // 2
    low = value.astype(LOW)
    return low[:, :width], low[:, width:]


def band(t):
    keys = slice(0, BAND) if t % 2 == 0 else slice(SPAN - BAND, SPAN)
    return t // 2, keys, slice(t * 128, (t + 1) * 128)


def two_heads(pair):
    zero = jnp.zeros((HEAD, pair.shape[1]), LOW)
    first = jnp.concatenate([pair[:HEAD], zero], axis=0)
    second = jnp.concatenate([zero, pair[HEAD:]], axis=0)
    return jnp.concatenate([first, second], axis=1)


def two_heads_rows(pair):
    left = iota(pair.shape, 1) < HEAD
    zero = jnp.zeros(pair.shape, LOW)
    return jnp.concatenate([jnp.where(left, pair, zero), jnp.where(left, zero, pair)], axis=0)


def softmax_keys(s):
    e = jnp.exp(s - jnp.max(s, axis=0, keepdims=True))
    return (e * (1.0 / jnp.sum(e, axis=0, keepdims=True))).astype(LOW)


def kernel_a(
    counts_hbm, ids_hbm, segs_hbm, cot_hbm,
    table_hbm, g1_hbm, wq_hbm, wk_hbm, wv_hbm, wo_hbm, g2_hbm, up_hbm, down_hbm, proj_hbm,
    wg1_hbm, wwq_hbm, wwk_hbm, wwv_hbm, wwo_hbm, wg2_hbm, wup_hbm, wdown_hbm,
    keptl_hbm, kepts_hbm, keptm_hbm, kepti_hbm, turns_ref,
    keep_ref, send_ref, outk_ref, outs_ref, gain_ref,
    first_low_ref, first_slope_ref, first_mid_ref,
    q_ref, k_ref, v_ref, probs_ref, mixt_ref, normed_ref, xhat_ref, winv_ref, md_ref, pooled_ref, pa_ref,
    counts_ref, ids_ref, segs_ref,
    table_ref, g1_ref, wq_ref, wk_ref, wv_ref, wo_ref, g2_ref, up_ref, down_ref, proj_ref, wg1_ref, wg2_ref,
    cot, wwq, wwk, wwv, wwo, wup, wdown,
    tab_t, wqkv_t, wo_t, up_t, ids_t, slow, sslope, smid, sinfo, pa, pm, rowinfo, firsts_v, firsts, before_s, act_s, found_s,
    mid_s, word_s, old_s, back_s,
    csem, wsem, ksem,
):
    phase = lax.axis_index("phase")
    tiny = [
        pltpu.make_async_copy(src.at[phase], dst, csem.at[12 + i])
        for i, (src, dst) in enumerate(((counts_hbm, counts_ref), (ids_hbm, ids_ref), (segs_hbm, segs_ref)))
    ]
    for load in tiny:
        load.start()
    early = [
        pltpu.make_async_copy(src, dst, csem.at[i])
        for i, (src, dst) in enumerate(
            ((g1_hbm, g1_ref), (g2_hbm, g2_ref), (table_hbm, table_ref), (wq_hbm, wq_ref), (wk_hbm, wk_ref),
             (wv_hbm, wv_ref), (wo_hbm, wo_ref), (up_hbm, up_ref), (down_hbm, down_ref), (proj_hbm, proj_ref),
             (wg1_hbm, wg1_ref), (wg2_hbm, wg2_ref))
        )
    ]
    for load in early:
        load.start()
    loads = [
        pltpu.make_async_copy(src, dst, wsem.at[i])
        for i, (src, dst) in enumerate(
            ((wwq_hbm, wwq), (wwk_hbm, wwk), (wwv_hbm, wwv), (wwo_hbm, wwo),
             (wup_hbm, wup), (wdown_hbm, wdown), (cot_hbm.at[phase, 0], cot))
        )
    ]
    pa[...] = jnp.zeros_like(pa)
    pm[...] = jnp.zeros_like(pm)
    for slot in range(2):
        slow[slot, R_P:R_P + CHAR_HEADS * SPAN] = jnp.zeros((CHAR_HEADS * SPAN, WIDE), LOW)
    for load in tiny:
        load.wait()
    counts_row = counts_ref[...].astype(F32)
    starts = word_starts(counts_row)
    counts = row_to_column(counts_row)
    blocks = jnp.floor((starts + 0.5) * (1.0 / STEP))
    places = starts + (SPAN - STEP) * blocks
    n_turns = jnp.max(places).astype(jnp.int32) // WIDE + 1
    turns_ref[0] = n_turns
    bases = (iota((1, 128), 1) * WIDE).astype(F32)
    first = jnp.sum(jnp.where(places < bases, 1.0, 0.0), axis=0, keepdims=True)
    firsts_v[...] = jnp.broadcast_to(first, (8, 128)).astype(jnp.int32)
    first_copy = pltpu.make_async_copy(firsts_v, firsts, wsem.at[7])
    first_copy.start()
    ids = ids_ref[...]
    ids_t[...] = jnp.concatenate(
        [ids[:, 128 * a:128 * a + 128] for a in range(32)], axis=0
    ).astype(F32).T.astype(LOW)
    places_row = column_to_row(places)
    none = jnp.zeros((1, 1), F32)
    rowinfo[...] = jnp.concatenate(
        [places_row - jnp.concatenate([none, places_row[:, :-1]], axis=1),
         counts_row - jnp.concatenate([none, counts_row[:, :-1]], axis=1),
         jnp.ones((1, WORDS), F32), jnp.zeros((13, WORDS), F32)], axis=0
    ).astype(LOW)
    for load in early:
        load.wait()
    for load in loads:
        load.start()
    tab_t[...] = table_ref[...].T
    wqkv_t[0:CD] = (wq_ref[...] * 0.125).T
    wqkv_t[CD:2 * CD] = wk_ref[...].T
    wqkv_t[2 * CD:] = wv_ref[...].T
    wo_t[...] = wo_ref[...].T
    up_t[...] = up_ref[...].T
    g1 = row_to_column(g1_ref[...].astype(F32)[None, :])
    g2 = row_to_column(g2_ref[...].astype(F32)[None, :])
    first_copy.wait()

    def find(turn):
        place = (iota((1, WIDE), 1) + turn * WIDE).astype(F32)
        begun = jnp.where(places <= place, 1.0, 0.0).astype(LOW)
        info = nn(rowinfo[...], begun)
        word = info[2:3] - 1.0
        slot = place - info[0:1]
        flat = (word * 16.0 + slot).astype(jnp.int32)
        chosen = jnp.where(iota((32, WIDE), 0) == (flat >> 7), 1.0, 0.0).astype(LOW)
        lanes = nn(ids_t[...], chosen)
        ident = jnp.sum(jnp.where(iota((128, WIDE), 0) == (flat & 127), lanes, 0.0), axis=0, keepdims=True)
        valid = slot < info[1:2]
        none = jnp.full((6, WIDE), -1.0, F32)
        return jnp.concatenate([jnp.where(valid, ident, -1.0), jnp.where(valid, word, -1.0), none], axis=0)

    found_s[...] = find(jnp.int32(0))

    def copies_one(b):
        slot = lax.rem(b, 2)
        return (
            pltpu.make_async_copy(slow.at[slot], keptl_hbm.at[b], ksem.at[0, slot]),
            pltpu.make_async_copy(smid.at[slot], keptm_hbm.at[b], ksem.at[2, slot]),
            pltpu.make_async_copy(sinfo.at[slot], kepti_hbm.at[b], ksem.at[3, slot]),
        )

    def copies_two(b):
        slot = lax.rem(b, 2)
        return (pltpu.make_async_copy(sslope.at[slot], kepts_hbm.at[b], ksem.at[1, slot]),)

    def start(copies):
        for c in copies:
            c.start()

    def wait(copies):
        for c in copies:
            c.wait()

    def near_words(b):
        first = (firsts[0, b] // 16) * 16
        return first, (firsts[0, b + 1] - first + WINDOW - 1) // WINDOW

    def window(first):
        return pl.ds(pl.multiple_of(first, 16), WINDOW)

    def attend(b):
        slot = lax.rem(b, 2)
        ident = found_s[0:1]
        word = found_s[1:2]
        hot = jnp.where(iota((CVOC, WIDE), 0).astype(F32) == ident, 1.0, 0.0).astype(LOW)
        emb = nn(tab_t[...], hot)
        inv1 = lax.rsqrt(jnp.mean(emb * emb, axis=0, keepdims=True) + epsilon)
        normed = (emb * inv1 * g1).astype(LOW)
        yield
        qkv = []
        for i in range(3):
            qkv.append(nn(wqkv_t[i * CD:(i + 1) * CD], normed).astype(LOW))
            yield
        query_t, key_t, value_t = qkv
        slow[slot, R_EMB:R_EMB + CD] = emb.astype(LOW)
        slow[slot, R_Q:R_Q + CD] = query_t
        slow[slot, R_K:R_K + CD] = key_t
        key_rows = [key_t[:, u * SPAN:(u + 1) * SPAN].T for u in range(2)]
        word_col = jnp.broadcast_to(jnp.where(word < 0.0, -2.0, word), (8, WIDE)).T[:, 0:1]
        yield
        scores = []
        for t in range(4):
            u, ks, ql = band(t)
            for pair in range(CHAR_HEADS // 2):
                fs = slice(pair * 128, pair * 128 + 128)
                scores.append(nn(key_rows[u][ks, fs], two_heads(query_t[fs, ql])))
                yield
        for u in range(2):
            us = slice(u * SPAN, (u + 1) * SPAN)
            slow[slot, R_V:R_V + SPAN, us] = value_t[:, us].T
        for t in range(4):
            u, ks, ql = band(t)
            bias = jnp.where(word_col[u * SPAN + ks.start:u * SPAN + ks.stop] == word[:, ql], 0.0, floor_score)
            for pair in range(CHAR_HEADS // 2):
                s = scores[t * 2 + pair]
                for i in range(2):
                    p = softmax_keys(s[:, i * 128:i * 128 + 128] + bias)
                    row = (pair * 2 + i) * SPAN
                    slow[slot, R_P + row + ks.start:R_P + row + ks.stop, ql] = p
        yield
        mixed = [[], []]
        for u in range(2):
            us = slice(u * SPAN, (u + 1) * SPAN)
            for h in range(CHAR_HEADS):
                hs = slice(h * HEAD, (h + 1) * HEAD)
                mixed[u].append(nn(value_t[hs, us], slow[slot, R_P + h * SPAN:R_P + (h + 1) * SPAN, us]).astype(LOW))
                yield
        mixed = jnp.concatenate([jnp.concatenate(part, axis=0) for part in mixed], axis=1)
        slow[slot, R_MIX:R_MIX + CD] = mixed
        middle = emb + nn(wo_t[...], mixed)
        yield
        inv2 = lax.rsqrt(jnp.mean(middle * middle, axis=0, keepdims=True) + epsilon)
        smid[slot] = middle
        sinfo[slot] = jnp.concatenate([inv1, inv2, ident, word, jnp.zeros((4, WIDE), F32)], axis=0)
        normed_two = (middle * inv2 * g2).astype(LOW)
        middle_low = middle.astype(LOW)
        yield
        for c in range(CFF // 256):
            cs = slice(c * 256, (c + 1) * 256)
            before_s[cs] = nn(up_t[cs], normed_two)
            if c == 0:
                found_s[...] = find(b + 1)
            if c == 1:
                first, _ = near_words(b)
                pm[window(first), :] += nt(members(word, first, WINDOW), middle_low)
                mid_s[...] = middle_low
            if c == 3:
                old_s[0:1] = word_s[0:1]
                word_s[0:1] = word
            yield

    def feed(b):
        slot = lax.rem(b, 2)
        first, _ = near_words(b)
        near = members(word_s[0:1], first, WINDOW, 0.5)
        for c in range(CFF // 256):
            for d in range(8):
                cs = slice(c * 256 + d * 32, c * 256 + (d + 1) * 32)
                act, slope = gelu_twice(before_s[cs])
                sslope[slot, cs] = slope.astype(LOW)
                act_s[cs] = act.astype(LOW)
            cs = slice(c * 256, (c + 1) * 256)
            pa[window(first), cs] += nt(near, act_s[cs])
            yield

    def run(order, one, two):
        parts = {"a": one, "f": two}
        for step in order:
            next(parts[step])

    def more_one(b):
        first, windows = near_words(b)

        def more(i, carry):
            at = first + i * WINDOW
            pm[window(at), :] += nt(members(word_s[0:1], at, WINDOW), mid_s[...])
            return carry

        lax.fori_loop(1, windows, more, 0)

    def more_two(b, word):
        first, windows = near_words(b)

        def more(i, carry):
            at = first + i * WINDOW
            pa[window(at), :] += nt(members(word[0:1], at, WINDOW, 0.5), act_s[...])
            return carry

        lax.fori_loop(1, windows, more, 0)

    run("a" * 28, attend(jnp.int32(0)), None)
    more_one(jnp.int32(0))
    start(copies_one(jnp.int32(0)))
    first_low_ref[...] = slow[0]
    first_mid_ref[...] = smid[0]

    def turn(b, carry):
        @pl.when(b >= 2)
        def _():
            wait(copies_one(b - 2))

        @pl.when(b >= 3)
        def _():
            wait(copies_two(b - 3))

        run(SCHEDULE, attend(b), feed(b - 1))
        more_one(b)
        more_two(b - 1, old_s)

        @pl.when(b == 1)
        def _():
            first_slope_ref[...] = sslope[0]

        start(copies_one(b))
        start(copies_two(b - 1))
        return carry

    lax.fori_loop(1, n_turns, turn, 0)

    @pl.when(n_turns >= 3)
    def _():
        wait(copies_two(n_turns - 3))

    for load in loads:
        load.wait()
    cot_low = cot[...]
    last = feed(n_turns - 1)
    for c in range(4):
        cs = slice(c * 512, (c + 1) * 512)
        back_s[:, cs] = nt(cot_low, wdown[cs, :])
        next(last)
    more_two(n_turns - 1, word_s)

    @pl.when(n_turns == 1)
    def _():
        first_slope_ref[...] = sslope[0]

    start(copies_two(n_turns - 1))

    pa_hi = pa[0:WORDS].astype(LOW)
    per_count = 1.0 / counts
    pooled = (pm[0:WORDS] + nn(pa_hi, down_ref[...])) * per_count
    pooled_low = pooled.astype(LOW)
    pooled_ref[...] = pooled_low
    pa_ref[...] = pa_hi
    x = nn(pooled_low, proj_ref[...]).astype(LOW).astype(F32)
    wg1 = wg1_ref[...].astype(F32)[None, :]
    wg2 = wg2_ref[...].astype(F32)[None, :]
    winv1 = lax.rsqrt(jnp.mean(x * x, axis=1, keepdims=True) + epsilon)
    xhat = x * winv1
    normed = (xhat * wg1).astype(LOW)
    xhat_ref[...] = xhat
    winv_ref[...] = jnp.broadcast_to(winv1, (WORDS, 128))
    normed_ref[...] = normed
    q = (nn(normed, wwq[...]) * 0.125).astype(LOW)
    k = nn(normed, wwk[...]).astype(LOW)
    v = nn(normed, wwv[...]).astype(LOW)
    seg_row = segs_ref[...].astype(F32)
    seg_col = row_to_column(seg_row)
    allowed = (seg_row == seg_col) & (iota((WORDS, WORDS), 0) <= iota((WORDS, WORDS), 1))
    bias = jnp.where(allowed, 0.0, floor_score)
    q_ref[...] = q
    k_ref[...] = k
    v_ref[...] = v
    v_t = v.T
    for h in range(WORD_HEADS):
        probs_ref[h, 128:, 0:128] = jnp.zeros((128, 128), LOW)
    halves = [(slice(0, 128 * (t + 1)), slice(128 * t, 128 * (t + 1))) for t in range(2)]
    pairs = [slice(pair * 128, pair * 128 + 128) for pair in range(WORD_HEADS // 2)]
    scores = [[nt(k[ks, fs], two_heads_rows(q[ql, fs])) for ks, ql in halves] for fs in pairs]
    mixed_t = []
    for pair in range(WORD_HEADS // 2):
        for (ks, ql), s in zip(halves, scores[pair]):
            for i in range(2):
                probs_ref[pair * 2 + i, ks, ql] = softmax_keys(s[:, i * 128:i * 128 + 128] + bias[ks, ql])
        for h in (pair * 2, pair * 2 + 1):
            mixed_t.append(nn(v_t[h * HEAD:(h + 1) * HEAD], probs_ref[h]).astype(LOW))
    mixed_t = jnp.concatenate(mixed_t, axis=0)
    mixt_ref[...] = mixed_t
    middle = x + nn(mixed_t.T, wwo[...])
    winv2 = lax.rsqrt(jnp.mean(middle * middle, axis=1, keepdims=True) + epsilon)
    normed_two = (middle * winv2 * wg2).astype(LOW)
    result = middle
    n2d = jnp.zeros((WORDS, WD), F32)
    n2_t = normed_two.T
    held = {}
    turns = (0, 2, 1, 3)
    quarter = [slice(c * 512, (c + 1) * 512) for c in range(4)]
    act, slope = gelu_pair(nn(normed_two, wup[:, quarter[0]]))
    for i, c in enumerate(turns):
        cs = quarter[c]
        act = act.astype(LOW)
        bd = (back_s[:, cs] * slope).astype(LOW)
        if i < 3:
            ahead = nn(normed_two, wup[:, quarter[turns[i + 1]]])
        result = result + nn(act, wdown[cs, :])
        gd = nn(act.T, cot_low)
        gu = nn(n2_t, bd).astype(LOW)
        n2d = n2d + nt(bd, wup[:, cs])
        if i < 3:
            act, slope = gelu_pair(ahead)
        put(keep_ref, send_ref, phase, lambda i, p: feed_order(c * 4 + i, p), F_DOWN, column_halves(gd), 128)
        if c < 2:
            held[c] = gu
        else:
            put(keep_ref, send_ref, phase, feed_order, F_UP + (c - 2) * 64, (held[c - 2], gu), 32)
    result = result.astype(LOW)
    front = phase == 0
    outk_ref[...] = jnp.where(front, result[:, :256], result[:, 256:])
    outs_ref[...] = jnp.where(front, result[:, 256:], result[:, :256])
    vhat = middle * winv2
    gain_ref[...] = jnp.broadcast_to(jnp.sum(n2d * vhat, axis=0, keepdims=True), (8, WD))
    lifted = n2d * wg2
    md_ref[...] = cot[...].astype(F32) + winv2 * (lifted - vhat * jnp.mean(lifted * vhat, axis=1, keepdims=True))

    def drain(b, carry):
        wait(copies_one(b))
        wait(copies_two(b))
        return carry

    lax.fori_loop(jnp.maximum(n_turns - 2, 0), n_turns, drain, 0)


def kernel_a2(
    counts_ref, q_ref, k_ref, v_ref, pw, mixt_ref, normed_ref, xhat_ref, winv_ref, md_ref, pooled_ref, pa_ref,
    wg1_ref, proj_ref, wwq, wwk, wwv, wwo,
    gw_ref, keep_ref, send_ref, gain_ref,
):
    phase = lax.axis_index("phase")
    wg1 = wg1_ref[...].astype(F32)[None, :]
    q, k, v, normed, pooled_low = q_ref[...], k_ref[...], v_ref[...], normed_ref[...], pooled_ref[...]
    per_count = 1.0 / row_to_column(counts_ref[phase].astype(F32))
    md = md_ref[...]
    md_low = md.astype(LOW)
    put(keep_ref, send_ref, phase, word_order, T_O, column_halves(nn(mixt_ref[...], md_low)), 32)
    k_t = k.T
    do = nt(md_low, wwo[...]).astype(LOW)
    dq_t, dk, dv = [], [], []
    left = iota((WORDS, 128), 1) < HEAD
    pairs = [slice(pair * 128, pair * 128 + 128) for pair in range(WORD_HEADS // 2)]
    halves = [(slice(0, 128 * (t + 1)), slice(128 * t, 128 * (t + 1))) for t in range(2)]
    deltas = [[nt(v[ks, fs], two_heads_rows(do[ql, fs])) for ks, ql in halves] for fs in pairs]

    def scores(pair):
        ds = []
        for (ks, ql), dp in zip(halves, deltas[pair]):
            for i in range(2):
                pf = pw[pair * 2 + i, ks, ql].astype(F32)
                dph = dp[:, i * 128:i * 128 + 128]
                d = (pf * (dph - jnp.sum(pf * dph, axis=0, keepdims=True))).astype(LOW)
                ds.append(d if ks.stop == WORDS else jnp.concatenate([d, jnp.zeros((128, 128), LOW)], axis=0))
        return [jnp.concatenate([ds[i], ds[i + 2]], axis=1) for i in range(2)]

    both = None
    for pair in range(WORD_HEADS // 2 + 1):
        ahead = scores(pair) if pair < WORD_HEADS // 2 else None
        if ahead is not None:
            fs = pairs[pair]
            dv.append(jnp.where(left, nn(pw[pair * 2], do[:, fs]), nn(pw[pair * 2 + 1], do[:, fs])).astype(LOW))
        if both is not None:
            fs = pairs[pair - 1]
            for i in range(2):
                h = (pair - 1) * 2 + i
                dq_t.append(nn(k_t[h * HEAD:(h + 1) * HEAD], both[i]))
            dk.append(jnp.where(left, nn(both[0], q[:, fs]), nn(both[1], q[:, fs])).astype(LOW))
        both = ahead
    dq = (jnp.concatenate(dq_t, axis=0) * 0.125).astype(LOW).T
    dk = jnp.concatenate(dk, axis=1)
    dv = jnp.concatenate(dv, axis=1)
    normed_t = normed.T
    nd = nt(dq, wwq[...]) + nt(dk, wwk[...]) + nt(dv, wwv[...])
    put(keep_ref, send_ref, phase, word_order, T_Q, column_halves(nn(normed_t, dq)), 32)
    put(keep_ref, send_ref, phase, word_order, T_K, column_halves(nn(normed_t, dk)), 32)
    put(keep_ref, send_ref, phase, word_order, T_V, column_halves(nn(normed_t, dv)), 32)
    vhat = xhat_ref[...]
    gain_ref[...] = jnp.broadcast_to(jnp.sum(nd * vhat, axis=0, keepdims=True), (8, WD))
    lifted = nd * wg1
    xd = md + winv_ref[:, 0:1] * (lifted - vhat * jnp.mean(lifted * vhat, axis=1, keepdims=True))
    vd = xd.astype(LOW)
    put(keep_ref, send_ref, phase, word_order, T_PROJ, column_halves(nn(pooled_low.T, vd)), 16)
    gw = (nt(vd, proj_ref[...]) * per_count).astype(LOW)
    gw_ref[...] = gw.T
    put(keep_ref, send_ref, phase, word_order, T_CDOWN, column_halves(nn(pa_ref[...].T, gw)), 64)


def kernel_b1(
    turns_ref, gw_ref, g2_ref, up_ref, down_ref, kepts_hbm, keptm_hbm, info_ref, f0_ref, f1_hbm, first_slope_ref, first_mid_ref,
    delta_ref, aup_ref, gain_ref, facc_ref,
    sslope, smid, given, aup, ag2, down, f1, ksem, fsem,
):
    n_turns = turns_ref[0]

    def kept_copies(b, slot):
        return (
            pltpu.make_async_copy(kepts_hbm.at[b], sslope.at[slot], ksem.at[0, slot]),
            pltpu.make_async_copy(keptm_hbm.at[b], smid.at[slot], ksem.at[1, slot]),
        )

    sslope[0] = first_slope_ref[...]
    smid[0] = first_mid_ref[...]
    a, _, _, _ = own_bits()
    load = pltpu.make_async_copy(f1_hbm.at[pl.ds(a * 8, 8)], f1, fsem.at[0])
    load.start()
    g2 = row_to_column(g2_ref[...].astype(F32)[None, :])
    down[...] = down_ref[...] * 0.5
    aup[...] = jnp.zeros_like(aup)
    ag2[...] = jnp.zeros_like(ag2)

    def give(b):
        given[...] = nn(gw_ref[...], members(info_ref[b, I_WORD:I_WORD + 1], 0, WORDS)).astype(LOW)

    give(0)

    def turn(b, carry):
        slot = lax.rem(b, 2)

        @pl.when(b + 1 < n_turns)
        def _():
            for c in kept_copies(b + 1, 1 - slot):
                c.start()

        @pl.when(b > 0)
        def _():
            for c in kept_copies(b, slot):
                c.wait()

        cuts = [slice(c * 256, (c + 1) * 256) for c in range(CFF // 256)]
        inv2 = info_ref[b, I_INV2:I_INV2 + 1]
        g_low = given[...]
        vhat = smid[slot] * inv2
        normed_two = (vhat * g2).astype(LOW)
        n2d = jnp.zeros((CD, WIDE), F32)
        ahead = nn(down[cuts[0], :], g_low)
        bds = []
        for c, cs in enumerate(cuts):
            bds.append((ahead * sslope[slot, cs].astype(F32)).astype(LOW))
            if c + 1 < len(cuts):
                ahead = nn(down[cuts[c + 1], :], g_low)
            n2d = n2d + nn(up_ref[:, cs], bds[c])
        aup[:, cuts[0]] += nt(normed_two, bds[0])
        ag2[...] += n2d * vhat
        lifted = n2d * g2
        aup[:, cuts[1]] += nt(normed_two, bds[1])
        mean = jnp.mean(lifted * vhat, axis=0, keepdims=True)
        aup[:, cuts[2]] += nt(normed_two, bds[2])
        md = g_low.astype(F32) + inv2 * (lifted - vhat * mean)
        delta_ref[b] = md.astype(LOW)
        aup[:, cuts[3]] += nt(normed_two, bds[3])
        give(jnp.minimum(b + 1, TURNS - 1))
        return carry

    lax.fori_loop(0, n_turns, turn, 0)
    aup_ref[...] = aup[...].astype(LOW)
    load.wait()
    add_up(facc_ref, f0_ref.at[pl.ds(a * 8, 8)], f1)
    gain_ref[...] = jnp.broadcast_to(jnp.sum(ag2[...], axis=1, keepdims=True), (CD, 8)).T


def kernel_b2(
    turns_ref, wgain1_ref, wgain2_ref, gain2_ref, aup_ref, g1_ref, wq_ref, wk_ref, wv_ref, wo_ref,
    keptl_hbm, first_low_ref, delta_ref, info_ref, facc_ref, f2_hbm, t0_ref, t1_hbm,
    keep_ref, send_ref, fnext_ref, tacc_ref,
    slow, up_next, dscore, wqkv, aqkv, ao, atab, ag1, f2, t1, ksem, fsem,
):
    phase = lax.axis_index("phase")
    n_turns = turns_ref[0]

    def kept_copies(b, slot):
        return [
            pltpu.make_async_copy(keptl_hbm.at[b, rows], slow.at[slot, rows], ksem.at[i, slot])
            for i, rows in enumerate((pl.ds(0, KEPT_FIRST), pl.ds(KEPT_FIRST, KEPT_LOW - KEPT_FIRST)))
        ]

    slow[0] = first_low_ref[...]
    _, _, low, _ = own_bits()
    quarter = pl.ds(own_plane() * 4, 4)
    loads = [
        pltpu.make_async_copy(src.at[at], dst, fsem.at[i])
        for i, (src, at, dst) in enumerate(((f2_hbm, pl.ds(low * 4, 4), f2), (t1_hbm, quarter, t1)))
    ]
    for load in loads:
        load.start()
    g1 = row_to_column(g1_ref[...].astype(F32)[None, :])
    for i, w in enumerate((wq_ref, wk_ref, wv_ref)):
        wqkv[:, i * CD:(i + 1) * CD] = w[...]
    for acc in (aqkv, ao, atab, ag1, dscore):
        acc[...] = jnp.zeros_like(acc)

    def step(b):
        up_next[...] = nn(wo_ref[...], delta_ref[b]).astype(LOW)

    step(0)

    def turn(b, carry):
        slot = lax.rem(b, 2)

        @pl.when(b + 1 < n_turns)
        def _():
            for c in kept_copies(b + 1, 1 - slot):
                c.start()

        @pl.when(b > 0)
        def _():
            for c in kept_copies(b, slot):
                c.wait()

        do = up_next[...]
        deltas = []
        for t in range(4):
            u, ks, ql = band(t)
            for pair in range(CHAR_HEADS // 2):
                fs = slice(u * SPAN + pair * 128, u * SPAN + pair * 128 + 128)
                deltas.append(nn(
                    slow[slot, R_V + ks.start:R_V + ks.stop, fs], two_heads(do[pair * 128:pair * 128 + 128, ql])
                ))
        dq, dk, dv = ([[None, None] for _ in range(CHAR_HEADS)] for _ in range(3))
        for t in range(4):
            u, ks, ql = band(t)
            for pair in range(CHAR_HEADS // 2):
                dp = deltas[t * 2 + pair]
                for i in range(2):
                    row = (pair * 2 + i) * SPAN
                    pf = slow[slot, R_P + row + ks.start:R_P + row + ks.stop, ql].astype(F32)
                    dph = dp[:, i * 128:i * 128 + 128]
                    d = pf * (dph - jnp.sum(pf * dph, axis=0, keepdims=True))
                    dscore[row + ks.start:row + ks.stop, ql] = d.astype(LOW)
                h, v = (t % 2) * 2 + pair, t // 2
                vs = slice(v * SPAN, (v + 1) * SPAN)
                dv[h][v] = nt(do[h * HEAD:(h + 1) * HEAD, vs], slow[slot, R_P + h * SPAN:R_P + (h + 1) * SPAN, vs]).astype(LOW)
        inv1 = info_ref[b, I_INV1:I_INV1 + 1]
        ident = info_ref[b, I_IDENT:I_IDENT + 1]
        md_low = delta_ref[b]
        emb = slow[slot, R_EMB:R_EMB + CD].astype(F32)
        ehat = emb * inv1
        normed = (ehat * g1).astype(LOW)
        hot = jnp.where(iota((CVOC, WIDE), 0).astype(F32) == ident, 1.0, 0.0).astype(LOW)
        for h in range(CHAR_HEADS):
            for u in range(2):
                us = slice(u * SPAN, (u + 1) * SPAN)
                ds = dscore[h * SPAN:(h + 1) * SPAN, us]
                dq[h][u] = (nn(slow[slot, R_K + h * HEAD:R_K + (h + 1) * HEAD, us], ds) * 0.125).astype(LOW)
                dk[h][u] = nt(slow[slot, R_Q + h * HEAD:R_Q + (h + 1) * HEAD, us], ds).astype(LOW)
        dqkv = jnp.concatenate([jnp.concatenate(pair, axis=1) for part in (dq, dk, dv) for pair in part], axis=0)
        nd = nn(wqkv[...], dqkv)
        aqkv[:, 0:CD] += nt(normed, dqkv[0:CD])
        ag1[...] += nd * ehat
        lifted = nd * g1
        aqkv[:, CD:2 * CD] += nt(normed, dqkv[CD:2 * CD])
        mean = jnp.mean(lifted * ehat, axis=0, keepdims=True)
        aqkv[:, 2 * CD:] += nt(normed, dqkv[2 * CD:])
        ed = md_low.astype(F32) + inv1 * (lifted - ehat * mean)
        step(jnp.minimum(b + 1, TURNS - 1))
        ao[...] += nt(slow[slot, R_MIX:R_MIX + CD], md_low)
        atab[...] += nt(hot, ed.astype(LOW))
        return carry

    lax.fori_loop(0, n_turns, turn, 0)

    for load in loads:
        load.wait()
    add_up(fnext_ref, facc_ref.at[pl.ds(low * 4, 4)], f2)
    add_up(tacc_ref, t0_ref.at[quarter], t1)
    put(keep_ref, send_ref, phase, plane_first, C_TABLE, column_halves(atab[...]), 16)
    put(keep_ref, send_ref, phase, plane_first, C_Q, column_halves(aqkv[:, 0:CD]), 16)
    put(keep_ref, send_ref, phase, plane_first, C_K, column_halves(aqkv[:, CD:2 * CD]), 16)
    put(keep_ref, send_ref, phase, plane_first, C_V, column_halves(aqkv[:, 2 * CD:]), 16)
    put(keep_ref, send_ref, phase, plane_first, C_O, column_halves(ao[...]), 16)
    put(keep_ref, send_ref, phase, plane_first, C_UP, column_halves(aup_ref[...]), 16)
    cg1 = jnp.broadcast_to(jnp.sum(ag1[...], axis=1, keepdims=True), (CD, 8)).T[0:1]
    cg2 = gain2_ref[0:1]
    for d in range(SHARES):
        rows = [
            jnp.concatenate([cg1[:, d * 16:d * 16 + 16], jnp.zeros((1, 112), F32)], axis=1),
            jnp.concatenate([cg2[:, d * 16:d * 16 + 16], jnp.zeros((1, 112), F32)], axis=1),
            jnp.concatenate([wgain1_ref[0:1, d * 32:d * 32 + 32], jnp.zeros((1, 96), F32)], axis=1),
            jnp.concatenate([wgain2_ref[0:1, d * 32:d * 32 + 32], jnp.zeros((1, 96), F32)], axis=1),
            jnp.zeros((12, 128), F32),
        ]
        tile = jnp.concatenate(rows, axis=0).astype(LOW)
        keep_ref[plane_first(d), C_GAIN:C_GAIN + 16, :] = tile
        send_ref[plane_first(d), C_GAIN:C_GAIN + 16, :] = tile


def kernel_add_one(f0_ref, f1_hbm, send_ref, f1, sem):
    a, _, _, _ = own_bits()
    loads = [
        pltpu.make_async_copy(f1_hbm.at[pl.ds((1 - a) * 8 + i, 2)], f1.at[pl.ds(i, 2)], sem.at[i // 2]) for i in range(0, 8, 2)
    ]
    for load in loads:
        load.start()
    for i, load in enumerate(loads):
        load.wait()
        at = pl.ds(i * 2, 2)
        add_up(send_ref.at[at], f0_ref.at[pl.ds((1 - a) * 8 + i * 2, 2)], f1.at[at])


def kernel_add_words(t0_ref, t1_hbm, ts1_ref, ts2_ref, ts3_ref, t1, sem):
    places = [pl.ds(lax.bitwise_xor(own_plane(), k) * 4, 4) for k in range(1, 4)]
    loads = [pltpu.make_async_copy(t1_hbm.at[at], t1.at[k], sem.at[k]) for k, at in enumerate(places)]
    for load in loads:
        load.start()
    for k, out in enumerate((ts1_ref, ts2_ref, ts3_ref)):
        loads[k].wait()
        add_up(out, t0_ref.at[places[k]], t1.at[k])


def kernel_add_two(facc_ref, f2_hbm, fsend_ref, f2, sem):
    _, _, low, _ = own_bits()
    half = pl.ds((1 - low) * 4, 4)
    load = pltpu.make_async_copy(f2_hbm.at[half], f2, sem.at[0])
    load.start()
    load.wait()
    add_up(fsend_ref, facc_ref.at[half], f2)


def kernel_add_three(
    facc_ref, f3_hbm, tacc_ref, tg1_hbm, tg2_hbm, tg3_hbm, fsend_ref, fkeep_ref, tsend_ref, tkeep_ref, f3, tg, sem
):
    _, b, low, _ = own_bits()
    loads = [pltpu.make_async_copy(src, tg.at[i], sem.at[0]) for i, src in enumerate((tg1_hbm, tg2_hbm, tg3_hbm))]
    loads.append(pltpu.make_async_copy(f3_hbm, f3, sem.at[1]))
    for load in loads:
        load.start()
    for load in loads[:3]:
        load.wait()
    for out, bit in ((tsend_ref, 1 - low), (tkeep_ref, low)):
        at = pl.ds(bit * 2, 2)
        add_up(out, tacc_ref.at[at], *(tg.at[k, at] for k in range(3)))
    loads[3].wait()
    for out, bit in ((fsend_ref, 1 - b), (fkeep_ref, b)):
        add_up(out, facc_ref.at[pl.ds(bit * 2, 2)], f3.at[pl.ds(bit * 2, 2)])


def kernel_f(
    f3, f4, t2, t3, last, c0, c1, c2, c3, c4, c5, c6, c7, outk, outg,
    word_out, d_table, d_g1, d_q, d_k, d_v, d_o, d_g2, d_up, d_down, d_proj,
    e_g1, e_q, e_k, e_v, e_o, e_g2, e_up, e_down,
):
    phase = lax.axis_index("phase")
    dp = lax.axis_index("dp")
    _, _, low, high = own_bits()
    line = lax.div(dp, 4)
    place = lax.rem(dp, 4) * 4 + line
    fs = ((f3, high), (f4, high), (last, 0))
    ts = ((t2, high), (t3, high), (last, F_ROWS))
    cs = ((c0, place), (c1, place), (c2, line), (c3, line), (c4, line), (c5, None), (c6, None), (c7, None))
    word_out[phase, 0] = outk[...]
    word_out[1 - phase, 0] = outg[...]

    def total(parts, row, n):
        t = None
        for part, at in parts:
            if part is last:
                piece = part[at + row:at + row + n]
            else:
                piece = part[row:row + n] if at is None else part[at, row:row + n]
            t = piece.astype(F32) if t is None else t + piece.astype(F32)
        return t

    f, t, c = partial(total, fs), partial(total, ts), partial(total, cs)
    d_table[...] = c(C_TABLE, 16)
    d_q[...] = c(C_Q, 16)
    d_k[...] = c(C_K, 16)
    d_v[...] = c(C_V, 16)
    d_o[...] = c(C_O, 16)
    for i in range(4):
        d_up[:, i * 128:(i + 1) * 128] = c(C_UP + i * 16, 16)
        e_up[:, i * 256:(i + 1) * 256] = f(F_UP + i * 32, 32)
    gains = c(C_GAIN, 16)
    d_g1[...] = gains[0, :16]
    d_g2[...] = gains[1, :16]
    e_g1[...] = gains[2, :32]
    e_g2[...] = gains[3, :32]
    cd = t(T_CDOWN, 32)
    d_down[0:32] = cd[:, :128]
    d_down[32:64] = cd[:, 128:]
    d_proj[...] = t(T_PROJ, 16)
    e_q[...] = t(T_Q, 32)
    e_k[...] = t(T_K, 32)
    e_v[...] = t(T_V, 32)
    e_o[...] = t(T_O, 32)
    e_down[...] = f(F_DOWN, 128)


ANYWHERE = pl.BlockSpec(memory_space=pltpu.HBM)
INSIDE = pl.BlockSpec(memory_space=pltpu.VMEM)
SCALARS = pl.BlockSpec(memory_space=pltpu.SMEM)
shape = jax.ShapeDtypeStruct


def params(mib):
    return pltpu.CompilerParams(vmem_limit_bytes=mib * 2**20)


def outside(dims, dtype):
    return pltpu.HBM(dims, dtype)


def kept_outside(*values):
    return tuple(pltpu.with_memory_space_constraint(v, pltpu.HBM) for v in values)


def call_a(char_counts, char_ids, segment_ids, out_cotangent, weights):
    v = pltpu.VMEM
    return pl.pallas_call(
        kernel_a,
        out_shape=(
            outside((TURNS, KEPT_LOW, WIDE), LOW),
            outside((TURNS, CFF, WIDE), LOW),
            outside((TURNS, CD, WIDE), F32),
            outside((TURNS, 8, WIDE), F32),
            shape((1,), jnp.int32),
            v((SHARES, F_ROWS, 256), LOW),
            v((SHARES, F_ROWS, 256), LOW),
            shape((WORDS, WD // 2), LOW),
            shape((WORDS, WD // 2), LOW),
            shape((8, WD), F32),
            v((KEPT_LOW, WIDE), LOW), v((CFF, WIDE), LOW), v((CD, WIDE), F32),
            shape((WORDS, WD), LOW), shape((WORDS, WD), LOW), shape((WORDS, WD), LOW),
            shape((WORD_HEADS, WORDS, WORDS), LOW), shape((WD, WORDS), LOW), shape((WORDS, WD), LOW),
            shape((WORDS, WD), F32), shape((WORDS, 128), F32), shape((WORDS, WD), F32),
            shape((WORDS, CD), LOW), shape((WORDS, CFF), LOW),
        ),
        in_specs=[ANYWHERE] * 22,
        out_specs=(ANYWHERE,) * 4 + (SCALARS,) + (INSIDE,) * 19,
        scratch_shapes=[
            v((1, WORDS), jnp.int32), v((1, WORDS * CPW), jnp.int32), v((1, WORDS), jnp.int32),
            v((CVOC, CD), LOW), v((CD,), LOW), v((CD, CD), LOW), v((CD, CD), LOW), v((CD, CD), LOW), v((CD, CD), LOW),
            v((CD,), LOW), v((CD, CFF), LOW), v((CFF, CD), LOW), v((CD, WD), LOW), v((WD,), LOW), v((WD,), LOW),
            v((WORDS, WD), LOW),
            v((WD, WD), LOW), v((WD, WD), LOW), v((WD, WD), LOW), v((WD, WD), LOW),
            v((WD, WFF), LOW), v((WFF, WD), LOW),
            v((CD, CVOC), LOW), v((3 * CD, CD), LOW), v((CD, CD), LOW), v((CFF, CD), LOW), v((128, 32), LOW),
            v((2, KEPT_LOW, WIDE), LOW), v((2, CFF, WIDE), LOW), v((2, CD, WIDE), F32), v((2, 8, WIDE), F32),
            v((WORDS + WINDOW, CFF), F32), v((WORDS + WINDOW, CD), F32), v((16, WORDS), LOW),
            v((8, 128), jnp.int32), pltpu.SMEM((8, 128), jnp.int32),
            v((CFF, WIDE), F32), v((CFF, WIDE), LOW), v((8, WIDE), F32),
            v((CD, WIDE), LOW), v((8, WIDE), F32), v((8, WIDE), F32), v((WORDS, WFF), F32),
            pltpu.SemaphoreType.DMA((15,)),
            pltpu.SemaphoreType.DMA((8,)),
            pltpu.SemaphoreType.DMA((4, 2)),
        ],
        compiler_params=params(38),
        cost_estimate=pl.CostEstimate(flops=200 * 10**9, bytes_accessed=60 * 10**6, transcendentals=10**6),
        name="forward_and_words",
    )(*kept_outside(char_counts, char_ids, segment_ids, out_cotangent, *weights))


def call_a2(char_counts, kept, gain, project, weights):
    v = pltpu.VMEM
    return pl.pallas_call(
        kernel_a2,
        out_shape=(
            shape((CD, WORDS), LOW),
            v((SHARES, T_ROWS, 256), LOW),
            v((SHARES, T_ROWS, 256), LOW),
            shape((8, WD), F32),
        ),
        in_specs=[INSIDE] * 18,
        out_specs=(INSIDE,) * 4,
        compiler_params=params(20),
        cost_estimate=pl.CostEstimate(flops=200 * 10**9, bytes_accessed=10 * 10**6, transcendentals=10**6),
        name="word_attention_backward",
    )(char_counts, *kept, gain, project, *weights)


def call_b1(turns, gw, gain, up, down, kepts, keptm, kepti, f0, f1, first):
    v = pltpu.VMEM
    return pl.pallas_call(
        kernel_b1,
        out_shape=(v((TURNS, CD, WIDE), LOW), shape((CD, CFF), LOW), shape((8, CD), F32), v((8, F_ROWS, 256), LOW)),
        in_specs=[SCALARS] + [INSIDE] * 4 + [ANYWHERE] * 2 + [INSIDE] * 2 + [ANYWHERE] + [INSIDE] * 2,
        out_specs=(INSIDE,) * 4,
        scratch_shapes=[
            v((2, CFF, WIDE), LOW), v((2, CD, WIDE), F32), v((CD, WIDE), LOW),
            v((CD, CFF), F32), v((CD, WIDE), F32), v((CFF, CD), LOW),
            v((8, F_ROWS, 256), LOW),
            pltpu.SemaphoreType.DMA((2, 2)),
            pltpu.SemaphoreType.DMA((1,)),
        ],
        compiler_params=params(18),
        cost_estimate=pl.CostEstimate(flops=200 * 10**9, bytes_accessed=20 * 10**6, transcendentals=10**6),
        name="character_backward_one",
    )(turns, gw, gain, up, down, *kept_outside(kepts, keptm), kepti, f0, *kept_outside(f1), *first)


def call_b2(turns, wgain1, wgain2, gain2, aup, weights, keptl, first, keptd, kepti, facc, f2, t0, t1):
    v = pltpu.VMEM
    return pl.pallas_call(
        kernel_b2,
        out_shape=(
            v((SHARES, C_ROWS, 128), LOW), v((SHARES, C_ROWS, 128), LOW), v((4, F_ROWS, 256), LOW), v((4, T_ROWS, 256), LOW)
        ),
        in_specs=[SCALARS] + [INSIDE] * 9 + [ANYWHERE] + [INSIDE] * 4 + [ANYWHERE, INSIDE, ANYWHERE],
        out_specs=(INSIDE,) * 4,
        scratch_shapes=[
            v((2, KEPT_LOW, WIDE), LOW), v((CD, WIDE), LOW),
            v((CHAR_HEADS * SPAN, WIDE), LOW),
            v((CD, 3 * CD), LOW),
            v((CD, 3 * CD), F32), v((CD, CD), F32), v((CVOC, CD), F32), v((CD, WIDE), F32),
            v((4, F_ROWS, 256), LOW), v((4, T_ROWS, 256), LOW),
            pltpu.SemaphoreType.DMA((3, 2)),
            pltpu.SemaphoreType.DMA((2,)),
        ],
        compiler_params=params(24),
        cost_estimate=pl.CostEstimate(flops=200 * 10**9, bytes_accessed=40 * 10**6, transcendentals=10**6),
        name="character_backward_two",
    )(turns, wgain1, wgain2, gain2, aup, *weights, *kept_outside(keptl), first, keptd, kepti, facc, *kept_outside(f2), t0, *kept_outside(t1))


def call_add(kernel, name, outs, parts, specs, scratch):
    v = pltpu.VMEM
    return pl.pallas_call(
        kernel,
        out_shape=tuple(v(s, LOW) for s in outs),
        in_specs=specs,
        out_specs=(INSIDE,) * len(outs),
        scratch_shapes=[v(s, LOW) for s in scratch] + [pltpu.SemaphoreType.DMA((4,))],
        compiler_params=params(12),
        name=name,
    )(*parts)


def add_one(f0, f1):
    half = (8, F_ROWS, 256)
    return call_add(kernel_add_one, "add_one", (half,), (f0, *kept_outside(f1)), [INSIDE, ANYWHERE], (half,))[0]


def add_words(t0, t1):
    ts = (4, T_ROWS, 256)
    return call_add(
        kernel_add_words, "add_words", (ts, ts, ts), (t0, *kept_outside(t1)), [INSIDE, ANYWHERE], ((3,) + ts,)
    )


def add_two(facc, f2):
    fs = (4, F_ROWS, 256)
    return call_add(kernel_add_two, "add_two", (fs,), (facc, *kept_outside(f2)), [INSIDE, ANYWHERE], (fs,))[0]


def add_three(facc, f3, tacc, tgot):
    fs, ts = (2, F_ROWS, 256), (2, T_ROWS, 256)
    return call_add(
        kernel_add_three, "add_three", (fs, fs, ts, ts), (facc, *kept_outside(f3), tacc, *kept_outside(*tgot)),
        [INSIDE, ANYWHERE] * 2 + [ANYWHERE] * 2, ((4, F_ROWS, 256), (3, 4, T_ROWS, 256)),
    )


def call_f(words, c, outk, outg):
    v = pltpu.VMEM
    outs = ((CVOC, CD), (CD,), (CD, CD), (CD, CD), (CD, CD), (CD, CD), (CD,), (CD, CFF), (CFF, CD), (CD, WD),
            (WD,), (WD, WD), (WD, WD), (WD, WD), (WD, WD), (WD,), (WD, WFF), (WFF, WD))
    outs = [(s[0] // SHARES,) + tuple(n // 2 for n in s[1:]) for s in outs]
    return pl.pallas_call(
        kernel_f,
        out_shape=(shape((2, 1, WORDS, WD // 2), LOW),) + tuple(shape(s, F32) for s in outs),
        in_specs=[INSIDE] * 15,
        out_specs=(INSIDE,) * 19,
        compiler_params=params(8),
        name="finish",
    )(*words, *c, outk, outg)


def flip(value, axis, bits):
    count = lax.axis_size(axis)
    return lax.ppermute(value, axis, [(i, i ^ bits) for i in range(count)])


def flip_both(value, first, second):
    pairs = [(i, i ^ first) for i in range(SHARES)] + [(SHARES + i, SHARES + (i ^ second)) for i in range(SHARES)]
    return lax.ppermute(value, ("phase", "dp"), pairs)


def pick(value, index):
    return lax.dynamic_index_in_dim(value, index, 0, keepdims=False)


def plus(*parts):
    total = parts[0].astype(F32)
    for part in parts[1:]:
        total = total + part.astype(F32)
    return total.astype(LOW)


def across(value, side):
    return flip_both(value, *((1, 2), (2, 1), (4, 4), (8, 8))[side])


def half(bit, *parts):
    return plus(*(lax.dynamic_slice_in_dim(part, bit * (part.shape[0] // 2), part.shape[0] // 2, 0) for part in parts))


def after(value, *others):
    return lax.optimization_barrier((value,) + others)[0]


def together(*values):
    return lax.optimization_barrier(values)


def body(
    char_ids, char_counts, segment_ids, out_cotangent,
    char_table, char_gain_one, char_query, char_key, char_value, char_output, char_gain_two, char_up, char_down,
    char_project,
    word_gain_one, word_query, word_key, word_value, word_output, word_gain_two, word_up, word_down,
):
    keptl, kepts, keptm, kepti, turns, fkeep, fsend, outk, outs, wgain2, flow, fslope, fmid, *words = call_a(
        char_counts, char_ids, segment_ids, out_cotangent,
        (char_table, char_gain_one, char_query, char_key, char_value, char_output, char_gain_two, char_up, char_down,
         char_project,
         word_gain_one, word_query, word_key, word_value, word_output, word_gain_two, word_up, word_down),
    )
    fgot = flip(fsend, "phase", 1)
    outg = flip(outs, "phase", 1)
    gw, tkeep, tsend, wgain1 = call_a2(
        char_counts, words, word_gain_one, char_project, (word_query, word_key, word_value, word_output)
    )
    one = (char_gain_two, char_up, char_down, kepts, keptm, kepti)
    two = (char_gain_one, char_query, char_key, char_value, char_output)
    if lax.axis_size("dp") != SHARES:
        keptd, aup, gain2, facc = call_b1(turns, gw, *one, fkeep, fgot, (fslope, fmid))
        tgot = flip(tsend, "phase", 1)
        ckeep, csend, _, _ = call_b2(turns, wgain1, wgain2, gain2, aup, two, keptl, flow, keptd, kepti, facc, facc, tkeep, tgot)
        return general_sums(outk, outg, (fkeep, fgot), (tkeep, tgot), (ckeep, flip(csend, "phase", 1)))
    gw, tsend, fgot, outg = together(gw, tsend, fgot, outg)
    gw, fsend = together(gw, add_one(fkeep, fgot))
    f2, tgot = across(fsend, 0), flip(tsend, "phase", 1)
    keptd, aup, gain2, facc = call_b1(turns, gw, *one, fkeep, fgot, (fslope, fmid))
    keptd, tgot = together(keptd, tgot)
    tsends = add_words(tkeep, tgot)
    tparts = [flip(send, "dp", k) for k, send in enumerate(tsends, 1)]
    f2 = after(f2, *tsends)
    fsend = add_two(facc, f2)
    keptd, fsend = together(keptd, fsend)
    f3 = across(fsend, 2)
    ckeep, csend, facc, tacc = call_b2(
        turns, wgain1, wgain2, gain2, aup, two, keptl, flow, keptd, kepti, facc, f2, tkeep, tgot
    )
    ckeep, csend, facc, f3, *tparts = together(ckeep, csend, facc, f3, *tparts)
    _, _, low, high = own_bits()
    cphase = flip(csend, "phase", 1)
    fsend, facc, tsend, tacc = add_three(facc, f3, tacc, tparts)
    f4, t3 = across(fsend, 1), across(tsend, 2)
    dp = lax.axis_index("dp")
    plane, line = lax.rem(dp, 4), lax.div(dp, 4)
    c = [ckeep.reshape(4, 4, C_ROWS, 128), cphase.reshape(4, 4, C_ROWS, 128)]
    sends = [plus(*(pick(part, lax.bitwise_xor(plane, k)) for part in c)) for k in range(1, 4)]
    cgot = [flip(send, "dp", k) for k, send in enumerate(sends, 1)]
    f4, t3 = after(f4, *sends), after(t3, *sends)
    last = jnp.concatenate([pick(half(1 - high, facc, f4), 0), pick(half(1 - high, tacc, t3), 0)], axis=0)
    last = across(last, 3)
    c = [pick(part, plane) for part in c] + cgot
    sends = [plus(*(pick(part, lax.bitwise_xor(line, k)) for part in c)) for k in range(1, 4)]
    cline = [flip(send, "dp", 4 * k) for k, send in enumerate(sends, 1)]
    return call_f((facc, f4, tacc, t3, last), (ckeep, cphase, *cgot, *cline), outk, outg)


def general_sums(outk, outg, fs, ts, cs):
    phase = lax.axis_index("phase")
    first = phase == 0
    outs = jnp.stack([jnp.where(first, outk, outg), jnp.where(first, outg, outk)])[:, None]
    def order(places):
        plain, swapped = (jnp.asarray([places(d, core) for d in range(SHARES)]) for core in range(2))
        return jnp.where(first, plain, swapped)

    def natural(pair, order):
        return jnp.take(pair[0].astype(F32) + pair[1].astype(F32), order, axis=0)

    f, t, c = natural(fs, order(feed_order)), natural(ts, order(word_order)), natural(cs, jnp.asarray([plane_first(d) for d in range(SHARES)]))

    def whole(rows):
        return rows.reshape(-1, rows.shape[-1])

    def wide(rows, pieces):
        n = rows.shape[1] // pieces
        return whole(rows.reshape(SHARES, pieces, n, rows.shape[-1]).transpose(0, 2, 1, 3).reshape(SHARES, n, -1))

    cdown = t[:, T_CDOWN:T_CDOWN + 32]
    cdown = jnp.concatenate([cdown[..., :128], cdown[..., 128:]], axis=1)
    parts = (
        whole(c[:, C_TABLE:C_TABLE + 16]), c[:, C_GAIN, :16].reshape(-1),
        whole(c[:, C_Q:C_Q + 16]), whole(c[:, C_K:C_K + 16]), whole(c[:, C_V:C_V + 16]), whole(c[:, C_O:C_O + 16]),
        c[:, C_GAIN + 1, :16].reshape(-1),
        wide(c[:, C_UP:C_UP + 64], 4), whole(cdown), whole(t[:, T_PROJ:T_PROJ + 16]),
        c[:, C_GAIN + 2, :32].reshape(-1),
        whole(t[:, T_Q:T_Q + 32]), whole(t[:, T_K:T_K + 32]), whole(t[:, T_V:T_V + 32]), whole(t[:, T_O:T_O + 32]),
        c[:, C_GAIN + 3, :32].reshape(-1),
        wide(f[:, F_UP:F_UP + 128], 4), whole(f[:, F_DOWN:F_DOWN + 128]),
    )
    return (outs,) + tuple(lax.psum_scatter(p, "dp", scatter_dimension=0, tiled=True) for p in parts)


def solution(mesh):
    rows = P(None, "dp", None)
    both = P("dp", "phase")
    one = P("dp")
    return jax.shard_map(
        body,
        mesh=mesh,
        in_specs=(rows, rows, rows, P(None, "dp", None, None)) + (P(),) * 18,
        out_specs=(
            P(None, "dp", None, "phase"),
            both, one, both, both, both, both, one, both, both, both,
            one, both, both, both, both, one, both, both,
        ),
        check_vma=False,
    )
```
